32 devices in a mesh: dp: 16 (over z, y, core), mp: 2 (over x).
Axes of the slice: x: 2, y: 2, z: 4, core: 2. Of those that a mesh axis runs over, the one named last changes fastest.
Arguments:
- inputs: bfloat16 [16384, 768], P('dp'), may hold values from -6 to 6
- segment_ids: int32 [16384], P('dp'), may hold values from 0 to 16383, as said below
- pair_index: int32 [256], P('dp'), may hold values from 0 to 255, as said below
- w_qkv: bfloat16 [3, 768, 768], P(None, None, 'mp'), may hold values from -0.21875 to 0.21875
- bias_qv: float32 [2, 768], P(None, 'mp'), may hold values from -1.8 to 1.8
- w_out: bfloat16 [768, 768], P('mp'), may hold values from -0.4375 to 0.4375
- w_in: bfloat16 [768, 3072], P(None, 'mp'), may hold values from -0.21875 to 0.21875
- bias_in: float32 [3072], P('mp'), may hold values from -1.8 to 1.8
- w_back: bfloat16 [3072, 768], P('mp'), may hold values from -0.109375 to 0.109375
- w_pool: bfloat16 [768, 768], replicated, may hold values from -0.21875 to 0.21875
- norm_gains: float32 [2, 768], replicated, may hold values from 0.5 to 1.5
- shifts: float32 [5, 768], replicated, may hold values from -1.8 to 1.8
- logit_scale: float32 [1], replicated, may hold values from 30 to 60
- out_grad: bfloat16 [16384, 768], P('dp'), may hold values from -6 to 6
Outputs:
- block_out: bfloat16 [16384, 768], P('dp')
- loss_value: float32 [1], replicated
- grad_inputs: float32 [16384, 768], P('dp')
- grad_qkv: float32 [3, 768, 768], P(None, 'dp', 'mp')
- grad_bias_qv: float32 [2, 768], P(None, ('mp', 'dp'))
- grad_out: float32 [768, 768], P(('mp', 'dp'))
- grad_in: float32 [768, 3072], P('dp', 'mp')
- grad_bias_in: float32 [3072], P(('mp', 'dp'))
- grad_back: float32 [3072, 768], P(('mp', 'dp'))
- grad_pool: float32 [768, 768], P('dp')
- grad_gains: float32 [2, 768], P(None, 'dp')
- grad_shifts: float32 [4, 768], P(None, 'dp')
- grad_pool_bias: float32 [768], P('dp')
- grad_scale: float32 [1], replicated
- new_scale: float32 [1], replicated
The draws below stay inside these ranges and needn't reach their ends.
Inputs may be any that keep to these rules, and one draw needn't show every extreme that they name: segment_ids never fall; the first token of each aligned block of 64 tokens starts a new segment, and a block holds one to three segments; the last token's id is 16383. pair_index pairs the 256 blocks off: pair_index[pair_index[a]] = a and pair_index[a] != a for every block a.
All inputs are finite; a program needn't handle non-finite values.
Results may differ from the reference program's by a relative error of at most 0.012.
The reference program's roundings to bfloat16 on the way count: a program that leaves them out, or rounds other values in their place, can miss the bound.
Values may be sent and summed in bfloat16 or wider, within the bound.
A program may use at most 128 MiB of HBM per device.

```python
import math
from functools import partial
import jax
import jax.numpy as jnp
from jax import lax

D = 768
HEADS = 12
HEAD_DIM = 64
FF = 3072
SEG_LEN = 64
TOKENS = 16384
SEGS = 256


def draw_segment_ids(key, part):
    key = jax.random.fold_in(key, 11)
    blocks = TOKENS // SEG_LEN
    cut_points = jax.random.randint(key, (blocks, 2), 1, SEG_LEN).astype(jnp.int32)
    cut_points = cut_points.at[blocks - 1, 1].set(SEG_LEN - 1)
    within = jnp.arange(SEG_LEN, dtype=jnp.int32)
    first_cut = jnp.where(cut_points[:, :1] <= within[None, :], cut_points[:, :1], 0)
    second_cut = jnp.where(cut_points[:, 1:] <= within[None, :], cut_points[:, 1:], 0)
    block_base = jnp.arange(blocks, dtype=jnp.int32)[:, None] * SEG_LEN
    return (block_base + jnp.maximum(first_cut, second_cut)).reshape(TOKENS).astype(jnp.int32)


def draw_pair_index(key, part):
    key = jax.random.fold_in(key, 23)
    shuffled = jax.random.permutation(key, SEGS).astype(jnp.int32)
    even_side = shuffled[0::2]
    odd_side = shuffled[1::2]
    paired = jnp.zeros((SEGS,), jnp.int32).at[even_side].set(odd_side)
    return paired.at[odd_side].set(even_side).astype(jnp.int32)


def steps_of(stream_key, dims, cuts, smallest, largest):
    factor_of, own = 1.0, jax.random.fold_in(stream_key, 6)
    for dim, parts in cuts:
        steps = jnp.exp(jax.random.uniform(jax.random.fold_in(own, dim), (parts,), jnp.float32, smallest / len(cuts), largest / len(cuts)))
        factor_of = factor_of * jnp.repeat(steps, dims[dim] // parts).reshape([-1 if axis == dim else 1 for axis in range(len(dims))])
    return factor_of


def gaussian(stream_key, dims, spread, bound, shards=(), kind=jnp.bfloat16):
    entries = spread * jax.random.normal(stream_key, dims, jnp.float32)
    if shards:
        entries = entries * steps_of(stream_key, dims, shards, -0.22, 0.18)
    return jnp.clip(entries, -bound, bound).astype(kind)


def setup_inputs(seed: int = 0) -> dict:
    seeds = jax.random.split(jax.random.key(seed), 15)
    return {
        "inputs": gaussian(seeds[0], (TOKENS, D), 1.0, 6.0, ((0, 16),)),
        "segment_ids": draw_segment_ids(jax.random.fold_in(seeds[14], 71), 0),
        "pair_index": draw_pair_index(jax.random.fold_in(seeds[14], 71), 0),
        "w_qkv": gaussian(seeds[3], (3, D, D), D ** -0.5, 0.21875, ((2, 2),)),
        "bias_qv": gaussian(seeds[4], (2, D), 0.3, 1.8, ((1, 2),), jnp.float32),
        "w_out": gaussian(seeds[5], (D, D), (D // 4) ** -0.5, 0.4375, ((0, 2),)),
        "w_in": gaussian(seeds[6], (D, FF), D ** -0.5, 0.21875, ((1, 2),)),
        "bias_in": gaussian(seeds[7], (FF,), 0.3, 1.8, ((0, 2),), jnp.float32),
        "w_back": gaussian(seeds[8], (FF, D), FF ** -0.5, 0.109375, ((0, 2),)),
        "w_pool": gaussian(seeds[9], (D, D), D ** -0.5, 0.21875),
        "norm_gains": jnp.clip(1.0 + 0.1 * jax.random.normal(seeds[10], (2, D), jnp.float32), 0.5, 1.5),
        "shifts": gaussian(seeds[11], (5, D), 0.3, 1.8, (), jnp.float32),
        "logit_scale": jnp.clip(jax.random.uniform(seeds[12], (1,), jnp.float32, 30.0, 60.0), 30.0, 60.0),
        "out_grad": gaussian(seeds[13], (TOKENS, D), 1.0, 6.0, ((0, 16),)),
    }


epsilon = 1e-12
margin = 0.3
step_rate = 0.1
masked_out = -1e+30
highest = lax.Precision.HIGHEST

@jax.custom_vjp
def low(v):
    return lax.optimization_barrier(v.astype(jnp.bfloat16)).astype(jnp.float32)

@jax.custom_vjp
def low_back(v):
    return v

def low_keep(v):
    return (low(v), None)

def low_pass(kept, grad):
    return (grad,)

def back_keep(v):
    return (v, None)

def back_low(kept, grad):
    return (low(grad),)
low.defvjp(low_keep, low_pass)
low_back.defvjp(back_keep, back_low)

def layer_norm(values, gain, shift):
    row_mean = lax.optimization_barrier(jnp.mean(values, axis=-1, keepdims=True))
    centred = values - row_mean
    row_var = lax.optimization_barrier(jnp.mean(centred * centred, axis=-1, keepdims=True))
    return centred * lax.rsqrt(row_var + epsilon) * gain + shift

def block_rows(params, rows_in, seg_rows):
    w_qkv, bias_qv, w_out, w_in, bias_in, w_back, norm_gains, shifts = params
    count = rows_in.shape[0]
    blocks = count // SEG_LEN
    rounded = low(rows_in)
    queries = low(low_back(jnp.dot(rounded, w_qkv[0], precision=highest) + bias_qv[0]))
    key_rows = low(low_back(jnp.dot(rounded, w_qkv[1], precision=highest)))
    values = low(low_back(jnp.dot(rounded, w_qkv[2], precision=highest) + bias_qv[1]))
    shape_four = (blocks, SEG_LEN, HEADS, HEAD_DIM)
    scores = jnp.einsum('bqhd,bkhd->bhqk', queries.reshape(shape_four), key_rows.reshape(shape_four), precision=highest) * HEAD_DIM ** (-0.5)
    seg_blocks = seg_rows.reshape(blocks, SEG_LEN)
    same_seg = seg_blocks[:, None, :, None] == seg_blocks[:, None, None, :]
    scores = low_back(jnp.where(same_seg, scores, masked_out))
    row_max = lax.optimization_barrier(jnp.max(scores, axis=-1, keepdims=True))
    shifted = jnp.exp(scores - row_max)
    probs = low(shifted / lax.optimization_barrier(jnp.sum(shifted, axis=-1, keepdims=True)))
    context = jnp.einsum('bhqk,bkhd->bqhd', probs, values.reshape(shape_four), precision=highest).reshape(count, D)
    context = low(low_back(context))
    attended = low_back(jnp.dot(context, w_out, precision=highest) + shifts[0])
    hidden_one = layer_norm(rows_in + attended, norm_gains[0], shifts[1])
    inner = low_back(jnp.dot(low(hidden_one), w_in, precision=highest) + bias_in)
    activated = low(jax.nn.gelu(inner, approximate=False))
    branch = low_back(jnp.dot(activated, w_back, precision=highest) + shifts[2])
    return layer_norm(hidden_one + branch, norm_gains[1], shifts[3])

def log_sum_exp(logits, axis_index):
    top_value = lax.optimization_barrier(jnp.max(logits, axis=axis_index, keepdims=True))
    summed = lax.optimization_barrier(jnp.sum(jnp.exp(logits - top_value), axis=axis_index, keepdims=True))
    return jnp.squeeze(top_value + jnp.log(summed), axis=axis_index)

def pair_loss(firsts, pair_index, w_pool, bias_pool, logit_scale):
    seg_count = firsts.shape[0]
    pooled = jnp.tanh(low_back(jnp.dot(low(firsts), w_pool, precision=highest) + bias_pool))
    unit_rows = low(pooled * lax.rsqrt(lax.optimization_barrier(jnp.sum(pooled * pooled, axis=-1, keepdims=True)) + 1e-06))
    cosine = low_back(jnp.dot(unit_rows, unit_rows.T, precision=highest))
    seg_order = jnp.arange(seg_count, dtype=jnp.int32)
    self_pair = seg_order[:, None] == seg_order[None, :]
    positive = seg_order[None, :] == pair_index[:, None]
    logits = logit_scale[0] * (cosine - margin * positive.astype(jnp.float32))
    logits = jnp.where(self_pair, masked_out, logits)
    row_lse = log_sum_exp(logits, 1)
    col_lse = log_sum_exp(logits, 0)
    pos_sum = jnp.sum(jnp.where(positive, logits, 0.0))
    return (jnp.sum(row_lse) + jnp.sum(col_lse) - 2.0 * pos_sum) / (2.0 * seg_count)

def objective(inputs_f, w_qkv, bias_qv, w_out, w_in, bias_in, w_back, w_pool, norm_gains, shifts, logit_scale, segment_ids, pair_index, grad_rows):
    total_rows = inputs_f.shape[0]
    span = math.gcd(total_rows, 4096)
    steps = total_rows // span
    params = (w_qkv, bias_qv, w_out, w_in, bias_in, w_back, norm_gains, shifts)
    run_rows = jax.checkpoint(partial(block_rows, params))

    def advance(running, item):
        rows_in, seg_rows, cot_rows = item
        hidden_two = run_rows(rows_in, seg_rows)
        return (running + jnp.sum(hidden_two * cot_rows), hidden_two)
    dotted, hidden_all = lax.scan(advance, jnp.zeros((), jnp.float32), (inputs_f.reshape(steps, span, D), segment_ids.reshape(steps, span), grad_rows.reshape(steps, span, D)))
    hidden_all = hidden_all.reshape(total_rows, D)
    firsts = hidden_all.reshape(total_rows // SEG_LEN, SEG_LEN, D)[:, 0]
    loss_value = pair_loss(firsts, pair_index, w_pool, shifts[4], logit_scale)
    return (dotted + loss_value, (hidden_all, loss_value))

def reference(inputs, segment_ids, pair_index, w_qkv, bias_qv, w_out, w_in, bias_in, w_back, w_pool, norm_gains, shifts, logit_scale, out_grad):
    grad_rows = out_grad.astype(jnp.float32)

    def wrapped(inputs_f, w_qkv_f, bias_qv_f, w_out_f, w_in_f, bias_in_f, w_back_f, w_pool_f, gains_f, shifts_f, scale_f):
        return objective(inputs_f, w_qkv_f, bias_qv_f, w_out_f, w_in_f, bias_in_f, w_back_f, w_pool_f, gains_f, shifts_f, scale_f, segment_ids, pair_index, grad_rows)
    total, pullback, extras = jax.vjp(wrapped, inputs.astype(jnp.float32), w_qkv.astype(jnp.float32), bias_qv.astype(jnp.float32), w_out.astype(jnp.float32), w_in.astype(jnp.float32), bias_in.astype(jnp.float32), w_back.astype(jnp.float32), w_pool.astype(jnp.float32), norm_gains.astype(jnp.float32), shifts.astype(jnp.float32), logit_scale.astype(jnp.float32), has_aux=True)
    hidden_all, loss_value = extras
    grads = pullback(jnp.ones((), jnp.float32))
    grad_scale = grads[10]
    new_scale = logit_scale - step_rate * grad_scale
    return (hidden_all.astype(jnp.bfloat16), jnp.reshape(loss_value, (1,)), grads[0], grads[1], grads[2], grads[3], grads[4], grads[5], grads[6], grads[7], grads[8], grads[9][:4], grads[9][4], grad_scale, new_scale)
```

```python
from functools import partial

import jax
import jax.numpy as jnp
from jax import lax
from jax.experimental import pallas as pl
from jax.experimental.pallas import tpu as pltpu
from jax.sharding import PartitionSpec as P

HEAD_DIM = 64
SEG_LEN = 64
PAIR = 2 * HEAD_DIM
GROUP = 128

epsilon = 1e-12
margin = 0.3
step_rate = 0.1
masked_out = -1e30
f32 = jnp.float32
bf16 = jnp.bfloat16

NT = (((1,), (1,)), ((), ()))
TN = (((0,), (0,)), ((), ()))


def mm(a, b):
    return jnp.dot(a, b, preferred_element_type=f32)


def mm_nt(a, b):
    return lax.dot_general(a, b, NT, preferred_element_type=f32)


def mm_tn(a, b):
    return lax.dot_general(a, b, TN, preferred_element_type=f32)


def params(mib=40):
    return pltpu.CompilerParams(vmem_limit_bytes=mib * 1024 * 1024)


def cost(flops, moved):
    return pl.CostEstimate(flops=int(flops), bytes_accessed=int(moved), transcendentals=0)


def lane_masks():
    lane = lax.broadcasted_iota(jnp.int32, (1, PAIR), 1)
    first = (lane < HEAD_DIM).astype(f32)
    return first, 1.0 - first


def two_heads(rows):
    first, second = lane_masks()
    return jnp.concatenate([rows * first.astype(bf16), rows * second.astype(bf16)], axis=0)


def join_heads(both):
    first, second = lane_masks()
    half = both.shape[0] // 2
    return both[:half] * first + both[half:] * second


def pair_probs(q_two, k_pair, same):
    scores = mm_nt(q_two, k_pair) * (HEAD_DIM ** (-0.5))
    scores = jnp.where(same, scores, masked_out)
    shifted = jnp.exp(scores - jnp.max(scores, axis=1, keepdims=True))
    return shifted / jnp.sum(shifted, axis=1, keepdims=True)


def same_segment(seg_col, seg_row, rows):
    own = seg_col[rows, :]
    other = seg_row[:, rows]
    one = own == other
    return jnp.concatenate([one, one], axis=0)


def attention_kernel(x_ref, w_ref, b_ref, segc_ref, segr_ref, q_ref, k_ref, v_ref, c_ref):
    x = x_ref[...]
    q_ref[...] = (mm(x, w_ref[0]) + b_ref[0:1]).astype(bf16)
    k_ref[...] = mm(x, w_ref[1]).astype(bf16)
    v_ref[...] = (mm(x, w_ref[2]) + b_ref[1:2]).astype(bf16)
    for group in range(x.shape[0] // GROUP):
        rows = slice(group * GROUP, (group + 1) * GROUP)
        same = same_segment(segc_ref, segr_ref, rows)
        for pair in range(q_ref.shape[1] // PAIR):
            cols = slice(pair * PAIR, (pair + 1) * PAIR)
            probs = pair_probs(two_heads(q_ref[rows, cols]), k_ref[rows, cols], same)
            c_ref[rows, cols] = join_heads(mm(probs.astype(bf16), v_ref[rows, cols])).astype(bf16)


def attention_half(x, w, b, segc, segr):
    rows, cols = x.shape[0], w.shape[2]
    out = jax.ShapeDtypeStruct((rows, cols), bf16)
    return pl.pallas_call(
        attention_kernel,
        out_shape=(out,) * 4,
        compiler_params=params(),
        cost_estimate=cost(2 * rows * 768 * cols * 3 * 2, 6 * rows * cols * 2),
        name="attention",
    )(x, w, b, segc, segr)


def norm_rows(values):
    row_mean = jnp.mean(values, axis=-1, keepdims=True)
    centred = values - row_mean
    inv_std = lax.rsqrt(jnp.mean(centred * centred, axis=-1, keepdims=True) + epsilon)
    return centred * inv_std, inv_std


def norm_back(grad, normed, inv_std, gain):
    scaled = grad * gain
    return inv_std * (
        scaled
        - jnp.mean(scaled, axis=-1, keepdims=True)
        - normed * jnp.mean(scaled * normed, axis=-1, keepdims=True)
    )


def first_norm_kernel(co_ref, cp_ref, wo_ref, wp_ref, x_ref, g_ref, s_ref, n_ref, inv_ref, low_ref):
    for at in range(0, x_ref.shape[0], 128):
        rows = slice(at, at + 128)
        attended = mm(co_ref[rows], wo_ref[...]) + mm(cp_ref[rows], wp_ref[...]) + s_ref[0:1]
        normed, inv_std = norm_rows(x_ref[rows].astype(f32) + attended)
        n_ref[rows] = normed
        inv_ref[rows] = inv_std
        low_ref[rows] = (normed * g_ref[0:1] + s_ref[1:2]).astype(bf16)


def first_norm(ctx_o, ctx_p, wo, wp, x, gains, shifts):
    rows, width = x.shape
    return pl.pallas_call(
        first_norm_kernel,
        out_shape=(
            jax.ShapeDtypeStruct((rows, width), f32),
            jax.ShapeDtypeStruct((rows, 1), f32),
            jax.ShapeDtypeStruct((rows, width), bf16),
        ),
        compiler_params=params(),
        cost_estimate=cost(2 * rows * width * width, 12 * rows * width),
        name="first_norm",
    )(ctx_o, ctx_p, wo, wp, x, gains, shifts)


def inner_kernel(h_ref, w_ref, b_ref, act_ref, slope_ref):
    for at in range(0, h_ref.shape[0], 128):
        rows = slice(at, at + 128)
        inner = mm(h_ref[rows], w_ref[...]) + b_ref[...]
        cumulative = 0.5 * (1.0 + lax.erf(inner * 0.7071067811865476))
        density = jnp.exp(-0.5 * inner * inner) * 0.3989422804014327
        act_ref[rows] = (inner * cumulative).astype(bf16)
        slope_ref[rows] = (cumulative + inner * density).astype(bf16)


def inner_half(low, w, b):
    rows, width = low.shape
    units = w.shape[1]
    tile = 256
    out = jax.ShapeDtypeStruct((rows, units), bf16)
    return pl.pallas_call(
        inner_kernel,
        grid=(units // tile,),
        in_specs=[
            pl.BlockSpec((rows, width), lambda n: (0, 0)),
            pl.BlockSpec((width, tile), lambda n: (0, n)),
            pl.BlockSpec((1, tile), lambda n: (0, n)),
        ],
        out_specs=[pl.BlockSpec((rows, tile), lambda n: (0, n))] * 2,
        out_shape=(out, out),
        compiler_params=params(),
        cost_estimate=cost(4 * rows * width * units, 8 * rows * units),
        name="inner",
    )(low, w, b)


def branch_kernel(act_ref, w_ref, out_ref):
    for at in range(0, act_ref.shape[0], 128):
        rows = slice(at, at + 128)
        out_ref[rows] = mm(act_ref[rows], w_ref[...])


def branch_half(act, w):
    rows, units = act.shape
    width = w.shape[1]
    return pl.pallas_call(
        branch_kernel,
        out_shape=jax.ShapeDtypeStruct((rows, width), f32),
        compiler_params=params(),
        cost_estimate=cost(2 * rows * width * units, 4 * rows * units),
        name="branch",
    )(act, w)


def second_norm_kernel(act_ref, w_ref, part_ref, n1_ref, g_ref, s_ref, n_ref, inv_ref, out_ref):
    for at in range(0, act_ref.shape[0], 128):
        rows = slice(at, at + 128)
        branch = mm(act_ref[rows], w_ref[...]) + part_ref[rows] + s_ref[2:3]
        hidden_one = n1_ref[rows] * g_ref[0:1] + s_ref[1:2]
        normed, inv_std = norm_rows(hidden_one + branch)
        n_ref[rows] = normed
        inv_ref[rows] = inv_std
        out_ref[rows] = (normed * g_ref[1:2] + s_ref[3:4]).astype(bf16)


def second_norm(act, w, part, normed_one, gains, shifts):
    rows, units = act.shape
    width = w.shape[1]
    return pl.pallas_call(
        second_norm_kernel,
        out_shape=(
            jax.ShapeDtypeStruct((rows, width), f32),
            jax.ShapeDtypeStruct((rows, 1), f32),
            jax.ShapeDtypeStruct((rows, width), bf16),
        ),
        compiler_params=params(),
        cost_estimate=cost(2 * rows * width * units, 4 * rows * units),
        name="second_norm",
    )(act, w, part, normed_one, gains, shifts)


def loss_kernel(
    pos_ref, rel_ref, w_ref, bias_ref, scale_ref,
    loss_ref, gscale_ref, pre_ref, bias_grad_ref, first_grad_ref, firsts_out_ref,
    all_ref, pooled_ref, len_ref, unit_ref, lse_col_ref, lse_row_ref, pre_f_ref,
):
    count, width = pooled_ref.shape
    slots = count // 8
    chunk = min(count, 256)
    steps = count // chunk
    mine = pos_ref[0]
    here = pos_ref[1]
    scale = scale_ref[0]

    @pl.loop(0, slots)
    def _(slot):
        source = pl.multiple_of(slot * 8, 8)
        target = pl.multiple_of(jnp.bitwise_xor(slot, mine) * 8, 8)
        all_ref[pl.ds(target, 8), :] = rel_ref[pl.ds(source, 8), :].astype(f32)

    def pool(at):
        firsts = all_ref[pl.ds(at, chunk), :width].astype(bf16)
        firsts_out_ref[pl.ds(at, chunk), :] = firsts
        pooled = jnp.tanh(mm(firsts, w_ref[...]) + bias_ref[...])
        inv_len = lax.rsqrt(jnp.sum(pooled * pooled, axis=-1, keepdims=True) + 1e-06)
        pooled_ref[pl.ds(at, chunk), :] = pooled
        len_ref[pl.ds(at, chunk), :] = inv_len
        unit_ref[pl.ds(at, chunk), :] = (pooled * inv_len).astype(bf16)

    def positions(at):
        own = at + lax.broadcasted_iota(jnp.int32, (chunk, count), 0)
        other = lax.broadcasted_iota(jnp.int32, (chunk, count), 1)
        paired = all_ref[pl.ds(at, chunk), width:width + 1] * 64.0 + all_ref[pl.ds(at, chunk), width + 1:width + 2]
        positive = paired.astype(jnp.int32) == other
        return own == other, positive

    def logits_of(at):
        cosine = mm_nt(unit_ref[pl.ds(at, chunk), :], unit_ref[...])
        own, positive = positions(at)
        shifted = cosine - jnp.where(positive, margin, 0.0)
        return shifted, own, positive

    def first_pass(at, run):
        shifted, own, positive = logits_of(at)
        logits = jnp.where(own, masked_out, scale * shifted)
        top = jnp.max(logits, axis=1, keepdims=True)
        lse = top + jnp.log(jnp.sum(jnp.exp(logits - top), axis=1, keepdims=True))
        lse_col_ref[pl.ds(at, chunk), :] = lse
        eye = lax.broadcasted_iota(jnp.int32, (chunk, chunk), 0) == lax.broadcasted_iota(
            jnp.int32, (chunk, chunk), 1
        )
        lse_row_ref[:, pl.ds(at, chunk)] = jnp.sum(jnp.where(eye, lse, 0.0), axis=0, keepdims=True)
        return run + jnp.sum(lse) - jnp.sum(jnp.where(positive, logits, 0.0))

    def second_pass(at, run):
        run_scale, run_bias = run
        shifted, own, positive = logits_of(at)
        logits = scale * shifted
        factor = 1.0 / (2.0 * count)
        grad = (
            jnp.exp(logits - lse_col_ref[pl.ds(at, chunk), :])
            + jnp.exp(logits - lse_row_ref[...])
            - jnp.where(positive, 2.0, 0.0)
        ) * factor
        grad = jnp.where(own, 0.0, grad)
        run_scale = run_scale + jnp.sum(grad * shifted)
        unit_grad = 2.0 * mm((scale * grad).astype(bf16), unit_ref[...])
        pooled = pooled_ref[pl.ds(at, chunk), :]
        inv_len = len_ref[pl.ds(at, chunk), :]
        along = jnp.sum(pooled * unit_grad, axis=-1, keepdims=True)
        pooled_grad = inv_len * unit_grad - pooled * (inv_len * inv_len * inv_len) * along
        pre_grad = (pooled_grad * (1.0 - pooled * pooled)).astype(bf16)
        pre_ref[pl.ds(at, chunk), :] = pre_grad
        pre_f_ref[pl.ds(at, chunk), :] = pre_grad.astype(f32)
        return run_scale, run_bias + jnp.sum(pre_grad.astype(f32), axis=0, keepdims=True)

    def each(body, run):
        if steps == 1:
            return body(0, run)
        return lax.fori_loop(0, steps, lambda s, r: body(pl.multiple_of(s * chunk, chunk), r), run)

    each(lambda at, run: (pool(at), run)[1], 0)
    total = each(first_pass, jnp.float32(0.0))
    run_scale, run_bias = each(second_pass, (jnp.float32(0.0), jnp.zeros((1, width), f32)))
    loss_ref[0] = total / count
    gscale_ref[0] = run_scale
    bias_grad_ref[...] = run_bias
    own_rows = pre_f_ref[pl.ds(pl.multiple_of(here * 8, 8), 8), :].astype(bf16)
    first_grad_ref[...] = mm_nt(own_rows, w_ref[...])


def pair_loss(position, rel, w_pool, bias, scale):
    count, wide = rel.shape
    width = w_pool.shape[0]
    smem = pl.BlockSpec(memory_space=pltpu.SMEM)
    vmem = pl.BlockSpec(memory_space=pltpu.VMEM)
    return pl.pallas_call(
        loss_kernel,
        in_specs=[smem, vmem, vmem, vmem, smem],
        out_specs=[smem, smem, vmem, vmem, vmem, vmem],
        out_shape=(
            jax.ShapeDtypeStruct((1,), f32),
            jax.ShapeDtypeStruct((1,), f32),
            jax.ShapeDtypeStruct((count, width), bf16),
            jax.ShapeDtypeStruct((1, width), f32),
            jax.ShapeDtypeStruct((8, width), f32),
            jax.ShapeDtypeStruct((count, width), bf16),
        ),
        scratch_shapes=[
            pltpu.VMEM((count, wide), f32),
            pltpu.VMEM((count, width), f32),
            pltpu.VMEM((count, 1), f32),
            pltpu.VMEM((count, width), bf16),
            pltpu.VMEM((count, 1), f32),
            pltpu.VMEM((1, count), f32),
            pltpu.VMEM((count, width), f32),
        ],
        compiler_params=params(56),
        cost_estimate=cost(2e9, 4e6),
        name="pair_loss",
    )(position, rel, w_pool, bias, scale)


def put_slabs(pos_ref, source, keep_ref, send_ref, lead):
    slab = source.shape[0] // 16
    for place in range(16):
        at = pl.multiple_of(jnp.bitwise_xor(pos_ref[0], place) * slab, slab)
        target = send_ref if place % 2 else keep_ref
        target[lead + (place // 2,)] = source[pl.ds(at, slab), :].astype(bf16)


def second_back_kernel(
    og_ref, fg_ref, n_ref, inv_ref, g_ref, grad_ref, low_ref, sums_ref
):
    rows_all, width = og_ref.shape
    sums_ref[...] = jnp.zeros_like(sums_ref)
    for at in range(0, rows_all, 64):
        rows = slice(at, at + 64)
        block = at // 64
        is_first = lax.broadcasted_iota(jnp.int32, (64, width), 0) == 0
        grad = og_ref[rows].astype(f32) + jnp.where(is_first, fg_ref[block:block + 1], 0.0)
        normed = n_ref[rows]
        value = norm_back(grad, normed, inv_ref[rows], g_ref[1:2])
        low = value.astype(bf16)
        grad_ref[rows] = value
        low_ref[rows] = low
        sums_ref[0:1] += jnp.sum(grad * normed, axis=0, keepdims=True)
        sums_ref[1:2] += jnp.sum(grad, axis=0, keepdims=True)
        sums_ref[2:3] += jnp.sum(low.astype(f32), axis=0, keepdims=True)


def second_back(out_grad, first_grad, normed, inv_std, gains):
    rows, width = out_grad.shape
    return pl.pallas_call(
        second_back_kernel,
        out_shape=(
            jax.ShapeDtypeStruct((rows, width), f32),
            jax.ShapeDtypeStruct((rows, width), bf16),
            jax.ShapeDtypeStruct((8, width), f32),
        ),
        compiler_params=params(),
        cost_estimate=cost(20 * rows * width, 12 * rows * width),
        name="second_back",
    )(out_grad, first_grad, normed, inv_std, gains)


def slab_shape(rows, cols):
    return jax.ShapeDtypeStruct((8, rows // 16, cols), bf16)


def back_weight_kernel(pos_ref, act_ref, branch_ref, keep_ref, send_ref, whole):
    for at in range(0, whole.shape[0], 256):
        rows = slice(at, at + 256)
        whole[rows] = mm_tn(act_ref[:, rows], branch_ref[...])
    put_slabs(pos_ref, whole, keep_ref, send_ref, ())


def back_weight(pos, act, branch):
    rows, units = act.shape
    width = branch.shape[1]
    smem = pl.BlockSpec(memory_space=pltpu.SMEM)
    vmem = pl.BlockSpec(memory_space=pltpu.VMEM)
    return pl.pallas_call(
        back_weight_kernel,
        in_specs=[smem, vmem, vmem],
        out_specs=[vmem, vmem],
        out_shape=(slab_shape(units, width),) * 2,
        scratch_shapes=[pltpu.VMEM((units, width), f32)],
        compiler_params=params(),
        cost_estimate=cost(2 * rows * width * units, 4 * units * width),
        name="back_weight",
    )(pos, act, branch)


def inner_back_kernel(pos_ref, branch_ref, wb_ref, slope_ref, low_ref, wi_ref, part_ref,
                      keep_ref, send_ref, bias_ref, out_ref, grad, whole):
    units = slope_ref.shape[1]
    for at in range(0, units, 256):
        cols = slice(at, at + 256)
        inner_grad = (mm_nt(branch_ref[...], wb_ref[cols]) * slope_ref[:, cols].astype(f32)).astype(bf16)
        grad[:, cols] = inner_grad
        bias_ref[:, cols] = jnp.sum(inner_grad.astype(f32), axis=0, keepdims=True)
        whole[:, cols] = mm_tn(low_ref[...], inner_grad)
    put_slabs(pos_ref, whole, keep_ref, send_ref, ())
    for at in range(0, low_ref.shape[0], 128):
        rows = slice(at, at + 128)
        out_ref[rows] = part_ref[rows] + mm_nt(grad[rows], wi_ref[...])


def inner_back(pos, branch, w_back, slope, low, w_in, part):
    rows, units = slope.shape
    width = low.shape[1]
    smem = pl.BlockSpec(memory_space=pltpu.SMEM)
    vmem = pl.BlockSpec(memory_space=pltpu.VMEM)
    return pl.pallas_call(
        inner_back_kernel,
        in_specs=[smem] + [vmem] * 6,
        out_specs=[vmem] * 4,
        out_shape=(slab_shape(width, units),) * 2
        + (jax.ShapeDtypeStruct((1, units), f32), jax.ShapeDtypeStruct((rows, width), f32)),
        scratch_shapes=[pltpu.VMEM((rows, units), bf16), pltpu.VMEM((width, units), f32)],
        compiler_params=params(),
        cost_estimate=cost(6 * rows * width * units, 4 * units * width),
        name="inner_back",
    )(pos, branch, w_back, slope, low, w_in, part)


def first_back_kernel(pos_ref, grad_ref, n_ref, inv_ref, g_ref, co_ref, cp_ref, wo_ref, wp_ref,
                      one_ref, sums_ref, dco_ref, dcp_ref, keep_ref, send_ref, low, whole):
    width = grad_ref.shape[1]
    sums_ref[...] = jnp.zeros_like(sums_ref)
    for at in range(0, grad_ref.shape[0], 128):
        rows = slice(at, at + 128)
        grad = grad_ref[rows]
        normed = n_ref[rows]
        value = norm_back(grad, normed, inv_ref[rows], g_ref[0:1])
        low_rows = value.astype(bf16)
        one_ref[rows] = value
        low[rows] = low_rows
        dco_ref[rows] = mm_nt(low_rows, wo_ref[...]).astype(bf16)
        dcp_ref[rows] = mm_nt(low_rows, wp_ref[...]).astype(bf16)
        sums_ref[0:1] += jnp.sum(grad * normed, axis=0, keepdims=True)
        sums_ref[1:2] += jnp.sum(grad, axis=0, keepdims=True)
        sums_ref[2:3] += jnp.sum(low_rows.astype(f32), axis=0, keepdims=True)
    for side, ctx_ref in enumerate((co_ref, cp_ref)):
        whole[...] = mm_tn(ctx_ref[...], low[...])
        put_slabs(pos_ref, whole, keep_ref.at[side], send_ref.at[side], ())


def first_back(pos, grad, normed, inv_std, gains, ctx_o, ctx_p, wo, wp):
    rows, width = grad.shape
    cols = ctx_o.shape[1]
    smem = pl.BlockSpec(memory_space=pltpu.SMEM)
    vmem = pl.BlockSpec(memory_space=pltpu.VMEM)
    return pl.pallas_call(
        first_back_kernel,
        in_specs=[smem] + [vmem] * 8,
        out_specs=[vmem] * 6,
        out_shape=(
            jax.ShapeDtypeStruct((rows, width), f32),
            jax.ShapeDtypeStruct((8, width), f32),
            jax.ShapeDtypeStruct((rows, cols), bf16),
            jax.ShapeDtypeStruct((rows, cols), bf16),
        )
        + (jax.ShapeDtypeStruct((2, 8, cols // 16, width), bf16),) * 2,
        scratch_shapes=[pltpu.VMEM((rows, width), bf16), pltpu.VMEM((cols, width), f32)],
        compiler_params=params(),
        cost_estimate=cost(8 * rows * width * cols, 12 * rows * width),
        name="first_back",
    )(pos, grad, normed, inv_std, gains, ctx_o, ctx_p, wo, wp)


def attention_back_kernel(pos_ref, x_ref, w_ref, segc_ref, segr_ref, q_ref, k_ref, v_ref, dc_ref, part_ref,
                          keep_ref, send_ref, bias_ref, out_ref, dq, dk, dv, whole):
    scale = HEAD_DIM ** (-0.5)
    for group in range(x_ref.shape[0] // GROUP):
        rows = slice(group * GROUP, (group + 1) * GROUP)
        same = same_segment(segc_ref, segr_ref, rows)
        for pair in range(q_ref.shape[1] // PAIR):
            cols = slice(pair * PAIR, (pair + 1) * PAIR)
            q_two = two_heads(q_ref[rows, cols])
            dc_two = two_heads(dc_ref[rows, cols])
            k_pair = k_ref[rows, cols]
            probs = pair_probs(q_two, k_pair, same)
            prob_grad = mm_nt(dc_two, v_ref[rows, cols])
            score_grad = (
                probs * (prob_grad - jnp.sum(prob_grad * probs, axis=1, keepdims=True))
            ).astype(bf16)
            dq[rows, cols] = (join_heads(mm(score_grad, k_pair)) * scale).astype(bf16)
            dk[rows, cols] = (mm_tn(score_grad, q_two) * scale).astype(bf16)
            dv[rows, cols] = mm_tn(probs.astype(bf16), dc_two).astype(bf16)
    bias_ref[0:1] = jnp.sum(dq[...].astype(f32), axis=0, keepdims=True)
    bias_ref[1:2] = jnp.sum(dv[...].astype(f32), axis=0, keepdims=True)
    for s, grad in enumerate((dq, dk, dv)):
        whole[...] = mm_tn(x_ref[...], grad[...])
        put_slabs_at(pos_ref, whole, keep_ref, send_ref, s)
    for at in range(0, x_ref.shape[0], 128):
        rows = slice(at, at + 128)
        out_ref[rows] = (
            part_ref[rows] + mm_nt(dq[rows], w_ref[0]) + mm_nt(dk[rows], w_ref[1]) + mm_nt(dv[rows], w_ref[2])
        )


def put_slabs_at(pos_ref, source, keep_ref, send_ref, s):
    slab = source.shape[0] // 16
    for place in range(16):
        at = pl.multiple_of(jnp.bitwise_xor(pos_ref[0], place) * slab, slab)
        target = send_ref if place % 2 else keep_ref
        target[place // 2, s] = source[pl.ds(at, slab), :].astype(bf16)


def attention_back(pos, x, w, segc, segr, q, k, v, dc, part):
    rows, width = x.shape
    cols = q.shape[1]
    smem = pl.BlockSpec(memory_space=pltpu.SMEM)
    vmem = pl.BlockSpec(memory_space=pltpu.VMEM)
    slabs = jax.ShapeDtypeStruct((8, 3, width // 16, cols), bf16)
    return pl.pallas_call(
        attention_back_kernel,
        in_specs=[smem] + [vmem] * 9,
        out_specs=[vmem] * 4,
        out_shape=(slabs, slabs, jax.ShapeDtypeStruct((2, cols), f32), jax.ShapeDtypeStruct((rows, width), f32)),
        scratch_shapes=[pltpu.VMEM((rows, cols), bf16)] * 3 + [pltpu.VMEM((width, cols), f32)],
        compiler_params=params(),
        cost_estimate=cost(20 * rows * width * cols, 4 * 3 * width * cols),
        name="attention_back",
    )(pos, x, w, segc, segr, q, k, v, dc, part)


def swap_mp(values):
    return lax.ppermute(values, "mp", [(0, 1), (1, 0)])


def swap_dp(values, bit):
    size = lax.axis_size("dp")
    return lax.ppermute(values, "dp", [(at, at ^ bit) for at in range(size)])


def fetch(own, axis, place):
    size = own.shape[axis] // 4
    first = swap_mp(lax.dynamic_slice_in_dim(own, place * size, size, axis))
    second = swap_dp(first, 2)
    third = swap_dp(first, 1)
    fourth = swap_dp(second, 1)
    whole = jnp.zeros_like(own)
    for bits, part in ((0, first), (2, second), (1, third), (3, fourth)):
        whole = lax.dynamic_update_slice_in_dim(whole, part, (place ^ bits) * size, axis)
    return whole


def gather_rows(rows):
    size = lax.axis_size("dp")
    if size != 16:
        return lax.all_gather(rows, ("dp", "mp"), axis=0, tiled=True)
    rows = jnp.concatenate([rows, swap_mp(rows)], axis=0)
    for bit in (1, 2, 4, 8):
        rows = jnp.concatenate([rows, swap_dp(rows, bit)], axis=0)
    return rows


def add(a, b):
    return (a.astype(f32) + b.astype(f32)).astype(a.dtype)


def scatter_sum(keep, send, order):
    size = lax.axis_size("dp")
    if size != 16:
        rest = keep.shape[2:]
        both = jnp.stack([keep, send], axis=2)
        both = both.reshape((2, 16) + rest)
        mine = add(both[0], swap_mp(both[1]))
        return mine
    got = swap_dp(send, 1)
    rest = keep.shape[2:]
    names = ["x", "z1", "z0", "y"]
    keep = keep.reshape((2, 2, 2, 2) + rest)
    got = got.reshape((2, 2, 2, 2) + rest)
    bit_of = {"y": 2, "z0": 4, "z1": 8}
    for name in order:
        axis = names.index(name)
        names.remove(name)
        pick = lambda values, at: lax.index_in_dim(values, at, axis, keepdims=False)
        out = add(pick(keep, 1), pick(got, 1))
        out = swap_mp(out) if name == "x" else swap_dp(out, bit_of[name])
        keep = add(pick(keep, 0), pick(got, 0))
        got = out
    return add(keep, got)


def swap_order(values, axis, place):
    shape = values.shape
    split = values.reshape(shape[:axis] + (2, 2, 2, 2) + shape[axis + 1:])
    for at, bit in enumerate((8, 4, 2, 1)):
        low = lax.index_in_dim(split, 0, axis + at)
        high = lax.index_in_dim(split, 1, axis + at)
        flipped = jnp.concatenate([high, low], axis=axis + at)
        split = jnp.where((place & bit) != 0, flipped, split)
    return split.reshape(shape)


def shards(
    inputs, segment_ids, pair_index, w_qkv, bias_qv, w_out, w_in, bias_in, w_back,
    w_pool, norm_gains, shifts, logit_scale, out_grad,
):
    tok_rows, width = inputs.shape
    size = lax.axis_size("dp")
    dp, mp = lax.axis_index("dp"), lax.axis_index("mp")
    rows = tok_rows // 2
    blocks = rows // SEG_LEN
    place = dp % 4
    slots = dp if size == 16 else 0 * dp
    pos = jnp.reshape(slots, (1,)).astype(jnp.int32)

    x = lax.dynamic_slice_in_dim(inputs, mp * rows, rows, 0)
    cot = lax.dynamic_slice_in_dim(out_grad, mp * rows, rows, 0)
    seg = lax.dynamic_slice_in_dim(segment_ids, mp * rows, rows, 0)
    segc, segr = seg.reshape(rows, 1), seg.reshape(1, rows)
    pairs = lax.dynamic_slice_in_dim(pair_index, mp * blocks, blocks, 0)

    cols = w_qkv.shape[2]
    units = w_in.shape[1]
    biases = swap_mp(jnp.concatenate([bias_qv.reshape(-1), bias_in]))
    bias_qv_p, bias_in_p = biases[:2 * cols].reshape(2, cols), biases[2 * cols:]
    w_qkv_p = fetch(w_qkv, 1, place)
    w_out_p = fetch(w_out, 0, place)
    w_in_p = fetch(w_in, 0, place)
    w_back_p = fetch(w_back, 0, place)

    q_o, k_o, v_o, ctx_o = attention_half(x, w_qkv, bias_qv, segc, segr)
    q_p, k_p, v_p, ctx_p = attention_half(x, w_qkv_p, bias_qv_p, segc, segr)
    normed_one, inv_one, low_one = first_norm(ctx_o, ctx_p, w_out, w_out_p, x, norm_gains, shifts)
    act_o, slope_o = inner_half(low_one, w_in, bias_in.reshape(1, -1))
    part = branch_half(act_o, w_back)
    act_p, slope_p = inner_half(low_one, w_in_p, bias_in_p.reshape(1, -1))
    normed_two, inv_two, own_out = second_norm(act_p, w_back_p, part, normed_one, norm_gains, shifts)

    firsts = own_out.reshape(blocks, SEG_LEN, width)[:, 0]
    tail = jnp.concatenate(
        [(pairs // 64).astype(bf16)[:, None], (pairs % 64).astype(bf16)[:, None], jnp.zeros((blocks, 126), bf16)],
        axis=1,
    )
    rel = gather_rows(jnp.concatenate([firsts, tail], axis=1))
    linear = dp * 2 + mp
    position = jnp.stack([linear if size == 16 else 0 * linear, linear]).astype(jnp.int32)
    loss_value, grad_scale, pre_all, pool_bias, first_grad, firsts_all = pair_loss(
        position, rel, w_pool, shifts[4:5], logit_scale
    )
    pool_rows = width // size
    grad_pool = lax.dot_general(
        lax.dynamic_slice_in_dim(firsts_all, dp * pool_rows, pool_rows, 1), pre_all, TN, preferred_element_type=f32
    )
    grad_pool_bias = lax.dynamic_slice_in_dim(pool_bias[0], dp * pool_rows, pool_rows, 0)

    grad_two, branch, sums_two = second_back(cot, first_grad, normed_two, inv_two, norm_gains)
    keep_bo, send_bo = back_weight(pos, act_o, branch)
    keep_bp, send_bp = back_weight(pos, act_p, branch)
    keep_io, send_io, bias_io, part_one = inner_back(pos, branch, w_back, slope_o, low_one, w_in, grad_two)
    keep_ip, send_ip, bias_ip, part_two = inner_back(pos, branch, w_back_p, slope_p, low_one, w_in_p, part_one)
    grad_one, sums_one, dc_o, dc_p, keep_w, send_w = first_back(
        pos, part_two, normed_one, inv_one, norm_gains, ctx_o, ctx_p, w_out, w_out_p
    )
    keep_qo, send_qo, bias_qo, in_one = attention_back(pos, x, w_qkv, segc, segr, q_o, k_o, v_o, dc_o, grad_one)
    keep_qp, send_qp, bias_qp, in_two = attention_back(pos, x, w_qkv_p, segc, segr, q_p, k_p, v_p, dc_p, in_one)

    both = lambda a, b: jnp.stack([a, b])
    mine_back = scatter_sum(both(keep_bo, keep_bp), both(send_bo, send_bp), ("x", "y", "z0", "z1"))
    mine_in = scatter_sum(both(keep_io, keep_ip), both(send_io, send_ip), ("y", "x", "z0", "z1"))
    mine_out = scatter_sum(keep_w, send_w, ("x", "y", "z0", "z1"))
    mine_qkv = scatter_sum(both(keep_qo, keep_qp), both(send_qo, send_qp), ("y", "x", "z0", "z1"))

    vectors = jnp.concatenate([sums_one[0:1], sums_two[0:1], sums_one[2:3], sums_one[1:2], sums_two[2:3], sums_two[1:2]])
    by_dp = vectors.reshape(6, 16, width // 16).transpose(1, 0, 2).reshape(16, -1)
    by_dp = jnp.broadcast_to(by_dp[None], (2,) + by_dp.shape)
    bias_q = both(bias_qo, bias_qp).reshape(2, 2, 16, cols // 16).transpose(0, 2, 1, 3).reshape(2, 16, -1)
    bias_i = both(bias_io, bias_ip).reshape(2, 16, units // 16)
    packed = jnp.concatenate([by_dp, bias_q, bias_i], axis=2)
    packed = swap_order(packed, 1, slots).reshape(2, 8, 2, -1)
    mine_small = scatter_sum(packed[:, :, 0], packed[:, :, 1], ("y", "x", "z0", "z1"))

    if size != 16:
        fold = lambda values: lax.psum_scatter(values, "dp", scatter_dimension=0, tiled=True)
        grad_back = fold(mine_back.reshape(units, width).astype(f32))
        grad_in = fold(mine_in.reshape(width, units).astype(f32))
        grad_qkv = fold(mine_qkv.transpose(0, 2, 1, 3).reshape(width, 3, cols).astype(f32)).transpose(1, 0, 2)
        small = mine_small
        n_vec = 6 * (width // 16)
        n_q = 2 * (cols // 16)
        n_i = units // 16
        vec = small[:, :n_vec].reshape(16, 6, -1).transpose(0, 2, 1).reshape(width, 6)
        vec = fold(vec).T
        grad_bias_qv = fold(small[:, n_vec:n_vec + n_q].reshape(16, 2, -1).transpose(0, 2, 1).reshape(cols, 2)).T
        grad_bias_in = fold(small[:, n_vec + n_q:n_vec + n_q + n_i].reshape(units))
        grad_out = fold(mine_out.reshape(cols, width).astype(f32))
    else:
        grad_back = mine_back.astype(f32)
        grad_in = mine_in.astype(f32)
        grad_qkv = mine_qkv.astype(f32)
        small = mine_small
        n_vec = 6 * (width // 16)
        n_q = 2 * (cols // 16)
        n_i = units // 16
        vec = small[:n_vec].reshape(6, -1)
        grad_bias_qv = small[n_vec:n_vec + n_q].reshape(2, -1)
        grad_bias_in = small[n_vec + n_q:n_vec + n_q + n_i]
        grad_out = mine_out.astype(f32)

    def both_halves(own):
        other = swap_mp(own)
        return jnp.concatenate([jnp.where(mp == 0, own, other), jnp.where(mp == 0, other, own)], axis=0)

    block_out = both_halves(own_out)
    grad_inputs = both_halves(in_two.astype(bf16)).astype(f32)
    new_scale = logit_scale - step_rate * grad_scale
    return (
        block_out, loss_value, grad_inputs, grad_qkv, grad_bias_qv, grad_out, grad_in, grad_bias_in,
        grad_back, grad_pool, vec[:2], vec[2:], grad_pool_bias, grad_scale, new_scale,
    )


def solution(mesh):
    return jax.shard_map(
        shards,
        mesh=mesh,
        in_specs=(
            P("dp", None), P("dp"), P("dp"), P(None, None, "mp"), P(None, "mp"), P("mp", None), P(None, "mp"),
            P("mp"), P("mp", None), P(), P(), P(), P(), P("dp", None),
        ),
        out_specs=(
            P("dp", None), P(), P("dp", None), P(None, "dp", "mp"), P(None, ("mp", "dp")), P(("mp", "dp"), None),
            P("dp", "mp"), P(("mp", "dp")), P(("mp", "dp"), None), P("dp", None), P(None, "dp"), P(None, "dp"),
            P("dp"), P(), P(),
        ),
        check_vma=False,
    )
```

```python
from functools import partial

import jax
import jax.numpy as jnp
from jax import lax
from jax.experimental import pallas as pl
from jax.experimental.pallas import tpu as pltpu
from jax.sharding import PartitionSpec as P

HEAD_DIM = 64
SEG_LEN = 64
PAIR = 2 * HEAD_DIM
GROUP = 128

epsilon = 1e-12
margin = 0.3
step_rate = 0.1
masked_out = -1e30
f32 = jnp.float32
bf16 = jnp.bfloat16

NT = (((1,), (1,)), ((), ()))
TN = (((0,), (0,)), ((), ()))


def mm(a, b):
    return jnp.dot(a, b, preferred_element_type=f32)


def mm_nt(a, b):
    return lax.dot_general(a, b, NT, preferred_element_type=f32)


def mm_tn(a, b):
    return lax.dot_general(a, b, TN, preferred_element_type=f32)


def params(mib=40):
    return pltpu.CompilerParams(vmem_limit_bytes=mib * 1024 * 1024)


def cost(flops, moved):
    return pl.CostEstimate(flops=int(flops), bytes_accessed=int(moved), transcendentals=0)


def lane_masks():
    lane = lax.broadcasted_iota(jnp.int32, (1, PAIR), 1)
    first = (lane < HEAD_DIM).astype(f32)
    return first, 1.0 - first


def two_heads(rows):
    first, second = lane_masks()
    return jnp.concatenate([rows * first.astype(bf16), rows * second.astype(bf16)], axis=0)


def join_heads(both):
    first, second = lane_masks()
    half = both.shape[0] // 2
    return both[:half] * first + both[half:] * second


def pair_probs(q_two, k_pair, same):
    scores = mm_nt(q_two, k_pair) * (HEAD_DIM ** (-0.5))
    scores = jnp.where(same, scores, masked_out)
    shifted = jnp.exp(scores - jnp.max(scores, axis=1, keepdims=True))
    return shifted / jnp.sum(shifted, axis=1, keepdims=True)


def same_segment(seg_col, seg_row, rows):
    own = seg_col[rows, :]
    other = seg_row[:, rows]
    one = own == other
    return jnp.concatenate([one, one], axis=0)


def attention_kernel(x_ref, w_ref, b_ref, segc_ref, segr_ref, q_ref, k_ref, v_ref, c_ref):
    x = x_ref[...]
    q_ref[...] = (mm(x, w_ref[0]) + b_ref[0:1]).astype(bf16)
    k_ref[...] = mm(x, w_ref[1]).astype(bf16)
    v_ref[...] = (mm(x, w_ref[2]) + b_ref[1:2]).astype(bf16)
    for group in range(x.shape[0] // GROUP):
        rows = slice(group * GROUP, (group + 1) * GROUP)
        same = same_segment(segc_ref, segr_ref, rows)
        for pair in range(q_ref.shape[1] // PAIR):
            cols = slice(pair * PAIR, (pair + 1) * PAIR)
            probs = pair_probs(two_heads(q_ref[rows, cols]), k_ref[rows, cols], same)
            c_ref[rows, cols] = join_heads(mm(probs.astype(bf16), v_ref[rows, cols])).astype(bf16)


def attention_half(x, w, b, segc, segr):
    rows, cols = x.shape[0], w.shape[2]
    out = jax.ShapeDtypeStruct((rows, cols), bf16)
    return pl.pallas_call(
        attention_kernel,
        out_shape=(out,) * 4,
        compiler_params=params(),
        cost_estimate=cost(2 * rows * 768 * cols * 3 * 2, 6 * rows * cols * 2),
        name="attention",
    )(x, w, b, segc, segr)


def norm_rows(values):
    row_mean = jnp.mean(values, axis=-1, keepdims=True)
    centred = values - row_mean
    inv_std = lax.rsqrt(jnp.mean(centred * centred, axis=-1, keepdims=True) + epsilon)
    return centred * inv_std, inv_std


def norm_back(grad, normed, inv_std, gain):
    scaled = grad * gain
    return inv_std * (
        scaled
        - jnp.mean(scaled, axis=-1, keepdims=True)
        - normed * jnp.mean(scaled * normed, axis=-1, keepdims=True)
    )


def first_norm_kernel(co_ref, cp_ref, wo_ref, wp_ref, x_ref, g_ref, s_ref, n_ref, inv_ref, low_ref):
    for at in range(0, x_ref.shape[0], 128):
        rows = slice(at, at + 128)
        attended = mm(co_ref[rows], wo_ref[...]) + mm(cp_ref[rows], wp_ref[...]) + s_ref[0:1]
        normed, inv_std = norm_rows(x_ref[rows].astype(f32) + attended)
        n_ref[rows] = normed
        inv_ref[rows] = inv_std
        low_ref[rows] = (normed * g_ref[0:1] + s_ref[1:2]).astype(bf16)


def first_norm(ctx_o, ctx_p, wo, wp, x, gains, shifts):
    rows, width = x.shape
    return pl.pallas_call(
        first_norm_kernel,
        out_shape=(
            jax.ShapeDtypeStruct((rows, width), f32),
            jax.ShapeDtypeStruct((rows, 1), f32),
            jax.ShapeDtypeStruct((rows, width), bf16),
        ),
        compiler_params=params(),
        cost_estimate=cost(2 * rows * width * width, 12 * rows * width),
        name="first_norm",
    )(ctx_o, ctx_p, wo, wp, x, gains, shifts)


def inner_kernel(h_ref, w_ref, b_ref, act_ref, slope_ref):
    for at in range(0, h_ref.shape[0], 128):
        rows = slice(at, at + 128)
        inner = mm(h_ref[rows], w_ref[...]) + b_ref[...]
        cumulative = 0.5 * (1.0 + lax.erf(inner * 0.7071067811865476))
        density = jnp.exp(-0.5 * inner * inner) * 0.3989422804014327
        act_ref[rows] = (inner * cumulative).astype(bf16)
        slope_ref[rows] = (cumulative + inner * density).astype(bf16)


def inner_half(low, w, b):
    rows, width = low.shape
    units = w.shape[1]
    tile = 256
    out = jax.ShapeDtypeStruct((rows, units), bf16)
    return pl.pallas_call(
        inner_kernel,
        grid=(units // tile,),
        in_specs=[
            pl.BlockSpec((rows, width), lambda n: (0, 0)),
            pl.BlockSpec((width, tile), lambda n: (0, n)),
            pl.BlockSpec((1, tile), lambda n: (0, n)),
        ],
        out_specs=[pl.BlockSpec((rows, tile), lambda n: (0, n))] * 2,
        out_shape=(out, out),
        compiler_params=params(),
        cost_estimate=cost(4 * rows * width * units, 8 * rows * units),
        name="inner",
    )(low, w, b)


def branch_kernel(act_ref, w_ref, out_ref):
    for at in range(0, act_ref.shape[0], 128):
        rows = slice(at, at + 128)
        out_ref[rows] = mm(act_ref[rows], w_ref[...])


def branch_half(act, w):
    rows, units = act.shape
    width = w.shape[1]
    return pl.pallas_call(
        branch_kernel,
        out_shape=jax.ShapeDtypeStruct((rows, width), f32),
        compiler_params=params(),
        cost_estimate=cost(2 * rows * width * units, 4 * rows * units),
        name="branch",
    )(act, w)


def second_norm_kernel(act_ref, w_ref, part_ref, n1_ref, g_ref, s_ref, n_ref, inv_ref, out_ref):
    for at in range(0, act_ref.shape[0], 128):
        rows = slice(at, at + 128)
        branch = mm(act_ref[rows], w_ref[...]) + part_ref[rows] + s_ref[2:3]
        hidden_one = n1_ref[rows] * g_ref[0:1] + s_ref[1:2]
        normed, inv_std = norm_rows(hidden_one + branch)
        n_ref[rows] = normed
        inv_ref[rows] = inv_std
        out_ref[rows] = (normed * g_ref[1:2] + s_ref[3:4]).astype(bf16)


def second_norm(act, w, part, normed_one, gains, shifts):
    rows, units = act.shape
    width = w.shape[1]
    return pl.pallas_call(
        second_norm_kernel,
        out_shape=(
            jax.ShapeDtypeStruct((rows, width), f32),
            jax.ShapeDtypeStruct((rows, 1), f32),
            jax.ShapeDtypeStruct((rows, width), bf16),
        ),
        compiler_params=params(),
        cost_estimate=cost(2 * rows * width * units, 4 * rows * units),
        name="second_norm",
    )(act, w, part, normed_one, gains, shifts)


def loss_kernel(
    pos_ref, rel_ref, w_ref, bias_ref, scale_ref,
    loss_ref, gscale_ref, pre_ref, bias_grad_ref, first_grad_ref, firsts_out_ref,
    all_ref, pooled_ref, len_ref, unit_ref, lse_col_ref, lse_row_ref, pre_f_ref,
):
    @pl.loop(0, pooled_ref.shape[0] // 8)
    def _(slot):
        source = pl.multiple_of(slot * 8, 8)
        target = pl.multiple_of(jnp.bitwise_xor(slot, pos_ref[0]) * 8, 8)
        all_ref[pl.ds(target, 8), :] = rel_ref[pl.ds(source, 8), :].astype(f32)

    loss_passes(
        pos_ref[1], scale_ref[0], w_ref, bias_ref[...],
        loss_ref, gscale_ref, pre_ref, bias_grad_ref, first_grad_ref, firsts_out_ref,
        all_ref, pooled_ref, len_ref, unit_ref, lse_col_ref, lse_row_ref, pre_f_ref,
    )


def loss_passes(
    here, scale, w_ref, bias,
    loss_ref, gscale_ref, pre_ref, bias_grad_ref, first_grad_ref, firsts_out_ref,
    all_ref, pooled_ref, len_ref, unit_ref, lse_col_ref, lse_row_ref, pre_f_ref,
):
    count, width = pooled_ref.shape
    chunk = min(count, 256)
    steps = count // chunk

    def pool(at):
        firsts = all_ref[pl.ds(at, chunk), :width].astype(bf16)
        firsts_out_ref[pl.ds(at, chunk), :] = firsts
        pooled = jnp.tanh(mm(firsts, w_ref[...]) + bias)
        inv_len = lax.rsqrt(jnp.sum(pooled * pooled, axis=-1, keepdims=True) + 1e-06)
        pooled_ref[pl.ds(at, chunk), :] = pooled
        len_ref[pl.ds(at, chunk), :] = inv_len
        unit_ref[pl.ds(at, chunk), :] = (pooled * inv_len).astype(bf16)

    def positions(at):
        own = at + lax.broadcasted_iota(jnp.int32, (chunk, count), 0)
        other = lax.broadcasted_iota(jnp.int32, (chunk, count), 1)
        paired = all_ref[pl.ds(at, chunk), width:width + 1] * 64.0 + all_ref[pl.ds(at, chunk), width + 1:width + 2]
        positive = paired.astype(jnp.int32) == other
        return own == other, positive

    def logits_of(at):
        cosine = mm_nt(unit_ref[pl.ds(at, chunk), :], unit_ref[...])
        own, positive = positions(at)
        shifted = cosine - jnp.where(positive, margin, 0.0)
        return shifted, own, positive

    def first_pass(at, run):
        shifted, own, positive = logits_of(at)
        logits = jnp.where(own, masked_out, scale * shifted)
        top = jnp.max(logits, axis=1, keepdims=True)
        lse = top + jnp.log(jnp.sum(jnp.exp(logits - top), axis=1, keepdims=True))
        lse_col_ref[pl.ds(at, chunk), :] = lse
        eye = lax.broadcasted_iota(jnp.int32, (chunk, chunk), 0) == lax.broadcasted_iota(
            jnp.int32, (chunk, chunk), 1
        )
        lse_row_ref[:, pl.ds(at, chunk)] = jnp.sum(jnp.where(eye, lse, 0.0), axis=0, keepdims=True)
        return run + jnp.sum(lse) - jnp.sum(jnp.where(positive, logits, 0.0))

    def second_pass(at, run):
        run_scale, run_bias = run
        shifted, own, positive = logits_of(at)
        logits = scale * shifted
        factor = 1.0 / (2.0 * count)
        grad = (
            jnp.exp(logits - lse_col_ref[pl.ds(at, chunk), :])
            + jnp.exp(logits - lse_row_ref[...])
            - jnp.where(positive, 2.0, 0.0)
        ) * factor
        grad = jnp.where(own, 0.0, grad)
        run_scale = run_scale + jnp.sum(grad * shifted)
        unit_grad = 2.0 * mm((scale * grad).astype(bf16), unit_ref[...])
        pooled = pooled_ref[pl.ds(at, chunk), :]
        inv_len = len_ref[pl.ds(at, chunk), :]
        along = jnp.sum(pooled * unit_grad, axis=-1, keepdims=True)
        pooled_grad = inv_len * unit_grad - pooled * (inv_len * inv_len * inv_len) * along
        pre_grad = (pooled_grad * (1.0 - pooled * pooled)).astype(bf16)
        pre_ref[pl.ds(at, chunk), :] = pre_grad
        pre_f_ref[pl.ds(at, chunk), :] = pre_grad.astype(f32)
        return run_scale, run_bias + jnp.sum(pre_grad.astype(f32), axis=0, keepdims=True)

    def each(body, run):
        if steps == 1:
            return body(0, run)
        return lax.fori_loop(0, steps, lambda s, r: body(pl.multiple_of(s * chunk, chunk), r), run)

    each(lambda at, run: (pool(at), run)[1], 0)
    total = each(first_pass, jnp.float32(0.0))
    run_scale, run_bias = each(second_pass, (jnp.float32(0.0), jnp.zeros((1, width), f32)))
    loss_ref[0] = total / count
    gscale_ref[0] = run_scale
    bias_grad_ref[...] = run_bias
    own_rows = pre_f_ref[pl.ds(pl.multiple_of(here * 8, 8), 8), :].astype(bf16)
    first_grad_ref[...] = mm_nt(own_rows, w_ref[...])


def pair_loss(position, rel, w_pool, bias, scale):
    count, wide = rel.shape
    width = w_pool.shape[0]
    smem = pl.BlockSpec(memory_space=pltpu.SMEM)
    vmem = pl.BlockSpec(memory_space=pltpu.VMEM)
    return pl.pallas_call(
        loss_kernel,
        in_specs=[smem, vmem, vmem, vmem, smem],
        out_specs=[smem, smem, vmem, vmem, vmem, vmem],
        out_shape=(
            jax.ShapeDtypeStruct((1,), f32),
            jax.ShapeDtypeStruct((1,), f32),
            jax.ShapeDtypeStruct((count, width), bf16),
            jax.ShapeDtypeStruct((1, width), f32),
            jax.ShapeDtypeStruct((8, width), f32),
            jax.ShapeDtypeStruct((count, width), bf16),
        ),
        scratch_shapes=[
            pltpu.VMEM((count, wide), f32),
            pltpu.VMEM((count, width), f32),
            pltpu.VMEM((count, 1), f32),
            pltpu.VMEM((count, width), bf16),
            pltpu.VMEM((count, 1), f32),
            pltpu.VMEM((1, count), f32),
            pltpu.VMEM((count, width), f32),
        ],
        compiler_params=params(56),
        cost_estimate=cost(2e9, 4e6),
        name="pair_loss",
    )(position, rel, w_pool, bias, scale)


def put_slabs(pos_ref, source, keep_ref, send_ref, lead):
    slab = source.shape[0] // 16
    for place in range(16):
        at = pl.multiple_of(jnp.bitwise_xor(pos_ref[0], place) * slab, slab)
        target = send_ref if place % 2 else keep_ref
        target[lead + (place // 2,)] = source[pl.ds(at, slab), :].astype(bf16)


def second_back_kernel(
    og_ref, fg_ref, n_ref, inv_ref, g_ref, grad_ref, low_ref, sums_ref
):
    rows_all, width = og_ref.shape
    sums_ref[...] = jnp.zeros_like(sums_ref)
    for at in range(0, rows_all, 64):
        rows = slice(at, at + 64)
        block = at // 64
        is_first = lax.broadcasted_iota(jnp.int32, (64, width), 0) == 0
        grad = og_ref[rows].astype(f32) + jnp.where(is_first, fg_ref[block:block + 1], 0.0)
        normed = n_ref[rows]
        value = norm_back(grad, normed, inv_ref[rows], g_ref[1:2])
        low = value.astype(bf16)
        grad_ref[rows] = value
        low_ref[rows] = low
        sums_ref[0:1] += jnp.sum(grad * normed, axis=0, keepdims=True)
        sums_ref[1:2] += jnp.sum(grad, axis=0, keepdims=True)
        sums_ref[2:3] += jnp.sum(low.astype(f32), axis=0, keepdims=True)


def second_back(out_grad, first_grad, normed, inv_std, gains):
    rows, width = out_grad.shape
    return pl.pallas_call(
        second_back_kernel,
        out_shape=(
            jax.ShapeDtypeStruct((rows, width), f32),
            jax.ShapeDtypeStruct((rows, width), bf16),
            jax.ShapeDtypeStruct((8, width), f32),
        ),
        compiler_params=params(),
        cost_estimate=cost(20 * rows * width, 12 * rows * width),
        name="second_back",
    )(out_grad, first_grad, normed, inv_std, gains)


def slab_shape(rows, cols):
    return jax.ShapeDtypeStruct((8, rows // 16, cols), bf16)


def back_weight_kernel(pos_ref, act_ref, branch_ref, keep_ref, send_ref, whole):
    for at in range(0, whole.shape[0], 256):
        rows = slice(at, at + 256)
        whole[rows] = mm_tn(act_ref[:, rows], branch_ref[...])
    put_slabs(pos_ref, whole, keep_ref, send_ref, ())


def back_weight(pos, act, branch):
    rows, units = act.shape
    width = branch.shape[1]
    smem = pl.BlockSpec(memory_space=pltpu.SMEM)
    vmem = pl.BlockSpec(memory_space=pltpu.VMEM)
    return pl.pallas_call(
        back_weight_kernel,
        in_specs=[smem, vmem, vmem],
        out_specs=[vmem, vmem],
        out_shape=(slab_shape(units, width),) * 2,
        scratch_shapes=[pltpu.VMEM((units, width), f32)],
        compiler_params=params(),
        cost_estimate=cost(2 * rows * width * units, 4 * units * width),
        name="back_weight",
    )(pos, act, branch)


def inner_back_kernel(pos_ref, branch_ref, wb_ref, slope_ref, low_ref, wi_ref, part_ref,
                      keep_ref, send_ref, bias_ref, out_ref, grad, whole):
    units = slope_ref.shape[1]
    for at in range(0, units, 256):
        cols = slice(at, at + 256)
        inner_grad = (mm_nt(branch_ref[...], wb_ref[cols]) * slope_ref[:, cols].astype(f32)).astype(bf16)
        grad[:, cols] = inner_grad
        bias_ref[:, cols] = jnp.sum(inner_grad.astype(f32), axis=0, keepdims=True)
        whole[:, cols] = mm_tn(low_ref[...], inner_grad)
    put_slabs(pos_ref, whole, keep_ref, send_ref, ())
    for at in range(0, low_ref.shape[0], 128):
        rows = slice(at, at + 128)
        out_ref[rows] = part_ref[rows] + mm_nt(grad[rows], wi_ref[...])


def inner_back(pos, branch, w_back, slope, low, w_in, part):
    rows, units = slope.shape
    width = low.shape[1]
    smem = pl.BlockSpec(memory_space=pltpu.SMEM)
    vmem = pl.BlockSpec(memory_space=pltpu.VMEM)
    return pl.pallas_call(
        inner_back_kernel,
        in_specs=[smem] + [vmem] * 6,
        out_specs=[vmem] * 4,
        out_shape=(slab_shape(width, units),) * 2
        + (jax.ShapeDtypeStruct((1, units), f32), jax.ShapeDtypeStruct((rows, width), f32)),
        scratch_shapes=[pltpu.VMEM((rows, units), bf16), pltpu.VMEM((width, units), f32)],
        compiler_params=params(),
        cost_estimate=cost(6 * rows * width * units, 4 * units * width),
        name="inner_back",
    )(pos, branch, w_back, slope, low, w_in, part)


def first_back_kernel(pos_ref, grad_ref, n_ref, inv_ref, g_ref, co_ref, cp_ref, wo_ref, wp_ref,
                      one_ref, sums_ref, dco_ref, dcp_ref, keep_ref, send_ref, low, whole):
    width = grad_ref.shape[1]
    sums_ref[...] = jnp.zeros_like(sums_ref)
    for at in range(0, grad_ref.shape[0], 128):
        rows = slice(at, at + 128)
        grad = grad_ref[rows]
        normed = n_ref[rows]
        value = norm_back(grad, normed, inv_ref[rows], g_ref[0:1])
        low_rows = value.astype(bf16)
        one_ref[rows] = value
        low[rows] = low_rows
        dco_ref[rows] = mm_nt(low_rows, wo_ref[...]).astype(bf16)
        dcp_ref[rows] = mm_nt(low_rows, wp_ref[...]).astype(bf16)
        sums_ref[0:1] += jnp.sum(grad * normed, axis=0, keepdims=True)
        sums_ref[1:2] += jnp.sum(grad, axis=0, keepdims=True)
        sums_ref[2:3] += jnp.sum(low_rows.astype(f32), axis=0, keepdims=True)
    for side, ctx_ref in enumerate((co_ref, cp_ref)):
        whole[...] = mm_tn(ctx_ref[...], low[...])
        put_slabs(pos_ref, whole, keep_ref.at[side], send_ref.at[side], ())


def first_back(pos, grad, normed, inv_std, gains, ctx_o, ctx_p, wo, wp):
    rows, width = grad.shape
    cols = ctx_o.shape[1]
    smem = pl.BlockSpec(memory_space=pltpu.SMEM)
    vmem = pl.BlockSpec(memory_space=pltpu.VMEM)
    return pl.pallas_call(
        first_back_kernel,
        in_specs=[smem] + [vmem] * 8,
        out_specs=[vmem] * 6,
        out_shape=(
            jax.ShapeDtypeStruct((rows, width), f32),
            jax.ShapeDtypeStruct((8, width), f32),
            jax.ShapeDtypeStruct((rows, cols), bf16),
            jax.ShapeDtypeStruct((rows, cols), bf16),
        )
        + (jax.ShapeDtypeStruct((2, 8, cols // 16, width), bf16),) * 2,
        scratch_shapes=[pltpu.VMEM((rows, width), bf16), pltpu.VMEM((cols, width), f32)],
        compiler_params=params(),
        cost_estimate=cost(8 * rows * width * cols, 12 * rows * width),
        name="first_back",
    )(pos, grad, normed, inv_std, gains, ctx_o, ctx_p, wo, wp)


def attention_back_kernel(pos_ref, x_ref, w_ref, segc_ref, segr_ref, q_ref, k_ref, v_ref, dc_ref, part_ref,
                          keep_ref, send_ref, bias_ref, out_ref, dq, dk, dv, whole):
    scale = HEAD_DIM ** (-0.5)
    for group in range(x_ref.shape[0] // GROUP):
        rows = slice(group * GROUP, (group + 1) * GROUP)
        same = same_segment(segc_ref, segr_ref, rows)
        for pair in range(q_ref.shape[1] // PAIR):
            cols = slice(pair * PAIR, (pair + 1) * PAIR)
            q_two = two_heads(q_ref[rows, cols])
            dc_two = two_heads(dc_ref[rows, cols])
            k_pair = k_ref[rows, cols]
            probs = pair_probs(q_two, k_pair, same)
            prob_grad = mm_nt(dc_two, v_ref[rows, cols])
            score_grad = (
                probs * (prob_grad - jnp.sum(prob_grad * probs, axis=1, keepdims=True))
            ).astype(bf16)
            dq[rows, cols] = (join_heads(mm(score_grad, k_pair)) * scale).astype(bf16)
            dk[rows, cols] = (mm_tn(score_grad, q_two) * scale).astype(bf16)
            dv[rows, cols] = mm_tn(probs.astype(bf16), dc_two).astype(bf16)
    bias_ref[0:1] = jnp.sum(dq[...].astype(f32), axis=0, keepdims=True)
    bias_ref[1:2] = jnp.sum(dv[...].astype(f32), axis=0, keepdims=True)
    for s, grad in enumerate((dq, dk, dv)):
        whole[...] = mm_tn(x_ref[...], grad[...])
        put_slabs_at(pos_ref, whole, keep_ref, send_ref, s)
    for at in range(0, x_ref.shape[0], 128):
        rows = slice(at, at + 128)
        out_ref[rows] = (
            part_ref[rows] + mm_nt(dq[rows], w_ref[0]) + mm_nt(dk[rows], w_ref[1]) + mm_nt(dv[rows], w_ref[2])
        )


def put_slabs_at(pos_ref, source, keep_ref, send_ref, s):
    slab = source.shape[0] // 16
    for place in range(16):
        at = pl.multiple_of(jnp.bitwise_xor(pos_ref[0], place) * slab, slab)
        target = send_ref if place % 2 else keep_ref
        target[place // 2, s] = source[pl.ds(at, slab), :].astype(bf16)


def attention_back(pos, x, w, segc, segr, q, k, v, dc, part):
    rows, width = x.shape
    cols = q.shape[1]
    smem = pl.BlockSpec(memory_space=pltpu.SMEM)
    vmem = pl.BlockSpec(memory_space=pltpu.VMEM)
    slabs = jax.ShapeDtypeStruct((8, 3, width // 16, cols), bf16)
    return pl.pallas_call(
        attention_back_kernel,
        in_specs=[smem] + [vmem] * 9,
        out_specs=[vmem] * 4,
        out_shape=(slabs, slabs, jax.ShapeDtypeStruct((2, cols), f32), jax.ShapeDtypeStruct((rows, width), f32)),
        scratch_shapes=[pltpu.VMEM((rows, cols), bf16)] * 3 + [pltpu.VMEM((width, cols), f32)],
        compiler_params=params(),
        cost_estimate=cost(20 * rows * width * cols, 4 * 3 * width * cols),
        name="attention_back",
    )(pos, x, w, segc, segr, q, k, v, dc, part)


def flip(value, bit):
    return value + bit - 2 * bit * ((value // bit) % 2)


class Copies:
    def __init__(self, send, recv, local):
        self.send, self.recv, self.local = send, recv, local
        self.sent, self.kept = [], []

    def remote(self, source, target, device):
        at = len(self.sent)
        copy = pltpu.make_async_remote_copy(
            src_ref=source, dst_ref=target, send_sem=self.send.at[at], recv_sem=self.recv.at[at],
            device_id=device, device_id_type=pl.DeviceIdType.MESH,
        )
        copy.start()
        self.sent.append(copy)
        return copy

    def here(self, source, target):
        copy = pltpu.make_async_copy(source, target, self.local.at[len(self.kept)])
        copy.start()
        self.kept.append(copy)
        return copy


def greet(devices):
    barrier = pltpu.get_barrier_semaphore()
    for device in devices:
        pl.semaphore_signal(barrier, inc=1, device_id=device, device_id_type=pl.DeviceIdType.MESH)
    pl.semaphore_wait(barrier, len(devices))


N_CHUNK = 3


def forward_kernel(
    x_ref, segc_ref, segr_ref, w_qkv_ref, b_qv_ref, b_in_ref, g_ref, s_ref, ids_ref, w_pool_ref, scale_ref,
    w_qkv_any, w_out_any, w_in_any, w_back_any,
    block_out, p_qkv, p_out_any, p_in_any, p_back_any, q_any, k_any, v_any, n1_any, i1_any, lowt_any, xt_any, ctxt_any,
    actt_any, slope_any, n2_any, i2_any,
    loss_ref, gscale_ref, new_scale_ref, first_grad_ref, b_qv_p, pool_ref, pool_bias_ref,
    w_out, w_in, w_back, p_out, p_in, p_back, b_in_p, q, k, v, qf, kf, vf, ctx_far, ctx_o, ctx_p,
    n1, i1, low, act, slope, part, n2, i2, own_out, lowt, xt, ctxt, actt, firsts, gathered,
    pre_ref, bias_grad_ref, firsts_out_ref, all_ref, pooled_ref, len_ref, unit_ref, lse_col_ref, lse_row_ref, pre_f_ref,
    send_sem, recv_sem, local_sem,
):
    dp, mp = lax.axis_index("dp"), lax.axis_index("mp")
    rows = q.shape[0]
    width = x_ref.shape[1]
    units = w_in.shape[1]
    near = {"x": {"mp": 1 - mp}, "y": {"dp": flip(dp, 2)}, "z": {"dp": flip(dp, 4)}, "c": {"dp": flip(dp, 1)}}
    far = ({"dp": flip(dp, 8)}, {"dp": flip(flip(dp, 4), 8)})
    run = Copies(send_sem, recv_sem, local_sem)
    own = dp % 8
    bit = {"y": 2, "z": 4}

    out_block, in_block, unit_chunk = w_out.shape[0] // 8, width // 8, units // N_CHUNK
    back_block = unit_chunk // 8

    def out_at(ref):
        return lambda b: ref.at[pl.ds(pl.multiple_of(b * out_block, 16), out_block)]

    def in_at(ref, n):
        return lambda b: ref.at[pl.ds(pl.multiple_of(b * in_block, 16), in_block), pl.ds(n * unit_chunk, unit_chunk)]

    def back_at(ref, n):
        return lambda b: ref.at[pl.ds(pl.multiple_of(n * unit_chunk + b * back_block, 16), back_block)]

    def qkv_at(ref):
        return lambda b: ref.at[:, pl.ds(pl.multiple_of(b * in_block, 16), in_block)]

    chunks = [(out_at(w_out_any), out_at(p_out), "zy")]
    for n in range(N_CHUNK):
        chunks.append((in_at(w_in_any, n), in_at(p_in, n), "yz" if n % 2 == 0 else "zy"))
    for n in range(N_CHUNK):
        chunks.append((back_at(w_back_any, n), back_at(p_back, n), "zy" if n % 2 == 0 else "yz"))
    chunks += [None, None, (qkv_at(w_qkv_any), qkv_at(p_qkv), "yz")]
    total = len(chunks)
    hops = [[None] * 4 for _ in chunks]

    def step(at, stage):
        if not 0 <= at < total or chunks[at] is None:
            return
        source, target, route = chunks[at]
        one = flip(own, bit[route[0]])
        if stage == 0:
            hops[at][0] = [run.remote(source(own), target(own), near["x"])]
            return
        for copy in hops[at][stage - 1]:
            copy.wait_recv()
        if stage == 1:
            hops[at][1] = [run.remote(target(own), target(own), near[route[0]])]
        elif stage == 2:
            hops[at][2] = [run.remote(target(b), target(b), near[route[1]]) for b in (own, one)]
        elif stage == 3:
            two = bit[route[1]]
            hops[at][3] = [
                run.remote(target(b), target(b), near["c"]) for b in (own, one, flip(own, two), flip(one, two))
            ]

    def wave(at):
        step(at - 7, 4)
        step(at - 6, 3)
        step(at - 4, 2)
        step(at - 2, 1)
        step(at, 0)

    greet(list(near.values()) + list(far))
    wave(0)
    b_copies = [run.remote(b_in_ref, b_in_p, near["x"]), run.remote(b_qv_ref, b_qv_p, near["x"])]
    wave(1)
    loads = [run.here(a, b) for a, b in ((w_out_any, w_out), (w_in_any, w_in), (w_back_any, w_back))]

    def project(base, q_to, k_to, v_to):
        x = x_ref[pl.ds(base, rows)]
        q_to[...] = (mm(x, w_qkv_ref[0]) + b_qv_ref[0:1]).astype(bf16)
        k_to[...] = mm(x, w_qkv_ref[1]).astype(bf16)
        v_to[...] = (mm(x, w_qkv_ref[2]) + b_qv_ref[1:2]).astype(bf16)

    def attend(base, q_from, k_from, v_from, target):
        for group in range(rows // GROUP):
            at = slice(group * GROUP, (group + 1) * GROUP)
            here = pl.ds(pl.multiple_of(base + group * GROUP, GROUP), GROUP)
            one = segc_ref[here, :] == segr_ref[:, here]
            same = jnp.concatenate([one, one], axis=0)
            for pair in range(q_from.shape[1] // PAIR):
                cols = slice(pair * PAIR, (pair + 1) * PAIR)
                probs = pair_probs(two_heads(q_from[at, cols]), k_from[at, cols], same)
                target[at, cols] = join_heads(mm(probs.astype(bf16), v_from[at, cols])).astype(bf16)

    far_base = pl.multiple_of((1 - mp) * rows, rows)
    own_base = pl.multiple_of(mp * rows, rows)
    project(far_base, qf, kf, vf)
    attend(far_base, qf, kf, vf, ctx_far)
    wave(2)
    project(own_base, q, k, v)
    wave(3)
    attend(own_base, q, k, v, ctx_o)
    for a, b in ((q, q_any), (k, k_any), (v, v_any)):
        run.here(a, b)
    wave(4)
    for at in range(0, rows, 128):
        here = slice(at, at + 128)
        xt[:, here] = x_ref[pl.ds(pl.multiple_of(own_base + at, 128), 128)].T
        ctxt[0, :, here] = ctx_o[here].T
    loads[0].wait()
    for at in range(0, rows, 128):
        part[at:at + 128] = mm(ctx_o[at:at + 128], w_out[...])
    wave(5)
    wave(6)
    c_copy = run.remote(ctx_far, ctx_p, near["x"])
    wave(7)
    wave(8)
    c_copy.wait_recv()
    for at in range(0, rows, 128):
        here = slice(at, at + 128)
        x = x_ref[pl.ds(pl.multiple_of(own_base + at, 128), 128)].astype(f32)
        normed, inv_std = norm_rows(x + part[here] + mm(ctx_p[here], p_out[...]) + s_ref[0:1])
        n1[here] = normed
        i1[here] = jnp.broadcast_to(inv_std, (128, 128))
        rounded = (normed * g_ref[0:1] + s_ref[1:2]).astype(bf16)
        low[here] = rounded
        lowt[:, here] = rounded.T
        ctxt[1, :, here] = ctx_p[here].T
    for a, b in ((p_out, p_out_any), (n1, n1_any), (i1, i1_any), (lowt, lowt_any), (xt, xt_any), (ctxt, ctxt_any)):
        run.here(a, b)

    def inner(side, n, w, b):
        for at in range(n * unit_chunk, (n + 1) * unit_chunk, 256):
            cols = slice(at, at + 256)
            for top in range(0, rows, 128):
                here = slice(top, top + 128)
                value = mm(low[here], w[:, cols]) + b[:, cols]
                cumulative = 0.5 * (1.0 + lax.erf(value * 0.7071067811865476))
                density = jnp.exp(-0.5 * value * value) * 0.3989422804014327
                rounded = (value * cumulative).astype(bf16)
                act[side, here, cols] = rounded
                actt[side, cols, here] = rounded.T
                slope[side, here, cols] = (cumulative + value * density).astype(bf16)

    def branch(side, n, w, first=False):
        cols = slice(n * unit_chunk, (n + 1) * unit_chunk)
        for top in range(0, rows, 128):
            here = slice(top, top + 128)
            value = mm(act[side, here, cols], w[cols])
            part[here] = value if first else part[here] + value

    loads[1].wait()
    loads[2].wait()
    inner(0, 0, w_in, b_in_ref)
    wave(9)
    inner(0, 1, w_in, b_in_ref)
    wave(10)
    inner(0, 2, w_in, b_in_ref)
    for n in range(N_CHUNK):
        branch(0, n, w_back, first=n == 0)
    for copy in b_copies:
        copy.wait_recv()
    wave(11)
    inner(1, 0, p_in, b_in_p)
    inner(1, 1, p_in, b_in_p)
    wave(12)
    inner(1, 2, p_in, b_in_p)
    for a, b in ((actt, actt_any), (slope, slope_any), (p_in, p_in_any)):
        run.here(a, b)
    branch(1, 0, p_back)
    wave(13)
    branch(1, 1, p_back)
    last = slice(2 * unit_chunk, units)
    for at in range(0, rows, 64):
        here = slice(at, at + 64)
        value = mm(act[1, here, last], p_back[last]) + part[here] + s_ref[2:3]
        normed, inv_std = norm_rows(n1[here] * g_ref[0:1] + s_ref[1:2] + value)
        n2[here] = normed
        i2[here] = jnp.broadcast_to(inv_std, (64, 128))
        hidden = (normed * g_ref[1:2] + s_ref[3:4]).astype(bf16)
        own_out[here] = hidden
        firsts[at // 64:at // 64 + 1] = hidden[0:1].astype(f32)

    out_rows = block_out.at[pl.ds(own_base, rows)]
    out_copy = run.remote(own_out, out_rows, near["x"])
    run.here(own_out, out_rows)
    wave(14)

    z, y, c = dp // 4, (dp // 2) % 2, dp % 2
    half = width // 2
    gathered[z, y, c, mp] = jnp.concatenate(
        [
            jnp.concatenate([firsts[:, :half], ids_ref[...]], axis=1),
            jnp.concatenate([firsts[:, half:], ids_ref[...]], axis=1),
        ],
        axis=0,
    ).astype(bf16)
    slot = gathered.at[z, y, c, mp]
    for copy in [run.remote(slot, slot, device) for device in (far[1], far[0], near["z"])]:
        copy.wait_recv()
    slot = gathered.at[:, y, c, mp]
    run.remote(slot, slot, near["y"]).wait_recv()
    slot = gathered.at[:, :, c, mp]
    run.remote(slot, slot, near["x"]).wait_recv()
    slot = gathered.at[:, :, c]
    last_copy = run.remote(slot, slot, near["c"])
    wave(15)
    last_copy.wait_recv()

    for a, b in ((n2, n2_any), (i2, i2_any), (p_back, p_back_any)):
        run.here(a, b)

    @pl.loop(0, 32)
    def _(at):
        values = gathered[at // 8, (at // 4) % 2, (at // 2) % 2, at % 2].astype(f32)
        here = pl.ds(pl.multiple_of(at * 8, 8), 8)
        all_ref[here, :half] = values[:8, :half]
        all_ref[here, half:width] = values[8:, :half]
        all_ref[here, width:] = values[:8, half:]

    loss_passes(
        dp * 2 + mp, scale_ref[0], w_pool_ref, s_ref[4:5],
        loss_ref, gscale_ref, pre_ref, bias_grad_ref, first_grad_ref, firsts_out_ref,
        all_ref, pooled_ref, len_ref, unit_ref, lse_col_ref, lse_row_ref, pre_f_ref,
    )
    new_scale_ref[0] = scale_ref[0] - step_rate * gscale_ref[0]
    per = width // 16
    own_firsts = mm(firsts_out_ref[...], pick(width, dp * per, per).astype(bf16)).astype(bf16)
    pool_ref[...] = mm_tn(own_firsts, pre_ref[...])
    pool_bias_ref[...] = exact(bias_grad_ref[...], pick(width, dp * per, per))
    wave(16)
    out_copy.wait_recv()
    for copy in run.sent:
        copy.wait_send()
    for copy in run.kept[3:]:
        copy.wait()


def forward(x, segc, segr, w_qkv, b_qv, b_in, gains, shifts, ids, w_pool, scale, w_out, w_in, w_back):
    rows, width = x.shape[0] // 2, x.shape[1]
    cols, units = w_qkv.shape[2], w_in.shape[1]
    count = 2 * lax.axis_size("dp") * 8
    any_ = pl.BlockSpec(memory_space=pl.ANY)
    smem = pl.BlockSpec(memory_space=pltpu.SMEM)
    vmem = pl.BlockSpec(memory_space=pltpu.VMEM)
    S = jax.ShapeDtypeStruct
    head = (rows, cols)
    kept = [
        ((2 * rows, width), bf16), (w_qkv.shape, bf16), (w_out.shape, bf16), (w_in.shape, bf16), (w_back.shape, bf16),
        (head, bf16), (head, bf16), (head, bf16),
        ((rows, width), f32), ((rows, 128), f32), ((width, rows), bf16), ((width, rows), bf16), ((2, cols, rows), bf16),
        ((2, units, rows), bf16), ((2, rows, units), bf16), ((rows, width), f32), ((rows, 128), f32),
    ]
    scratch = [
        (w_out.shape, bf16), (w_in.shape, bf16), (w_back.shape, bf16),
        (w_out.shape, bf16), (w_in.shape, bf16), (w_back.shape, bf16), ((1, units), f32),
    ] + [(head, bf16)] * 9 + [
        ((rows, width), f32), ((rows, 128), f32), ((rows, width), bf16),
        ((2, rows, units), bf16), ((2, rows, units), bf16), ((rows, width), f32), ((rows, width), f32),
        ((rows, 128), f32), ((rows, width), bf16),
        ((width, rows), bf16), ((width, rows), bf16), ((2, cols, rows), bf16), ((2, units, rows), bf16),
        ((8, width), f32), ((4, 2, 2, 2, 16, width // 2 + 128), bf16),
        ((count, width), bf16), ((1, width), f32), ((count, width), bf16),
        ((count, width + 128), f32), ((count, width), f32), ((count, 1), f32), ((count, width), bf16),
        ((count, 1), f32), ((1, count), f32), ((count, width), f32),
    ]
    return pl.pallas_call(
        forward_kernel,
        in_specs=[vmem] * 10 + [smem] + [any_] * 4,
        out_specs=[any_] * len(kept) + [smem] * 3 + [vmem] * 4,
        out_shape=tuple(S(*k) for k in kept) + (
            S((1,), f32), S((1,), f32), S((1,), f32), S((8, width), f32), S(b_qv.shape, f32),
            S((width // 16, width), f32), S((1, width // 16), f32),
        ),
        scratch_shapes=[pltpu.VMEM(*s) for s in scratch] + [
            pltpu.SemaphoreType.DMA((80,)), pltpu.SemaphoreType.DMA((80,)), pltpu.SemaphoreType.DMA((24,)),
        ],
        compiler_params=pltpu.CompilerParams(
            vmem_limit_bytes=56 * 1024 * 1024, collective_id=0, has_side_effects=True
        ),
        name="forward",
    )(x, segc, segr, w_qkv, b_qv, b_in, gains, shifts, ids, w_pool, scale, w_qkv, w_out, w_in, w_back)


def pick(size, start, count):
    return (
        lax.broadcasted_iota(jnp.int32, (size, count), 0)
        == start + lax.broadcasted_iota(jnp.int32, (size, count), 1)
    ).astype(f32)


def exact(a, b):
    return jnp.dot(a, b, preferred_element_type=f32, precision=lax.Precision.HIGHEST)


ORDERS = (
    ("x", "y", "z", "w"), ("y", "x", "z", "w"), ("z", "y", "x", "w"),
    ("y", "x", "z", "w"), ("z", "y", "x", "w"), ("y", "x", "z", "w"),
)
TILE = 384


def backward_kernel(
    segc_ref, segr_ref, g_ref, first_grad_ref, b_qv_ref,
    x_any, og_any, n2_any, i2_any, n1_any, i1_any, act_any, slope_any, low_any, xt_any, ctx_any, q_any, k_any, v_any,
    wb_o_any, wb_p_any, wi_o_any, wi_p_any, wo_o_any, wo_p_any, wq_o_any, wq_p_any,
    grad_in_any, o_back, o_in, o_qkv, o_out, o_gains, o_shifts, o_bqv, o_bin,
    one_buf, two_buf, three_buf, grad, i2, n1, i1, act, slope, low, xt, ctx, q, k, v, wb, wi, wo, wq, deltas,
    unit_a, unit_b, got_a, got_b, next_a, next_b, late_a, late_b, last_a, last_b, end_a, end_b, sums, sums_got,
    send_sem, recv_sem, local_sem,
):
    dp, mp = lax.axis_index("dp"), lax.axis_index("mp")
    rows, width = one_buf.shape
    units = slope.shape[2]
    cols = q.shape[2]
    own_base = pl.multiple_of(mp * rows, rows)
    near = {
        "x": {"mp": 1 - mp}, "y": {"dp": flip(dp, 2)}, "z": {"dp": flip(dp, 4)}, "w": {"dp": flip(dp, 8)},
        "c": {"dp": flip(dp, 1)},
    }
    run = Copies(send_sem, recv_sem, local_sem)
    greet(list(near.values()))
    load = lambda pairs: [run.here(a, b) for a, b in pairs]
    own_rows = lambda ref: ref.at[pl.ds(own_base, rows)]
    loads_one = load(((own_rows(og_any), one_buf), (n2_any, grad), (i2_any, i2), (act_any, act)))
    loads_two = load(((wb_o_any, wb.at[0]), (wb_p_any, wb.at[1]), (slope_any, slope)))

    bits = {"y": 2, "z": 4, "w": 8}
    stores = [unit_a.at[n] for n in range(4)] + [unit_b.at[n] for n in range(2)]
    stages = [
        [got_a.at[n], next_a.at[n], late_a.at[n], last_a.at[n], end_a.at[n]] for n in range(4)
    ] + [[got_b.at[n], next_b.at[n], late_b.at[n], last_b.at[n], end_b.at[n]] for n in range(2)]
    flight = {}

    def place(unit, side, dest):
        at = 0
        for weight, name in zip((8, 4, 2, 1), ORDERS[unit]):
            other = side if name == "x" else (dest // bits[name] + dp // bits[name]) % 2
            at = at + weight * other
        return (dest + dp) % 2, at

    def put(unit, side, dest, value, where=slice(None)):
        core, at = place(unit, side, dest)
        stores[unit][core, at, where] = value.astype(bf16)

    def begin(unit):
        flight[unit, 0] = run.remote(stores[unit].at[1], stages[unit][0], near["c"])

    def step(unit, stage):
        flight[unit, stage - 1].wait_recv()
        mine, got = stores[unit].at[0], stages[unit][stage - 1]
        count = 16 >> (stage - 1)
        half = count // 2
        if stage == 5:
            return mine[0].astype(f32) + got[0].astype(f32)
        for at in range(half, count):
            mine[at] = mine[at] + got[at]
        flight[unit, stage] = run.remote(
            mine.at[pl.ds(half, half)], stages[unit][stage], near[ORDERS[unit][stage - 1]]
        )
        for at in range(half):
            mine[at] = mine[at] + got[at]

    def wait(copies):
        for copy in copies:
            copy.wait()

    wait(loads_one[:3])
    gain_two, shift_two, bias_two = 0.0, 0.0, 0.0
    for at in range(0, rows, 64):
        here = slice(at, at + 64)
        is_first = lax.broadcasted_iota(jnp.int32, (64, width), 0) == 0
        value = one_buf[here].astype(f32) + jnp.where(is_first, first_grad_ref[at // 64:at // 64 + 1], 0.0)
        normed = grad[here]
        out = norm_back(value, normed, i2[here, 0:1], g_ref[1:2])
        rounded = out.astype(bf16)
        grad[here] = out
        two_buf[here] = rounded
        gain_two += jnp.sum(value * normed, axis=0, keepdims=True)
        shift_two += jnp.sum(value, axis=0, keepdims=True)
        bias_two += jnp.sum(rounded.astype(f32), axis=0, keepdims=True)
    sums[0] = jnp.zeros(sums.shape[1:], f32)
    sums[0, 1:2] = gain_two
    sums[0, 4:5] = bias_two
    sums[0, 5:6] = shift_two

    def back_weight(side):
        for top in range(0, units, TILE):
            tile = mm(act[side, top:top + TILE], two_buf[...])
            for at in range(0, TILE, 96):
                dest = (top + at) // 96
                put(0, side, dest, tile[at:at + 48])
                put(1, side, dest, tile[at + 48:at + 96])

    wait(loads_one[3:])
    back_weight(0)
    back_weight(1)
    begin(0)
    begin(1)
    loads_three = load(((wi_o_any, wi.at[0]), (wi_p_any, wi.at[1])))
    loads_four = load(((n1_any, n1), (i1_any, i1), (wo_o_any, wo.at[0]), (wo_p_any, wo.at[1])))
    wait(loads_two)

    def inner_grads(side):
        owner = mp + side - 2 * mp * side
        for at in range(0, units, 256):
            here = slice(at, at + 256)
            value = (mm_nt(two_buf[...], wb[side, here]) * slope[side, :, here].astype(f32)).astype(bf16)
            slope[side, :, here] = value
            sums[0, pl.ds(8 + 2 * owner + at // width, 1), at % width:at % width + 256] = jnp.sum(
                value.astype(f32), axis=0, keepdims=True
            )

    inner_grads(0)
    step(0, 1)
    step(1, 1)
    inner_grads(1)
    loads_five = load(((low_any, low), (ctx_any, ctx), (own_rows(x_any), three_buf), (wq_p_any, wq.at[1])))
    wait(loads_three)
    for at in range(0, rows, 128):
        here = slice(at, at + 128)
        grad[here] = grad[here] + mm_nt(slope[0, here], wi[0]) + mm_nt(slope[1, here], wi[1])
    loads_six = load(
        ((q_any, q.at[0]), (k_any, k.at[0]), (v_any, v.at[0]), (xt_any, xt), (wq_o_any, wq.at[0]))
    )

    wait(loads_four)
    gain_one, shift_one, bias_one = 0.0, 0.0, 0.0
    for at in range(0, rows, 64):
        here = slice(at, at + 64)
        value = grad[here]
        normed = n1[here]
        out = norm_back(value, normed, i1[here, 0:1], g_ref[0:1])
        rounded = out.astype(bf16)
        grad[here] = out
        one_buf[here] = rounded
        gain_one += jnp.sum(value * normed, axis=0, keepdims=True)
        shift_one += jnp.sum(value, axis=0, keepdims=True)
        bias_one += jnp.sum(rounded.astype(f32), axis=0, keepdims=True)
    sums[0, 0:1] = gain_one
    sums[0, 2:3] = bias_one
    sums[0, 3:4] = shift_one

    def in_weight(half):
        for side in range(2):
            for top in range(0, width, TILE):
                tile = mm(low[top:top + TILE], slope[side, :, half * width:(half + 1) * width])
                for at in range(0, TILE, 48):
                    put(2 + half, side, (top + at) // 48, tile[at:at + 48])

    wait(loads_five)
    in_weight(0)
    begin(2)
    for side in range(2):
        two_buf[:, side * cols:(side + 1) * cols] = mm_nt(one_buf[...], wo[side]).astype(bf16)
    in_weight(1)
    begin(3)
    step(2, 1)

    q[1] = (mm(three_buf[...], wq[1, 0]) + b_qv_ref[0:1]).astype(bf16)
    k[1] = mm(three_buf[...], wq[1, 1]).astype(bf16)
    v[1] = (mm(three_buf[...], wq[1, 2]) + b_qv_ref[1:2]).astype(bf16)
    step(3, 1)
    wait(loads_six)

    def attend_back(side, groups):
        scale = HEAD_DIM ** (-0.5)
        for group in groups:
            at = slice(group * GROUP, (group + 1) * GROUP)
            here = pl.ds(pl.multiple_of(own_base + group * GROUP, GROUP), GROUP)
            one = segc_ref[here, :] == segr_ref[:, here]
            same = jnp.concatenate([one, one], axis=1)
            for pair in range(cols // PAIR):
                lanes = slice(pair * PAIR, (pair + 1) * PAIR)
                q_two = two_heads(q[side, at, lanes])
                dc_two = two_heads(two_buf[at, side * cols + pair * PAIR:side * cols + (pair + 1) * PAIR])
                k_pair, v_pair = k[side, at, lanes], v[side, at, lanes]
                scores = jnp.where(same, mm_nt(k_pair, q_two) * scale, masked_out)
                shifted = jnp.exp(scores - jnp.max(scores, axis=0, keepdims=True))
                probs = shifted / jnp.sum(shifted, axis=0, keepdims=True)
                prob_grad = mm_nt(v_pair, dc_two)
                score_grad = (
                    probs * (prob_grad - jnp.sum(prob_grad * probs, axis=0, keepdims=True))
                ).astype(bf16)
                deltas[side, 0, at, lanes] = (join_heads(mm_tn(score_grad, k_pair)) * scale).astype(bf16)
                deltas[side, 1, at, lanes] = (mm(score_grad, q_two) * scale).astype(bf16)
                deltas[side, 2, at, lanes] = mm(probs.astype(bf16), dc_two).astype(bf16)

    attend_back(0, (0, 1))
    step(0, 2)
    attend_back(0, (2, 3))
    step(1, 2)
    attend_back(1, (0, 1))
    step(2, 2)
    step(0, 3)
    attend_back(1, (2, 3))
    step(1, 3)

    def qkv_weight(side):
        for s in range(3):
            for top in range(0, width, TILE):
                tile = mm(xt[top:top + TILE], deltas[side, s])
                for at in range(0, TILE, 48):
                    unit, first = ((4, 0), (4, 48), (5, 0))[s]
                    put(unit, side, (top + at) // 48, tile[at:at + 48], slice(first, first + 48))
        tile = mm(ctx[side], one_buf[...])
        for dest in range(16):
            part = tile[dest * 24:(dest + 1) * 24]
            put(5, side, dest, jnp.concatenate([part[:, :cols], part[:, cols:]], axis=0), slice(48, 96))
        owner = mp + side - 2 * mp * side
        lanes = pl.ds(pl.multiple_of(owner * cols, 128), cols)
        sums[0, 6:7, lanes] = jnp.sum(deltas[side, 0].astype(f32), axis=0, keepdims=True)
        sums[0, 7:8, lanes] = jnp.sum(deltas[side, 2].astype(f32), axis=0, keepdims=True)

    qkv_weight(0)
    qkv_weight(1)
    begin(4)
    begin(5)

    def sum_step(stage):
        if stage:
            flight["sums", stage - 1].wait_recv()
            sums[stage] = sums[stage - 1] + sums_got[stage - 1]
        if stage < 5:
            name = ("c", "x", "y", "z", "w")[stage]
            flight["sums", stage] = run.remote(sums.at[stage], sums_got.at[stage], near[name])

    sum_step(0)
    for at in range(0, rows, 128):
        here = slice(at, at + 128)
        value = grad[here]
        for side in range(2):
            for s in range(3):
                value = value + mm_nt(deltas[side, s, here], wq[side, s])
        three_buf[here] = value.astype(bf16)
    last_copy = run.remote(three_buf, own_rows(grad_in_any), near["x"])
    run.here(three_buf, own_rows(grad_in_any))
    sum_step(1)
    step(4, 1)
    step(5, 1)
    step(3, 2)
    step(2, 3)
    step(0, 4)
    step(1, 4)
    sum_step(2)
    step(3, 3)
    step(2, 4)
    o_back[0:48] = step(0, 5)
    o_back[48:96] = step(1, 5)
    step(3, 4)
    sum_step(3)
    step(4, 2)
    step(5, 2)
    o_in[:, :width] = step(2, 5)
    o_in[:, width:] = step(3, 5)
    sum_step(4)
    step(4, 3)
    step(5, 3)
    step(4, 4)
    step(5, 4)
    sum_step(5)

    total = sums[5]
    vectors = exact(total[0:8], pick(width, dp * (width // 16), width // 16))
    o_gains[...] = vectors[0:2]
    o_shifts[...] = vectors[2:6]
    o_bqv[...] = exact(total[0:8], pick(width, mp * cols + dp * (cols // 16), cols // 16))[6:8]
    per = units // 16
    o_bin[...] = exact(sums[5, pl.ds(8 + 2 * mp + dp // 8, 1), :], pick(width, (dp % 8) * per, per))

    value = step(4, 5)
    o_qkv[0] = value[:48]
    o_qkv[1] = value[48:]
    value = step(5, 5)
    o_qkv[2] = value[:48]
    o_out[:, :cols] = value[48:72]
    o_out[:, cols:] = value[72:]
    last_copy.wait_recv()
    for copy in run.sent:
        copy.wait_send()
    run.kept[-1].wait()


def backward(segc, segr, gains, first_grad, b_qv, *arrays):
    rows, width = arrays[2].shape
    units = arrays[7].shape[2]
    cols = arrays[11].shape[1]
    any_ = pl.BlockSpec(memory_space=pl.ANY)
    vmem = pl.BlockSpec(memory_space=pltpu.VMEM)
    S = jax.ShapeDtypeStruct
    per = width // 16
    a, b = (per, width), (2 * per, cols)
    scratch = [((rows, width), bf16)] * 3 + [
        ((rows, width), f32), ((rows, 128), f32), ((rows, width), f32), ((rows, 128), f32),
        ((2, units, rows), bf16), ((2, rows, units), bf16), ((width, rows), bf16), ((width, rows), bf16),
        ((2, cols, rows), bf16), ((2, rows, cols), bf16), ((2, rows, cols), bf16), ((2, rows, cols), bf16),
        ((2, units, width), bf16), ((2, width, units), bf16), ((2, cols, width), bf16), ((2, 3, width, cols), bf16),
        ((2, 3, rows, cols), bf16),
        ((4, 2, 16) + a, bf16), ((2, 2, 16) + b, bf16),
        ((4, 16) + a, bf16), ((2, 16) + b, bf16), ((4, 8) + a, bf16), ((2, 8) + b, bf16),
        ((4, 4) + a, bf16), ((2, 4) + b, bf16), ((4, 2) + a, bf16), ((2, 2) + b, bf16),
        ((4, 1) + a, bf16), ((2, 1) + b, bf16), ((6, 16, width), f32), ((5, 16, width), f32),
    ]
    return pl.pallas_call(
        backward_kernel,
        in_specs=[vmem] * 5 + [any_] * len(arrays),
        out_specs=[any_] + [vmem] * 8,
        out_shape=(
            S((2 * rows, width), bf16), S((2 * per, width), f32), S((per, 2 * width), f32), S((3, per, cols), f32),
            S((cols // 16, width), f32), S((2, per), f32), S((4, per), f32), S((2, cols // 16), f32),
            S((1, units // 16), f32),
        ),
        scratch_shapes=[pltpu.VMEM(*s) for s in scratch] + [
            pltpu.SemaphoreType.DMA((40,)), pltpu.SemaphoreType.DMA((40,)), pltpu.SemaphoreType.DMA((28,)),
        ],
        compiler_params=pltpu.CompilerParams(
            vmem_limit_bytes=63 * 1024 * 1024, collective_id=1, has_side_effects=True
        ),
        name="backward",
    )(segc, segr, gains, first_grad, b_qv, *arrays)


def swap_mp(values):
    return lax.ppermute(values, "mp", [(0, 1), (1, 0)])


def swap_dp(values, bit):
    size = lax.axis_size("dp")
    return lax.ppermute(values, "dp", [(at, at ^ bit) for at in range(size)])


def fetch(own, axis, place):
    size = own.shape[axis] // 4
    first = swap_mp(lax.dynamic_slice_in_dim(own, place * size, size, axis))
    second = swap_dp(first, 2)
    third = swap_dp(first, 1)
    fourth = swap_dp(second, 1)
    whole = jnp.zeros_like(own)
    for bits, part in ((0, first), (2, second), (1, third), (3, fourth)):
        whole = lax.dynamic_update_slice_in_dim(whole, part, (place ^ bits) * size, axis)
    return whole


def gather_rows(rows):
    size = lax.axis_size("dp")
    if size != 16:
        return lax.all_gather(rows, ("dp", "mp"), axis=0, tiled=True)
    rows = jnp.concatenate([rows, swap_mp(rows)], axis=0)
    for bit in (1, 2, 4, 8):
        rows = jnp.concatenate([rows, swap_dp(rows, bit)], axis=0)
    return rows


def both_halves(own, mp):
    other = swap_mp(own)
    return jnp.concatenate([jnp.where(mp == 0, own, other), jnp.where(mp == 0, other, own)], axis=0)


def add(a, b):
    return (a.astype(f32) + b.astype(f32)).astype(a.dtype)


def scatter_sum(keep, send, order):
    size = lax.axis_size("dp")
    if size != 16:
        rest = keep.shape[2:]
        both = jnp.stack([keep, send], axis=2)
        both = both.reshape((2, 16) + rest)
        mine = add(both[0], swap_mp(both[1]))
        return mine
    got = swap_dp(send, 1)
    rest = keep.shape[2:]
    names = ["x", "z1", "z0", "y"]
    keep = keep.reshape((2, 2, 2, 2) + rest)
    got = got.reshape((2, 2, 2, 2) + rest)
    bit_of = {"y": 2, "z0": 4, "z1": 8}
    for name in order:
        axis = names.index(name)
        names.remove(name)
        pick = lambda values, at: lax.index_in_dim(values, at, axis, keepdims=False)
        out = add(pick(keep, 1), pick(got, 1))
        out = swap_mp(out) if name == "x" else swap_dp(out, bit_of[name])
        keep = add(pick(keep, 0), pick(got, 0))
        got = out
    return add(keep, got)


def swap_order(values, axis, place):
    shape = values.shape
    split = values.reshape(shape[:axis] + (2, 2, 2, 2) + shape[axis + 1:])
    for at, bit in enumerate((8, 4, 2, 1)):
        low = lax.index_in_dim(split, 0, axis + at)
        high = lax.index_in_dim(split, 1, axis + at)
        flipped = jnp.concatenate([high, low], axis=axis + at)
        split = jnp.where((place & bit) != 0, flipped, split)
    return split.reshape(shape)


def shards(
    inputs, segment_ids, pair_index, w_qkv, bias_qv, w_out, w_in, bias_in, w_back,
    w_pool, norm_gains, shifts, logit_scale, out_grad,
):
    tok_rows, width = inputs.shape
    size = lax.axis_size("dp")
    dp, mp = lax.axis_index("dp"), lax.axis_index("mp")
    rows = tok_rows // 2
    blocks = rows // SEG_LEN
    place = dp % 4
    slots = 0 * dp
    pos = jnp.reshape(slots, (1,)).astype(jnp.int32)

    x = lax.dynamic_slice_in_dim(inputs, mp * rows, rows, 0)
    cot = lax.dynamic_slice_in_dim(out_grad, mp * rows, rows, 0)
    seg = lax.dynamic_slice_in_dim(segment_ids, mp * rows, rows, 0)
    segc, segr = seg.reshape(rows, 1), seg.reshape(1, rows)
    pairs = lax.dynamic_slice_in_dim(pair_index, mp * blocks, blocks, 0)

    cols = w_qkv.shape[2]
    units = w_in.shape[1]
    ids = jnp.pad(jnp.stack([pairs // 64, pairs % 64], axis=1).astype(f32), ((0, 0), (0, 126)))
    if size == 16:
        segc, segr = segment_ids.reshape(-1, 1), segment_ids.reshape(1, -1)
        (
            block_out, w_qkv_p, w_out_p, w_in_p, w_back_p, q, k, v, n1, i1, lowt, xt, ctxt, actt, slope, n2, i2,
            loss_value, grad_scale, new_scale, first_grad, bias_qv_p, grad_pool, grad_pool_bias,
        ) = forward(
            inputs, segc, segr, w_qkv, bias_qv, bias_in.reshape(1, -1),
            norm_gains, shifts, ids, w_pool, logit_scale, w_out, w_in, w_back,
        )
        grad_inputs, grad_back, grad_in, grad_qkv, grad_out, gains, shift_grads, grad_bias_qv, grad_bias_in = backward(
            segc, segr, norm_gains, first_grad, bias_qv_p,
            inputs, out_grad, n2, i2, n1, i1, actt, slope, lowt, xt, ctxt, q, k, v,
            w_back, w_back_p, w_in, w_in_p, w_out, w_out_p, w_qkv, w_qkv_p,
        )
        return (
            block_out, loss_value, grad_inputs.astype(f32), grad_qkv, grad_bias_qv, grad_out, grad_in,
            grad_bias_in[0], grad_back, grad_pool, gains, shift_grads, grad_pool_bias[0], grad_scale, new_scale,
        )

    biases = swap_mp(bias_qv)
    bias_qv_p, bias_in_p = biases, swap_mp(bias_in)
    w_qkv_p = fetch(w_qkv, 1, place)
    w_out_p = fetch(w_out, 0, place)
    w_in_p = fetch(w_in, 0, place)
    w_back_p = fetch(w_back, 0, place)

    q_o, k_o, v_o, ctx_o = attention_half(x, w_qkv, bias_qv, segc, segr)
    q_p, k_p, v_p, ctx_p = attention_half(x, w_qkv_p, bias_qv_p, segc, segr)
    normed_one, inv_one, low_one = first_norm(ctx_o, ctx_p, w_out, w_out_p, x, norm_gains, shifts)
    act_o, slope_o = inner_half(low_one, w_in, bias_in.reshape(1, -1))
    part = branch_half(act_o, w_back)
    act_p, slope_p = inner_half(low_one, w_in_p, bias_in_p.reshape(1, -1))
    normed_two, inv_two, own_out = second_norm(act_p, w_back_p, part, normed_one, norm_gains, shifts)

    firsts = own_out.reshape(blocks, SEG_LEN, width)[:, 0]
    rel = gather_rows(jnp.concatenate([firsts, ids.astype(bf16)], axis=1))
    linear = dp * 2 + mp
    position = jnp.stack([linear if size == 16 else 0 * linear, linear]).astype(jnp.int32)
    loss_value, grad_scale, pre_all, pool_bias, first_grad, firsts_all = pair_loss(
        position, rel, w_pool, shifts[4:5], logit_scale
    )
    block_out = both_halves(own_out, mp)
    pool_rows = width // size
    grad_pool = lax.dot_general(
        lax.dynamic_slice_in_dim(firsts_all, dp * pool_rows, pool_rows, 1), pre_all, TN, preferred_element_type=f32
    )
    grad_pool_bias = lax.dynamic_slice_in_dim(pool_bias[0], dp * pool_rows, pool_rows, 0)

    grad_two, branch, sums_two = second_back(cot, first_grad, normed_two, inv_two, norm_gains)
    keep_bo, send_bo = back_weight(pos, act_o, branch)
    keep_bp, send_bp = back_weight(pos, act_p, branch)
    keep_io, send_io, bias_io, part_one = inner_back(pos, branch, w_back, slope_o, low_one, w_in, grad_two)
    keep_ip, send_ip, bias_ip, part_two = inner_back(pos, branch, w_back_p, slope_p, low_one, w_in_p, part_one)
    grad_one, sums_one, dc_o, dc_p, keep_w, send_w = first_back(
        pos, part_two, normed_one, inv_one, norm_gains, ctx_o, ctx_p, w_out, w_out_p
    )
    keep_qo, send_qo, bias_qo, in_one = attention_back(pos, x, w_qkv, segc, segr, q_o, k_o, v_o, dc_o, grad_one)
    keep_qp, send_qp, bias_qp, in_two = attention_back(pos, x, w_qkv_p, segc, segr, q_p, k_p, v_p, dc_p, in_one)

    both = lambda a, b: jnp.stack([a, b])
    mine_back = scatter_sum(both(keep_bo, keep_bp), both(send_bo, send_bp), ("x", "y", "z0", "z1"))
    mine_in = scatter_sum(both(keep_io, keep_ip), both(send_io, send_ip), ("y", "x", "z0", "z1"))
    mine_out = scatter_sum(keep_w, send_w, ("x", "y", "z0", "z1"))
    mine_qkv = scatter_sum(both(keep_qo, keep_qp), both(send_qo, send_qp), ("y", "x", "z0", "z1"))

    vectors = jnp.concatenate([sums_one[0:1], sums_two[0:1], sums_one[2:3], sums_one[1:2], sums_two[2:3], sums_two[1:2]])
    by_dp = vectors.reshape(6, 16, width // 16).transpose(1, 0, 2).reshape(16, -1)
    by_dp = jnp.broadcast_to(by_dp[None], (2,) + by_dp.shape)
    bias_q = both(bias_qo, bias_qp).reshape(2, 2, 16, cols // 16).transpose(0, 2, 1, 3).reshape(2, 16, -1)
    bias_i = both(bias_io, bias_ip).reshape(2, 16, units // 16)
    packed = jnp.concatenate([by_dp, bias_q, bias_i], axis=2)
    packed = swap_order(packed, 1, slots).reshape(2, 8, 2, -1)
    mine_small = scatter_sum(packed[:, :, 0], packed[:, :, 1], ("y", "x", "z0", "z1"))

    if size != 16:
        fold = lambda values: lax.psum_scatter(values, "dp", scatter_dimension=0, tiled=True)
        grad_back = fold(mine_back.reshape(units, width).astype(f32))
        grad_in = fold(mine_in.reshape(width, units).astype(f32))
        grad_qkv = fold(mine_qkv.transpose(0, 2, 1, 3).reshape(width, 3, cols).astype(f32)).transpose(1, 0, 2)
        small = mine_small
        n_vec = 6 * (width // 16)
        n_q = 2 * (cols // 16)
        n_i = units // 16
        vec = small[:, :n_vec].reshape(16, 6, -1).transpose(0, 2, 1).reshape(width, 6)
        vec = fold(vec).T
        grad_bias_qv = fold(small[:, n_vec:n_vec + n_q].reshape(16, 2, -1).transpose(0, 2, 1).reshape(cols, 2)).T
        grad_bias_in = fold(small[:, n_vec + n_q:n_vec + n_q + n_i].reshape(units))
        grad_out = fold(mine_out.reshape(cols, width).astype(f32))
    else:
        grad_back = mine_back.astype(f32)
        grad_in = mine_in.astype(f32)
        grad_qkv = mine_qkv.astype(f32)
        small = mine_small
        n_vec = 6 * (width // 16)
        n_q = 2 * (cols // 16)
        n_i = units // 16
        vec = small[:n_vec].reshape(6, -1)
        grad_bias_qv = small[n_vec:n_vec + n_q].reshape(2, -1)
        grad_bias_in = small[n_vec + n_q:n_vec + n_q + n_i]
        grad_out = mine_out.astype(f32)

    grad_inputs = both_halves(in_two.astype(bf16), mp).astype(f32)
    new_scale = logit_scale - step_rate * grad_scale
    return (
        block_out, loss_value, grad_inputs, grad_qkv, grad_bias_qv, grad_out, grad_in, grad_bias_in,
        grad_back, grad_pool, vec[:2], vec[2:], grad_pool_bias, grad_scale, new_scale,
    )


def solution(mesh):
    return jax.shard_map(
        shards,
        mesh=mesh,
        in_specs=(
            P("dp", None), P("dp"), P("dp"), P(None, None, "mp"), P(None, "mp"), P("mp", None), P(None, "mp"),
            P("mp"), P("mp", None), P(), P(), P(), P(), P("dp", None),
        ),
        out_specs=(
            P("dp", None), P(), P("dp", None), P(None, "dp", "mp"), P(None, ("mp", "dp")), P(("mp", "dp"), None),
            P("dp", "mp"), P(("mp", "dp")), P(("mp", "dp"), None), P("dp", None), P(None, "dp"), P(None, "dp"),
            P("dp"), P(), P(),
        ),
        check_vma=False,
    )
```

```python
from functools import partial

import jax
import jax.numpy as jnp
from jax import lax
from jax.experimental import pallas as pl
from jax.experimental.pallas import tpu as pltpu
from jax.sharding import PartitionSpec as P

HEAD_DIM = 64
SEG_LEN = 64
PAIR = 2 * HEAD_DIM
GROUP = 128

epsilon = 1e-12
margin = 0.3
step_rate = 0.1
masked_out = -1e30
f32 = jnp.float32
bf16 = jnp.bfloat16

NT = (((1,), (1,)), ((), ()))
TN = (((0,), (0,)), ((), ()))


def mm(a, b):
    return jnp.dot(a, b, preferred_element_type=f32)


def mm_nt(a, b):
    return lax.dot_general(a, b, NT, preferred_element_type=f32)


def mm_tn(a, b):
    return lax.dot_general(a, b, TN, preferred_element_type=f32)


def params(mib=40):
    return pltpu.CompilerParams(vmem_limit_bytes=mib * 1024 * 1024)


def cost(flops, moved):
    return pl.CostEstimate(flops=int(flops), bytes_accessed=int(moved), transcendentals=0)


def lane_masks():
    lane = lax.broadcasted_iota(jnp.int32, (1, PAIR), 1)
    first = (lane < HEAD_DIM).astype(f32)
    return first, 1.0 - first


def two_heads(rows):
    first, second = lane_masks()
    return jnp.concatenate([rows * first.astype(bf16), rows * second.astype(bf16)], axis=0)


def join_heads(both):
    first, second = lane_masks()
    half = both.shape[0] // 2
    return both[:half] * first + both[half:] * second


def pair_probs(q_two, k_pair, same):
    scores = mm_nt(q_two, k_pair) * (HEAD_DIM ** (-0.5))
    scores = jnp.where(same, scores, masked_out)
    shifted = jnp.exp(scores - jnp.max(scores, axis=1, keepdims=True))
    return shifted / jnp.sum(shifted, axis=1, keepdims=True)


def same_segment(seg_col, seg_row, rows):
    own = seg_col[rows, :]
    other = seg_row[:, rows]
    one = own == other
    return jnp.concatenate([one, one], axis=0)


def attention_kernel(x_ref, w_ref, b_ref, segc_ref, segr_ref, q_ref, k_ref, v_ref, c_ref):
    x = x_ref[...]
    q_ref[...] = (mm(x, w_ref[0]) + b_ref[0:1]).astype(bf16)
    k_ref[...] = mm(x, w_ref[1]).astype(bf16)
    v_ref[...] = (mm(x, w_ref[2]) + b_ref[1:2]).astype(bf16)
    for group in range(x.shape[0] // GROUP):
        rows = slice(group * GROUP, (group + 1) * GROUP)
        same = same_segment(segc_ref, segr_ref, rows)
        for pair in range(q_ref.shape[1] // PAIR):
            cols = slice(pair * PAIR, (pair + 1) * PAIR)
            probs = pair_probs(two_heads(q_ref[rows, cols]), k_ref[rows, cols], same)
            c_ref[rows, cols] = join_heads(mm(probs.astype(bf16), v_ref[rows, cols])).astype(bf16)


def attention_half(x, w, b, segc, segr):
    rows, cols = x.shape[0], w.shape[2]
    out = jax.ShapeDtypeStruct((rows, cols), bf16)
    return pl.pallas_call(
        attention_kernel,
        out_shape=(out,) * 4,
        compiler_params=params(),
        cost_estimate=cost(2 * rows * 768 * cols * 3 * 2, 6 * rows * cols * 2),
        name="attention",
    )(x, w, b, segc, segr)


def norm_rows(values):
    row_mean = jnp.mean(values, axis=-1, keepdims=True)
    centred = values - row_mean
    inv_std = lax.rsqrt(jnp.mean(centred * centred, axis=-1, keepdims=True) + epsilon)
    return centred * inv_std, inv_std


def norm_back(grad, normed, inv_std, gain):
    scaled = grad * gain
    return inv_std * (
        scaled
        - jnp.mean(scaled, axis=-1, keepdims=True)
        - normed * jnp.mean(scaled * normed, axis=-1, keepdims=True)
    )


def first_norm_kernel(co_ref, cp_ref, wo_ref, wp_ref, x_ref, g_ref, s_ref, n_ref, inv_ref, low_ref):
    for at in range(0, x_ref.shape[0], 128):
        rows = slice(at, at + 128)
        attended = mm(co_ref[rows], wo_ref[...]) + mm(cp_ref[rows], wp_ref[...]) + s_ref[0:1]
        normed, inv_std = norm_rows(x_ref[rows].astype(f32) + attended)
        n_ref[rows] = normed
        inv_ref[rows] = inv_std
        low_ref[rows] = (normed * g_ref[0:1] + s_ref[1:2]).astype(bf16)


def first_norm(ctx_o, ctx_p, wo, wp, x, gains, shifts):
    rows, width = x.shape
    return pl.pallas_call(
        first_norm_kernel,
        out_shape=(
            jax.ShapeDtypeStruct((rows, width), f32),
            jax.ShapeDtypeStruct((rows, 1), f32),
            jax.ShapeDtypeStruct((rows, width), bf16),
        ),
        compiler_params=params(),
        cost_estimate=cost(2 * rows * width * width, 12 * rows * width),
        name="first_norm",
    )(ctx_o, ctx_p, wo, wp, x, gains, shifts)


def inner_kernel(h_ref, w_ref, b_ref, act_ref, slope_ref):
    for at in range(0, h_ref.shape[0], 128):
        rows = slice(at, at + 128)
        inner = mm(h_ref[rows], w_ref[...]) + b_ref[...]
        cumulative = 0.5 * (1.0 + lax.erf(inner * 0.7071067811865476))
        density = jnp.exp(-0.5 * inner * inner) * 0.3989422804014327
        act_ref[rows] = (inner * cumulative).astype(bf16)
        slope_ref[rows] = (cumulative + inner * density).astype(bf16)


def inner_half(low, w, b):
    rows, width = low.shape
    units = w.shape[1]
    tile = 256
    out = jax.ShapeDtypeStruct((rows, units), bf16)
    return pl.pallas_call(
        inner_kernel,
        grid=(units // tile,),
        in_specs=[
            pl.BlockSpec((rows, width), lambda n: (0, 0)),
            pl.BlockSpec((width, tile), lambda n: (0, n)),
            pl.BlockSpec((1, tile), lambda n: (0, n)),
        ],
        out_specs=[pl.BlockSpec((rows, tile), lambda n: (0, n))] * 2,
        out_shape=(out, out),
        compiler_params=params(),
        cost_estimate=cost(4 * rows * width * units, 8 * rows * units),
        name="inner",
    )(low, w, b)


def branch_kernel(act_ref, w_ref, out_ref):
    for at in range(0, act_ref.shape[0], 128):
        rows = slice(at, at + 128)
        out_ref[rows] = mm(act_ref[rows], w_ref[...])


def branch_half(act, w):
    rows, units = act.shape
    width = w.shape[1]
    return pl.pallas_call(
        branch_kernel,
        out_shape=jax.ShapeDtypeStruct((rows, width), f32),
        compiler_params=params(),
        cost_estimate=cost(2 * rows * width * units, 4 * rows * units),
        name="branch",
    )(act, w)


def second_norm_kernel(act_ref, w_ref, part_ref, n1_ref, g_ref, s_ref, n_ref, inv_ref, out_ref):
    for at in range(0, act_ref.shape[0], 128):
        rows = slice(at, at + 128)
        branch = mm(act_ref[rows], w_ref[...]) + part_ref[rows] + s_ref[2:3]
        hidden_one = n1_ref[rows] * g_ref[0:1] + s_ref[1:2]
        normed, inv_std = norm_rows(hidden_one + branch)
        n_ref[rows] = normed
        inv_ref[rows] = inv_std
        out_ref[rows] = (normed * g_ref[1:2] + s_ref[3:4]).astype(bf16)


def second_norm(act, w, part, normed_one, gains, shifts):
    rows, units = act.shape
    width = w.shape[1]
    return pl.pallas_call(
        second_norm_kernel,
        out_shape=(
            jax.ShapeDtypeStruct((rows, width), f32),
            jax.ShapeDtypeStruct((rows, 1), f32),
            jax.ShapeDtypeStruct((rows, width), bf16),
        ),
        compiler_params=params(),
        cost_estimate=cost(2 * rows * width * units, 4 * rows * units),
        name="second_norm",
    )(act, w, part, normed_one, gains, shifts)


def loss_kernel(
    pos_ref, rel_ref, w_ref, bias_ref, scale_ref,
    loss_ref, gscale_ref, pre_ref, bias_grad_ref, first_grad_ref, firsts_out_ref,
    all_ref, pooled_ref, len_ref, unit_ref, lse_col_ref, lse_row_ref, pre_f_ref,
):
    @pl.loop(0, pooled_ref.shape[0] // 8)
    def _(slot):
        source = pl.multiple_of(slot * 8, 8)
        target = pl.multiple_of(jnp.bitwise_xor(slot, pos_ref[0]) * 8, 8)
        all_ref[pl.ds(target, 8), :] = rel_ref[pl.ds(source, 8), :].astype(f32)

    loss_passes(
        pos_ref[1], scale_ref[0], w_ref, bias_ref[...],
        loss_ref, gscale_ref, pre_ref, bias_grad_ref, first_grad_ref, firsts_out_ref,
        all_ref, pooled_ref, len_ref, unit_ref, lse_col_ref, lse_row_ref, pre_f_ref,
    )


def loss_passes(
    here, scale, w_ref, bias,
    loss_ref, gscale_ref, pre_ref, bias_grad_ref, first_grad_ref, firsts_out_ref,
    all_ref, pooled_ref, len_ref, unit_ref, lse_col_ref, lse_row_ref, pre_f_ref,
):
    count, width = pooled_ref.shape
    chunk = min(count, 256)
    steps = count // chunk

    def pool(at):
        firsts = all_ref[pl.ds(at, chunk), :width].astype(bf16)
        firsts_out_ref[pl.ds(at, chunk), :] = firsts
        pooled = jnp.tanh(mm(firsts, w_ref[...]) + bias)
        inv_len = lax.rsqrt(jnp.sum(pooled * pooled, axis=-1, keepdims=True) + 1e-06)
        pooled_ref[pl.ds(at, chunk), :] = pooled
        len_ref[pl.ds(at, chunk), :] = inv_len
        unit_ref[pl.ds(at, chunk), :] = (pooled * inv_len).astype(bf16)

    def positions(at):
        own = at + lax.broadcasted_iota(jnp.int32, (chunk, count), 0)
        other = lax.broadcasted_iota(jnp.int32, (chunk, count), 1)
        paired = all_ref[pl.ds(at, chunk), width:width + 1] * 64.0 + all_ref[pl.ds(at, chunk), width + 1:width + 2]
        positive = paired.astype(jnp.int32) == other
        return own == other, positive

    def logits_of(at):
        cosine = mm_nt(unit_ref[pl.ds(at, chunk), :], unit_ref[...])
        own, positive = positions(at)
        shifted = cosine - jnp.where(positive, margin, 0.0)
        return shifted, own, positive

    def first_pass(at, run):
        shifted, own, positive = logits_of(at)
        logits = jnp.where(own, masked_out, scale * shifted)
        top = jnp.max(logits, axis=1, keepdims=True)
        lse = top + jnp.log(jnp.sum(jnp.exp(logits - top), axis=1, keepdims=True))
        lse_col_ref[pl.ds(at, chunk), :] = lse
        eye = lax.broadcasted_iota(jnp.int32, (chunk, chunk), 0) == lax.broadcasted_iota(
            jnp.int32, (chunk, chunk), 1
        )
        lse_row_ref[:, pl.ds(at, chunk)] = jnp.sum(jnp.where(eye, lse, 0.0), axis=0, keepdims=True)
        return run + jnp.sum(lse) - jnp.sum(jnp.where(positive, logits, 0.0))

    def second_pass(at, run):
        run_scale, run_bias = run
        shifted, own, positive = logits_of(at)
        logits = scale * shifted
        factor = 1.0 / (2.0 * count)
        grad = (
            jnp.exp(logits - lse_col_ref[pl.ds(at, chunk), :])
            + jnp.exp(logits - lse_row_ref[...])
            - jnp.where(positive, 2.0, 0.0)
        ) * factor
        grad = jnp.where(own, 0.0, grad)
        run_scale = run_scale + jnp.sum(grad * shifted)
        unit_grad = 2.0 * mm((scale * grad).astype(bf16), unit_ref[...])
        pooled = pooled_ref[pl.ds(at, chunk), :]
        inv_len = len_ref[pl.ds(at, chunk), :]
        along = jnp.sum(pooled * unit_grad, axis=-1, keepdims=True)
        pooled_grad = inv_len * unit_grad - pooled * (inv_len * inv_len * inv_len) * along
        pre_grad = (pooled_grad * (1.0 - pooled * pooled)).astype(bf16)
        pre_ref[pl.ds(at, chunk), :] = pre_grad
        pre_f_ref[pl.ds(at, chunk), :] = pre_grad.astype(f32)
        return run_scale, run_bias + jnp.sum(pre_grad.astype(f32), axis=0, keepdims=True)

    def each(body, run):
        if steps == 1:
            return body(0, run)
        return lax.fori_loop(0, steps, lambda s, r: body(pl.multiple_of(s * chunk, chunk), r), run)

    each(lambda at, run: (pool(at), run)[1], 0)
    total = each(first_pass, jnp.float32(0.0))
    run_scale, run_bias = each(second_pass, (jnp.float32(0.0), jnp.zeros((1, width), f32)))
    loss_ref[0] = total / count
    gscale_ref[0] = run_scale
    bias_grad_ref[...] = run_bias
    own_rows = pre_f_ref[pl.ds(pl.multiple_of(here * 8, 8), 8), :].astype(bf16)
    first_grad_ref[...] = mm_nt(own_rows, w_ref[...])


def pair_loss(position, rel, w_pool, bias, scale):
    count, wide = rel.shape
    width = w_pool.shape[0]
    smem = pl.BlockSpec(memory_space=pltpu.SMEM)
    vmem = pl.BlockSpec(memory_space=pltpu.VMEM)
    return pl.pallas_call(
        loss_kernel,
        in_specs=[smem, vmem, vmem, vmem, smem],
        out_specs=[smem, smem, vmem, vmem, vmem, vmem],
        out_shape=(
            jax.ShapeDtypeStruct((1,), f32),
            jax.ShapeDtypeStruct((1,), f32),
            jax.ShapeDtypeStruct((count, width), bf16),
            jax.ShapeDtypeStruct((1, width), f32),
            jax.ShapeDtypeStruct((8, width), f32),
            jax.ShapeDtypeStruct((count, width), bf16),
        ),
        scratch_shapes=[
            pltpu.VMEM((count, wide), f32),
            pltpu.VMEM((count, width), f32),
            pltpu.VMEM((count, 1), f32),
            pltpu.VMEM((count, width), bf16),
            pltpu.VMEM((count, 1), f32),
            pltpu.VMEM((1, count), f32),
            pltpu.VMEM((count, width), f32),
        ],
        compiler_params=params(56),
        cost_estimate=cost(2e9, 4e6),
        name="pair_loss",
    )(position, rel, w_pool, bias, scale)


def put_slabs(pos_ref, source, keep_ref, send_ref, lead):
    slab = source.shape[0] // 16
    for place in range(16):
        at = pl.multiple_of(jnp.bitwise_xor(pos_ref[0], place) * slab, slab)
        target = send_ref if place % 2 else keep_ref
        target[lead + (place // 2,)] = source[pl.ds(at, slab), :].astype(bf16)


def second_back_kernel(
    og_ref, fg_ref, n_ref, inv_ref, g_ref, grad_ref, low_ref, sums_ref
):
    rows_all, width = og_ref.shape
    sums_ref[...] = jnp.zeros_like(sums_ref)
    for at in range(0, rows_all, 64):
        rows = slice(at, at + 64)
        block = at // 64
        is_first = lax.broadcasted_iota(jnp.int32, (64, width), 0) == 0
        grad = og_ref[rows].astype(f32) + jnp.where(is_first, fg_ref[block:block + 1], 0.0)
        normed = n_ref[rows]
        value = norm_back(grad, normed, inv_ref[rows], g_ref[1:2])
        low = value.astype(bf16)
        grad_ref[rows] = value
        low_ref[rows] = low
        sums_ref[0:1] += jnp.sum(grad * normed, axis=0, keepdims=True)
        sums_ref[1:2] += jnp.sum(grad, axis=0, keepdims=True)
        sums_ref[2:3] += jnp.sum(low.astype(f32), axis=0, keepdims=True)


def second_back(out_grad, first_grad, normed, inv_std, gains):
    rows, width = out_grad.shape
    return pl.pallas_call(
        second_back_kernel,
        out_shape=(
            jax.ShapeDtypeStruct((rows, width), f32),
            jax.ShapeDtypeStruct((rows, width), bf16),
            jax.ShapeDtypeStruct((8, width), f32),
        ),
        compiler_params=params(),
        cost_estimate=cost(20 * rows * width, 12 * rows * width),
        name="second_back",
    )(out_grad, first_grad, normed, inv_std, gains)


def slab_shape(rows, cols):
    return jax.ShapeDtypeStruct((8, rows // 16, cols), bf16)


def back_weight_kernel(pos_ref, act_ref, branch_ref, keep_ref, send_ref, whole):
    for at in range(0, whole.shape[0], 256):
        rows = slice(at, at + 256)
        whole[rows] = mm_tn(act_ref[:, rows], branch_ref[...])
    put_slabs(pos_ref, whole, keep_ref, send_ref, ())


def back_weight(pos, act, branch):
    rows, units = act.shape
    width = branch.shape[1]
    smem = pl.BlockSpec(memory_space=pltpu.SMEM)
    vmem = pl.BlockSpec(memory_space=pltpu.VMEM)
    return pl.pallas_call(
        back_weight_kernel,
        in_specs=[smem, vmem, vmem],
        out_specs=[vmem, vmem],
        out_shape=(slab_shape(units, width),) * 2,
        scratch_shapes=[pltpu.VMEM((units, width), f32)],
        compiler_params=params(),
        cost_estimate=cost(2 * rows * width * units, 4 * units * width),
        name="back_weight",
    )(pos, act, branch)


def inner_back_kernel(pos_ref, branch_ref, wb_ref, slope_ref, low_ref, wi_ref, part_ref,
                      keep_ref, send_ref, bias_ref, out_ref, grad, whole):
    units = slope_ref.shape[1]
    for at in range(0, units, 256):
        cols = slice(at, at + 256)
        inner_grad = (mm_nt(branch_ref[...], wb_ref[cols]) * slope_ref[:, cols].astype(f32)).astype(bf16)
        grad[:, cols] = inner_grad
        bias_ref[:, cols] = jnp.sum(inner_grad.astype(f32), axis=0, keepdims=True)
        whole[:, cols] = mm_tn(low_ref[...], inner_grad)
    put_slabs(pos_ref, whole, keep_ref, send_ref, ())
    for at in range(0, low_ref.shape[0], 128):
        rows = slice(at, at + 128)
        out_ref[rows] = part_ref[rows] + mm_nt(grad[rows], wi_ref[...])


def inner_back(pos, branch, w_back, slope, low, w_in, part):
    rows, units = slope.shape
    width = low.shape[1]
    smem = pl.BlockSpec(memory_space=pltpu.SMEM)
    vmem = pl.BlockSpec(memory_space=pltpu.VMEM)
    return pl.pallas_call(
        inner_back_kernel,
        in_specs=[smem] + [vmem] * 6,
        out_specs=[vmem] * 4,
        out_shape=(slab_shape(width, units),) * 2
        + (jax.ShapeDtypeStruct((1, units), f32), jax.ShapeDtypeStruct((rows, width), f32)),
        scratch_shapes=[pltpu.VMEM((rows, units), bf16), pltpu.VMEM((width, units), f32)],
        compiler_params=params(),
        cost_estimate=cost(6 * rows * width * units, 4 * units * width),
        name="inner_back",
    )(pos, branch, w_back, slope, low, w_in, part)


def first_back_kernel(pos_ref, grad_ref, n_ref, inv_ref, g_ref, co_ref, cp_ref, wo_ref, wp_ref,
                      one_ref, sums_ref, dco_ref, dcp_ref, keep_ref, send_ref, low, whole):
    width = grad_ref.shape[1]
    sums_ref[...] = jnp.zeros_like(sums_ref)
    for at in range(0, grad_ref.shape[0], 128):
        rows = slice(at, at + 128)
        grad = grad_ref[rows]
        normed = n_ref[rows]
        value = norm_back(grad, normed, inv_ref[rows], g_ref[0:1])
        low_rows = value.astype(bf16)
        one_ref[rows] = value
        low[rows] = low_rows
        dco_ref[rows] = mm_nt(low_rows, wo_ref[...]).astype(bf16)
        dcp_ref[rows] = mm_nt(low_rows, wp_ref[...]).astype(bf16)
        sums_ref[0:1] += jnp.sum(grad * normed, axis=0, keepdims=True)
        sums_ref[1:2] += jnp.sum(grad, axis=0, keepdims=True)
        sums_ref[2:3] += jnp.sum(low_rows.astype(f32), axis=0, keepdims=True)
    for side, ctx_ref in enumerate((co_ref, cp_ref)):
        whole[...] = mm_tn(ctx_ref[...], low[...])
        put_slabs(pos_ref, whole, keep_ref.at[side], send_ref.at[side], ())


def first_back(pos, grad, normed, inv_std, gains, ctx_o, ctx_p, wo, wp):
    rows, width = grad.shape
    cols = ctx_o.shape[1]
    smem = pl.BlockSpec(memory_space=pltpu.SMEM)
    vmem = pl.BlockSpec(memory_space=pltpu.VMEM)
    return pl.pallas_call(
        first_back_kernel,
        in_specs=[smem] + [vmem] * 8,
        out_specs=[vmem] * 6,
        out_shape=(
            jax.ShapeDtypeStruct((rows, width), f32),
            jax.ShapeDtypeStruct((8, width), f32),
            jax.ShapeDtypeStruct((rows, cols), bf16),
            jax.ShapeDtypeStruct((rows, cols), bf16),
        )
        + (jax.ShapeDtypeStruct((2, 8, cols // 16, width), bf16),) * 2,
        scratch_shapes=[pltpu.VMEM((rows, width), bf16), pltpu.VMEM((cols, width), f32)],
        compiler_params=params(),
        cost_estimate=cost(8 * rows * width * cols, 12 * rows * width),
        name="first_back",
    )(pos, grad, normed, inv_std, gains, ctx_o, ctx_p, wo, wp)


def attention_back_kernel(pos_ref, x_ref, w_ref, segc_ref, segr_ref, q_ref, k_ref, v_ref, dc_ref, part_ref,
                          keep_ref, send_ref, bias_ref, out_ref, dq, dk, dv, whole):
    scale = HEAD_DIM ** (-0.5)
    for group in range(x_ref.shape[0] // GROUP):
        rows = slice(group * GROUP, (group + 1) * GROUP)
        same = same_segment(segc_ref, segr_ref, rows)
        for pair in range(q_ref.shape[1] // PAIR):
            cols = slice(pair * PAIR, (pair + 1) * PAIR)
            q_two = two_heads(q_ref[rows, cols])
            dc_two = two_heads(dc_ref[rows, cols])
            k_pair = k_ref[rows, cols]
            probs = pair_probs(q_two, k_pair, same)
            prob_grad = mm_nt(dc_two, v_ref[rows, cols])
            score_grad = (
                probs * (prob_grad - jnp.sum(prob_grad * probs, axis=1, keepdims=True))
            ).astype(bf16)
            dq[rows, cols] = (join_heads(mm(score_grad, k_pair)) * scale).astype(bf16)
            dk[rows, cols] = (mm_tn(score_grad, q_two) * scale).astype(bf16)
            dv[rows, cols] = mm_tn(probs.astype(bf16), dc_two).astype(bf16)
    bias_ref[0:1] = jnp.sum(dq[...].astype(f32), axis=0, keepdims=True)
    bias_ref[1:2] = jnp.sum(dv[...].astype(f32), axis=0, keepdims=True)
    for s, grad in enumerate((dq, dk, dv)):
        whole[...] = mm_tn(x_ref[...], grad[...])
        put_slabs_at(pos_ref, whole, keep_ref, send_ref, s)
    for at in range(0, x_ref.shape[0], 128):
        rows = slice(at, at + 128)
        out_ref[rows] = (
            part_ref[rows] + mm_nt(dq[rows], w_ref[0]) + mm_nt(dk[rows], w_ref[1]) + mm_nt(dv[rows], w_ref[2])
        )


def put_slabs_at(pos_ref, source, keep_ref, send_ref, s):
    slab = source.shape[0] // 16
    for place in range(16):
        at = pl.multiple_of(jnp.bitwise_xor(pos_ref[0], place) * slab, slab)
        target = send_ref if place % 2 else keep_ref
        target[place // 2, s] = source[pl.ds(at, slab), :].astype(bf16)


def attention_back(pos, x, w, segc, segr, q, k, v, dc, part):
    rows, width = x.shape
    cols = q.shape[1]
    smem = pl.BlockSpec(memory_space=pltpu.SMEM)
    vmem = pl.BlockSpec(memory_space=pltpu.VMEM)
    slabs = jax.ShapeDtypeStruct((8, 3, width // 16, cols), bf16)
    return pl.pallas_call(
        attention_back_kernel,
        in_specs=[smem] + [vmem] * 9,
        out_specs=[vmem] * 4,
        out_shape=(slabs, slabs, jax.ShapeDtypeStruct((2, cols), f32), jax.ShapeDtypeStruct((rows, width), f32)),
        scratch_shapes=[pltpu.VMEM((rows, cols), bf16)] * 3 + [pltpu.VMEM((width, cols), f32)],
        compiler_params=params(),
        cost_estimate=cost(20 * rows * width * cols, 4 * 3 * width * cols),
        name="attention_back",
    )(pos, x, w, segc, segr, q, k, v, dc, part)


def flip(value, bit):
    return value + bit - 2 * bit * ((value // bit) % 2)


class Copies:
    def __init__(self, send, recv, local):
        self.send, self.recv, self.local = send, recv, local
        self.sent, self.kept = [], []

    def remote(self, source, target, device):
        at = len(self.sent)
        copy = pltpu.make_async_remote_copy(
            src_ref=source, dst_ref=target, send_sem=self.send.at[at], recv_sem=self.recv.at[at],
            device_id=device, device_id_type=pl.DeviceIdType.MESH,
        )
        copy.start()
        self.sent.append(copy)
        return copy

    def here(self, source, target):
        copy = pltpu.make_async_copy(source, target, self.local.at[len(self.kept)])
        copy.start()
        self.kept.append(copy)
        return copy


def greet(devices):
    barrier = pltpu.get_barrier_semaphore()
    for device in devices:
        pl.semaphore_signal(barrier, inc=1, device_id=device, device_id_type=pl.DeviceIdType.MESH)
    pl.semaphore_wait(barrier, len(devices))


def same_block(row):
    across = jnp.broadcast_to(row.astype(f32), (GROUP, GROUP))
    return across == across.T


def arrive(*copies):
    for copy in copies:
        copy.wait_recv()


N_CHUNK = 3


def forward_kernel(
    x_ref, segr_ref, w_qkv_ref, b_qv_ref, b_in_ref, g_ref, s_ref, w_pool_ref, scale_ref, pairs_ref,
    w_qkv_any, w_out_any, w_in_any, w_back_any,
    block_out, p_qkv, p_out_any, p_in_any, p_back_any, q_any, k_any, v_any, n1_any, i1_any, lowt_any, xt_any, ctxt_any,
    actt_any, slope_any, n2_any, i2_any,
    loss_ref, gscale_ref, new_scale_ref, first_grad_ref, b_qv_p, pool_ref, pool_bias_ref,
    w_out, w_in, w_back, p_out, p_in, p_back, b_in_p, q, k, v, qf, kf, vf, ctx_far, ctx_o, ctx_p,
    n1, i1, low, act, slope, part, n2, i2, own_out, lowt, xt, ctxt, actt, firsts, gathered,
    pre_ref, bias_grad_ref, firsts_out_ref, all_ref, pooled_ref, len_ref, unit_ref, lse_col_ref, lse_row_ref, pre_f_ref,
    send_sem, recv_sem, local_sem,
):
    dp, mp = lax.axis_index("dp"), lax.axis_index("mp")
    rows = q.shape[0]
    width = x_ref.shape[1]
    units = w_in.shape[1]
    near = {"x": {"mp": 1 - mp}, "y": {"dp": flip(dp, 2)}, "z": {"dp": flip(dp, 4)}, "c": {"dp": flip(dp, 1)}}
    far = ({"dp": flip(dp, 8)}, {"dp": flip(flip(dp, 4), 8)})
    run = Copies(send_sem, recv_sem, local_sem)
    own = dp % 8
    bit = {"y": 2, "z": 4}

    out_block, in_block, unit_chunk = w_out.shape[0] // 8, width // 8, units // N_CHUNK
    back_block = unit_chunk // 8

    def out_at(ref):
        return lambda b: ref.at[pl.ds(pl.multiple_of(b * out_block, 16), out_block)]

    def in_at(ref, n):
        return lambda b: ref.at[pl.ds(pl.multiple_of(b * in_block, 16), in_block), pl.ds(n * unit_chunk, unit_chunk)]

    def back_at(ref, n):
        return lambda b: ref.at[pl.ds(pl.multiple_of(n * unit_chunk + b * back_block, 16), back_block)]

    def qkv_at(ref):
        return lambda b: ref.at[:, pl.ds(pl.multiple_of(b * 2 * in_block, 16), 2 * in_block)]

    chunks = [(out_at(w_out_any), out_at(p_out), "zy")]
    for n in range(N_CHUNK):
        chunks.append((in_at(w_in_any, n), in_at(p_in, n), "yz" if n % 2 == 0 else "zy"))
    for n in range(N_CHUNK):
        chunks.append((back_at(w_back_any, n), back_at(p_back, n), "zy" if n % 2 == 0 else "yz"))
    chunks.append((qkv_at(w_qkv_any), qkv_at(p_qkv), "y"))
    total = len(chunks)
    hops = [[None] * 4 for _ in chunks]

    def step(at, stage):
        source, target, route = chunks[at]
        first = own if len(route) == 2 else dp % 4
        if stage == 0:
            hops[at][0] = [run.remote(source(first), target(first), near["x"])]
            return
        for copy in hops[at][stage - 1]:
            copy.wait_recv()
        one = flip(first, bit[route[0]])
        blocks = [first, one]
        if len(route) == 2:
            blocks += [flip(b, bit[route[1]]) for b in blocks]
        if stage == 1:
            hops[at][1] = [run.remote(target(first), target(first), near[route[0]])]
        elif stage == len(route) + 1:
            hops[at][stage] = [run.remote(target(b), target(b), near["c"]) for b in blocks]
        elif stage == 2:
            hops[at][2] = [run.remote(target(b), target(b), near[route[1]]) for b in blocks[:2]]

    greet(list(near.values()) + list(far))
    for at in range(total - 1):
        step(at, 0)
    b_copies = [run.remote(b_in_ref, b_in_p, near["x"]), run.remote(b_qv_ref, b_qv_p, near["x"])]
    loads = [run.here(a, b) for a, b in ((w_out_any, w_out), (w_in_any, w_in), (w_back_any, w_back))]

    def project(base, q_to, k_to, v_to):
        x = x_ref[pl.ds(base, rows)]
        q_to[...] = (mm(x, w_qkv_ref[0]) + b_qv_ref[0:1]).astype(bf16)
        k_to[...] = mm(x, w_qkv_ref[1]).astype(bf16)
        v_to[...] = (mm(x, w_qkv_ref[2]) + b_qv_ref[1:2]).astype(bf16)

    def attend(base, q_from, k_from, v_from, target):
        for group in range(rows // GROUP):
            at = slice(group * GROUP, (group + 1) * GROUP)
            one = same_block(segr_ref[:, pl.ds(pl.multiple_of(base + group * GROUP, GROUP), GROUP)])
            same = jnp.concatenate([one, one], axis=0)
            for pair in range(q_from.shape[1] // PAIR):
                cols = slice(pair * PAIR, (pair + 1) * PAIR)
                probs = pair_probs(two_heads(q_from[at, cols]), k_from[at, cols], same)
                target[at, cols] = join_heads(mm(probs.astype(bf16), v_from[at, cols])).astype(bf16)

    far_base = pl.multiple_of((1 - mp) * rows, rows)
    own_base = pl.multiple_of(mp * rows, rows)
    project(far_base, qf, kf, vf)
    attend(far_base, qf, kf, vf, ctx_far)
    c_copy = run.remote(ctx_far, ctx_p, near["x"])
    step(7, 0)
    project(own_base, q, k, v)
    step(0, 1)
    attend(own_base, q, k, v, ctx_o)
    step(1, 1)
    for a, b in ((q, q_any), (k, k_any), (v, v_any)):
        run.here(a, b)
    for at in range(0, rows, 128):
        here = slice(at, at + 128)
        xt[:, here] = x_ref[pl.ds(pl.multiple_of(own_base + at, 128), 128)].T
        ctxt[0, :, here] = ctx_o[here].T
    step(2, 1)
    loads[0].wait()
    part[...] = mm(ctx_o[...], w_out[...])
    for at, stage in (
        (0, 2), (3, 1), (1, 2), (4, 1), (2, 2), (5, 1), (0, 3), (6, 1), (4, 2), (0, 4), (3, 2), (2, 3), (1, 3), (2, 4),
        (6, 2), (1, 4), (5, 2),
    ):
        step(at, stage)

    def inner(side, n, w, b):
        for at in range(n * unit_chunk, (n + 1) * unit_chunk, 256):
            cols = slice(at, at + 256)
            bias = jnp.concatenate([b[at // 128:at // 128 + 1], b[at // 128 + 1:at // 128 + 2]], axis=1)
            for top in range(0, rows, 128):
                here = slice(top, top + 128)
                value = mm(low[here], w[:, cols]) + bias
                cumulative = 0.5 * (1.0 + lax.erf(value * 0.7071067811865476))
                density = jnp.exp(-0.5 * value * value) * 0.3989422804014327
                rounded = (value * cumulative).astype(bf16)
                act[side, here, cols] = rounded
                actt[side, cols, here] = rounded.T
                slope[side, here, cols] = (cumulative + value * density).astype(bf16)

    def branch(side, n, w, first=False):
        cols = slice(n * unit_chunk, (n + 1) * unit_chunk)
        for top in range(0, rows, 128):
            here = slice(top, top + 128)
            value = mm(act[side, here, cols], w[cols])
            part[here] = value if first else part[here] + value

    c_copy.wait_recv()
    for at in range(0, rows, 128):
        here = slice(at, at + 128)
        x = x_ref[pl.ds(pl.multiple_of(own_base + at, 128), 128)].astype(f32)
        normed, inv_std = norm_rows(x + part[here] + mm(ctx_p[here], p_out[...]) + s_ref[0:1])
        n1[here] = normed
        i1[here] = jnp.broadcast_to(inv_std, (128, 128))
        rounded = (normed * g_ref[0:1] + s_ref[1:2]).astype(bf16)
        low[here] = rounded
        lowt[:, here] = rounded.T
        ctxt[1, :, here] = ctx_p[here].T
    for a, b in ((p_out, p_out_any), (n1, n1_any), (i1, i1_any), (lowt, lowt_any), (xt, xt_any), (ctxt, ctxt_any)):
        run.here(a, b)
    loads[1].wait()
    loads[2].wait()
    inner(0, 0, w_in, b_in_ref)
    inner(0, 1, w_in, b_in_ref)
    step(3, 3)
    inner(0, 2, w_in, b_in_ref)
    step(4, 3)
    for n in range(N_CHUNK):
        branch(0, n, w_back, first=n == 0)
    step(3, 4)
    for copy in b_copies:
        copy.wait_recv()
    inner(1, 0, p_in, b_in_p)
    step(4, 4)
    inner(1, 1, p_in, b_in_p)
    step(5, 3)
    inner(1, 2, p_in, b_in_p)
    step(6, 3)
    for a, b in ((actt, actt_any), (slope, slope_any), (p_in, p_in_any)):
        run.here(a, b)
    branch(1, 0, p_back)
    step(5, 4)
    branch(1, 1, p_back)
    step(6, 4)
    step(7, 1)
    last = slice(2 * unit_chunk, units)
    for at in range(0, rows, 64):
        here = slice(at, at + 64)
        value = mm(act[1, here, last], p_back[last]) + part[here] + s_ref[2:3]
        normed, inv_std = norm_rows(n1[here] * g_ref[0:1] + s_ref[1:2] + value)
        n2[here] = normed
        i2[here] = jnp.broadcast_to(inv_std, (64, 128))
        hidden = (normed * g_ref[1:2] + s_ref[3:4]).astype(bf16)
        own_out[here] = hidden
        firsts[at // 64:at // 64 + 1] = hidden[0:1].astype(f32)

    z, y, c = dp // 4, (dp // 2) % 2, dp % 2
    half = width // 2
    row_of = lax.broadcasted_iota(jnp.int32, (8, 128), 0)
    lane_of = lax.broadcasted_iota(jnp.int32, (8, 128), 1)
    ids = jnp.zeros((8, 128), f32)
    for at in range(8):
        pair = pairs_ref[mp * 8 + at]
        ids = jnp.where((row_of == at) & (lane_of == 0), (pair // 64).astype(f32), ids)
        ids = jnp.where((row_of == at) & (lane_of == 1), (pair % 64).astype(f32), ids)
    gathered[z, y, c, mp] = jnp.concatenate(
        [jnp.concatenate([firsts[:, :half], ids], axis=1), jnp.concatenate([firsts[:, half:], ids], axis=1)], axis=0
    ).astype(bf16)
    slot = gathered.at[z, y, c, mp]
    copy = run.remote(slot, slot, near["x"])
    out_rows = block_out.at[pl.ds(own_base, rows)]
    out_copy = run.remote(own_out, out_rows, near["x"])
    run.here(own_out, out_rows)
    arrive(copy)
    slot = gathered.at[z, y, c]
    copies = [run.remote(slot, slot, device) for device in (far[1], far[0], near["z"])]
    arrive(*copies)
    slot = gathered.at[:, y, c]
    arrive(run.remote(slot, slot, near["y"]))
    slot = gathered.at[:, :, c]
    arrive(run.remote(slot, slot, near["c"]))

    for a, b in ((n2, n2_any), (i2, i2_any), (p_back, p_back_any)):
        run.here(a, b)

    @pl.loop(0, 32)
    def _(at):
        values = gathered[at // 8, (at // 4) % 2, (at // 2) % 2, at % 2].astype(f32)
        here = pl.ds(pl.multiple_of(at * 8, 8), 8)
        all_ref[here, :half] = values[:8, :half]
        all_ref[here, half:width] = values[8:, :half]
        all_ref[here, width:] = values[:8, half:]

    loss_passes(
        dp * 2 + mp, scale_ref[0], w_pool_ref, s_ref[4:5],
        loss_ref, gscale_ref, pre_ref, bias_grad_ref, first_grad_ref, firsts_out_ref,
        all_ref, pooled_ref, len_ref, unit_ref, lse_col_ref, lse_row_ref, pre_f_ref,
    )
    new_scale_ref[0] = scale_ref[0] - step_rate * gscale_ref[0]
    per = width // 16
    own_firsts = mm(firsts_out_ref[...], pick(width, dp * per, per).astype(bf16)).astype(bf16)
    pool_ref[...] = mm_tn(own_firsts, pre_ref[...])
    pool_bias_ref[...] = exact(bias_grad_ref[...], pick(width, dp * per, per))
    step(7, 2)
    step(7, 3)
    out_copy.wait_recv()
    for copy in run.sent:
        copy.wait_send()
    for copy in run.kept[3:]:
        copy.wait()


def forward(x, segr, w_qkv, b_qv, b_in, gains, shifts, w_pool, scale, pairs, w_out, w_in, w_back):
    rows, width = x.shape[0] // 2, x.shape[1]
    cols, units = w_qkv.shape[2], w_in.shape[1]
    count = 2 * lax.axis_size("dp") * 8
    any_ = pl.BlockSpec(memory_space=pl.ANY)
    smem = pl.BlockSpec(memory_space=pltpu.SMEM)
    vmem = pl.BlockSpec(memory_space=pltpu.VMEM)
    S = jax.ShapeDtypeStruct
    head = (rows, cols)
    kept = [
        ((2 * rows, width), bf16), (w_qkv.shape, bf16), (w_out.shape, bf16), (w_in.shape, bf16), (w_back.shape, bf16),
        (head, bf16), (head, bf16), (head, bf16),
        ((rows, width), f32), ((rows, 128), f32), ((width, rows), bf16), ((width, rows), bf16), ((2, cols, rows), bf16),
        ((2, units, rows), bf16), ((2, rows, units), bf16), ((rows, width), f32), ((rows, 128), f32),
    ]
    scratch = [
        (w_out.shape, bf16), (w_in.shape, bf16), (w_back.shape, bf16),
        (w_out.shape, bf16), (w_in.shape, bf16), (w_back.shape, bf16), (b_in.shape, f32),
    ] + [(head, bf16)] * 9 + [
        ((rows, width), f32), ((rows, 128), f32), ((rows, width), bf16),
        ((2, rows, units), bf16), ((2, rows, units), bf16), ((rows, width), f32), ((rows, width), f32),
        ((rows, 128), f32), ((rows, width), bf16),
        ((width, rows), bf16), ((width, rows), bf16), ((2, cols, rows), bf16), ((2, units, rows), bf16),
        ((8, width), f32), ((4, 2, 2, 2, 16, width // 2 + 128), bf16),
        ((count, width), bf16), ((1, width), f32), ((count, width), bf16),
        ((count, width + 128), f32), ((count, width), f32), ((count, 1), f32), ((count, width), bf16),
        ((count, 1), f32), ((1, count), f32), ((count, width), f32),
    ]
    return pl.pallas_call(
        forward_kernel,
        in_specs=[vmem] * 8 + [smem] * 2 + [any_] * 4,
        out_specs=[any_] * len(kept) + [smem] * 3 + [vmem] * 4,
        out_shape=tuple(S(*k) for k in kept) + (
            S((1,), f32), S((1,), f32), S((1,), f32), S((8, width), f32), S(b_qv.shape, f32),
            S((width // 16, width), f32), S((1, width // 16), f32),
        ),
        scratch_shapes=[pltpu.VMEM(*s) for s in scratch] + [
            pltpu.SemaphoreType.DMA((80,)), pltpu.SemaphoreType.DMA((80,)), pltpu.SemaphoreType.DMA((24,)),
        ],
        compiler_params=pltpu.CompilerParams(
            vmem_limit_bytes=56 * 1024 * 1024, collective_id=0, has_side_effects=True
        ),
        name="forward",
    )(x, segr, w_qkv, b_qv, b_in, gains, shifts, w_pool, scale, pairs, w_qkv, w_out, w_in, w_back)


def pick(size, start, count):
    return (
        lax.broadcasted_iota(jnp.int32, (size, count), 0)
        == start + lax.broadcasted_iota(jnp.int32, (size, count), 1)
    ).astype(f32)


def exact(a, b):
    return jnp.dot(a, b, preferred_element_type=f32, precision=lax.Precision.HIGHEST)


ORDERS = (
    ("y", "x", "w", "z"), ("x", "y", "w", "z"), ("w", "x", "y", "z"),
    ("x", "z", "y", "w"), ("z", "x", "w", "y"), ("y", "z", "x", "w"),
    ("x", "y", "w", "z"), ("x", "y", "z", "w"), ("z", "y", "w", "x"),
    ("y", "z", "w", "x"), ("x", "y", "z", "w"), ("y", "z", "x", "w"),
)
TILE = 384


def backward_kernel(
    segr_ref, g_ref, first_grad_ref, b_qv_ref,
    x_any, og_any, n2_any, i2_any, n1_any, i1_any, act_any, slope_any, low_any, xt_any, ctx_any, q_any, k_any, v_any,
    wb_o_any, wb_p_any, wi_o_any, wi_p_any, wo_o_any, wo_p_any, wq_o_any, wq_p_any,
    grad_in_any, o_back, o_in, o_qkv, o_out, o_gains, o_shifts, o_bqv, o_bin,
    one_buf, two_buf, three_buf, grad, i2, n1, i1, act, slope, low, xt, ctx, q, k, v, wb, wi, wo, wq, deltas,
    unit, got_one, got_two, got_three, got_four, got_five, sums, sums_got,
    send_sem, recv_sem, local_sem,
):
    dp, mp = lax.axis_index("dp"), lax.axis_index("mp")
    rows, width = one_buf.shape
    units = slope.shape[2]
    cols = q.shape[2]
    per = width // 16
    own_base = pl.multiple_of(mp * rows, rows)
    near = {
        "x": {"mp": 1 - mp}, "y": {"dp": flip(dp, 2)}, "z": {"dp": flip(dp, 4)}, "w": {"dp": flip(dp, 8)},
        "c": {"dp": flip(dp, 1)},
    }
    run = Copies(send_sem, recv_sem, local_sem)
    greet(list(near.values()))
    own_rows = lambda ref: ref.at[pl.ds(own_base, rows)]
    pending = {}

    def load(*pairs):
        for source, target, name in pairs:
            pending.setdefault(name, []).append(run.here(source, target))

    def need(*names):
        for name in names:
            for copy in pending.pop(name, ()):
                copy.wait()

    load((own_rows(og_any), one_buf, "two"), (n2_any, grad, "two"), (i2_any, i2, "two"))
    load((act_any, act, "act"), (wb_o_any, wb.at[0], "wb"), (wb_p_any, wb.at[1], "wb"), (slope_any, slope, "slope"))

    bits = {"y": 2, "z": 4, "w": 8}
    flight = {}

    def put(at, side, dest, value):
        spot = 0
        for weight, name in zip((8, 4, 2, 1), ORDERS[at]):
            spot = spot + weight * (side if name == "x" else (dest // bits[name] + dp // bits[name]) % 2)
        unit[at, (dest + dp) % 2, spot] = value.astype(bf16)

    def arrivals(at, stage):
        return (got_one, got_two, got_three, got_four, got_five)[stage].at[at]

    def begin(at):
        flight[at, 0] = run.remote(unit.at[at, 1], arrivals(at, 0), near["c"])

    def step(at, stage):
        flight[at, stage - 1].wait_recv()
        mine, got = unit.at[at, 0], arrivals(at, stage - 1)
        count = 16 >> (stage - 1)
        half = count // 2
        if stage == 5:
            total = mine[0].astype(f32) + got[0].astype(f32)
            if at < 4:
                o_back[at % 2 * per:(at % 2 + 1) * per, at // 2 * TILE:(at // 2 + 1) * TILE] = total
            elif at < 8:
                o_in[:, (at - 4) * TILE:(at - 3) * TILE] = total
            elif at < 11:
                o_qkv[at - 8] = total
            else:
                o_out[:, :cols] = total[:per // 2]
                o_out[:, cols:] = total[per // 2:]
            return
        for n in range(half, count):
            mine[n] = mine[n] + got[n]
        flight[at, stage] = run.remote(mine.at[pl.ds(half, half)], arrivals(at, stage), near[ORDERS[at][stage - 1]])
        for n in range(half):
            mine[n] = mine[n] + got[n]

    def sum_step(stage):
        if stage:
            flight["sums", stage - 1].wait_recv()
            sums[stage] = sums[stage - 1] + sums_got[stage - 1]
        if stage < 5:
            name = ("c", "x", "y", "z", "w")[stage]
            flight["sums", stage] = run.remote(sums.at[stage], sums_got.at[stage], near[name])

    def norm_grads(source, extra, normed_ref, inv_ref, gain, low_ref, places):
        gain_sum, shift_sum, low_sum = 0.0, 0.0, 0.0
        for at in range(0, rows, 64):
            here = slice(at, at + 64)
            value = source[here].astype(f32)
            if extra is not None:
                is_first = lax.broadcasted_iota(jnp.int32, (64, width), 0) == 0
                value = value + jnp.where(is_first, extra[at // 64:at // 64 + 1], 0.0)
            normed = normed_ref[here]
            out = norm_back(value, normed, inv_ref[here, 0:1], gain)
            rounded = out.astype(bf16)
            grad[here] = out
            low_ref[here] = rounded
            gain_sum += jnp.sum(value * normed, axis=0, keepdims=True)
            shift_sum += jnp.sum(value, axis=0, keepdims=True)
            low_sum += jnp.sum(rounded.astype(f32), axis=0, keepdims=True)
        for place, value in zip(places, (gain_sum, shift_sum, low_sum)):
            sums[0, place:place + 1] = value

    def second_norm():
        need("two")
        sums[0] = jnp.zeros(sums.shape[1:], f32)
        norm_grads(one_buf, first_grad_ref, grad, i2, g_ref[1:2], two_buf, (1, 5, 4))
        load((wi_o_any, wi.at[0], "wi"), (wi_p_any, wi.at[1], "wi"), (low_any, low, "low"))
        load((n1_any, n1, "one"), (i1_any, i1, "one"))

    def back_weight(half):
        need("act")
        for side in range(2):
            for top in range(0, units, TILE):
                tile = mm(act[side, top:top + TILE], two_buf[:, half * cols:(half + 1) * cols])
                for at in range(0, TILE, per):
                    put(2 * half + at // per % 2, side, (top + at) // (2 * per), tile[at:at + per])

    def inner_grads(side):
        need("wb", "slope")
        owner = mp + side - 2 * mp * side
        for at in range(0, units, 256):
            here = slice(at, at + 256)
            value = (mm_nt(two_buf[...], wb[side, here]) * slope[side, :, here].astype(f32)).astype(bf16)
            slope[side, :, here] = value
            sums[0, pl.ds(8 + 2 * owner + at // width, 1), at % width:at % width + 256] = jnp.sum(
                value.astype(f32), axis=0, keepdims=True
            )
        if side == 0:
            load((ctx_any, ctx, "ctx"), (wo_o_any, wo.at[0], "wo"), (wo_p_any, wo.at[1], "wo"))
            load((own_rows(x_any), three_buf, "x"), (wq_p_any, wq.at[1], "wq_p"))

    def feed_back():
        need("wi")
        for at in range(0, width, 256):
            here = slice(at, at + 256)
            grad[:, here] = grad[:, here] + mm_nt(slope[0], wi[0, here]) + mm_nt(slope[1], wi[1, here])
        load((q_any, q.at[0], "qkv"), (k_any, k.at[0], "qkv"), (v_any, v.at[0], "qkv"))
        load((xt_any, xt, "xt"), (wq_o_any, wq.at[0], "wq_o"))

    def first_norm_back():
        need("one")
        norm_grads(grad, None, n1, i1, g_ref[0:1], one_buf, (0, 3, 2))

    def in_weight(half):
        need("low")
        for at in range(2 * half, 2 * half + 2):
            for side in range(2):
                for top in range(0, width, TILE):
                    tile = mm(low[top:top + TILE], slope[side, :, at * TILE:(at + 1) * TILE])
                    for row in range(0, TILE, per):
                        put(4 + at, side, (top + row) // per, tile[row:row + per])

    def out_weight():
        need("ctx")
        for side in range(2):
            tile = mm(ctx[side], one_buf[...])
            for dest in range(16):
                part = tile[dest * per // 2:(dest + 1) * per // 2]
                put(11, side, dest, jnp.concatenate([part[:, :cols], part[:, cols:]], axis=0))

    def context_grads():
        need("wo")
        for side in range(2):
            two_buf[:, side * cols:(side + 1) * cols] = mm_nt(one_buf[...], wo[side]).astype(bf16)

    def again():
        need("x", "wq_p")
        q[1] = (mm(three_buf[...], wq[1, 0]) + b_qv_ref[0:1]).astype(bf16)
        k[1] = mm(three_buf[...], wq[1, 1]).astype(bf16)
        v[1] = (mm(three_buf[...], wq[1, 2]) + b_qv_ref[1:2]).astype(bf16)

    def attend_back(side, groups):
        need("qkv")
        scale = HEAD_DIM ** (-0.5)
        for group in groups:
            at = slice(group * GROUP, (group + 1) * GROUP)
            one = same_block(segr_ref[:, pl.ds(pl.multiple_of(own_base + group * GROUP, GROUP), GROUP)])
            same = jnp.concatenate([one, one], axis=1)
            for pair in range(cols // PAIR):
                lanes = slice(pair * PAIR, (pair + 1) * PAIR)
                q_two = two_heads(q[side, at, lanes])
                dc_two = two_heads(two_buf[at, side * cols + pair * PAIR:side * cols + (pair + 1) * PAIR])
                k_pair, v_pair = k[side, at, lanes], v[side, at, lanes]
                scores = jnp.where(same, mm_nt(k_pair, q_two) * scale, masked_out)
                shifted = jnp.exp(scores - jnp.max(scores, axis=0, keepdims=True))
                probs = shifted / jnp.sum(shifted, axis=0, keepdims=True)
                prob_grad = mm_nt(v_pair, dc_two)
                score_grad = (
                    probs * (prob_grad - jnp.sum(prob_grad * probs, axis=0, keepdims=True))
                ).astype(bf16)
                deltas[side, 0, at, lanes] = (join_heads(mm_tn(score_grad, k_pair)) * scale).astype(bf16)
                deltas[side, 1, at, lanes] = (mm(score_grad, q_two) * scale).astype(bf16)
                deltas[side, 2, at, lanes] = mm(probs.astype(bf16), dc_two).astype(bf16)

    def qkv_weight(s):
        need("xt")
        for side in range(2):
            for top in range(0, width, TILE):
                tile = mm(xt[top:top + TILE], deltas[side, s])
                for at in range(0, TILE, per):
                    put(8 + s, side, (top + at) // per, tile[at:at + per])
            if s != 1:
                owner = mp + side - 2 * mp * side
                lanes = pl.ds(pl.multiple_of(owner * cols, 128), cols)
                sums[0, 6 + s // 2:7 + s // 2, lanes] = jnp.sum(deltas[side, s].astype(f32), axis=0, keepdims=True)

    def input_grads():
        need("wq_o", "wq_p")
        for at in range(0, width, 256):
            here = slice(at, at + 256)
            value = grad[:, here]
            for side in range(2):
                for s in range(3):
                    value = value + mm_nt(deltas[side, s], wq[side, s, here])
            three_buf[:, here] = value.astype(bf16)
        flight["inputs"] = run.remote(three_buf, own_rows(grad_in_any), near["x"])
        run.here(three_buf, own_rows(grad_in_any))

    second_norm()
    back_weight(0)
    begin(0)
    begin(1)
    inner_grads(1)
    back_weight(1)
    begin(2)
    begin(3)
    step(0, 1)
    step(1, 1)
    inner_grads(0)
    step(2, 1)
    step(3, 1)
    feed_back()
    in_weight(0)
    begin(4)
    begin(5)
    first_norm_back()
    step(0, 2)
    step(1, 2)
    step(4, 1)
    out_weight()
    begin(11)
    step(5, 1)
    in_weight(1)
    begin(6)
    begin(7)
    step(11, 1)
    context_grads()
    step(3, 2)
    step(6, 1)
    step(7, 1)
    step(1, 3)
    attend_back(0, (2, 3))
    step(2, 2)
    step(4, 2)
    step(0, 3)
    again()
    step(3, 3)
    step(5, 2)
    attend_back(1, (0, 1))
    attend_back(0, (0, 1))
    step(6, 2)
    step(1, 4)
    step(11, 2)
    attend_back(1, (2, 3))
    step(3, 4)
    step(5, 3)
    step(0, 4)
    qkv_weight(0)
    begin(8)
    step(7, 2)
    step(1, 5)
    qkv_weight(2)
    begin(10)
    sum_step(0)
    step(6, 3)
    qkv_weight(1)
    begin(9)
    step(8, 1)
    step(11, 3)
    step(2, 3)
    step(3, 5)
    step(0, 5)
    step(10, 1)
    step(9, 1)
    step(4, 3)
    step(7, 3)
    sum_step(1)
    input_grads()
    step(5, 4)
    step(2, 4)
    step(11, 4)
    step(6, 4)
    step(8, 2)
    step(9, 2)
    step(10, 2)
    step(7, 4)
    sum_step(2)
    step(4, 4)
    step(2, 5)
    step(5, 5)
    step(8, 3)
    step(6, 5)
    step(11, 5)
    step(10, 3)
    step(9, 3)
    sum_step(3)
    step(4, 5)
    step(7, 5)
    step(10, 4)
    step(8, 4)
    sum_step(4)
    step(9, 4)
    step(10, 5)
    step(8, 5)
    step(9, 5)
    sum_step(5)
    total = sums[5]
    vectors = exact(total[0:8], pick(width, dp * per, per))
    o_gains[...] = vectors[0:2]
    o_shifts[...] = vectors[2:6]
    o_bqv[...] = exact(total[0:8], pick(width, mp * cols + dp * (per // 2), per // 2))[6:8]
    few = units // 16
    o_bin[...] = exact(sums[5, pl.ds(8 + 2 * mp + dp // 8, 1), :], pick(width, (dp % 8) * few, few))
    flight["inputs"].wait_recv()
    for copy in run.sent:
        copy.wait_send()
    run.kept[-1].wait()


def backward(segr, gains, first_grad, b_qv, *arrays):
    rows, width = arrays[2].shape
    units = arrays[7].shape[2]
    cols = arrays[11].shape[1]
    any_ = pl.BlockSpec(memory_space=pl.ANY)
    vmem = pl.BlockSpec(memory_space=pltpu.VMEM)
    S = jax.ShapeDtypeStruct
    per = width // 16
    count = len(ORDERS)
    scratch = [((rows, width), bf16)] * 3 + [
        ((rows, width), f32), ((rows, 128), f32), ((rows, width), f32), ((rows, 128), f32),
        ((2, units, rows), bf16), ((2, rows, units), bf16), ((width, rows), bf16), ((width, rows), bf16),
        ((2, cols, rows), bf16), ((2, rows, cols), bf16), ((2, rows, cols), bf16), ((2, rows, cols), bf16),
        ((2, units, width), bf16), ((2, width, units), bf16), ((2, cols, width), bf16), ((2, 3, width, cols), bf16),
        ((2, 3, rows, cols), bf16), ((count, 2, 16, per, TILE), bf16),
    ] + [((count, n, per, TILE), bf16) for n in (16, 8, 4, 2, 1)] + [((6, 16, width), f32), ((5, 16, width), f32)]
    return pl.pallas_call(
        backward_kernel,
        in_specs=[vmem] * 4 + [any_] * len(arrays),
        out_specs=[any_] + [vmem] * 8,
        out_shape=(
            S((2 * rows, width), bf16), S((2 * per, width), f32), S((per, 2 * width), f32), S((3, per, cols), f32),
            S((cols // 16, width), f32), S((2, per), f32), S((4, per), f32), S((2, cols // 16), f32),
            S((1, units // 16), f32),
        ),
        scratch_shapes=[pltpu.VMEM(*s) for s in scratch] + [
            pltpu.SemaphoreType.DMA((72,)), pltpu.SemaphoreType.DMA((72,)), pltpu.SemaphoreType.DMA((28,)),
        ],
        compiler_params=pltpu.CompilerParams(
            vmem_limit_bytes=63 * 1024 * 1024, collective_id=1, has_side_effects=True
        ),
        name="backward",
    )(segr, gains, first_grad, b_qv, *arrays)


def finish_kernel(*refs):
    count = len(refs) // 2
    refs[count][...] = refs[0][...].astype(f32)
    refs[count + 1][...] = refs[1][...]

    @pl.when(pl.program_id(0) == 0)
    def _():
        for source, target in zip(refs[2:count], refs[count + 2:]):
            target[...] = source[...]


def finish(grad_inputs, block_out, *arrays):
    rows, width = grad_inputs.shape
    block = pl.BlockSpec((rows // 4, width), lambda n: (n, 0))
    whole = [pl.BlockSpec(a.shape, lambda n, dims=a.ndim: (0,) * dims) for a in arrays]
    return pl.pallas_call(
        finish_kernel,
        grid=(4,),
        in_specs=[block, block] + whole,
        out_specs=[block, block] + whole,
        out_shape=(jax.ShapeDtypeStruct((rows, width), f32),)
        + tuple(jax.ShapeDtypeStruct(a.shape, a.dtype) for a in (block_out,) + arrays),
        compiler_params=params(60),
        name="finish",
    )(grad_inputs, block_out, *arrays)


def swap_mp(values):
    return lax.ppermute(values, "mp", [(0, 1), (1, 0)])


def swap_dp(values, bit):
    size = lax.axis_size("dp")
    return lax.ppermute(values, "dp", [(at, at ^ bit) for at in range(size)])


def fetch(own, axis, place):
    size = own.shape[axis] // 4
    first = swap_mp(lax.dynamic_slice_in_dim(own, place * size, size, axis))
    second = swap_dp(first, 2)
    third = swap_dp(first, 1)
    fourth = swap_dp(second, 1)
    whole = jnp.zeros_like(own)
    for bits, part in ((0, first), (2, second), (1, third), (3, fourth)):
        whole = lax.dynamic_update_slice_in_dim(whole, part, (place ^ bits) * size, axis)
    return whole


def gather_rows(rows):
    size = lax.axis_size("dp")
    if size != 16:
        return lax.all_gather(rows, ("dp", "mp"), axis=0, tiled=True)
    rows = jnp.concatenate([rows, swap_mp(rows)], axis=0)
    for bit in (1, 2, 4, 8):
        rows = jnp.concatenate([rows, swap_dp(rows, bit)], axis=0)
    return rows


def both_halves(own, mp):
    other = swap_mp(own)
    return jnp.concatenate([jnp.where(mp == 0, own, other), jnp.where(mp == 0, other, own)], axis=0)


def add(a, b):
    return (a.astype(f32) + b.astype(f32)).astype(a.dtype)


def scatter_sum(keep, send, order):
    size = lax.axis_size("dp")
    if size != 16:
        rest = keep.shape[2:]
        both = jnp.stack([keep, send], axis=2)
        both = both.reshape((2, 16) + rest)
        mine = add(both[0], swap_mp(both[1]))
        return mine
    got = swap_dp(send, 1)
    rest = keep.shape[2:]
    names = ["x", "z1", "z0", "y"]
    keep = keep.reshape((2, 2, 2, 2) + rest)
    got = got.reshape((2, 2, 2, 2) + rest)
    bit_of = {"y": 2, "z0": 4, "z1": 8}
    for name in order:
        axis = names.index(name)
        names.remove(name)
        pick = lambda values, at: lax.index_in_dim(values, at, axis, keepdims=False)
        out = add(pick(keep, 1), pick(got, 1))
        out = swap_mp(out) if name == "x" else swap_dp(out, bit_of[name])
        keep = add(pick(keep, 0), pick(got, 0))
        got = out
    return add(keep, got)


def swap_order(values, axis, place):
    shape = values.shape
    split = values.reshape(shape[:axis] + (2, 2, 2, 2) + shape[axis + 1:])
    for at, bit in enumerate((8, 4, 2, 1)):
        low = lax.index_in_dim(split, 0, axis + at)
        high = lax.index_in_dim(split, 1, axis + at)
        flipped = jnp.concatenate([high, low], axis=axis + at)
        split = jnp.where((place & bit) != 0, flipped, split)
    return split.reshape(shape)


def shards(
    inputs, segment_ids, pair_index, w_qkv, bias_qv, w_out, w_in, bias_in, w_back,
    w_pool, norm_gains, shifts, logit_scale, out_grad,
):
    tok_rows, width = inputs.shape
    size = lax.axis_size("dp")
    dp, mp = lax.axis_index("dp"), lax.axis_index("mp")
    rows = tok_rows // 2
    blocks = rows // SEG_LEN
    place = dp % 4
    slots = 0 * dp
    pos = jnp.reshape(slots, (1,)).astype(jnp.int32)

    x = lax.dynamic_slice_in_dim(inputs, mp * rows, rows, 0)
    cot = lax.dynamic_slice_in_dim(out_grad, mp * rows, rows, 0)
    seg = lax.dynamic_slice_in_dim(segment_ids, mp * rows, rows, 0)
    segc, segr = seg.reshape(rows, 1), seg.reshape(1, rows)
    pairs = lax.dynamic_slice_in_dim(pair_index, mp * blocks, blocks, 0)

    cols = w_qkv.shape[2]
    units = w_in.shape[1]
    ids = jnp.pad(jnp.stack([pairs // 64, pairs % 64], axis=1).astype(f32), ((0, 0), (0, 126)))
    if size == 16:
        segr = segment_ids.reshape(1, -1)
        (
            block_out, w_qkv_p, w_out_p, w_in_p, w_back_p, q, k, v, n1, i1, lowt, xt, ctxt, actt, slope, n2, i2,
            loss_value, grad_scale, new_scale, first_grad, bias_qv_p, grad_pool, pool_bias,
        ) = forward(
            inputs, segr, w_qkv, bias_qv, bias_in.reshape(-1, 128),
            norm_gains, shifts, w_pool, logit_scale, pair_index, w_out, w_in, w_back,
        )
        results = backward(
            segr, norm_gains, first_grad, bias_qv_p,
            inputs, out_grad, n2, i2, n1, i1, actt, slope, lowt, xt, ctxt, q, k, v,
            w_back, w_back_p, w_in, w_in_p, w_out, w_out_p, w_qkv, w_qkv_p,
        )
        (
            grad_inputs, block_out, grad_back, grad_in, grad_qkv, grad_out, gains, shift_grads, grad_bias_qv,
            grad_bias_in, grad_pool, pool_bias,
        ) = finish(results[0], block_out, *results[1:], grad_pool, pool_bias)
        return (
            block_out, loss_value, grad_inputs, grad_qkv, grad_bias_qv, grad_out, grad_in,
            grad_bias_in[0], grad_back, grad_pool, gains, shift_grads, pool_bias[0], grad_scale, new_scale,
        )

    biases = swap_mp(bias_qv)
    bias_qv_p, bias_in_p = biases, swap_mp(bias_in)
    w_qkv_p = fetch(w_qkv, 1, place)
    w_out_p = fetch(w_out, 0, place)
    w_in_p = fetch(w_in, 0, place)
    w_back_p = fetch(w_back, 0, place)

    q_o, k_o, v_o, ctx_o = attention_half(x, w_qkv, bias_qv, segc, segr)
    q_p, k_p, v_p, ctx_p = attention_half(x, w_qkv_p, bias_qv_p, segc, segr)
    normed_one, inv_one, low_one = first_norm(ctx_o, ctx_p, w_out, w_out_p, x, norm_gains, shifts)
    act_o, slope_o = inner_half(low_one, w_in, bias_in.reshape(1, -1))
    part = branch_half(act_o, w_back)
    act_p, slope_p = inner_half(low_one, w_in_p, bias_in_p.reshape(1, -1))
    normed_two, inv_two, own_out = second_norm(act_p, w_back_p, part, normed_one, norm_gains, shifts)

    firsts = own_out.reshape(blocks, SEG_LEN, width)[:, 0]
    rel = gather_rows(jnp.concatenate([firsts, ids.astype(bf16)], axis=1))
    linear = dp * 2 + mp
    position = jnp.stack([linear if size == 16 else 0 * linear, linear]).astype(jnp.int32)
    loss_value, grad_scale, pre_all, pool_bias, first_grad, firsts_all = pair_loss(
        position, rel, w_pool, shifts[4:5], logit_scale
    )
    block_out = both_halves(own_out, mp)
    pool_rows = width // size
    grad_pool = lax.dot_general(
        lax.dynamic_slice_in_dim(firsts_all, dp * pool_rows, pool_rows, 1), pre_all, TN, preferred_element_type=f32
    )
    grad_pool_bias = lax.dynamic_slice_in_dim(pool_bias[0], dp * pool_rows, pool_rows, 0)

    grad_two, branch, sums_two = second_back(cot, first_grad, normed_two, inv_two, norm_gains)
    keep_bo, send_bo = back_weight(pos, act_o, branch)
    keep_bp, send_bp = back_weight(pos, act_p, branch)
    keep_io, send_io, bias_io, part_one = inner_back(pos, branch, w_back, slope_o, low_one, w_in, grad_two)
    keep_ip, send_ip, bias_ip, part_two = inner_back(pos, branch, w_back_p, slope_p, low_one, w_in_p, part_one)
    grad_one, sums_one, dc_o, dc_p, keep_w, send_w = first_back(
        pos, part_two, normed_one, inv_one, norm_gains, ctx_o, ctx_p, w_out, w_out_p
    )
    keep_qo, send_qo, bias_qo, in_one = attention_back(pos, x, w_qkv, segc, segr, q_o, k_o, v_o, dc_o, grad_one)
    keep_qp, send_qp, bias_qp, in_two = attention_back(pos, x, w_qkv_p, segc, segr, q_p, k_p, v_p, dc_p, in_one)

    both = lambda a, b: jnp.stack([a, b])
    mine_back = scatter_sum(both(keep_bo, keep_bp), both(send_bo, send_bp), ("x", "y", "z0", "z1"))
    mine_in = scatter_sum(both(keep_io, keep_ip), both(send_io, send_ip), ("y", "x", "z0", "z1"))
    mine_out = scatter_sum(keep_w, send_w, ("x", "y", "z0", "z1"))
    mine_qkv = scatter_sum(both(keep_qo, keep_qp), both(send_qo, send_qp), ("y", "x", "z0", "z1"))

    vectors = jnp.concatenate([sums_one[0:1], sums_two[0:1], sums_one[2:3], sums_one[1:2], sums_two[2:3], sums_two[1:2]])
    by_dp = vectors.reshape(6, 16, width // 16).transpose(1, 0, 2).reshape(16, -1)
    by_dp = jnp.broadcast_to(by_dp[None], (2,) + by_dp.shape)
    bias_q = both(bias_qo, bias_qp).reshape(2, 2, 16, cols // 16).transpose(0, 2, 1, 3).reshape(2, 16, -1)
    bias_i = both(bias_io, bias_ip).reshape(2, 16, units // 16)
    packed = jnp.concatenate([by_dp, bias_q, bias_i], axis=2)
    packed = swap_order(packed, 1, slots).reshape(2, 8, 2, -1)
    mine_small = scatter_sum(packed[:, :, 0], packed[:, :, 1], ("y", "x", "z0", "z1"))

    if size != 16:
        fold = lambda values: lax.psum_scatter(values, "dp", scatter_dimension=0, tiled=True)
        grad_back = fold(mine_back.reshape(units, width).astype(f32))
        grad_in = fold(mine_in.reshape(width, units).astype(f32))
        grad_qkv = fold(mine_qkv.transpose(0, 2, 1, 3).reshape(width, 3, cols).astype(f32)).transpose(1, 0, 2)
        small = mine_small
        n_vec = 6 * (width // 16)
        n_q = 2 * (cols // 16)
        n_i = units // 16
        vec = small[:, :n_vec].reshape(16, 6, -1).transpose(0, 2, 1).reshape(width, 6)
        vec = fold(vec).T
        grad_bias_qv = fold(small[:, n_vec:n_vec + n_q].reshape(16, 2, -1).transpose(0, 2, 1).reshape(cols, 2)).T
        grad_bias_in = fold(small[:, n_vec + n_q:n_vec + n_q + n_i].reshape(units))
        grad_out = fold(mine_out.reshape(cols, width).astype(f32))
    else:
        grad_back = mine_back.astype(f32)
        grad_in = mine_in.astype(f32)
        grad_qkv = mine_qkv.astype(f32)
        small = mine_small
        n_vec = 6 * (width // 16)
        n_q = 2 * (cols // 16)
        n_i = units // 16
        vec = small[:n_vec].reshape(6, -1)
        grad_bias_qv = small[n_vec:n_vec + n_q].reshape(2, -1)
        grad_bias_in = small[n_vec + n_q:n_vec + n_q + n_i]
        grad_out = mine_out.astype(f32)

    grad_inputs = both_halves(in_two.astype(bf16), mp).astype(f32)
    new_scale = logit_scale - step_rate * grad_scale
    return (
        block_out, loss_value, grad_inputs, grad_qkv, grad_bias_qv, grad_out, grad_in, grad_bias_in,
        grad_back, grad_pool, vec[:2], vec[2:], grad_pool_bias, grad_scale, new_scale,
    )


def solution(mesh):
    return jax.shard_map(
        shards,
        mesh=mesh,
        in_specs=(
            P("dp", None), P("dp"), P("dp"), P(None, None, "mp"), P(None, "mp"), P("mp", None), P(None, "mp"),
            P("mp"), P("mp", None), P(), P(), P(), P(), P("dp", None),
        ),
        out_specs=(
            P("dp", None), P(), P("dp", None), P(None, "dp", "mp"), P(None, ("mp", "dp")), P(("mp", "dp"), None),
            P("dp", "mp"), P(("mp", "dp")), P(("mp", "dp"), None), P("dp", None), P(None, "dp"), P(None, "dp"),
            P("dp"), P(), P(),
        ),
        check_vma=False,
    )
```

```python
from functools import partial

import jax
import jax.numpy as jnp
from jax import lax
from jax.experimental import pallas as pl
from jax.experimental.pallas import tpu as pltpu
from jax.sharding import PartitionSpec as P

HEAD_DIM = 64
SEG_LEN = 64
PAIR = 2 * HEAD_DIM
GROUP = 128

epsilon = 1e-12
margin = 0.3
step_rate = 0.1
masked_out = -1e30
f32 = jnp.float32
bf16 = jnp.bfloat16

NT = (((1,), (1,)), ((), ()))
TN = (((0,), (0,)), ((), ()))


def mm(a, b):
    return jnp.dot(a, b, preferred_element_type=f32)


def mm_nt(a, b):
    return lax.dot_general(a, b, NT, preferred_element_type=f32)


def mm_tn(a, b):
    return lax.dot_general(a, b, TN, preferred_element_type=f32)


def params(mib=40):
    return pltpu.CompilerParams(vmem_limit_bytes=mib * 1024 * 1024)


def cost(flops, moved):
    return pl.CostEstimate(flops=int(flops), bytes_accessed=int(moved), transcendentals=0)


def lane_masks():
    lane = lax.broadcasted_iota(jnp.int32, (1, PAIR), 1)
    first = (lane < HEAD_DIM).astype(f32)
    return first, 1.0 - first


def two_heads(rows):
    first, second = lane_masks()
    return jnp.concatenate([rows * first.astype(bf16), rows * second.astype(bf16)], axis=0)


def join_heads(both):
    first, second = lane_masks()
    half = both.shape[0] // 2
    return both[:half] * first + both[half:] * second


def pair_probs(q_two, k_pair, same):
    scores = mm_nt(q_two, k_pair) * (HEAD_DIM ** (-0.5))
    scores = jnp.where(same, scores, masked_out)
    shifted = jnp.exp(scores - jnp.max(scores, axis=1, keepdims=True))
    return shifted / jnp.sum(shifted, axis=1, keepdims=True)


def same_segment(seg_col, seg_row, rows):
    own = seg_col[rows, :]
    other = seg_row[:, rows]
    one = own == other
    return jnp.concatenate([one, one], axis=0)


def attention_kernel(x_ref, w_ref, b_ref, segc_ref, segr_ref, q_ref, k_ref, v_ref, c_ref):
    x = x_ref[...]
    q_ref[...] = (mm(x, w_ref[0]) + b_ref[0:1]).astype(bf16)
    k_ref[...] = mm(x, w_ref[1]).astype(bf16)
    v_ref[...] = (mm(x, w_ref[2]) + b_ref[1:2]).astype(bf16)
    for group in range(x.shape[0] // GROUP):
        rows = slice(group * GROUP, (group + 1) * GROUP)
        same = same_segment(segc_ref, segr_ref, rows)
        for pair in range(q_ref.shape[1] // PAIR):
            cols = slice(pair * PAIR, (pair + 1) * PAIR)
            probs = pair_probs(two_heads(q_ref[rows, cols]), k_ref[rows, cols], same)
            c_ref[rows, cols] = join_heads(mm(probs.astype(bf16), v_ref[rows, cols])).astype(bf16)


def attention_half(x, w, b, segc, segr):
    rows, cols = x.shape[0], w.shape[2]
    out = jax.ShapeDtypeStruct((rows, cols), bf16)
    return pl.pallas_call(
        attention_kernel,
        out_shape=(out,) * 4,
        compiler_params=params(),
        cost_estimate=cost(2 * rows * 768 * cols * 3 * 2, 6 * rows * cols * 2),
        name="attention",
    )(x, w, b, segc, segr)


def norm_rows(values):
    row_mean = jnp.mean(values, axis=-1, keepdims=True)
    centred = values - row_mean
    inv_std = lax.rsqrt(jnp.mean(centred * centred, axis=-1, keepdims=True) + epsilon)
    return centred * inv_std, inv_std


def norm_back(grad, normed, inv_std, gain):
    scaled = grad * gain
    return inv_std * (
        scaled
        - jnp.mean(scaled, axis=-1, keepdims=True)
        - normed * jnp.mean(scaled * normed, axis=-1, keepdims=True)
    )


def first_norm_kernel(co_ref, cp_ref, wo_ref, wp_ref, x_ref, g_ref, s_ref, n_ref, inv_ref, low_ref):
    for at in range(0, x_ref.shape[0], 128):
        rows = slice(at, at + 128)
        attended = mm(co_ref[rows], wo_ref[...]) + mm(cp_ref[rows], wp_ref[...]) + s_ref[0:1]
        normed, inv_std = norm_rows(x_ref[rows].astype(f32) + attended)
        n_ref[rows] = normed
        inv_ref[rows] = inv_std
        low_ref[rows] = (normed * g_ref[0:1] + s_ref[1:2]).astype(bf16)


def first_norm(ctx_o, ctx_p, wo, wp, x, gains, shifts):
    rows, width = x.shape
    return pl.pallas_call(
        first_norm_kernel,
        out_shape=(
            jax.ShapeDtypeStruct((rows, width), f32),
            jax.ShapeDtypeStruct((rows, 1), f32),
            jax.ShapeDtypeStruct((rows, width), bf16),
        ),
        compiler_params=params(),
        cost_estimate=cost(2 * rows * width * width, 12 * rows * width),
        name="first_norm",
    )(ctx_o, ctx_p, wo, wp, x, gains, shifts)


def inner_kernel(h_ref, w_ref, b_ref, act_ref, slope_ref):
    for at in range(0, h_ref.shape[0], 128):
        rows = slice(at, at + 128)
        inner = mm(h_ref[rows], w_ref[...]) + b_ref[...]
        cumulative = 0.5 * (1.0 + lax.erf(inner * 0.7071067811865476))
        density = jnp.exp(-0.5 * inner * inner) * 0.3989422804014327
        act_ref[rows] = (inner * cumulative).astype(bf16)
        slope_ref[rows] = (cumulative + inner * density).astype(bf16)


def inner_half(low, w, b):
    rows, width = low.shape
    units = w.shape[1]
    tile = 256
    out = jax.ShapeDtypeStruct((rows, units), bf16)
    return pl.pallas_call(
        inner_kernel,
        grid=(units // tile,),
        in_specs=[
            pl.BlockSpec((rows, width), lambda n: (0, 0)),
            pl.BlockSpec((width, tile), lambda n: (0, n)),
            pl.BlockSpec((1, tile), lambda n: (0, n)),
        ],
        out_specs=[pl.BlockSpec((rows, tile), lambda n: (0, n))] * 2,
        out_shape=(out, out),
        compiler_params=params(),
        cost_estimate=cost(4 * rows * width * units, 8 * rows * units),
        name="inner",
    )(low, w, b)


def branch_kernel(act_ref, w_ref, out_ref):
    for at in range(0, act_ref.shape[0], 128):
        rows = slice(at, at + 128)
        out_ref[rows] = mm(act_ref[rows], w_ref[...])


def branch_half(act, w):
    rows, units = act.shape
    width = w.shape[1]
    return pl.pallas_call(
        branch_kernel,
        out_shape=jax.ShapeDtypeStruct((rows, width), f32),
        compiler_params=params(),
        cost_estimate=cost(2 * rows * width * units, 4 * rows * units),
        name="branch",
    )(act, w)


def second_norm_kernel(act_ref, w_ref, part_ref, n1_ref, g_ref, s_ref, n_ref, inv_ref, out_ref):
    for at in range(0, act_ref.shape[0], 128):
        rows = slice(at, at + 128)
        branch = mm(act_ref[rows], w_ref[...]) + part_ref[rows] + s_ref[2:3]
        hidden_one = n1_ref[rows] * g_ref[0:1] + s_ref[1:2]
        normed, inv_std = norm_rows(hidden_one + branch)
        n_ref[rows] = normed
        inv_ref[rows] = inv_std
        out_ref[rows] = (normed * g_ref[1:2] + s_ref[3:4]).astype(bf16)


def second_norm(act, w, part, normed_one, gains, shifts):
    rows, units = act.shape
    width = w.shape[1]
    return pl.pallas_call(
        second_norm_kernel,
        out_shape=(
            jax.ShapeDtypeStruct((rows, width), f32),
            jax.ShapeDtypeStruct((rows, 1), f32),
            jax.ShapeDtypeStruct((rows, width), bf16),
        ),
        compiler_params=params(),
        cost_estimate=cost(2 * rows * width * units, 4 * rows * units),
        name="second_norm",
    )(act, w, part, normed_one, gains, shifts)


def loss_kernel(
    pos_ref, rel_ref, w_ref, bias_ref, scale_ref,
    loss_ref, gscale_ref, pre_ref, bias_grad_ref, first_grad_ref, firsts_out_ref,
    all_ref, pooled_ref, len_ref, unit_ref, lse_col_ref, lse_row_ref, pre_f_ref,
):
    @pl.loop(0, pooled_ref.shape[0] // 8)
    def _(slot):
        source = pl.multiple_of(slot * 8, 8)
        target = pl.multiple_of(jnp.bitwise_xor(slot, pos_ref[0]) * 8, 8)
        all_ref[pl.ds(target, 8), :] = rel_ref[pl.ds(source, 8), :].astype(f32)

    loss_passes(
        pos_ref[1], scale_ref[0], w_ref, bias_ref[...],
        loss_ref, gscale_ref, pre_ref, bias_grad_ref, first_grad_ref, firsts_out_ref,
        all_ref, pooled_ref, len_ref, unit_ref, lse_col_ref, lse_row_ref, pre_f_ref,
    )


def loss_passes(
    here, scale, w_ref, bias,
    loss_ref, gscale_ref, pre_ref, bias_grad_ref, first_grad_ref, firsts_out_ref,
    all_ref, pooled_ref, len_ref, unit_ref, lse_col_ref, lse_row_ref, pre_f_ref,
):
    count, width = pooled_ref.shape
    chunk = min(count, 256)
    steps = count // chunk

    def pool(at):
        firsts = all_ref[pl.ds(at, chunk), :width].astype(bf16)
        firsts_out_ref[pl.ds(at, chunk), :] = firsts
        pooled = jnp.tanh(mm(firsts, w_ref[...]) + bias)
        inv_len = lax.rsqrt(jnp.sum(pooled * pooled, axis=-1, keepdims=True) + 1e-06)
        pooled_ref[pl.ds(at, chunk), :] = pooled
        len_ref[pl.ds(at, chunk), :] = inv_len
        unit_ref[pl.ds(at, chunk), :] = (pooled * inv_len).astype(bf16)

    def positions(at):
        own = at + lax.broadcasted_iota(jnp.int32, (chunk, count), 0)
        other = lax.broadcasted_iota(jnp.int32, (chunk, count), 1)
        paired = all_ref[pl.ds(at, chunk), width:width + 1]
        positive = paired.astype(jnp.int32) == other
        return own == other, positive

    def logits_of(at):
        cosine = mm_nt(unit_ref[pl.ds(at, chunk), :], unit_ref[...])
        own, positive = positions(at)
        shifted = cosine - jnp.where(positive, margin, 0.0)
        return shifted, own, positive

    def first_pass(at, run):
        shifted, own, positive = logits_of(at)
        logits = jnp.where(own, masked_out, scale * shifted)
        top = jnp.max(logits, axis=1, keepdims=True)
        lse = top + jnp.log(jnp.sum(jnp.exp(logits - top), axis=1, keepdims=True))
        lse_col_ref[pl.ds(at, chunk), :] = lse
        eye = lax.broadcasted_iota(jnp.int32, (chunk, chunk), 0) == lax.broadcasted_iota(
            jnp.int32, (chunk, chunk), 1
        )
        lse_row_ref[:, pl.ds(at, chunk)] = jnp.sum(jnp.where(eye, lse, 0.0), axis=0, keepdims=True)
        return run + jnp.sum(lse) - jnp.sum(jnp.where(positive, logits, 0.0))

    def second_pass(at, run):
        run_scale, run_bias = run
        shifted, own, positive = logits_of(at)
        logits = scale * shifted
        factor = 1.0 / (2.0 * count)
        grad = (
            jnp.exp(logits - lse_col_ref[pl.ds(at, chunk), :])
            + jnp.exp(logits - lse_row_ref[...])
            - jnp.where(positive, 2.0, 0.0)
        ) * factor
        grad = jnp.where(own, 0.0, grad)
        run_scale = run_scale + jnp.sum(grad * shifted)
        unit_grad = 2.0 * mm((scale * grad).astype(bf16), unit_ref[...])
        pooled = pooled_ref[pl.ds(at, chunk), :]
        inv_len = len_ref[pl.ds(at, chunk), :]
        along = jnp.sum(pooled * unit_grad, axis=-1, keepdims=True)
        pooled_grad = inv_len * unit_grad - pooled * (inv_len * inv_len * inv_len) * along
        pre_grad = (pooled_grad * (1.0 - pooled * pooled)).astype(bf16)
        pre_ref[pl.ds(at, chunk), :] = pre_grad
        pre_f_ref[pl.ds(at, chunk), :] = pre_grad.astype(f32)
        return run_scale, run_bias + jnp.sum(pre_grad.astype(f32), axis=0, keepdims=True)

    def each(body, run):
        if steps == 1:
            return body(0, run)
        return lax.fori_loop(0, steps, lambda s, r: body(pl.multiple_of(s * chunk, chunk), r), run)

    each(lambda at, run: (pool(at), run)[1], 0)
    total = each(first_pass, jnp.float32(0.0))
    run_scale, run_bias = each(second_pass, (jnp.float32(0.0), jnp.zeros((1, width), f32)))
    loss_ref[0] = total / count
    gscale_ref[0] = run_scale
    bias_grad_ref[...] = run_bias
    own_rows = pre_f_ref[pl.ds(pl.multiple_of(here * 8, 8), 8), :].astype(bf16)
    first_grad_ref[...] = mm_nt(own_rows, w_ref[...])


def pair_loss(position, rel, w_pool, bias, scale):
    count, wide = rel.shape
    width = w_pool.shape[0]
    smem = pl.BlockSpec(memory_space=pltpu.SMEM)
    vmem = pl.BlockSpec(memory_space=pltpu.VMEM)
    return pl.pallas_call(
        loss_kernel,
        in_specs=[smem, vmem, vmem, vmem, smem],
        out_specs=[smem, smem, vmem, vmem, vmem, vmem],
        out_shape=(
            jax.ShapeDtypeStruct((1,), f32),
            jax.ShapeDtypeStruct((1,), f32),
            jax.ShapeDtypeStruct((count, width), bf16),
            jax.ShapeDtypeStruct((1, width), f32),
            jax.ShapeDtypeStruct((8, width), f32),
            jax.ShapeDtypeStruct((count, width), bf16),
        ),
        scratch_shapes=[
            pltpu.VMEM((count, wide), f32),
            pltpu.VMEM((count, width), f32),
            pltpu.VMEM((count, 1), f32),
            pltpu.VMEM((count, width), bf16),
            pltpu.VMEM((count, 1), f32),
            pltpu.VMEM((1, count), f32),
            pltpu.VMEM((count, width), f32),
        ],
        compiler_params=params(56),
        cost_estimate=cost(2e9, 4e6),
        name="pair_loss",
    )(position, rel, w_pool, bias, scale)


def put_slabs(pos_ref, source, keep_ref, send_ref, lead):
    slab = source.shape[0] // 16
    for place in range(16):
        at = pl.multiple_of(jnp.bitwise_xor(pos_ref[0], place) * slab, slab)
        target = send_ref if place % 2 else keep_ref
        target[lead + (place // 2,)] = source[pl.ds(at, slab), :].astype(bf16)


def second_back_kernel(
    og_ref, fg_ref, n_ref, inv_ref, g_ref, grad_ref, low_ref, sums_ref
):
    rows_all, width = og_ref.shape
    sums_ref[...] = jnp.zeros_like(sums_ref)
    for at in range(0, rows_all, 64):
        rows = slice(at, at + 64)
        block = at // 64
        is_first = lax.broadcasted_iota(jnp.int32, (64, width), 0) == 0
        grad = og_ref[rows].astype(f32) + jnp.where(is_first, fg_ref[block:block + 1], 0.0)
        normed = n_ref[rows]
        value = norm_back(grad, normed, inv_ref[rows], g_ref[1:2])
        low = value.astype(bf16)
        grad_ref[rows] = value
        low_ref[rows] = low
        sums_ref[0:1] += jnp.sum(grad * normed, axis=0, keepdims=True)
        sums_ref[1:2] += jnp.sum(grad, axis=0, keepdims=True)
        sums_ref[2:3] += jnp.sum(low.astype(f32), axis=0, keepdims=True)


def second_back(out_grad, first_grad, normed, inv_std, gains):
    rows, width = out_grad.shape
    return pl.pallas_call(
        second_back_kernel,
        out_shape=(
            jax.ShapeDtypeStruct((rows, width), f32),
            jax.ShapeDtypeStruct((rows, width), bf16),
            jax.ShapeDtypeStruct((8, width), f32),
        ),
        compiler_params=params(),
        cost_estimate=cost(20 * rows * width, 12 * rows * width),
        name="second_back",
    )(out_grad, first_grad, normed, inv_std, gains)


def slab_shape(rows, cols):
    return jax.ShapeDtypeStruct((8, rows // 16, cols), bf16)


def back_weight_kernel(pos_ref, act_ref, branch_ref, keep_ref, send_ref, whole):
    for at in range(0, whole.shape[0], 256):
        rows = slice(at, at + 256)
        whole[rows] = mm_tn(act_ref[:, rows], branch_ref[...])
    put_slabs(pos_ref, whole, keep_ref, send_ref, ())


def back_weight(pos, act, branch):
    rows, units = act.shape
    width = branch.shape[1]
    smem = pl.BlockSpec(memory_space=pltpu.SMEM)
    vmem = pl.BlockSpec(memory_space=pltpu.VMEM)
    return pl.pallas_call(
        back_weight_kernel,
        in_specs=[smem, vmem, vmem],
        out_specs=[vmem, vmem],
        out_shape=(slab_shape(units, width),) * 2,
        scratch_shapes=[pltpu.VMEM((units, width), f32)],
        compiler_params=params(),
        cost_estimate=cost(2 * rows * width * units, 4 * units * width),
        name="back_weight",
    )(pos, act, branch)


def inner_back_kernel(pos_ref, branch_ref, wb_ref, slope_ref, low_ref, wi_ref, part_ref,
                      keep_ref, send_ref, bias_ref, out_ref, grad, whole):
    units = slope_ref.shape[1]
    for at in range(0, units, 256):
        cols = slice(at, at + 256)
        inner_grad = (mm_nt(branch_ref[...], wb_ref[cols]) * slope_ref[:, cols].astype(f32)).astype(bf16)
        grad[:, cols] = inner_grad
        bias_ref[:, cols] = jnp.sum(inner_grad.astype(f32), axis=0, keepdims=True)
        whole[:, cols] = mm_tn(low_ref[...], inner_grad)
    put_slabs(pos_ref, whole, keep_ref, send_ref, ())
    for at in range(0, low_ref.shape[0], 128):
        rows = slice(at, at + 128)
        out_ref[rows] = part_ref[rows] + mm_nt(grad[rows], wi_ref[...])


def inner_back(pos, branch, w_back, slope, low, w_in, part):
    rows, units = slope.shape
    width = low.shape[1]
    smem = pl.BlockSpec(memory_space=pltpu.SMEM)
    vmem = pl.BlockSpec(memory_space=pltpu.VMEM)
    return pl.pallas_call(
        inner_back_kernel,
        in_specs=[smem] + [vmem] * 6,
        out_specs=[vmem] * 4,
        out_shape=(slab_shape(width, units),) * 2
        + (jax.ShapeDtypeStruct((1, units), f32), jax.ShapeDtypeStruct((rows, width), f32)),
        scratch_shapes=[pltpu.VMEM((rows, units), bf16), pltpu.VMEM((width, units), f32)],
        compiler_params=params(),
        cost_estimate=cost(6 * rows * width * units, 4 * units * width),
        name="inner_back",
    )(pos, branch, w_back, slope, low, w_in, part)


def first_back_kernel(pos_ref, grad_ref, n_ref, inv_ref, g_ref, co_ref, cp_ref, wo_ref, wp_ref,
                      one_ref, sums_ref, dco_ref, dcp_ref, keep_ref, send_ref, low, whole):
    width = grad_ref.shape[1]
    sums_ref[...] = jnp.zeros_like(sums_ref)
    for at in range(0, grad_ref.shape[0], 128):
        rows = slice(at, at + 128)
        grad = grad_ref[rows]
        normed = n_ref[rows]
        value = norm_back(grad, normed, inv_ref[rows], g_ref[0:1])
        low_rows = value.astype(bf16)
        one_ref[rows] = value
        low[rows] = low_rows
        dco_ref[rows] = mm_nt(low_rows, wo_ref[...]).astype(bf16)
        dcp_ref[rows] = mm_nt(low_rows, wp_ref[...]).astype(bf16)
        sums_ref[0:1] += jnp.sum(grad * normed, axis=0, keepdims=True)
        sums_ref[1:2] += jnp.sum(grad, axis=0, keepdims=True)
        sums_ref[2:3] += jnp.sum(low_rows.astype(f32), axis=0, keepdims=True)
    for side, ctx_ref in enumerate((co_ref, cp_ref)):
        whole[...] = mm_tn(ctx_ref[...], low[...])
        put_slabs(pos_ref, whole, keep_ref.at[side], send_ref.at[side], ())


def first_back(pos, grad, normed, inv_std, gains, ctx_o, ctx_p, wo, wp):
    rows, width = grad.shape
    cols = ctx_o.shape[1]
    smem = pl.BlockSpec(memory_space=pltpu.SMEM)
    vmem = pl.BlockSpec(memory_space=pltpu.VMEM)
    return pl.pallas_call(
        first_back_kernel,
        in_specs=[smem] + [vmem] * 8,
        out_specs=[vmem] * 6,
        out_shape=(
            jax.ShapeDtypeStruct((rows, width), f32),
            jax.ShapeDtypeStruct((8, width), f32),
            jax.ShapeDtypeStruct((rows, cols), bf16),
            jax.ShapeDtypeStruct((rows, cols), bf16),
        )
        + (jax.ShapeDtypeStruct((2, 8, cols // 16, width), bf16),) * 2,
        scratch_shapes=[pltpu.VMEM((rows, width), bf16), pltpu.VMEM((cols, width), f32)],
        compiler_params=params(),
        cost_estimate=cost(8 * rows * width * cols, 12 * rows * width),
        name="first_back",
    )(pos, grad, normed, inv_std, gains, ctx_o, ctx_p, wo, wp)


def attention_back_kernel(pos_ref, x_ref, w_ref, segc_ref, segr_ref, q_ref, k_ref, v_ref, dc_ref, part_ref,
                          keep_ref, send_ref, bias_ref, out_ref, dq, dk, dv, whole):
    scale = HEAD_DIM ** (-0.5)
    for group in range(x_ref.shape[0] // GROUP):
        rows = slice(group * GROUP, (group + 1) * GROUP)
        same = same_segment(segc_ref, segr_ref, rows)
        for pair in range(q_ref.shape[1] // PAIR):
            cols = slice(pair * PAIR, (pair + 1) * PAIR)
            q_two = two_heads(q_ref[rows, cols])
            dc_two = two_heads(dc_ref[rows, cols])
            k_pair = k_ref[rows, cols]
            probs = pair_probs(q_two, k_pair, same)
            prob_grad = mm_nt(dc_two, v_ref[rows, cols])
            score_grad = (
                probs * (prob_grad - jnp.sum(prob_grad * probs, axis=1, keepdims=True))
            ).astype(bf16)
            dq[rows, cols] = (join_heads(mm(score_grad, k_pair)) * scale).astype(bf16)
            dk[rows, cols] = (mm_tn(score_grad, q_two) * scale).astype(bf16)
            dv[rows, cols] = mm_tn(probs.astype(bf16), dc_two).astype(bf16)
    bias_ref[0:1] = jnp.sum(dq[...].astype(f32), axis=0, keepdims=True)
    bias_ref[1:2] = jnp.sum(dv[...].astype(f32), axis=0, keepdims=True)
    for s, grad in enumerate((dq, dk, dv)):
        whole[...] = mm_tn(x_ref[...], grad[...])
        put_slabs_at(pos_ref, whole, keep_ref, send_ref, s)
    for at in range(0, x_ref.shape[0], 128):
        rows = slice(at, at + 128)
        out_ref[rows] = (
            part_ref[rows] + mm_nt(dq[rows], w_ref[0]) + mm_nt(dk[rows], w_ref[1]) + mm_nt(dv[rows], w_ref[2])
        )


def put_slabs_at(pos_ref, source, keep_ref, send_ref, s):
    slab = source.shape[0] // 16
    for place in range(16):
        at = pl.multiple_of(jnp.bitwise_xor(pos_ref[0], place) * slab, slab)
        target = send_ref if place % 2 else keep_ref
        target[place // 2, s] = source[pl.ds(at, slab), :].astype(bf16)


def attention_back(pos, x, w, segc, segr, q, k, v, dc, part):
    rows, width = x.shape
    cols = q.shape[1]
    smem = pl.BlockSpec(memory_space=pltpu.SMEM)
    vmem = pl.BlockSpec(memory_space=pltpu.VMEM)
    slabs = jax.ShapeDtypeStruct((8, 3, width // 16, cols), bf16)
    return pl.pallas_call(
        attention_back_kernel,
        in_specs=[smem] + [vmem] * 9,
        out_specs=[vmem] * 4,
        out_shape=(slabs, slabs, jax.ShapeDtypeStruct((2, cols), f32), jax.ShapeDtypeStruct((rows, width), f32)),
        scratch_shapes=[pltpu.VMEM((rows, cols), bf16)] * 3 + [pltpu.VMEM((width, cols), f32)],
        compiler_params=params(),
        cost_estimate=cost(20 * rows * width * cols, 4 * 3 * width * cols),
        name="attention_back",
    )(pos, x, w, segc, segr, q, k, v, dc, part)


def flip(value, bit):
    return value + bit - 2 * bit * ((value // bit) % 2)


class Copies:
    def __init__(self, send, recv, local):
        self.send, self.recv, self.local = send, recv, local
        self.sent, self.kept = [], []

    def remote(self, source, target, device):
        at = len(self.sent)
        copy = pltpu.make_async_remote_copy(
            src_ref=source, dst_ref=target, send_sem=self.send.at[at], recv_sem=self.recv.at[at],
            device_id=device, device_id_type=pl.DeviceIdType.MESH,
        )
        copy.start()
        self.sent.append(copy)
        return copy

    def here(self, source, target):
        copy = pltpu.make_async_copy(source, target, self.local.at[len(self.kept)])
        copy.start()
        self.kept.append(copy)
        return copy


def greet(devices):
    barrier = pltpu.get_barrier_semaphore()
    for device in devices:
        pl.semaphore_signal(barrier, inc=1, device_id=device, device_id_type=pl.DeviceIdType.MESH)
    pl.semaphore_wait(barrier, len(devices))


def same_block(row):
    across = jnp.broadcast_to(row.astype(f32), (GROUP, GROUP))
    return across == across.T


def arrive(*copies):
    for copy in copies:
        copy.wait_recv()


N_CHUNK = 3


def forward_kernel(
    segr_ref, b_qv_ref, b_in_ref, g_ref, s_ref, scale_ref, pairs_ref,
    x_any, w_pool_any, w_qkv_any, w_out_any, w_in_any, w_back_any,
    block_out, p_qkv, p_out_any, p_in_any, p_back_any, q_any, k_any, v_any, n1_any, i1_any, lowt_any, xt_any, ctxt_any,
    actt_any, slope_any, n2_any, i2_any,
    loss_ref, gscale_ref, new_scale_ref, first_grad_ref, b_qv_p, pool_ref, pool_bias_ref,
    x_ref, w_pool_ref, w_qkv_ref, w_out, w_in, w_back, p_out, p_in, p_back, b_in_p, q, k, v, qf, kf, vf, ctx_far, ctx_o, ctx_p,
    n1, i1, low, act, slope, part, n2, i2, own_out, lowt, xt, ctxt, actt, act_firsts, gathered, ids,
    pre_ref, bias_grad_ref, firsts_out_ref, all_ref, pooled_ref, len_ref, unit_ref, lse_col_ref, lse_row_ref, pre_f_ref,
    send_sem, recv_sem, local_sem,
):
    dp, mp = lax.axis_index("dp"), lax.axis_index("mp")
    rows = q.shape[0]
    width = x_ref.shape[1]
    units = w_in.shape[1]
    near = {"x": {"mp": 1 - mp}, "y": {"dp": flip(dp, 2)}, "z": {"dp": flip(dp, 4)}, "c": {"dp": flip(dp, 1)}}
    far = ({"dp": flip(dp, 8)}, {"dp": flip(flip(dp, 4), 8)})
    run = Copies(send_sem, recv_sem, local_sem)
    own = dp % 8
    bit = {"y": 2, "z": 4}

    out_block, in_block, unit_chunk = w_out.shape[0] // 8, width // 8, units // N_CHUNK
    back_block = unit_chunk // 8

    def out_at(ref):
        return lambda b: ref.at[pl.ds(pl.multiple_of(b * out_block, 16), out_block)]

    def in_at(ref, n):
        return lambda b: ref.at[pl.ds(pl.multiple_of(b * in_block, 16), in_block), pl.ds(n * unit_chunk, unit_chunk)]

    def back_at(ref, n):
        return lambda b: ref.at[pl.ds(pl.multiple_of(n * unit_chunk + b * back_block, 16), back_block)]

    def qkv_at(ref, n):
        return lambda b: ref.at[:, pl.ds(pl.multiple_of((2 * b + n) * in_block, 16), in_block)]

    chunks = [(out_at(w_out_any), out_at(p_out), "zy")]
    for n in range(N_CHUNK):
        chunks.append((in_at(w_in_any, n), in_at(p_in, n), "yz" if n % 2 == 0 else "zy"))
    for n in range(N_CHUNK):
        chunks.append((back_at(w_back_any, n), back_at(p_back, n), "zy" if n % 2 == 0 else "yz"))
    chunks += [(qkv_at(w_qkv_any, n), qkv_at(p_qkv, n), "yz"[n]) for n in range(2)]
    total = len(chunks)
    hops = [[None] * 4 for _ in chunks]

    def step(at, stage):
        source, target, route = chunks[at]
        first = own if len(route) == 2 else dp % 2 + 2 * ((dp // bit[route]) % 2)
        if stage == 0:
            hops[at][0] = [run.remote(source(first), target(first), near["x"])]
            return
        for copy in hops[at][stage - 1]:
            copy.wait_recv()
        one = flip(first, bit[route[0]] if len(route) == 2 else 2)
        blocks = [first, one]
        if len(route) == 2:
            blocks += [flip(b, bit[route[1]]) for b in blocks]
        if stage == 1:
            hops[at][1] = [run.remote(target(first), target(first), near[route[0]])]
        elif stage == len(route) + 1:
            hops[at][stage] = [run.remote(target(b), target(b), near["c"]) for b in blocks]
        elif stage == 2:
            hops[at][2] = [run.remote(target(b), target(b), near[route[1]]) for b in blocks[:2]]

    loads = [
        run.here(a, b)
        for a, b in (
            (x_any, x_ref), (w_qkv_any, w_qkv_ref), (w_out_any, w_out), (w_in_any, w_in), (w_back_any, w_back),
            (w_pool_any, w_pool_ref),
        )
    ]
    z, y, c = dp // 4, (dp // 2) % 2, dp % 2
    row_of = lax.broadcasted_iota(jnp.int32, (8, 128), 0)
    paired = jnp.zeros((8, 128), f32)
    for at in range(8):
        paired = jnp.where(row_of == at, pairs_ref[mp * 8 + at].astype(f32), paired)
    ids[z, y, c, mp] = paired
    greet(list(near.values()) + list(far))
    pair_hops = [[run.remote(ids.at[z, y, c, mp], ids.at[z, y, c, mp], near["x"])]]
    for at in range(total - 2):
        step(at, 0)
    b_copies = [run.remote(b_in_ref, b_in_p, near["x"]), run.remote(b_qv_ref, b_qv_p, near["x"])]

    def project(base, q_to, k_to, v_to):
        x = x_ref[pl.ds(base, rows)]
        q_to[...] = (mm(x, w_qkv_ref[0]) + b_qv_ref[0:1]).astype(bf16)
        k_to[...] = mm(x, w_qkv_ref[1]).astype(bf16)
        v_to[...] = (mm(x, w_qkv_ref[2]) + b_qv_ref[1:2]).astype(bf16)

    def attend(base, q_from, k_from, v_from, target):
        for group in range(rows // GROUP):
            at = slice(group * GROUP, (group + 1) * GROUP)
            one = same_block(segr_ref[:, pl.ds(pl.multiple_of(base + group * GROUP, GROUP), GROUP)])
            same = jnp.concatenate([one, one], axis=0)
            for pair in range(q_from.shape[1] // PAIR):
                cols = slice(pair * PAIR, (pair + 1) * PAIR)
                probs = pair_probs(two_heads(q_from[at, cols]), k_from[at, cols], same)
                target[at, cols] = join_heads(mm(probs.astype(bf16), v_from[at, cols])).astype(bf16)

    far_base = pl.multiple_of((1 - mp) * rows, rows)
    own_base = pl.multiple_of(mp * rows, rows)
    loads[0].wait()
    loads[1].wait()
    project(far_base, qf, kf, vf)
    attend(far_base, qf, kf, vf, ctx_far)
    c_copy = run.remote(ctx_far, ctx_p, near["x"])
    step(7, 0)
    step(8, 0)
    project(own_base, q, k, v)
    arrive(*pair_hops[0])
    slot = ids.at[z, y, c]
    pair_hops.append([run.remote(slot, slot, device) for device in (far[1], far[0], near["z"])])
    step(0, 1)
    attend(own_base, q, k, v, ctx_o)
    step(1, 1)
    for a, b in ((q, q_any), (k, k_any), (v, v_any)):
        run.here(a, b)
    for at in range(0, rows, 128):
        here = slice(at, at + 128)
        xt[:, here] = x_ref[pl.ds(pl.multiple_of(own_base + at, 128), 128)].T
        ctxt[0, :, here] = ctx_o[here].T
    step(2, 1)
    arrive(*pair_hops[1])
    slot = ids.at[:, y, c]
    pair_hops.append([run.remote(slot, slot, near["y"])])
    loads[2].wait()
    part[...] = mm(ctx_o[...], w_out[...])
    for at, stage in (
        (0, 2), (3, 1), (1, 2), (4, 1), (2, 2), (5, 1), (0, 3), (6, 1), (4, 2), (0, 4), (3, 2), (2, 3), (1, 3), (2, 4),
        (6, 2), (1, 4), (5, 2),
    ):
        step(at, stage)

    def inner(side, n, w, b):
        for at in range(n * unit_chunk, (n + 1) * unit_chunk, 256):
            cols = slice(at, at + 256)
            bias = jnp.concatenate([b[at // 128:at // 128 + 1], b[at // 128 + 1:at // 128 + 2]], axis=1)
            for top in range(0, rows, 128):
                here = slice(top, top + 128)
                value = mm(low[here], w[:, cols]) + bias
                cumulative = 0.5 * (1.0 + lax.erf(value * 0.7071067811865476))
                density = jnp.exp(-0.5 * value * value) * 0.3989422804014327
                rounded = (value * cumulative).astype(bf16)
                act[side, here, cols] = rounded
                actt[side, cols, here] = rounded.T
                if side == 1 and n == N_CHUNK - 1:
                    for row in range(0, 128, SEG_LEN):
                        block = (top + row) // SEG_LEN
                        act_firsts[block:block + 1, at % unit_chunk:at % unit_chunk + 256] = rounded[row:row + 1].astype(f32)
                slope[side, here, cols] = (cumulative + value * density).astype(bf16)

    def branch(side, n, w, first=False):
        cols = slice(n * unit_chunk, (n + 1) * unit_chunk)
        for top in range(0, rows, 128):
            here = slice(top, top + 128)
            value = mm(act[side, here, cols], w[cols])
            part[here] = value if first else part[here] + value

    c_copy.wait_recv()
    for at in range(0, rows, 128):
        here = slice(at, at + 128)
        x = x_ref[pl.ds(pl.multiple_of(own_base + at, 128), 128)].astype(f32)
        normed, inv_std = norm_rows(x + part[here] + mm(ctx_p[here], p_out[...]) + s_ref[0:1])
        n1[here] = normed
        i1[here] = jnp.broadcast_to(inv_std, (128, 128))
        rounded = (normed * g_ref[0:1] + s_ref[1:2]).astype(bf16)
        low[here] = rounded
        lowt[:, here] = rounded.T
        ctxt[1, :, here] = ctx_p[here].T
    for a, b in ((p_out, p_out_any), (n1, n1_any), (i1, i1_any), (lowt, lowt_any), (xt, xt_any), (ctxt, ctxt_any)):
        run.here(a, b)
    arrive(*pair_hops[2])
    slot = ids.at[:, :, c]
    pair_hops.append([run.remote(slot, slot, near["c"])])
    loads[3].wait()
    loads[4].wait()
    inner(0, 0, w_in, b_in_ref)
    inner(0, 1, w_in, b_in_ref)
    step(3, 3)
    inner(0, 2, w_in, b_in_ref)
    step(4, 3)
    for n in range(N_CHUNK):
        branch(0, n, w_back, first=n == 0)
    step(3, 4)
    for copy in b_copies:
        copy.wait_recv()
    inner(1, 0, p_in, b_in_p)
    step(4, 4)
    inner(1, 1, p_in, b_in_p)
    step(5, 3)
    step(7, 1)
    inner(1, 2, p_in, b_in_p)
    step(6, 3)
    for a, b in ((actt, actt_any), (slope, slope_any), (p_in, p_in_any)):
        run.here(a, b)
    branch(1, 0, p_back)
    step(5, 4)
    step(8, 1)
    branch(1, 1, p_back)
    step(6, 4)
    last = slice(2 * unit_chunk, units)

    def second_norm(part_rows, n1_rows, act_rows):
        value = mm(act_rows, p_back[last]) + part_rows + s_ref[2:3]
        normed, inv_std = norm_rows(n1_rows * g_ref[0:1] + s_ref[1:2] + value)
        return normed, inv_std, (normed * g_ref[1:2] + s_ref[3:4]).astype(bf16)

    half = width // 2
    every = lambda ref: jnp.concatenate([ref[at:at + 1] for at in range(0, rows, SEG_LEN)], axis=0)
    firsts = second_norm(every(part), every(n1), act_firsts[...].astype(bf16))[2].astype(f32)
    gathered[z, y, c, mp] = jnp.concatenate([firsts[:, :half], firsts[:, half:]], axis=0).astype(bf16)
    slot = gathered.at[z, y, c, mp]
    copy = run.remote(slot, slot, near["x"])
    for at in range(0, rows, 64):
        here = slice(at, at + 64)
        normed, inv_std, hidden = second_norm(part[here], n1[here], act[1, here, last])
        n2[here] = normed
        i2[here] = jnp.broadcast_to(inv_std, (64, 128))
        own_out[here] = hidden
    out_copy = run.remote(
        own_out.at[pl.ds(0, rows // 2)], block_out.at[pl.ds(own_base, rows // 2)], near["x"]
    )
    run.here(own_out, block_out.at[pl.ds(own_base, rows)])
    arrive(copy)
    slot = gathered.at[z, y, c]
    copies = [run.remote(slot, slot, device) for device in (far[1], far[0], near["z"])]
    arrive(*pair_hops[3])
    arrive(*copies)
    slot = gathered.at[:, y, c]
    copy = run.remote(slot, slot, near["y"])
    step(7, 2)
    step(8, 2)
    arrive(copy)
    slot = gathered.at[:, :, c]
    arrive(run.remote(slot, slot, near["c"]))
    loads[5].wait()

    for a, b in ((n2, n2_any), (i2, i2_any), (p_back, p_back_any)):
        run.here(a, b)

    @pl.loop(0, 32)
    def _(at):
        slot = (at // 8, (at // 4) % 2, (at // 2) % 2, at % 2)
        values = gathered[slot].astype(f32)
        here = pl.ds(pl.multiple_of(at * 8, 8), 8)
        all_ref[here, :half] = values[:8]
        all_ref[here, half:width] = values[8:]
        all_ref[here, width:] = ids[slot]

    loss_passes(
        dp * 2 + mp, scale_ref[0], w_pool_ref, s_ref[4:5],
        loss_ref, gscale_ref, pre_ref, bias_grad_ref, first_grad_ref, firsts_out_ref,
        all_ref, pooled_ref, len_ref, unit_ref, lse_col_ref, lse_row_ref, pre_f_ref,
    )
    new_scale_ref[0] = scale_ref[0] - step_rate * gscale_ref[0]
    per = width // 16
    own_firsts = mm(firsts_out_ref[...], pick(width, dp * per, per).astype(bf16)).astype(bf16)
    pool_ref[...] = mm_tn(own_firsts, pre_ref[...])
    pool_bias_ref[...] = exact(bias_grad_ref[...], pick(width, dp * per, per))
    step(7, 3)
    step(8, 3)
    out_copy.wait_recv()
    for copy in run.sent:
        copy.wait_send()
    for copy in run.kept[len(loads):]:
        copy.wait()


def forward(x, segr, w_qkv, b_qv, b_in, gains, shifts, w_pool, scale, pairs, w_out, w_in, w_back):
    rows, width = x.shape[0] // 2, x.shape[1]
    cols, units = w_qkv.shape[2], w_in.shape[1]
    count = 2 * lax.axis_size("dp") * 8
    any_ = pl.BlockSpec(memory_space=pl.ANY)
    smem = pl.BlockSpec(memory_space=pltpu.SMEM)
    vmem = pl.BlockSpec(memory_space=pltpu.VMEM)
    S = jax.ShapeDtypeStruct
    head = (rows, cols)
    kept = [
        ((2 * rows, width), bf16), (w_qkv.shape, bf16), (w_out.shape, bf16), (w_in.shape, bf16), (w_back.shape, bf16),
        (head, bf16), (head, bf16), (head, bf16),
        ((rows, width), f32), ((rows, 128), f32), ((width, rows), bf16), ((width, rows), bf16), ((2, cols, rows), bf16),
        ((2, units, rows), bf16), ((2, rows, units), bf16), ((rows, width), f32), ((rows, 128), f32),
    ]
    scratch = [
        (x.shape, bf16), (w_pool.shape, bf16), (w_qkv.shape, bf16),
        (w_out.shape, bf16), (w_in.shape, bf16), (w_back.shape, bf16),
        (w_out.shape, bf16), (w_in.shape, bf16), (w_back.shape, bf16), (b_in.shape, f32),
    ] + [(head, bf16)] * 9 + [
        ((rows, width), f32), ((rows, 128), f32), ((rows, width), bf16),
        ((2, rows, units), bf16), ((2, rows, units), bf16), ((rows, width), f32), ((rows, width), f32),
        ((rows, 128), f32), ((rows, width), bf16),
        ((width, rows), bf16), ((width, rows), bf16), ((2, cols, rows), bf16), ((2, units, rows), bf16),
        ((8, units // N_CHUNK), f32), ((4, 2, 2, 2, 16, width // 2), bf16), ((4, 2, 2, 2, 8, 128), f32),
        ((count, width), bf16), ((1, width), f32), ((count, width), bf16),
        ((count, width + 128), f32), ((count, width), f32), ((count, 1), f32), ((count, width), bf16),
        ((count, 1), f32), ((1, count), f32), ((count, width), f32),
    ]
    return pl.pallas_call(
        forward_kernel,
        in_specs=[vmem] * 5 + [smem] * 2 + [any_] * 6,
        out_specs=[any_] * len(kept) + [smem] * 3 + [vmem] * 4,
        out_shape=tuple(S(*k) for k in kept) + (
            S((1,), f32), S((1,), f32), S((1,), f32), S((8, width), f32), S(b_qv.shape, f32),
            S((width // 16, width), f32), S((1, width // 16), f32),
        ),
        scratch_shapes=[pltpu.VMEM(*s) for s in scratch] + [
            pltpu.SemaphoreType.DMA((80,)), pltpu.SemaphoreType.DMA((80,)), pltpu.SemaphoreType.DMA((24,)),
        ],
        compiler_params=pltpu.CompilerParams(
            vmem_limit_bytes=56 * 1024 * 1024, collective_id=0, has_side_effects=True
        ),
        name="forward",
    )(segr, b_qv, b_in, gains, shifts, scale, pairs, x, w_pool, w_qkv, w_out, w_in, w_back)


def pick(size, start, count):
    return (
        lax.broadcasted_iota(jnp.int32, (size, count), 0)
        == start + lax.broadcasted_iota(jnp.int32, (size, count), 1)
    ).astype(f32)


def exact(a, b):
    return jnp.dot(a, b, preferred_element_type=f32, precision=lax.Precision.HIGHEST)


ORDERS = (
    ("y", "z", "x", "w"), ("z", "y", "x", "w"), ("z", "y", "x", "w"),
    ("x", "z", "y", "w"), ("y", "z", "w", "x"), ("x", "y", "z", "w"),
    ("x", "z", "y", "w"), ("x", "z", "y", "w"), ("y", "z", "x", "w"),
    ("y", "z", "x", "w"), ("x", "y", "w", "z"), ("y", "z", "x", "w"),
)
TILE = 384


def backward_kernel(
    segr_ref, g_ref, first_grad_ref, b_qv_ref,
    out_any, x_any, og_any, n2_any, i2_any, n1_any, i1_any, act_any, slope_any, low_any, xt_any, ctx_any, q_any, k_any, v_any,
    wb_o_any, wb_p_any, wi_o_any, wi_p_any, wo_o_any, wo_p_any, wq_o_any, wq_p_any,
    grad_in_any, out_half, o_back, o_in, o_qkv, o_out, o_gains, o_shifts, o_bqv, o_bin,
    one_buf, two_buf, three_buf, grad, i2, n1, i1, act, slope, low, xt, ctx, q, k, v, wb, wi, wo, wq, deltas,
    unit, got_one, got_two, got_three, got_four, got_five, sums, sums_got,
    send_sem, recv_sem, local_sem,
):
    dp, mp = lax.axis_index("dp"), lax.axis_index("mp")
    rows, width = one_buf.shape
    units = slope.shape[2]
    cols = q.shape[2]
    per = width // 16
    own_base = pl.multiple_of(mp * rows, rows)
    near = {
        "x": {"mp": 1 - mp}, "y": {"dp": flip(dp, 2)}, "z": {"dp": flip(dp, 4)}, "w": {"dp": flip(dp, 8)},
        "c": {"dp": flip(dp, 1)},
    }
    run = Copies(send_sem, recv_sem, local_sem)
    own_rows = lambda ref: ref.at[pl.ds(own_base, rows)]
    pending = {}

    def load(*pairs):
        for source, target, name in pairs:
            pending.setdefault(name, []).append(run.here(source, target))

    def need(*names):
        for name in names:
            for copy in pending.pop(name, ()):
                copy.wait()

    load((own_rows(og_any), one_buf, "two"), (n2_any, grad, "two"), (i2_any, i2, "two"))
    load((act_any, act, "act"), (wb_o_any, wb.at[0], "wb"), (wb_p_any, wb.at[1], "wb"), (slope_any, slope, "slope"))

    greet(list(near.values()))
    flight = {"outs": run.remote(out_any.at[pl.ds(own_base + rows // 2, rows // 2)], out_half, near["x"])}
    bits = {"y": 2, "z": 4, "w": 8}

    def put(at, side, dest, value):
        spot = 0
        for weight, name in zip((8, 4, 2, 1), ORDERS[at]):
            spot = spot + weight * (side if name == "x" else (dest // bits[name] + dp // bits[name]) % 2)
        unit[at, (dest + dp) % 2, spot] = value.astype(bf16)

    def arrivals(at, stage):
        return (got_one, got_two, got_three, got_four, got_five)[stage].at[at]

    def begin(at):
        flight[at, 0] = run.remote(unit.at[at, 1], arrivals(at, 0), near["c"])

    def step(at, stage):
        flight[at, stage - 1].wait_recv()
        mine, got = unit.at[at, 0], arrivals(at, stage - 1)
        count = 16 >> (stage - 1)
        half = count // 2
        if stage == 5:
            total = mine[0].astype(f32) + got[0].astype(f32)
            if at < 4:
                o_back[at % 2 * per:(at % 2 + 1) * per, at // 2 * TILE:(at // 2 + 1) * TILE] = total
            elif at < 8:
                o_in[:, (at - 4) * TILE:(at - 3) * TILE] = total
            elif at < 11:
                o_qkv[at - 8] = total
            else:
                o_out[:, :cols] = total[:per // 2]
                o_out[:, cols:] = total[per // 2:]
            return
        for n in range(half, count):
            mine[n] = mine[n] + got[n]
        flight[at, stage] = run.remote(mine.at[pl.ds(half, half)], arrivals(at, stage), near[ORDERS[at][stage - 1]])
        for n in range(half):
            mine[n] = mine[n] + got[n]

    def sum_step(stage):
        if stage:
            flight["sums", stage - 1].wait_recv()
            sums[stage] = sums[stage - 1] + sums_got[stage - 1]
        if stage < 5:
            name = ("c", "x", "y", "z", "w")[stage]
            flight["sums", stage] = run.remote(sums.at[stage], sums_got.at[stage], near[name])

    def norm_grads(source, extra, normed_ref, inv_ref, gain, low_ref, places):
        gain_sum, shift_sum, low_sum = 0.0, 0.0, 0.0
        for at in range(0, rows, 64):
            here = slice(at, at + 64)
            value = source[here].astype(f32)
            if extra is not None:
                is_first = lax.broadcasted_iota(jnp.int32, (64, width), 0) == 0
                value = value + jnp.where(is_first, extra[at // 64:at // 64 + 1], 0.0)
            normed = normed_ref[here]
            out = norm_back(value, normed, inv_ref[here, 0:1], gain)
            rounded = out.astype(bf16)
            grad[here] = out
            low_ref[here] = rounded
            gain_sum += jnp.sum(value * normed, axis=0, keepdims=True)
            shift_sum += jnp.sum(value, axis=0, keepdims=True)
            low_sum += jnp.sum(rounded.astype(f32), axis=0, keepdims=True)
        for place, value in zip(places, (gain_sum, shift_sum, low_sum)):
            sums[0, place:place + 1] = value

    def second_norm():
        need("two")
        sums[0] = jnp.zeros(sums.shape[1:], f32)
        norm_grads(one_buf, first_grad_ref, grad, i2, g_ref[1:2], two_buf, (1, 5, 4))
        load((wi_o_any, wi.at[0], "wi"), (wi_p_any, wi.at[1], "wi"), (low_any, low, "low"))
        load((n1_any, n1, "one"), (i1_any, i1, "one"))

    def back_weight(half):
        need("act")
        for side in range(2):
            for top in range(0, units, TILE):
                tile = mm(act[side, top:top + TILE], two_buf[:, half * cols:(half + 1) * cols])
                for at in range(0, TILE, per):
                    put(2 * half + at // per % 2, side, (top + at) // (2 * per), tile[at:at + per])

    def inner_grads(side):
        need("wb", "slope")
        owner = mp + side - 2 * mp * side
        for at in range(0, units, 256):
            here = slice(at, at + 256)
            value = (mm_nt(two_buf[...], wb[side, here]) * slope[side, :, here].astype(f32)).astype(bf16)
            slope[side, :, here] = value
            sums[0, pl.ds(8 + 2 * owner + at // width, 1), at % width:at % width + 256] = jnp.sum(
                value.astype(f32), axis=0, keepdims=True
            )
        if side == 0:
            load((ctx_any, ctx, "ctx"), (wo_o_any, wo.at[0], "wo"), (wo_p_any, wo.at[1], "wo"))
            load((own_rows(x_any), three_buf, "x"), (wq_p_any, wq.at[1], "wq_p"))

    def feed_back():
        need("wi")
        for at in range(0, width, 256):
            here = slice(at, at + 256)
            grad[:, here] = grad[:, here] + mm_nt(slope[0], wi[0, here]) + mm_nt(slope[1], wi[1, here])
        load((q_any, q.at[0], "qkv"), (k_any, k.at[0], "qkv"), (v_any, v.at[0], "qkv"))
        load((xt_any, xt, "xt"), (wq_o_any, wq.at[0], "wq_o"))

    def first_norm_back():
        need("one")
        norm_grads(grad, None, n1, i1, g_ref[0:1], one_buf, (0, 3, 2))

    def in_weight(half):
        need("low")
        for at in range(2 * half, 2 * half + 2):
            for side in range(2):
                for top in range(0, width, TILE):
                    tile = mm(low[top:top + TILE], slope[side, :, at * TILE:(at + 1) * TILE])
                    for row in range(0, TILE, per):
                        put(4 + at, side, (top + row) // per, tile[row:row + per])

    def out_weight():
        need("ctx")
        for side in range(2):
            tile = mm(ctx[side], one_buf[...])
            for dest in range(16):
                part = tile[dest * per // 2:(dest + 1) * per // 2]
                put(11, side, dest, jnp.concatenate([part[:, :cols], part[:, cols:]], axis=0))

    def context_grads():
        need("wo")
        for side in range(2):
            two_buf[:, side * cols:(side + 1) * cols] = mm_nt(one_buf[...], wo[side]).astype(bf16)

    def again():
        need("x", "wq_p")
        q[1] = (mm(three_buf[...], wq[1, 0]) + b_qv_ref[0:1]).astype(bf16)
        k[1] = mm(three_buf[...], wq[1, 1]).astype(bf16)
        v[1] = (mm(three_buf[...], wq[1, 2]) + b_qv_ref[1:2]).astype(bf16)

    def attend_back(side, groups):
        need("qkv")
        scale = HEAD_DIM ** (-0.5)
        for group in groups:
            at = slice(group * GROUP, (group + 1) * GROUP)
            one = same_block(segr_ref[:, pl.ds(pl.multiple_of(own_base + group * GROUP, GROUP), GROUP)])
            same = jnp.concatenate([one, one], axis=1)
            for pair in range(cols // PAIR):
                lanes = slice(pair * PAIR, (pair + 1) * PAIR)
                q_two = two_heads(q[side, at, lanes])
                dc_two = two_heads(two_buf[at, side * cols + pair * PAIR:side * cols + (pair + 1) * PAIR])
                k_pair, v_pair = k[side, at, lanes], v[side, at, lanes]
                scores = jnp.where(same, mm_nt(k_pair, q_two) * scale, masked_out)
                shifted = jnp.exp(scores - jnp.max(scores, axis=0, keepdims=True))
                probs = shifted / jnp.sum(shifted, axis=0, keepdims=True)
                prob_grad = mm_nt(v_pair, dc_two)
                score_grad = (
                    probs * (prob_grad - jnp.sum(prob_grad * probs, axis=0, keepdims=True))
                ).astype(bf16)
                deltas[side, 0, at, lanes] = (join_heads(mm_tn(score_grad, k_pair)) * scale).astype(bf16)
                deltas[side, 1, at, lanes] = (mm(score_grad, q_two) * scale).astype(bf16)
                deltas[side, 2, at, lanes] = mm(probs.astype(bf16), dc_two).astype(bf16)

    def qkv_weight(s):
        need("xt")
        for side in range(2):
            for top in range(0, width, TILE):
                tile = mm(xt[top:top + TILE], deltas[side, s])
                for at in range(0, TILE, per):
                    put(8 + s, side, (top + at) // per, tile[at:at + per])
            if s != 1:
                owner = mp + side - 2 * mp * side
                lanes = pl.ds(pl.multiple_of(owner * cols, 128), cols)
                sums[0, 6 + s // 2:7 + s // 2, lanes] = jnp.sum(deltas[side, s].astype(f32), axis=0, keepdims=True)

    def input_grads():
        need("wq_o", "wq_p")
        for at in range(0, width, 256):
            here = slice(at, at + 256)
            value = grad[:, here]
            for side in range(2):
                for s in range(3):
                    value = value + mm_nt(deltas[side, s], wq[side, s, here])
            three_buf[:, here] = value.astype(bf16)
        flight["inputs"] = run.remote(three_buf, own_rows(grad_in_any), near["x"])
        run.here(three_buf, own_rows(grad_in_any))

    second_norm()
    back_weight(1)
    begin(2)
    begin(3)
    inner_grads(0)
    back_weight(0)
    begin(0)
    begin(1)
    step(2, 1)
    step(3, 1)
    inner_grads(1)
    step(0, 1)
    in_weight(1)
    begin(6)
    begin(7)
    step(1, 1)
    in_weight(0)
    begin(4)
    begin(5)
    step(6, 1)
    again()
    step(7, 1)
    step(4, 1)
    step(2, 2)
    step(3, 2)
    feed_back()
    step(5, 1)
    step(0, 2)
    first_norm_back()
    context_grads()
    step(1, 2)
    attend_back(0, (0, 1))
    step(6, 2)
    out_weight()
    begin(11)
    step(4, 2)
    step(3, 3)
    attend_back(1, (2, 3))
    step(2, 3)
    step(11, 1)
    step(0, 3)
    attend_back(0, (2, 3))
    step(7, 2)
    attend_back(1, (0, 1))
    step(1, 3)
    step(6, 3)
    step(3, 4)
    qkv_weight(2)
    begin(10)
    qkv_weight(0)
    sum_step(0)
    begin(8)
    step(4, 3)
    step(5, 2)
    qkv_weight(1)
    begin(9)
    sum_step(1)
    step(10, 1)
    step(2, 4)
    input_grads()
    step(1, 4)
    step(7, 3)
    sum_step(2)
    step(3, 5)
    step(6, 4)
    step(0, 4)
    step(11, 2)
    step(8, 1)
    step(9, 1)
    step(4, 4)
    step(5, 3)
    step(2, 5)
    step(7, 4)
    step(1, 5)
    sum_step(3)
    step(10, 2)
    step(6, 5)
    step(0, 5)
    step(11, 3)
    step(8, 2)
    step(5, 4)
    step(7, 5)
    sum_step(4)
    step(9, 2)
    step(8, 3)
    step(5, 5)
    step(10, 3)
    sum_step(5)
    total = sums[5]
    vectors = exact(total[0:8], pick(width, dp * per, per))
    o_gains[...] = vectors[0:2]
    o_shifts[...] = vectors[2:6]
    o_bqv[...] = exact(total[0:8], pick(width, mp * cols + dp * (per // 2), per // 2))[6:8]
    few = units // 16
    o_bin[...] = exact(sums[5, pl.ds(8 + 2 * mp + dp // 8, 1), :], pick(width, (dp % 8) * few, few))
    step(4, 5)
    step(9, 3)
    step(11, 4)
    step(8, 4)
    step(10, 4)
    step(9, 4)
    step(11, 5)
    step(8, 5)
    step(10, 5)
    step(9, 5)
    flight["inputs"].wait_recv()
    flight["outs"].wait_recv()
    for copy in run.sent:
        copy.wait_send()
    run.kept[-1].wait()


def backward(segr, gains, first_grad, b_qv, *arrays):
    rows, width = arrays[3].shape
    units = arrays[8].shape[2]
    cols = arrays[12].shape[1]
    any_ = pl.BlockSpec(memory_space=pl.ANY)
    vmem = pl.BlockSpec(memory_space=pltpu.VMEM)
    S = jax.ShapeDtypeStruct
    per = width // 16
    count = len(ORDERS)
    scratch = [((rows, width), bf16)] * 3 + [
        ((rows, width), f32), ((rows, 128), f32), ((rows, width), f32), ((rows, 128), f32),
        ((2, units, rows), bf16), ((2, rows, units), bf16), ((width, rows), bf16), ((width, rows), bf16),
        ((2, cols, rows), bf16), ((2, rows, cols), bf16), ((2, rows, cols), bf16), ((2, rows, cols), bf16),
        ((2, units, width), bf16), ((2, width, units), bf16), ((2, cols, width), bf16), ((2, 3, width, cols), bf16),
        ((2, 3, rows, cols), bf16), ((count, 2, 16, per, TILE), bf16),
    ] + [((count, n, per, TILE), bf16) for n in (16, 8, 4, 2, 1)] + [((6, 16, width), f32), ((5, 16, width), f32)]
    return pl.pallas_call(
        backward_kernel,
        in_specs=[vmem] * 4 + [any_] * len(arrays),
        out_specs=[any_] * 2 + [vmem] * 8,
        out_shape=(
            S((2 * rows, width), bf16), S((rows // 2, width), bf16), S((2 * per, width), f32), S((per, 2 * width), f32),
            S((3, per, cols), f32),
            S((cols // 16, width), f32), S((2, per), f32), S((4, per), f32), S((2, cols // 16), f32),
            S((1, units // 16), f32),
        ),
        scratch_shapes=[pltpu.VMEM(*s) for s in scratch] + [
            pltpu.SemaphoreType.DMA((72,)), pltpu.SemaphoreType.DMA((72,)), pltpu.SemaphoreType.DMA((28,)),
        ],
        compiler_params=pltpu.CompilerParams(
            vmem_limit_bytes=63 * 1024 * 1024, collective_id=1, has_side_effects=True
        ),
        name="backward",
    )(segr, gains, first_grad, b_qv, *arrays)


FINISH_PARTS = 4


def finish_kernel(*refs):
    grads_any, outs_any, half_any = refs[:3]
    count = (len(refs) - 8) // 3
    sources = refs[3:3 + count]
    wide_any, outs_to = refs[3 + count:5 + count]
    targets = refs[5 + count:5 + 2 * count]
    grads, wide, outs = refs[5 + 2 * count:8 + 2 * count]
    held = refs[8 + 2 * count:-2]
    load_sem, store_sem = refs[-2:]
    part = grads.shape[0] // FINISH_PARTS
    other = 1 - lax.axis_index("mp")
    loads, stores = [], []

    def copy(into, source, target, sem):
        into.append(pltpu.make_async_copy(source, target, sem.at[len(into)]))
        into[-1].start()

    def rows(ref, at):
        return ref.at[pl.ds(pl.multiple_of(at * part, part), part)]

    for at in range(FINISH_PARTS):
        copy(loads, rows(grads_any, at), rows(grads, at), load_sem)
    lates = 2 * other + 1
    kept = [2 * (1 - other), 2 * (1 - other) + 1, 2 * other]
    for at in kept:
        copy(loads, rows(outs_any, at), rows(outs, at), load_sem)
    copy(loads, half_any, rows(outs, lates), load_sem)
    for source, target in zip(sources, held):
        copy(loads, source, target, load_sem)
    for at in range(FINISH_PARTS):
        loads[at].wait()
        here = slice(at * part, (at + 1) * part)
        wide[here] = grads[here].astype(f32)
        copy(stores, rows(wide, at), rows(wide_any, at), store_sem)
    for n, at in enumerate(kept + [lates]):
        loads[FINISH_PARTS + n].wait()
        copy(stores, rows(outs, at), rows(outs_to, at), store_sem)
    for n in range(count):
        loads[2 * FINISH_PARTS + n].wait()
        copy(stores, held[n], targets[n], store_sem)
    for store in stores:
        store.wait()


def finish(grad_inputs, block_out, late_half, *arrays):
    any_ = pl.BlockSpec(memory_space=pl.ANY)
    results = (jax.ShapeDtypeStruct(grad_inputs.shape, f32),) + tuple(
        jax.ShapeDtypeStruct(a.shape, a.dtype) for a in (block_out,) + arrays
    )
    copies = 2 * FINISH_PARTS + len(arrays)
    return pl.pallas_call(
        finish_kernel,
        in_specs=[any_] * (3 + len(arrays)),
        out_specs=[any_] * len(results),
        out_shape=results,
        scratch_shapes=[
            pltpu.VMEM(grad_inputs.shape, bf16), pltpu.VMEM(grad_inputs.shape, f32), pltpu.VMEM(block_out.shape, bf16),
        ] + [pltpu.VMEM(a.shape, a.dtype) for a in arrays] + [
            pltpu.SemaphoreType.DMA((copies,)), pltpu.SemaphoreType.DMA((copies,)),
        ],
        compiler_params=params(60),
        name="finish",
    )(grad_inputs, block_out, late_half, *arrays)


def swap_mp(values):
    return lax.ppermute(values, "mp", [(0, 1), (1, 0)])


def swap_dp(values, bit):
    size = lax.axis_size("dp")
    return lax.ppermute(values, "dp", [(at, at ^ bit) for at in range(size)])


def fetch(own, axis, place):
    size = own.shape[axis] // 4
    first = swap_mp(lax.dynamic_slice_in_dim(own, place * size, size, axis))
    second = swap_dp(first, 2)
    third = swap_dp(first, 1)
    fourth = swap_dp(second, 1)
    whole = jnp.zeros_like(own)
    for bits, part in ((0, first), (2, second), (1, third), (3, fourth)):
        whole = lax.dynamic_update_slice_in_dim(whole, part, (place ^ bits) * size, axis)
    return whole


def gather_rows(rows):
    size = lax.axis_size("dp")
    if size != 16:
        return lax.all_gather(rows, ("dp", "mp"), axis=0, tiled=True)
    rows = jnp.concatenate([rows, swap_mp(rows)], axis=0)
    for bit in (1, 2, 4, 8):
        rows = jnp.concatenate([rows, swap_dp(rows, bit)], axis=0)
    return rows


def both_halves(own, mp):
    other = swap_mp(own)
    return jnp.concatenate([jnp.where(mp == 0, own, other), jnp.where(mp == 0, other, own)], axis=0)


def add(a, b):
    return (a.astype(f32) + b.astype(f32)).astype(a.dtype)


def scatter_sum(keep, send, order):
    size = lax.axis_size("dp")
    if size != 16:
        rest = keep.shape[2:]
        both = jnp.stack([keep, send], axis=2)
        both = both.reshape((2, 16) + rest)
        mine = add(both[0], swap_mp(both[1]))
        return mine
    got = swap_dp(send, 1)
    rest = keep.shape[2:]
    names = ["x", "z1", "z0", "y"]
    keep = keep.reshape((2, 2, 2, 2) + rest)
    got = got.reshape((2, 2, 2, 2) + rest)
    bit_of = {"y": 2, "z0": 4, "z1": 8}
    for name in order:
        axis = names.index(name)
        names.remove(name)
        pick = lambda values, at: lax.index_in_dim(values, at, axis, keepdims=False)
        out = add(pick(keep, 1), pick(got, 1))
        out = swap_mp(out) if name == "x" else swap_dp(out, bit_of[name])
        keep = add(pick(keep, 0), pick(got, 0))
        got = out
    return add(keep, got)


def swap_order(values, axis, place):
    shape = values.shape
    split = values.reshape(shape[:axis] + (2, 2, 2, 2) + shape[axis + 1:])
    for at, bit in enumerate((8, 4, 2, 1)):
        low = lax.index_in_dim(split, 0, axis + at)
        high = lax.index_in_dim(split, 1, axis + at)
        flipped = jnp.concatenate([high, low], axis=axis + at)
        split = jnp.where((place & bit) != 0, flipped, split)
    return split.reshape(shape)


def shards(
    inputs, segment_ids, pair_index, w_qkv, bias_qv, w_out, w_in, bias_in, w_back,
    w_pool, norm_gains, shifts, logit_scale, out_grad,
):
    tok_rows, width = inputs.shape
    size = lax.axis_size("dp")
    dp, mp = lax.axis_index("dp"), lax.axis_index("mp")
    rows = tok_rows // 2
    blocks = rows // SEG_LEN
    place = dp % 4
    slots = 0 * dp
    pos = jnp.reshape(slots, (1,)).astype(jnp.int32)

    x = lax.dynamic_slice_in_dim(inputs, mp * rows, rows, 0)
    cot = lax.dynamic_slice_in_dim(out_grad, mp * rows, rows, 0)
    seg = lax.dynamic_slice_in_dim(segment_ids, mp * rows, rows, 0)
    segc, segr = seg.reshape(rows, 1), seg.reshape(1, rows)
    pairs = lax.dynamic_slice_in_dim(pair_index, mp * blocks, blocks, 0)

    cols = w_qkv.shape[2]
    units = w_in.shape[1]
    if size == 16:
        segr = segment_ids.reshape(1, -1)
        (
            block_out, w_qkv_p, w_out_p, w_in_p, w_back_p, q, k, v, n1, i1, lowt, xt, ctxt, actt, slope, n2, i2,
            loss_value, grad_scale, new_scale, first_grad, bias_qv_p, grad_pool, pool_bias,
        ) = forward(
            inputs, segr, w_qkv, bias_qv, bias_in.reshape(-1, 128),
            norm_gains, shifts, w_pool, logit_scale, pair_index, w_out, w_in, w_back,
        )
        results = backward(
            segr, norm_gains, first_grad, bias_qv_p, block_out,
            inputs, out_grad, n2, i2, n1, i1, actt, slope, lowt, xt, ctxt, q, k, v,
            w_back, w_back_p, w_in, w_in_p, w_out, w_out_p, w_qkv, w_qkv_p,
        )
        (
            grad_inputs, block_out, grad_back, grad_in, grad_qkv, grad_out, gains, shift_grads, grad_bias_qv,
            grad_bias_in, grad_pool, pool_bias,
        ) = finish(results[0], block_out, results[1], *results[2:], grad_pool, pool_bias)
        return (
            block_out, loss_value, grad_inputs, grad_qkv, grad_bias_qv, grad_out, grad_in,
            grad_bias_in[0], grad_back, grad_pool, gains, shift_grads, pool_bias[0], grad_scale, new_scale,
        )

    biases = swap_mp(bias_qv)
    bias_qv_p, bias_in_p = biases, swap_mp(bias_in)
    w_qkv_p = fetch(w_qkv, 1, place)
    w_out_p = fetch(w_out, 0, place)
    w_in_p = fetch(w_in, 0, place)
    w_back_p = fetch(w_back, 0, place)

    q_o, k_o, v_o, ctx_o = attention_half(x, w_qkv, bias_qv, segc, segr)
    q_p, k_p, v_p, ctx_p = attention_half(x, w_qkv_p, bias_qv_p, segc, segr)
    normed_one, inv_one, low_one = first_norm(ctx_o, ctx_p, w_out, w_out_p, x, norm_gains, shifts)
    act_o, slope_o = inner_half(low_one, w_in, bias_in.reshape(1, -1))
    part = branch_half(act_o, w_back)
    act_p, slope_p = inner_half(low_one, w_in_p, bias_in_p.reshape(1, -1))
    normed_two, inv_two, own_out = second_norm(act_p, w_back_p, part, normed_one, norm_gains, shifts)

    firsts = own_out.reshape(blocks, SEG_LEN, width)[:, 0]
    ids = jnp.broadcast_to(pairs.astype(f32)[:, None], (blocks, 128))
    rel = jnp.concatenate([gather_rows(firsts).astype(f32), gather_rows(ids)], axis=1)
    linear = dp * 2 + mp
    position = jnp.stack([linear if size == 16 else 0 * linear, linear]).astype(jnp.int32)
    loss_value, grad_scale, pre_all, pool_bias, first_grad, firsts_all = pair_loss(
        position, rel, w_pool, shifts[4:5], logit_scale
    )
    block_out = both_halves(own_out, mp)
    pool_rows = width // size
    grad_pool = lax.dot_general(
        lax.dynamic_slice_in_dim(firsts_all, dp * pool_rows, pool_rows, 1), pre_all, TN, preferred_element_type=f32
    )
    grad_pool_bias = lax.dynamic_slice_in_dim(pool_bias[0], dp * pool_rows, pool_rows, 0)

    grad_two, branch, sums_two = second_back(cot, first_grad, normed_two, inv_two, norm_gains)
    keep_bo, send_bo = back_weight(pos, act_o, branch)
    keep_bp, send_bp = back_weight(pos, act_p, branch)
    keep_io, send_io, bias_io, part_one = inner_back(pos, branch, w_back, slope_o, low_one, w_in, grad_two)
    keep_ip, send_ip, bias_ip, part_two = inner_back(pos, branch, w_back_p, slope_p, low_one, w_in_p, part_one)
    grad_one, sums_one, dc_o, dc_p, keep_w, send_w = first_back(
        pos, part_two, normed_one, inv_one, norm_gains, ctx_o, ctx_p, w_out, w_out_p
    )
    keep_qo, send_qo, bias_qo, in_one = attention_back(pos, x, w_qkv, segc, segr, q_o, k_o, v_o, dc_o, grad_one)
    keep_qp, send_qp, bias_qp, in_two = attention_back(pos, x, w_qkv_p, segc, segr, q_p, k_p, v_p, dc_p, in_one)

    both = lambda a, b: jnp.stack([a, b])
    mine_back = scatter_sum(both(keep_bo, keep_bp), both(send_bo, send_bp), ("x", "y", "z0", "z1"))
    mine_in = scatter_sum(both(keep_io, keep_ip), both(send_io, send_ip), ("y", "x", "z0", "z1"))
    mine_out = scatter_sum(keep_w, send_w, ("x", "y", "z0", "z1"))
    mine_qkv = scatter_sum(both(keep_qo, keep_qp), both(send_qo, send_qp), ("y", "x", "z0", "z1"))

    vectors = jnp.concatenate([sums_one[0:1], sums_two[0:1], sums_one[2:3], sums_one[1:2], sums_two[2:3], sums_two[1:2]])
    by_dp = vectors.reshape(6, 16, width // 16).transpose(1, 0, 2).reshape(16, -1)
    by_dp = jnp.broadcast_to(by_dp[None], (2,) + by_dp.shape)
    bias_q = both(bias_qo, bias_qp).reshape(2, 2, 16, cols // 16).transpose(0, 2, 1, 3).reshape(2, 16, -1)
    bias_i = both(bias_io, bias_ip).reshape(2, 16, units // 16)
    packed = jnp.concatenate([by_dp, bias_q, bias_i], axis=2)
    packed = swap_order(packed, 1, slots).reshape(2, 8, 2, -1)
    mine_small = scatter_sum(packed[:, :, 0], packed[:, :, 1], ("y", "x", "z0", "z1"))

    if size != 16:
        fold = lambda values: lax.psum_scatter(values, "dp", scatter_dimension=0, tiled=True)
        grad_back = fold(mine_back.reshape(units, width).astype(f32))
        grad_in = fold(mine_in.reshape(width, units).astype(f32))
        grad_qkv = fold(mine_qkv.transpose(0, 2, 1, 3).reshape(width, 3, cols).astype(f32)).transpose(1, 0, 2)
        small = mine_small
        n_vec = 6 * (width // 16)
        n_q = 2 * (cols // 16)
        n_i = units // 16
        vec = small[:, :n_vec].reshape(16, 6, -1).transpose(0, 2, 1).reshape(width, 6)
        vec = fold(vec).T
        grad_bias_qv = fold(small[:, n_vec:n_vec + n_q].reshape(16, 2, -1).transpose(0, 2, 1).reshape(cols, 2)).T
        grad_bias_in = fold(small[:, n_vec + n_q:n_vec + n_q + n_i].reshape(units))
        grad_out = fold(mine_out.reshape(cols, width).astype(f32))
    else:
        grad_back = mine_back.astype(f32)
        grad_in = mine_in.astype(f32)
        grad_qkv = mine_qkv.astype(f32)
        small = mine_small
        n_vec = 6 * (width // 16)
        n_q = 2 * (cols // 16)
        n_i = units // 16
        vec = small[:n_vec].reshape(6, -1)
        grad_bias_qv = small[n_vec:n_vec + n_q].reshape(2, -1)
        grad_bias_in = small[n_vec + n_q:n_vec + n_q + n_i]
        grad_out = mine_out.astype(f32)

    grad_inputs = both_halves(in_two.astype(bf16), mp).astype(f32)
    new_scale = logit_scale - step_rate * grad_scale
    return (
        block_out, loss_value, grad_inputs, grad_qkv, grad_bias_qv, grad_out, grad_in, grad_bias_in,
        grad_back, grad_pool, vec[:2], vec[2:], grad_pool_bias, grad_scale, new_scale,
    )


def solution(mesh):
    return jax.shard_map(
        shards,
        mesh=mesh,
        in_specs=(
            P("dp", None), P("dp"), P("dp"), P(None, None, "mp"), P(None, "mp"), P("mp", None), P(None, "mp"),
            P("mp"), P("mp", None), P(), P(), P(), P(), P("dp", None),
        ),
        out_specs=(
            P("dp", None), P(), P("dp", None), P(None, "dp", "mp"), P(None, ("mp", "dp")), P(("mp", "dp"), None),
            P("dp", "mp"), P(("mp", "dp")), P(("mp", "dp"), None), P("dp", None), P(None, "dp"), P(None, "dp"),
            P("dp"), P(), P(),
        ),
        check_vma=False,
    )
```

```python
from functools import partial

import jax
import jax.numpy as jnp
from jax import lax
from jax.experimental import pallas as pl
from jax.experimental.pallas import tpu as pltpu
from jax.sharding import PartitionSpec as P

HEAD_DIM = 64
SEG_LEN = 64
PAIR = 2 * HEAD_DIM
GROUP = 128

epsilon = 1e-12
margin = 0.3
step_rate = 0.1
masked_out = -1e30
f32 = jnp.float32
bf16 = jnp.bfloat16

NT = (((1,), (1,)), ((), ()))
TN = (((0,), (0,)), ((), ()))


def mm(a, b):
    return jnp.dot(a, b, preferred_element_type=f32)


def mm_nt(a, b):
    return lax.dot_general(a, b, NT, preferred_element_type=f32)


def mm_tn(a, b):
    return lax.dot_general(a, b, TN, preferred_element_type=f32)


def params(mib=40):
    return pltpu.CompilerParams(vmem_limit_bytes=mib * 1024 * 1024)


def cost(flops, moved):
    return pl.CostEstimate(flops=int(flops), bytes_accessed=int(moved), transcendentals=0)


def lane_masks():
    lane = lax.broadcasted_iota(jnp.int32, (1, PAIR), 1)
    first = (lane < HEAD_DIM).astype(f32)
    return first, 1.0 - first


def two_heads(rows):
    first, second = lane_masks()
    return jnp.concatenate([rows * first.astype(bf16), rows * second.astype(bf16)], axis=0)


def join_heads(both):
    first, second = lane_masks()
    half = both.shape[0] // 2
    return both[:half] * first + both[half:] * second


def pair_probs(q_two, k_pair, same):
    scores = mm_nt(q_two, k_pair) * (HEAD_DIM ** (-0.5))
    scores = jnp.where(same, scores, masked_out)
    shifted = jnp.exp(scores - jnp.max(scores, axis=1, keepdims=True))
    return shifted / jnp.sum(shifted, axis=1, keepdims=True)


def same_segment(seg_col, seg_row, rows):
    own = seg_col[rows, :]
    other = seg_row[:, rows]
    one = own == other
    return jnp.concatenate([one, one], axis=0)


def attention_kernel(x_ref, w_ref, b_ref, segc_ref, segr_ref, q_ref, k_ref, v_ref, c_ref):
    x = x_ref[...]
    q_ref[...] = (mm(x, w_ref[0]) + b_ref[0:1]).astype(bf16)
    k_ref[...] = mm(x, w_ref[1]).astype(bf16)
    v_ref[...] = (mm(x, w_ref[2]) + b_ref[1:2]).astype(bf16)
    for group in range(x.shape[0] // GROUP):
        rows = slice(group * GROUP, (group + 1) * GROUP)
        same = same_segment(segc_ref, segr_ref, rows)
        for pair in range(q_ref.shape[1] // PAIR):
            cols = slice(pair * PAIR, (pair + 1) * PAIR)
            probs = pair_probs(two_heads(q_ref[rows, cols]), k_ref[rows, cols], same)
            c_ref[rows, cols] = join_heads(mm(probs.astype(bf16), v_ref[rows, cols])).astype(bf16)


def attention_half(x, w, b, segc, segr):
    rows, cols = x.shape[0], w.shape[2]
    out = jax.ShapeDtypeStruct((rows, cols), bf16)
    return pl.pallas_call(
        attention_kernel,
        out_shape=(out,) * 4,
        compiler_params=params(),
        cost_estimate=cost(2 * rows * 768 * cols * 3 * 2, 6 * rows * cols * 2),
        name="attention",
    )(x, w, b, segc, segr)


def norm_rows(values):
    row_mean = jnp.mean(values, axis=-1, keepdims=True)
    centred = values - row_mean
    inv_std = lax.rsqrt(jnp.mean(centred * centred, axis=-1, keepdims=True) + epsilon)
    return centred * inv_std, inv_std


def norm_back(grad, normed, inv_std, gain):
    scaled = grad * gain
    return inv_std * (
        scaled
        - jnp.mean(scaled, axis=-1, keepdims=True)
        - normed * jnp.mean(scaled * normed, axis=-1, keepdims=True)
    )


def first_norm_kernel(co_ref, cp_ref, wo_ref, wp_ref, x_ref, g_ref, s_ref, n_ref, inv_ref, low_ref):
    for at in range(0, x_ref.shape[0], 128):
        rows = slice(at, at + 128)
        attended = mm(co_ref[rows], wo_ref[...]) + mm(cp_ref[rows], wp_ref[...]) + s_ref[0:1]
        normed, inv_std = norm_rows(x_ref[rows].astype(f32) + attended)
        n_ref[rows] = normed
        inv_ref[rows] = inv_std
        low_ref[rows] = (normed * g_ref[0:1] + s_ref[1:2]).astype(bf16)


def first_norm(ctx_o, ctx_p, wo, wp, x, gains, shifts):
    rows, width = x.shape
    return pl.pallas_call(
        first_norm_kernel,
        out_shape=(
            jax.ShapeDtypeStruct((rows, width), f32),
            jax.ShapeDtypeStruct((rows, 1), f32),
            jax.ShapeDtypeStruct((rows, width), bf16),
        ),
        compiler_params=params(),
        cost_estimate=cost(2 * rows * width * width, 12 * rows * width),
        name="first_norm",
    )(ctx_o, ctx_p, wo, wp, x, gains, shifts)


def inner_kernel(h_ref, w_ref, b_ref, act_ref, slope_ref):
    for at in range(0, h_ref.shape[0], 128):
        rows = slice(at, at + 128)
        inner = mm(h_ref[rows], w_ref[...]) + b_ref[...]
        cumulative = 0.5 * (1.0 + lax.erf(inner * 0.7071067811865476))
        density = jnp.exp(-0.5 * inner * inner) * 0.3989422804014327
        act_ref[rows] = (inner * cumulative).astype(bf16)
        slope_ref[rows] = (cumulative + inner * density).astype(bf16)


def inner_half(low, w, b):
    rows, width = low.shape
    units = w.shape[1]
    tile = 256
    out = jax.ShapeDtypeStruct((rows, units), bf16)
    return pl.pallas_call(
        inner_kernel,
        grid=(units // tile,),
        in_specs=[
            pl.BlockSpec((rows, width), lambda n: (0, 0)),
            pl.BlockSpec((width, tile), lambda n: (0, n)),
            pl.BlockSpec((1, tile), lambda n: (0, n)),
        ],
        out_specs=[pl.BlockSpec((rows, tile), lambda n: (0, n))] * 2,
        out_shape=(out, out),
        compiler_params=params(),
        cost_estimate=cost(4 * rows * width * units, 8 * rows * units),
        name="inner",
    )(low, w, b)


def branch_kernel(act_ref, w_ref, out_ref):
    for at in range(0, act_ref.shape[0], 128):
        rows = slice(at, at + 128)
        out_ref[rows] = mm(act_ref[rows], w_ref[...])


def branch_half(act, w):
    rows, units = act.shape
    width = w.shape[1]
    return pl.pallas_call(
        branch_kernel,
        out_shape=jax.ShapeDtypeStruct((rows, width), f32),
        compiler_params=params(),
        cost_estimate=cost(2 * rows * width * units, 4 * rows * units),
        name="branch",
    )(act, w)


def second_norm_kernel(act_ref, w_ref, part_ref, n1_ref, g_ref, s_ref, n_ref, inv_ref, out_ref):
    for at in range(0, act_ref.shape[0], 128):
        rows = slice(at, at + 128)
        branch = mm(act_ref[rows], w_ref[...]) + part_ref[rows] + s_ref[2:3]
        hidden_one = n1_ref[rows] * g_ref[0:1] + s_ref[1:2]
        normed, inv_std = norm_rows(hidden_one + branch)
        n_ref[rows] = normed
        inv_ref[rows] = inv_std
        out_ref[rows] = (normed * g_ref[1:2] + s_ref[3:4]).astype(bf16)


def second_norm(act, w, part, normed_one, gains, shifts):
    rows, units = act.shape
    width = w.shape[1]
    return pl.pallas_call(
        second_norm_kernel,
        out_shape=(
            jax.ShapeDtypeStruct((rows, width), f32),
            jax.ShapeDtypeStruct((rows, 1), f32),
            jax.ShapeDtypeStruct((rows, width), bf16),
        ),
        compiler_params=params(),
        cost_estimate=cost(2 * rows * width * units, 4 * rows * units),
        name="second_norm",
    )(act, w, part, normed_one, gains, shifts)


def loss_kernel(
    pos_ref, rel_ref, w_ref, bias_ref, scale_ref,
    loss_ref, gscale_ref, pre_ref, bias_grad_ref, first_grad_ref, firsts_out_ref,
    all_ref, pooled_ref, len_ref, unit_ref, lse_col_ref, lse_row_ref, pre_f_ref,
):
    @pl.loop(0, pooled_ref.shape[0] // 8)
    def _(slot):
        source = pl.multiple_of(slot * 8, 8)
        target = pl.multiple_of(jnp.bitwise_xor(slot, pos_ref[0]) * 8, 8)
        all_ref[pl.ds(target, 8), :] = rel_ref[pl.ds(source, 8), :].astype(f32)

    loss_passes(
        pos_ref[1], scale_ref[0], w_ref, bias_ref[...],
        loss_ref, gscale_ref, pre_ref, bias_grad_ref, first_grad_ref, firsts_out_ref,
        all_ref, pooled_ref, len_ref, unit_ref, lse_col_ref, lse_row_ref, pre_f_ref,
    )


def loss_passes(
    here, scale, w_ref, bias,
    loss_ref, gscale_ref, pre_ref, bias_grad_ref, first_grad_ref, firsts_out_ref,
    all_ref, pooled_ref, len_ref, unit_ref, lse_col_ref, lse_row_ref, pre_f_ref,
):
    count, width = pooled_ref.shape
    chunk = min(count, 256)
    steps = count // chunk

    def pool(at):
        firsts = all_ref[pl.ds(at, chunk), :width].astype(bf16)
        firsts_out_ref[pl.ds(at, chunk), :] = firsts
        pooled = jnp.tanh(mm(firsts, w_ref[...]) + bias)
        inv_len = lax.rsqrt(jnp.sum(pooled * pooled, axis=-1, keepdims=True) + 1e-06)
        pooled_ref[pl.ds(at, chunk), :] = pooled
        len_ref[pl.ds(at, chunk), :] = inv_len
        unit_ref[pl.ds(at, chunk), :] = (pooled * inv_len).astype(bf16)

    def positions(at):
        own = at + lax.broadcasted_iota(jnp.int32, (chunk, count), 0)
        other = lax.broadcasted_iota(jnp.int32, (chunk, count), 1)
        paired = all_ref[pl.ds(at, chunk), width:width + 1]
        positive = paired.astype(jnp.int32) == other
        return own == other, positive

    def logits_of(at):
        cosine = mm_nt(unit_ref[pl.ds(at, chunk), :], unit_ref[...])
        own, positive = positions(at)
        shifted = cosine - jnp.where(positive, margin, 0.0)
        return shifted, own, positive

    def first_pass(at, run):
        shifted, own, positive = logits_of(at)
        logits = jnp.where(own, masked_out, scale * shifted)
        top = jnp.max(logits, axis=1, keepdims=True)
        lse = top + jnp.log(jnp.sum(jnp.exp(logits - top), axis=1, keepdims=True))
        lse_col_ref[pl.ds(at, chunk), :] = lse
        eye = lax.broadcasted_iota(jnp.int32, (chunk, chunk), 0) == lax.broadcasted_iota(
            jnp.int32, (chunk, chunk), 1
        )
        lse_row_ref[:, pl.ds(at, chunk)] = jnp.sum(jnp.where(eye, lse, 0.0), axis=0, keepdims=True)
        return run + jnp.sum(lse) - jnp.sum(jnp.where(positive, logits, 0.0))

    def second_pass(at, run):
        run_scale, run_bias = run
        shifted, own, positive = logits_of(at)
        logits = scale * shifted
        factor = 1.0 / (2.0 * count)
        grad = (
            jnp.exp(logits - lse_col_ref[pl.ds(at, chunk), :])
            + jnp.exp(logits - lse_row_ref[...])
            - jnp.where(positive, 2.0, 0.0)
        ) * factor
        grad = jnp.where(own, 0.0, grad)
        run_scale = run_scale + jnp.sum(grad * shifted)
        unit_grad = 2.0 * mm((scale * grad).astype(bf16), unit_ref[...])
        pooled = pooled_ref[pl.ds(at, chunk), :]
        inv_len = len_ref[pl.ds(at, chunk), :]
        along = jnp.sum(pooled * unit_grad, axis=-1, keepdims=True)
        pooled_grad = inv_len * unit_grad - pooled * (inv_len * inv_len * inv_len) * along
        pre_grad = (pooled_grad * (1.0 - pooled * pooled)).astype(bf16)
        pre_ref[pl.ds(at, chunk), :] = pre_grad
        pre_f_ref[pl.ds(at, chunk), :] = pre_grad.astype(f32)
        return run_scale, run_bias + jnp.sum(pre_grad.astype(f32), axis=0, keepdims=True)

    def each(body, run):
        if steps == 1:
            return body(0, run)
        return lax.fori_loop(0, steps, lambda s, r: body(pl.multiple_of(s * chunk, chunk), r), run)

    each(lambda at, run: (pool(at), run)[1], 0)
    total = each(first_pass, jnp.float32(0.0))
    run_scale, run_bias = each(second_pass, (jnp.float32(0.0), jnp.zeros((1, width), f32)))
    loss_ref[0] = total / count
    gscale_ref[0] = run_scale
    bias_grad_ref[...] = run_bias
    own_rows = pre_f_ref[pl.ds(pl.multiple_of(here * 8, 8), 8), :].astype(bf16)
    first_grad_ref[...] = mm_nt(own_rows, w_ref[...])


def pair_loss(position, rel, w_pool, bias, scale):
    count, wide = rel.shape
    width = w_pool.shape[0]
    smem = pl.BlockSpec(memory_space=pltpu.SMEM)
    vmem = pl.BlockSpec(memory_space=pltpu.VMEM)
    return pl.pallas_call(
        loss_kernel,
        in_specs=[smem, vmem, vmem, vmem, smem],
        out_specs=[smem, smem, vmem, vmem, vmem, vmem],
        out_shape=(
            jax.ShapeDtypeStruct((1,), f32),
            jax.ShapeDtypeStruct((1,), f32),
            jax.ShapeDtypeStruct((count, width), bf16),
            jax.ShapeDtypeStruct((1, width), f32),
            jax.ShapeDtypeStruct((8, width), f32),
            jax.ShapeDtypeStruct((count, width), bf16),
        ),
        scratch_shapes=[
            pltpu.VMEM((count, wide), f32),
            pltpu.VMEM((count, width), f32),
            pltpu.VMEM((count, 1), f32),
            pltpu.VMEM((count, width), bf16),
            pltpu.VMEM((count, 1), f32),
            pltpu.VMEM((1, count), f32),
            pltpu.VMEM((count, width), f32),
        ],
        compiler_params=params(56),
        cost_estimate=cost(2e9, 4e6),
        name="pair_loss",
    )(position, rel, w_pool, bias, scale)


def put_slabs(pos_ref, source, keep_ref, send_ref, lead):
    slab = source.shape[0] // 16
    for place in range(16):
        at = pl.multiple_of(jnp.bitwise_xor(pos_ref[0], place) * slab, slab)
        target = send_ref if place % 2 else keep_ref
        target[lead + (place // 2,)] = source[pl.ds(at, slab), :].astype(bf16)


def second_back_kernel(
    og_ref, fg_ref, n_ref, inv_ref, g_ref, grad_ref, low_ref, sums_ref
):
    rows_all, width = og_ref.shape
    sums_ref[...] = jnp.zeros_like(sums_ref)
    for at in range(0, rows_all, 64):
        rows = slice(at, at + 64)
        block = at // 64
        is_first = lax.broadcasted_iota(jnp.int32, (64, width), 0) == 0
        grad = og_ref[rows].astype(f32) + jnp.where(is_first, fg_ref[block:block + 1], 0.0)
        normed = n_ref[rows]
        value = norm_back(grad, normed, inv_ref[rows], g_ref[1:2])
        low = value.astype(bf16)
        grad_ref[rows] = value
        low_ref[rows] = low
        sums_ref[0:1] += jnp.sum(grad * normed, axis=0, keepdims=True)
        sums_ref[1:2] += jnp.sum(grad, axis=0, keepdims=True)
        sums_ref[2:3] += jnp.sum(low.astype(f32), axis=0, keepdims=True)


def second_back(out_grad, first_grad, normed, inv_std, gains):
    rows, width = out_grad.shape
    return pl.pallas_call(
        second_back_kernel,
        out_shape=(
            jax.ShapeDtypeStruct((rows, width), f32),
            jax.ShapeDtypeStruct((rows, width), bf16),
            jax.ShapeDtypeStruct((8, width), f32),
        ),
        compiler_params=params(),
        cost_estimate=cost(20 * rows * width, 12 * rows * width),
        name="second_back",
    )(out_grad, first_grad, normed, inv_std, gains)


def slab_shape(rows, cols):
    return jax.ShapeDtypeStruct((8, rows // 16, cols), bf16)


def back_weight_kernel(pos_ref, act_ref, branch_ref, keep_ref, send_ref, whole):
    for at in range(0, whole.shape[0], 256):
        rows = slice(at, at + 256)
        whole[rows] = mm_tn(act_ref[:, rows], branch_ref[...])
    put_slabs(pos_ref, whole, keep_ref, send_ref, ())


def back_weight(pos, act, branch):
    rows, units = act.shape
    width = branch.shape[1]
    smem = pl.BlockSpec(memory_space=pltpu.SMEM)
    vmem = pl.BlockSpec(memory_space=pltpu.VMEM)
    return pl.pallas_call(
        back_weight_kernel,
        in_specs=[smem, vmem, vmem],
        out_specs=[vmem, vmem],
        out_shape=(slab_shape(units, width),) * 2,
        scratch_shapes=[pltpu.VMEM((units, width), f32)],
        compiler_params=params(),
        cost_estimate=cost(2 * rows * width * units, 4 * units * width),
        name="back_weight",
    )(pos, act, branch)


def inner_back_kernel(pos_ref, branch_ref, wb_ref, slope_ref, low_ref, wi_ref, part_ref,
                      keep_ref, send_ref, bias_ref, out_ref, grad, whole):
    units = slope_ref.shape[1]
    for at in range(0, units, 256):
        cols = slice(at, at + 256)
        inner_grad = (mm_nt(branch_ref[...], wb_ref[cols]) * slope_ref[:, cols].astype(f32)).astype(bf16)
        grad[:, cols] = inner_grad
        bias_ref[:, cols] = jnp.sum(inner_grad.astype(f32), axis=0, keepdims=True)
        whole[:, cols] = mm_tn(low_ref[...], inner_grad)
    put_slabs(pos_ref, whole, keep_ref, send_ref, ())
    for at in range(0, low_ref.shape[0], 128):
        rows = slice(at, at + 128)
        out_ref[rows] = part_ref[rows] + mm_nt(grad[rows], wi_ref[...])


def inner_back(pos, branch, w_back, slope, low, w_in, part):
    rows, units = slope.shape
    width = low.shape[1]
    smem = pl.BlockSpec(memory_space=pltpu.SMEM)
    vmem = pl.BlockSpec(memory_space=pltpu.VMEM)
    return pl.pallas_call(
        inner_back_kernel,
        in_specs=[smem] + [vmem] * 6,
        out_specs=[vmem] * 4,
        out_shape=(slab_shape(width, units),) * 2
        + (jax.ShapeDtypeStruct((1, units), f32), jax.ShapeDtypeStruct((rows, width), f32)),
        scratch_shapes=[pltpu.VMEM((rows, units), bf16), pltpu.VMEM((width, units), f32)],
        compiler_params=params(),
        cost_estimate=cost(6 * rows * width * units, 4 * units * width),
        name="inner_back",
    )(pos, branch, w_back, slope, low, w_in, part)


def first_back_kernel(pos_ref, grad_ref, n_ref, inv_ref, g_ref, co_ref, cp_ref, wo_ref, wp_ref,
                      one_ref, sums_ref, dco_ref, dcp_ref, keep_ref, send_ref, low, whole):
    width = grad_ref.shape[1]
    sums_ref[...] = jnp.zeros_like(sums_ref)
    for at in range(0, grad_ref.shape[0], 128):
        rows = slice(at, at + 128)
        grad = grad_ref[rows]
        normed = n_ref[rows]
        value = norm_back(grad, normed, inv_ref[rows], g_ref[0:1])
        low_rows = value.astype(bf16)
        one_ref[rows] = value
        low[rows] = low_rows
        dco_ref[rows] = mm_nt(low_rows, wo_ref[...]).astype(bf16)
        dcp_ref[rows] = mm_nt(low_rows, wp_ref[...]).astype(bf16)
        sums_ref[0:1] += jnp.sum(grad * normed, axis=0, keepdims=True)
        sums_ref[1:2] += jnp.sum(grad, axis=0, keepdims=True)
        sums_ref[2:3] += jnp.sum(low_rows.astype(f32), axis=0, keepdims=True)
    for side, ctx_ref in enumerate((co_ref, cp_ref)):
        whole[...] = mm_tn(ctx_ref[...], low[...])
        put_slabs(pos_ref, whole, keep_ref.at[side], send_ref.at[side], ())


def first_back(pos, grad, normed, inv_std, gains, ctx_o, ctx_p, wo, wp):
    rows, width = grad.shape
    cols = ctx_o.shape[1]
    smem = pl.BlockSpec(memory_space=pltpu.SMEM)
    vmem = pl.BlockSpec(memory_space=pltpu.VMEM)
    return pl.pallas_call(
        first_back_kernel,
        in_specs=[smem] + [vmem] * 8,
        out_specs=[vmem] * 6,
        out_shape=(
            jax.ShapeDtypeStruct((rows, width), f32),
            jax.ShapeDtypeStruct((8, width), f32),
            jax.ShapeDtypeStruct((rows, cols), bf16),
            jax.ShapeDtypeStruct((rows, cols), bf16),
        )
        + (jax.ShapeDtypeStruct((2, 8, cols // 16, width), bf16),) * 2,
        scratch_shapes=[pltpu.VMEM((rows, width), bf16), pltpu.VMEM((cols, width), f32)],
        compiler_params=params(),
        cost_estimate=cost(8 * rows * width * cols, 12 * rows * width),
        name="first_back",
    )(pos, grad, normed, inv_std, gains, ctx_o, ctx_p, wo, wp)


def attention_back_kernel(pos_ref, x_ref, w_ref, segc_ref, segr_ref, q_ref, k_ref, v_ref, dc_ref, part_ref,
                          keep_ref, send_ref, bias_ref, out_ref, dq, dk, dv, whole):
    scale = HEAD_DIM ** (-0.5)
    for group in range(x_ref.shape[0] // GROUP):
        rows = slice(group * GROUP, (group + 1) * GROUP)
        same = same_segment(segc_ref, segr_ref, rows)
        for pair in range(q_ref.shape[1] // PAIR):
            cols = slice(pair * PAIR, (pair + 1) * PAIR)
            q_two = two_heads(q_ref[rows, cols])
            dc_two = two_heads(dc_ref[rows, cols])
            k_pair = k_ref[rows, cols]
            probs = pair_probs(q_two, k_pair, same)
            prob_grad = mm_nt(dc_two, v_ref[rows, cols])
            score_grad = (
                probs * (prob_grad - jnp.sum(prob_grad * probs, axis=1, keepdims=True))
            ).astype(bf16)
            dq[rows, cols] = (join_heads(mm(score_grad, k_pair)) * scale).astype(bf16)
            dk[rows, cols] = (mm_tn(score_grad, q_two) * scale).astype(bf16)
            dv[rows, cols] = mm_tn(probs.astype(bf16), dc_two).astype(bf16)
    bias_ref[0:1] = jnp.sum(dq[...].astype(f32), axis=0, keepdims=True)
    bias_ref[1:2] = jnp.sum(dv[...].astype(f32), axis=0, keepdims=True)
    for s, grad in enumerate((dq, dk, dv)):
        whole[...] = mm_tn(x_ref[...], grad[...])
        put_slabs_at(pos_ref, whole, keep_ref, send_ref, s)
    for at in range(0, x_ref.shape[0], 128):
        rows = slice(at, at + 128)
        out_ref[rows] = (
            part_ref[rows] + mm_nt(dq[rows], w_ref[0]) + mm_nt(dk[rows], w_ref[1]) + mm_nt(dv[rows], w_ref[2])
        )


def put_slabs_at(pos_ref, source, keep_ref, send_ref, s):
    slab = source.shape[0] // 16
    for place in range(16):
        at = pl.multiple_of(jnp.bitwise_xor(pos_ref[0], place) * slab, slab)
        target = send_ref if place % 2 else keep_ref
        target[place // 2, s] = source[pl.ds(at, slab), :].astype(bf16)


def attention_back(pos, x, w, segc, segr, q, k, v, dc, part):
    rows, width = x.shape
    cols = q.shape[1]
    smem = pl.BlockSpec(memory_space=pltpu.SMEM)
    vmem = pl.BlockSpec(memory_space=pltpu.VMEM)
    slabs = jax.ShapeDtypeStruct((8, 3, width // 16, cols), bf16)
    return pl.pallas_call(
        attention_back_kernel,
        in_specs=[smem] + [vmem] * 9,
        out_specs=[vmem] * 4,
        out_shape=(slabs, slabs, jax.ShapeDtypeStruct((2, cols), f32), jax.ShapeDtypeStruct((rows, width), f32)),
        scratch_shapes=[pltpu.VMEM((rows, cols), bf16)] * 3 + [pltpu.VMEM((width, cols), f32)],
        compiler_params=params(),
        cost_estimate=cost(20 * rows * width * cols, 4 * 3 * width * cols),
        name="attention_back",
    )(pos, x, w, segc, segr, q, k, v, dc, part)


def flip(value, bit):
    return value + bit - 2 * bit * ((value // bit) % 2)


class Copies:
    def __init__(self, send, recv, local):
        self.send, self.recv, self.local = send, recv, local
        self.sent, self.kept, self.ring = [], [], send.shape[0]

    def remote(self, source, target, device):
        at = len(self.sent)
        if at >= self.ring:
            self.sent[at - self.ring].wait_send()
        copy = pltpu.make_async_remote_copy(
            src_ref=source, dst_ref=target, send_sem=self.send.at[at % self.ring], recv_sem=self.recv.at[at],
            device_id=device, device_id_type=pl.DeviceIdType.MESH,
        )
        copy.start()
        self.sent.append(copy)
        return copy

    def here(self, source, target):
        copy = pltpu.make_async_copy(source, target, self.local.at[len(self.kept)])
        copy.start()
        self.kept.append(copy)
        return copy


def greet(devices):
    barrier = pltpu.get_barrier_semaphore()
    for device in devices:
        pl.semaphore_signal(barrier, inc=1, device_id=device, device_id_type=pl.DeviceIdType.MESH)
    pl.semaphore_wait(barrier, len(devices))


def same_block(row):
    across = jnp.broadcast_to(row.astype(f32), (GROUP, GROUP))
    return across == across.T


def arrive(*copies):
    for copy in copies:
        copy.wait_recv()


N_CHUNK = 3


def forward_kernel(
    segr_ref, b_qv_ref, b_in_ref, g_ref, s_ref, scale_ref, pairs_ref,
    x_any, w_pool_any, w_qkv_any, w_out_any, w_in_any, w_back_any,
    block_out, p_qkv, p_out_any, p_in_any, p_back_any, q_any, k_any, v_any, n1_any, i1_any, lowt_any, xt_any, ctxt_any,
    actt_any, slope_any, n2_any, i2_any,
    loss_ref, gscale_ref, new_scale_ref, first_any, b_qv_p, pool_any, pool_bias_any,
    first_grad_ref, pool_ref, pool_bias_ref, x_ref, w_pool_ref, w_qkv_ref, w_out, w_in, w_back, p_out, p_in, p_back, b_in_p, q, k, v, qf, kf, vf, ctx_far, ctx_o, ctx_p,
    n1, i1, low, act, slope, part, n2, i2, own_out, lowt, xt, ctxt, actt, ahead, ahead_got, gathered, ids,
    pre_ref, bias_grad_ref, firsts_out_ref, all_ref, pooled_ref, len_ref, unit_ref, lse_col_ref, lse_row_ref, pre_f_ref,
    send_sem, recv_sem, local_sem,
):
    dp, mp = lax.axis_index("dp"), lax.axis_index("mp")
    rows = q.shape[0]
    width = x_ref.shape[1]
    units = w_in.shape[1]
    near = {"x": {"mp": 1 - mp}, "y": {"dp": flip(dp, 2)}, "z": {"dp": flip(dp, 4)}, "c": {"dp": flip(dp, 1)}}
    far = ({"dp": flip(dp, 8)}, {"dp": flip(flip(dp, 4), 8)})
    run = Copies(send_sem, recv_sem, local_sem)
    own = dp % 8
    bit = {"y": 2, "z": 4}

    out_block, in_block, unit_chunk = w_out.shape[0] // 8, width // 8, units // N_CHUNK
    back_block = unit_chunk // 8

    def out_at(ref):
        return lambda b: ref.at[pl.ds(pl.multiple_of(b * out_block, 16), out_block)]

    def in_at(ref, n):
        return lambda b: ref.at[pl.ds(pl.multiple_of(b * in_block, 16), in_block), pl.ds(n * unit_chunk, unit_chunk)]

    def back_at(ref, n):
        return lambda b: ref.at[pl.ds(pl.multiple_of(n * unit_chunk + b * back_block, 16), back_block)]

    def qkv_at(ref, n):
        return lambda b: ref.at[:, pl.ds(pl.multiple_of((2 * b + n) * in_block, 16), in_block)]

    routes = ("zy", "zy", "yz", "zy", "yz", "zy", "yz")
    chunks = [(out_at(w_out_any), out_at(p_out), routes[0])]
    chunks += [(in_at(w_in_any, n), in_at(p_in, n), routes[1 + n]) for n in range(N_CHUNK)]
    chunks += [(back_at(w_back_any, n), back_at(p_back, n), routes[1 + N_CHUNK + n]) for n in range(N_CHUNK)]
    chunks += [(qkv_at(w_qkv_any, n), qkv_at(p_qkv, n), "yz"[n]) for n in range(2)]
    hops = [[None] * 4 for _ in chunks]

    def step(at, stage):
        source, target, route = chunks[at]
        first = own if len(route) == 2 else dp % 2 + 2 * ((dp // bit[route]) % 2)
        if stage == 0:
            hops[at][0] = [run.remote(source(first), target(first), near["x"])]
            return
        for copy in hops[at][stage - 1]:
            copy.wait_recv()
        one = flip(first, bit[route[0]] if len(route) == 2 else 2)
        blocks = [first, one]
        if len(route) == 2:
            blocks += [flip(b, bit[route[1]]) for b in blocks]
        if stage == 1:
            hops[at][1] = [run.remote(target(first), target(first), near[route[0]])]
        elif stage == len(route) + 1:
            hops[at][stage] = [run.remote(target(b), target(b), near["c"]) for b in blocks]
        elif stage == 2:
            hops[at][2] = [run.remote(target(b), target(b), near[route[1]]) for b in blocks[:2]]

    loads = [
        run.here(a, b)
        for a, b in (
            (x_any, x_ref), (w_qkv_any, w_qkv_ref), (w_out_any, w_out), (w_in_any, w_in), (w_back_any, w_back),
            (w_pool_any, w_pool_ref),
        )
    ]
    z, y, c = dp // 4, (dp // 2) % 2, dp % 2
    row_of = lax.broadcasted_iota(jnp.int32, (8, 128), 0)
    paired = jnp.zeros((8, 128), f32)
    for at in range(8):
        paired = jnp.where(row_of == at, pairs_ref[mp * 8 + at].astype(f32), paired)
    ids[z, y, c, mp] = paired
    greet(list(near.values()) + list(far))
    pair_hops = [[run.remote(ids.at[z, y, c, mp], ids.at[z, y, c, mp], near["x"])]]
    step(0, 0)
    b_copies = [run.remote(b_in_ref, b_in_p, near["x"]), run.remote(b_qv_ref, b_qv_p, near["x"])]

    def project(base, q_to, k_to, v_to):
        x = x_ref[pl.ds(base, rows)]
        q_to[...] = (mm(x, w_qkv_ref[0]) + b_qv_ref[0:1]).astype(bf16)
        k_to[...] = mm(x, w_qkv_ref[1]).astype(bf16)
        v_to[...] = (mm(x, w_qkv_ref[2]) + b_qv_ref[1:2]).astype(bf16)

    def attend(base, q_from, k_from, v_from, target):
        for group in range(rows // GROUP):
            at = slice(group * GROUP, (group + 1) * GROUP)
            one = same_block(segr_ref[:, pl.ds(pl.multiple_of(base + group * GROUP, GROUP), GROUP)])
            same = jnp.concatenate([one, one], axis=0)
            for pair in range(q_from.shape[1] // PAIR):
                cols = slice(pair * PAIR, (pair + 1) * PAIR)
                probs = pair_probs(two_heads(q_from[at, cols]), k_from[at, cols], same)
                target[at, cols] = join_heads(mm(probs.astype(bf16), v_from[at, cols])).astype(bf16)

    far_base = pl.multiple_of((1 - mp) * rows, rows)
    own_base = pl.multiple_of(mp * rows, rows)
    half = width // 2
    flight = {}

    def firsts_of(ref):
        return jnp.concatenate([ref[at:at + 1].astype(f32) for at in range(0, rows, SEG_LEN)], axis=0)

    def gelu_parts(value):
        cumulative = 0.5 * (1.0 + lax.erf(value * 0.7071067811865476))
        density = jnp.exp(-0.5 * value * value) * 0.3989422804014327
        return (value * cumulative).astype(bf16), cumulative + value * density

    def bias_of(b, at):
        return jnp.concatenate([b[at // 128:at // 128 + 1], b[at // 128 + 1:at // 128 + 2]], axis=1)

    def far_tokens():
        loads[0].wait()
        loads[1].wait()
        project(far_base, qf, kf, vf)
        attend(far_base, qf, kf, vf, ctx_far)

    def own_tokens():
        attend(own_base, q, k, v, ctx_o)
        for a, b in ((q, q_any), (k, k_any), (v, v_any)):
            run.here(a, b)

    def send_context(part):
        some = pl.ds(part * GROUP, GROUP)
        flight["context", part] = run.remote(ctx_far.at[some], ctx_p.at[some], near["x"])

    def ahead_out():
        loads[2].wait()
        both = jnp.concatenate([firsts_of(ctx_o), firsts_of(ctx_far)], axis=0).astype(bf16)
        ahead[0] = mm(both, w_out[...])
        flight["ahead"] = run.remote(ahead.at[0, pl.ds(8, 8)], ahead_got.at[0], near["x"])

    def ahead_norm():
        arrive(flight["ahead"])
        x = jnp.concatenate(
            [x_ref[pl.ds(pl.multiple_of(own_base + at, SEG_LEN), 16)][0:1].astype(f32) for at in range(0, rows, SEG_LEN)],
            axis=0,
        )
        hidden = norm_rows(x + ahead[0, 0:8] + ahead_got[0] + s_ref[0:1])[0] * g_ref[0:1] + s_ref[1:2]
        ahead[3, 0:8] = hidden
        ahead[1, 0:8] = hidden.astype(bf16).astype(f32)
        flight["ahead"] = run.remote(ahead.at[1, pl.ds(0, 8)], ahead.at[1, pl.ds(8, 8)], near["x"])

    def ahead_units():
        loads[3].wait()
        loads[4].wait()
        arrive(flight["ahead"])
        both = ahead[1].astype(bf16)
        total = jnp.zeros((16, width), f32)
        for at in range(0, units, 256):
            inside = gelu_parts(mm(both, w_in[:, at:at + 256]) + bias_of(b_in_ref, at))[0]
            total = total + mm(inside, w_back[at:at + 256])
        ahead[2] = total
        flight["ahead"] = run.remote(ahead.at[2, pl.ds(8, 8)], ahead_got.at[1], near["x"])

    def ahead_last():
        arrive(flight["ahead"])
        normed = norm_rows(ahead[3, 0:8] + (ahead[2, 0:8] + ahead_got[1] + s_ref[2:3]))[0]
        firsts = (normed * g_ref[1:2] + s_ref[3:4]).astype(bf16).astype(f32)
        gathered[z, y, c, mp] = jnp.concatenate([firsts[:, :half], firsts[:, half:]], axis=0).astype(bf16)
        slot = gathered.at[z, y, c, mp]
        flight["gather"] = [run.remote(slot, slot, near["x"])]

    def gather(hop):
        arrive(*flight["gather"])
        slot = (gathered.at[z, y, c], gathered.at[:, y, c], gathered.at[:, :, c])[hop]
        devices = ((far[1], far[0], near["z"]), (near["y"],), (near["c"],))[hop]
        flight["gather"] = [run.remote(slot, slot, device) for device in devices]

    def pair_hop(hop):
        arrive(*pair_hops[hop])
        slot = (ids.at[z, y, c], ids.at[:, y, c], ids.at[:, :, c])[hop]
        devices = ((far[1], far[0], near["z"]), (near["y"],), (near["c"],))[hop]
        pair_hops.append([run.remote(slot, slot, device) for device in devices])

    def turn():
        for at in range(0, rows, 128):
            here = slice(at, at + 128)
            xt[:, here] = x_ref[pl.ds(pl.multiple_of(own_base + at, 128), 128)].T
            ctxt[0, :, here] = ctx_o[here].T

    def own_out_part():
        part[...] = mm(ctx_o[...], w_out[...])

    def first_norm():
        arrive(*[flight["context", at] for at in range(rows // GROUP)])
        for at in range(0, rows, 128):
            here = slice(at, at + 128)
            x = x_ref[pl.ds(pl.multiple_of(own_base + at, 128), 128)].astype(f32)
            normed, inv_std = norm_rows(x + part[here] + mm(ctx_p[here], p_out[...]) + s_ref[0:1])
            n1[here] = normed
            i1[here] = jnp.broadcast_to(inv_std, (128, 128))
            rounded = (normed * g_ref[0:1] + s_ref[1:2]).astype(bf16)
            low[here] = rounded
            lowt[:, here] = rounded.T
            ctxt[1, :, here] = ctx_p[here].T
        for a, b in ((p_out, p_out_any), (n1, n1_any), (i1, i1_any), (lowt, lowt_any), (xt, xt_any), (ctxt, ctxt_any)):
            run.here(a, b)

    def inner(side, n):
        w, b = ((w_in, b_in_ref), (p_in, b_in_p))[side]
        if side == 1 and n == 0:
            arrive(*b_copies)
        for at in range(n * unit_chunk, (n + 1) * unit_chunk, 256):
            cols = slice(at, at + 256)
            bias = bias_of(b, at)
            for top in range(0, rows, 128):
                here = slice(top, top + 128)
                rounded, slopes = gelu_parts(mm(low[here], w[:, cols]) + bias)
                act[side, here, cols] = rounded
                actt[side, cols, here] = rounded.T
                slope[side, here, cols] = slopes.astype(bf16)
        if side == 1 and n == N_CHUNK - 1:
            for a, b in ((actt, actt_any), (slope, slope_any), (p_in, p_in_any)):
                run.here(a, b)

    def branch(side, n):
        w = (w_back, p_back)[side]
        cols = slice(n * unit_chunk, (n + 1) * unit_chunk)
        for top in range(0, rows, 128):
            here = slice(top, top + 128)
            value = mm(act[side, here, cols], w[cols])
            part[here] = value if (side, n) == (0, 0) else part[here] + value

    def second_norm():
        last = slice((N_CHUNK - 1) * unit_chunk, units)
        for at in range(0, rows, 64):
            here = slice(at, at + 64)
            value = mm(act[1, here, last], p_back[last]) + part[here] + s_ref[2:3]
            normed, inv_std = norm_rows(n1[here] * g_ref[0:1] + s_ref[1:2] + value)
            n2[here] = normed
            i2[here] = jnp.broadcast_to(inv_std, (64, 128))
            own_out[here] = (normed * g_ref[1:2] + s_ref[3:4]).astype(bf16)
        for a, b in ((n2, n2_any), (i2, i2_any), (p_back, p_back_any), (own_out, block_out)):
            run.here(a, b)

    far_tokens()
    step(1, 0)
    project(own_base, q, k, v)
    step(0, 1)
    pair_hop(0)
    own_tokens()
    step(2, 0)
    ahead_out()
    turn()
    own_out_part()
    step(1, 1)
    step(3, 0)
    step(0, 2)
    step(4, 0)
    step(2, 1)
    ahead_norm()
    step(1, 2)
    pair_hop(1)
    send_context(0)
    step(3, 1)
    step(0, 3)
    step(5, 0)
    step(4, 1)
    ahead_units()
    step(6, 0)
    step(0, 4)
    step(2, 2)
    step(3, 2)
    step(5, 1)
    send_context(3)
    step(1, 3)
    ahead_last()
    step(1, 4)
    send_context(2)
    step(4, 2)
    step(6, 1)
    send_context(1)
    step(2, 3)
    gather(0)
    step(2, 4)
    step(7, 0)
    step(3, 3)
    step(5, 2)
    step(3, 4)
    step(6, 2)
    first_norm()
    pair_hop(2)
    inner(0, 0)
    step(8, 0)
    step(4, 3)
    inner(0, 1)
    inner(0, 2)
    step(4, 4)
    gather(1)
    branch(0, 0)
    branch(0, 1)
    branch(0, 2)
    step(5, 3)
    step(7, 1)
    inner(1, 0)
    inner(1, 1)
    step(5, 4)
    step(6, 3)
    inner(1, 2)
    branch(1, 0)
    gather(2)
    branch(1, 1)
    step(6, 4)
    step(8, 1)
    second_norm()
    arrive(*pair_hops[3])
    arrive(*flight["gather"])
    loads[5].wait()

    @pl.loop(0, 32)
    def _(at):
        slot = (at // 8, (at // 4) % 2, (at // 2) % 2, at % 2)
        values = gathered[slot].astype(f32)
        here = pl.ds(pl.multiple_of(at * 8, 8), 8)
        all_ref[here, :half] = values[:8]
        all_ref[here, half:width] = values[8:]
        all_ref[here, width:] = ids[slot]

    loss_passes(
        dp * 2 + mp, scale_ref[0], w_pool_ref, s_ref[4:5],
        loss_ref, gscale_ref, pre_ref, bias_grad_ref, first_grad_ref, firsts_out_ref,
        all_ref, pooled_ref, len_ref, unit_ref, lse_col_ref, lse_row_ref, pre_f_ref,
    )
    new_scale_ref[0] = scale_ref[0] - step_rate * gscale_ref[0]
    per = width // 16
    own_firsts = mm(firsts_out_ref[...], pick(width, dp * per, per).astype(bf16)).astype(bf16)
    pool_ref[...] = mm_tn(own_firsts, pre_ref[...])
    pool_bias_ref[...] = exact(bias_grad_ref[...], pick(width, dp * per, per))
    for a, b in ((first_grad_ref, first_any), (pool_ref, pool_any), (pool_bias_ref, pool_bias_any)):
        run.here(a, b)
    step(7, 2)
    step(8, 2)
    step(7, 3)
    step(8, 3)
    for copy in run.sent[-run.ring:]:
        copy.wait_send()
    for copy in run.kept[len(loads):]:
        copy.wait()


def forward(x, segr, w_qkv, b_qv, b_in, gains, shifts, w_pool, scale, pairs, w_out, w_in, w_back):
    rows, width = x.shape[0] // 2, x.shape[1]
    cols, units = w_qkv.shape[2], w_in.shape[1]
    count = 2 * lax.axis_size("dp") * 8
    any_ = pl.BlockSpec(memory_space=pl.ANY)
    smem = pl.BlockSpec(memory_space=pltpu.SMEM)
    vmem = pl.BlockSpec(memory_space=pltpu.VMEM)
    S = jax.ShapeDtypeStruct
    head = (rows, cols)
    kept = [
        ((rows, width), bf16), (w_qkv.shape, bf16), (w_out.shape, bf16), (w_in.shape, bf16), (w_back.shape, bf16),
        (head, bf16), (head, bf16), (head, bf16),
        ((rows, width), f32), ((rows, 128), f32), ((width, rows), bf16), ((width, rows), bf16), ((2, cols, rows), bf16),
        ((2, units, rows), bf16), ((2, rows, units), bf16), ((rows, width), f32), ((rows, 128), f32),
    ]
    scratch = [
        ((8, width), f32), ((width // 16, width), f32), ((1, width // 16), f32),
        (x.shape, bf16), (w_pool.shape, bf16), (w_qkv.shape, bf16),
        (w_out.shape, bf16), (w_in.shape, bf16), (w_back.shape, bf16),
        (w_out.shape, bf16), (w_in.shape, bf16), (w_back.shape, bf16), (b_in.shape, f32),
    ] + [(head, bf16)] * 9 + [
        ((rows, width), f32), ((rows, 128), f32), ((rows, width), bf16),
        ((2, rows, units), bf16), ((2, rows, units), bf16), ((rows, width), f32), ((rows, width), f32),
        ((rows, 128), f32), ((rows, width), bf16),
        ((width, rows), bf16), ((width, rows), bf16), ((2, cols, rows), bf16), ((2, units, rows), bf16),
        ((4, 16, width), f32), ((2, 8, width), f32), ((4, 2, 2, 2, 16, width // 2), bf16), ((4, 2, 2, 2, 8, 128), f32),
        ((count, width), bf16), ((1, width), f32), ((count, width), bf16),
        ((count, width + 128), f32), ((count, width), f32), ((count, 1), f32), ((count, width), bf16),
        ((count, 1), f32), ((1, count), f32), ((count, width), f32),
    ]
    return pl.pallas_call(
        forward_kernel,
        in_specs=[vmem] * 5 + [smem] * 2 + [any_] * 6,
        out_specs=[any_] * len(kept) + [smem] * 3 + [any_] * 4,
        out_shape=tuple(S(*k) for k in kept) + (
            S((1,), f32), S((1,), f32), S((1,), f32), S((8, width), f32), S(b_qv.shape, f32),
            S((width // 16, width), f32), S((1, width // 16), f32),
        ),
        scratch_shapes=[pltpu.VMEM(*s) for s in scratch] + [
            pltpu.SemaphoreType.DMA((48,)), pltpu.SemaphoreType.DMA((90,)), pltpu.SemaphoreType.DMA((26,)),
        ],
        compiler_params=pltpu.CompilerParams(
            vmem_limit_bytes=56 * 1024 * 1024, collective_id=0, has_side_effects=True
        ),
        name="forward",
    )(segr, b_qv, b_in, gains, shifts, scale, pairs, x, w_pool, w_qkv, w_out, w_in, w_back)


def pick(size, start, count):
    return (
        lax.broadcasted_iota(jnp.int32, (size, count), 0)
        == start + lax.broadcasted_iota(jnp.int32, (size, count), 1)
    ).astype(f32)


def exact(a, b):
    return jnp.dot(a, b, preferred_element_type=f32, precision=lax.Precision.HIGHEST)


ORDERS = (
    ("z", "x", "y", "w"), ("y", "x", "q"), ("y", "z", "w", "x"),
    ("z", "x", "y", "w"), ("z", "x", "w", "y"), ("y", "z", "x", "w"),
    ("y", "z", "x", "w"), ("x", "z", "y", "w"), ("y", "x", "z", "w"),
    ("y", "z", "x", "w"), ("x", "y", "z", "w"), ("y", "x", "q"),
)
TILE = 384
PARTS = 4


def backward_kernel(
    segr_ref, g_ref, first_grad_ref, b_qv_ref,
    out_any, x_any, og_any, n2_any, i2_any, n1_any, i1_any, act_any, slope_any, low_any, xt_any, ctx_any, q_any, k_any, v_any,
    wb_o_any, wb_p_any, wi_o_any, wi_p_any, wo_o_any, wo_p_any, wq_o_any, wq_p_any,
    grad_in_any, out_other, o_back, o_in, o_qkv, o_out, a_gains, a_shifts, a_bqv, a_bin,
    o_gains, o_shifts, o_bqv, o_bin, one_buf, two_buf, three_buf, grad, i2, n1, i1, act, slope, low, xt, ctx, q, k, v, wb, wi, wo, wq, deltas,
    unit, got, ready, sums, sums_got,
    send_sem, recv_sem, local_sem,
):
    dp, mp = lax.axis_index("dp"), lax.axis_index("mp")
    rows, width = one_buf.shape
    units = slope.shape[2]
    cols = q.shape[2]
    per = width // 16
    own_base = pl.multiple_of(mp * rows, rows)
    near = {
        "x": {"mp": 1 - mp}, "y": {"dp": flip(dp, 2)}, "z": {"dp": flip(dp, 4)}, "w": {"dp": flip(dp, 8)},
        "c": {"dp": flip(dp, 1)},
    }
    quad = (near["z"], near["w"], {"dp": flip(flip(dp, 4), 8)})
    run = Copies(send_sem, recv_sem, local_sem)
    own_rows = lambda ref: ref.at[pl.ds(own_base, rows)]
    pending, results = {}, []

    def load(*pairs):
        for source, target, name in pairs:
            pending.setdefault(name, []).append(run.here(source, target))

    def need(*names):
        for name in names:
            for copy in pending.pop(name, ()):
                copy.wait()

    load((own_rows(og_any), one_buf, "two"), (n2_any, grad, "two"), (i2_any, i2, "two"))
    load((act_any, act, "act"), (wb_o_any, wb.at[0], "wb"), (wb_p_any, wb.at[1], "wb"), (slope_any, slope, "slope"))

    greet(list(near.values()) + [quad[2]])
    flight = {}
    bits = {"y": 2, "z": 4, "w": 8}

    def rel(name, side, dest):
        return side if name == "x" else (dest // bits[name] + dp // bits[name]) % 2

    def put(at, side, dest, value):
        spot, left = 0, 16
        for name in ORDERS[at]:
            left = left // (4 if name == "q" else 2)
            spot = spot + left * (2 * rel("w", side, dest) + rel("z", side, dest) if name == "q" else rel(name, side, dest))
        unit[at, (dest + dp) % 2, spot] = value.astype(bf16)

    def shape_of(at, stage):
        start, left = 0, 32
        for name in ("c",) + ORDERS[at][:stage]:
            held = left
            left = held // (4 if name == "q" else 2)
            begins, start = start, start + held - left
        return held, left, begins

    def begin(at):
        flight[at, 0] = [run.remote(unit.at[at, 1], got.at[at, pl.ds(0, 16)], near["c"])]

    def step(at, stage):
        arrive(*flight[at, stage - 1])
        held, count, begins = shape_of(at, stage - 1)
        mine = unit.at[at, 0]

        def added(n):
            if held == 2 * count:
                return mine[n] + got[at, begins + n]
            total = mine[n].astype(f32)
            for part in range(3):
                total = total + got[at, begins + part * count + n].astype(f32)
            return total.astype(bf16)

        if count == 1:
            total = mine[0].astype(f32)
            for part in range(held - 1):
                total = total + got[at, begins + part].astype(f32)
            ready[at] = total
            if at < 4:
                target = o_back.at[pl.ds(at % 2 * per, per), pl.ds(at // 2 * TILE, TILE)]
            elif at < 8:
                target = o_in.at[:, pl.ds((at - 4) * TILE, TILE)]
            elif at < 11:
                target = o_qkv.at[at - 8]
            else:
                results.append(run.here(ready.at[at, pl.ds(0, per // 2)], o_out.at[:, pl.ds(0, cols)]))
                results.append(run.here(ready.at[at, pl.ds(per // 2, per // 2)], o_out.at[:, pl.ds(cols, cols)]))
                return
            results.append(run.here(ready.at[at], target))
            return
        _, after, begins_next = shape_of(at, stage)
        for n in range(after, count):
            mine[n] = added(n)
        name = ORDERS[at][stage - 1]
        devices = quad if name == "q" else (near[name],)
        flight[at, stage] = [
            run.remote(
                mine.at[pl.ds((part + 1) * after, after)], got.at[at, pl.ds(begins_next + part * after, after)], device
            )
            for part, device in enumerate(devices)
        ]
        for n in range(after):
            mine[n] = added(n)

    def sum_step(stage):
        if stage:
            flight["sums", stage - 1].wait_recv()
            sums[stage] = sums[stage - 1] + sums_got[stage - 1]
        if stage < 5:
            name = ("c", "x", "y", "z", "w")[stage]
            flight["sums", stage] = run.remote(sums.at[stage], sums_got.at[stage], near[name])

    def norm_grads(source, extra, normed_ref, inv_ref, gain, low_ref, places):
        gain_sum, shift_sum, low_sum = 0.0, 0.0, 0.0
        for at in range(0, rows, 64):
            here = slice(at, at + 64)
            value = source[here].astype(f32)
            if extra is not None:
                is_first = lax.broadcasted_iota(jnp.int32, (64, width), 0) == 0
                value = value + jnp.where(is_first, extra[at // 64:at // 64 + 1], 0.0)
            normed = normed_ref[here]
            out = norm_back(value, normed, inv_ref[here, 0:1], gain)
            rounded = out.astype(bf16)
            grad[here] = out
            low_ref[here] = rounded
            gain_sum += jnp.sum(value * normed, axis=0, keepdims=True)
            shift_sum += jnp.sum(value, axis=0, keepdims=True)
            low_sum += jnp.sum(rounded.astype(f32), axis=0, keepdims=True)
        for place, value in zip(places, (gain_sum, shift_sum, low_sum)):
            sums[0, place:place + 1] = value

    def second_norm():
        need("two")
        sums[0] = jnp.zeros(sums.shape[1:], f32)
        norm_grads(one_buf, first_grad_ref, grad, i2, g_ref[1:2], two_buf, (1, 5, 4))
        load((wi_o_any, wi.at[0], "wi"), (wi_p_any, wi.at[1], "wi"), (low_any, low, "low"))
        load((n1_any, n1, "one"), (i1_any, i1, "one"))

    def back_weight(half):
        need("act")
        for side in range(2):
            for top in range(0, units, TILE):
                tile = mm(act[side, top:top + TILE], two_buf[:, half * cols:(half + 1) * cols])
                for at in range(0, TILE, per):
                    put(2 * half + at // per % 2, side, (top + at) // (2 * per), tile[at:at + per])

    def inner_grads(side):
        need("wb", "slope")
        owner = mp + side - 2 * mp * side
        for at in range(0, units, 256):
            here = slice(at, at + 256)
            value = (mm_nt(two_buf[...], wb[side, here]) * slope[side, :, here].astype(f32)).astype(bf16)
            slope[side, :, here] = value
            sums[0, pl.ds(8 + 2 * owner + at // width, 1), at % width:at % width + 256] = jnp.sum(
                value.astype(f32), axis=0, keepdims=True
            )
        if side == 0:
            load((ctx_any, ctx, "ctx"), (wo_o_any, wo.at[0], "wo"), (wo_p_any, wo.at[1], "wo"))
            load((own_rows(x_any), three_buf, "x"), (wq_p_any, wq.at[1], "wq_p"))

    def feed_back():
        need("wi")
        for at in range(0, width, 256):
            here = slice(at, at + 256)
            grad[:, here] = grad[:, here] + mm_nt(slope[0], wi[0, here]) + mm_nt(slope[1], wi[1, here])
        load((q_any, q.at[0], "qkv"), (k_any, k.at[0], "qkv"), (v_any, v.at[0], "qkv"))
        load((xt_any, xt, "xt"), (wq_o_any, wq.at[0], "wq_o"))

    def first_norm_back():
        need("one")
        norm_grads(grad, None, n1, i1, g_ref[0:1], one_buf, (0, 3, 2))

    def in_weight(half):
        need("low")
        for at in range(2 * half, 2 * half + 2):
            for side in range(2):
                for top in range(0, width, TILE):
                    tile = mm(low[top:top + TILE], slope[side, :, at * TILE:(at + 1) * TILE])
                    for row in range(0, TILE, per):
                        put(4 + at, side, (top + row) // per, tile[row:row + per])

    def out_weight():
        need("ctx")
        for side in range(2):
            tile = mm(ctx[side], one_buf[...])
            for dest in range(16):
                part = tile[dest * per // 2:(dest + 1) * per // 2]
                put(11, side, dest, jnp.concatenate([part[:, :cols], part[:, cols:]], axis=0))

    def context_grads():
        need("wo")
        for side in range(2):
            two_buf[:, side * cols:(side + 1) * cols] = mm_nt(one_buf[...], wo[side]).astype(bf16)

    def again():
        need("x", "wq_p")
        q[1] = (mm(three_buf[...], wq[1, 0]) + b_qv_ref[0:1]).astype(bf16)
        k[1] = mm(three_buf[...], wq[1, 1]).astype(bf16)
        v[1] = (mm(three_buf[...], wq[1, 2]) + b_qv_ref[1:2]).astype(bf16)

    def attend_back(side, groups):
        need("qkv")
        scale = HEAD_DIM ** (-0.5)
        for group in groups:
            at = slice(group * GROUP, (group + 1) * GROUP)
            one = same_block(segr_ref[:, pl.ds(pl.multiple_of(own_base + group * GROUP, GROUP), GROUP)])
            same = jnp.concatenate([one, one], axis=1)
            for pair in range(cols // PAIR):
                lanes = slice(pair * PAIR, (pair + 1) * PAIR)
                q_two = two_heads(q[side, at, lanes])
                dc_two = two_heads(two_buf[at, side * cols + pair * PAIR:side * cols + (pair + 1) * PAIR])
                k_pair, v_pair = k[side, at, lanes], v[side, at, lanes]
                scores = jnp.where(same, mm_nt(k_pair, q_two) * scale, masked_out)
                shifted = jnp.exp(scores - jnp.max(scores, axis=0, keepdims=True))
                probs = shifted / jnp.sum(shifted, axis=0, keepdims=True)
                prob_grad = mm_nt(v_pair, dc_two)
                score_grad = (
                    probs * (prob_grad - jnp.sum(prob_grad * probs, axis=0, keepdims=True))
                ).astype(bf16)
                deltas[side, 0, at, lanes] = (join_heads(mm_tn(score_grad, k_pair)) * scale).astype(bf16)
                deltas[side, 1, at, lanes] = (mm(score_grad, q_two) * scale).astype(bf16)
                deltas[side, 2, at, lanes] = mm(probs.astype(bf16), dc_two).astype(bf16)

    def qkv_weight(s):
        need("xt")
        for side in range(2):
            for top in range(0, width, TILE):
                tile = mm(xt[top:top + TILE], deltas[side, s])
                for at in range(0, TILE, per):
                    put(8 + s, side, (top + at) // per, tile[at:at + per])
            if s != 1:
                owner = mp + side - 2 * mp * side
                lanes = pl.ds(pl.multiple_of(owner * cols, 128), cols)
                sums[0, 6 + s // 2:7 + s // 2, lanes] = jnp.sum(deltas[side, s].astype(f32), axis=0, keepdims=True)

    def input_grads():
        need("wq_o", "wq_p")
        for at in range(0, width, 256):
            here = slice(at, at + 256)
            value = grad[:, here]
            for side in range(2):
                for s in range(3):
                    value = value + mm_nt(deltas[side, s], wq[side, s, here])
            three_buf[:, here] = value.astype(bf16)
        results.append(run.here(three_buf, own_rows(grad_in_any)))

    share = rows // PARTS

    def send_out(part):
        some = pl.ds(part * share, share)
        flight["out", part] = run.remote(out_any.at[some], out_other.at[some], near["x"])

    def send_inputs(part):
        some = pl.ds(pl.multiple_of(own_base + part * share, share), share)
        flight["inputs", part] = run.remote(
            three_buf.at[pl.ds(part * share, share)], grad_in_any.at[some], near["x"]
        )

    send_out(0)
    second_norm()
    back_weight(0)
    begin(0)
    begin(1)
    send_out(1)
    inner_grads(1)
    step(0, 1)
    back_weight(1)
    begin(2)
    begin(3)
    send_out(2)
    step(1, 1)
    inner_grads(0)
    in_weight(0)
    begin(4)
    begin(5)
    step(2, 1)
    send_out(3)
    step(3, 1)
    feed_back()
    step(5, 1)
    step(4, 1)
    step(0, 2)
    again()
    step(1, 2)
    first_norm_back()
    context_grads()
    in_weight(1)
    begin(6)
    begin(7)
    step(3, 2)
    step(0, 3)
    attend_back(1, (0, 1))
    step(2, 2)
    step(6, 1)
    attend_back(1, (2, 3))
    step(7, 1)
    step(1, 3)
    step(4, 2)
    attend_back(0, (2, 3))
    step(5, 2)
    step(3, 3)
    attend_back(0, (0, 1))
    step(2, 3)
    step(0, 4)
    qkv_weight(0)
    begin(8)
    qkv_weight(2)
    begin(10)
    sum_step(0)
    step(1, 4)
    qkv_weight(1)
    begin(9)
    step(8, 1)
    out_weight()
    begin(11)
    sum_step(1)
    step(7, 2)
    step(5, 3)
    step(10, 1)
    step(6, 2)
    step(9, 1)
    input_grads()
    sum_step(2)
    step(11, 1)
    step(4, 3)
    step(3, 4)
    step(2, 4)
    step(5, 4)
    step(0, 5)
    step(7, 3)
    step(8, 2)
    step(6, 3)
    step(10, 2)
    step(2, 5)
    send_inputs(0)
    step(4, 4)
    step(9, 2)
    sum_step(3)
    step(8, 3)
    step(3, 5)
    step(6, 4)
    step(5, 5)
    send_inputs(1)
    step(9, 3)
    sum_step(4)
    step(11, 2)
    step(8, 4)
    step(7, 4)
    step(6, 5)
    step(10, 3)
    send_inputs(2)
    step(9, 4)
    sum_step(5)
    total = sums[5]
    vectors = exact(total[0:8], pick(width, dp * per, per))
    o_gains[...] = vectors[0:2]
    o_shifts[...] = vectors[2:6]
    o_bqv[...] = exact(total[0:8], pick(width, mp * cols + dp * (per // 2), per // 2))[6:8]
    few = units // 16
    o_bin[...] = exact(sums[5, pl.ds(8 + 2 * mp + dp // 8, 1), :], pick(width, (dp % 8) * few, few))
    for source, target in ((o_gains, a_gains), (o_shifts, a_shifts), (o_bqv, a_bqv), (o_bin, a_bin)):
        results.append(run.here(source, target))
    step(8, 5)
    step(4, 5)
    step(11, 3)
    step(7, 5)
    send_inputs(3)
    step(10, 4)
    step(9, 5)
    step(11, 4)
    step(10, 5)
    for part in range(PARTS):
        arrive(flight["out", part], flight["inputs", part])
    for copy in run.sent[-run.ring:]:
        copy.wait_send()
    for copy in results:
        copy.wait()


def backward(segr, gains, first_grad, b_qv, *arrays):
    rows, width = arrays[3].shape
    units = arrays[8].shape[2]
    cols = arrays[12].shape[1]
    any_ = pl.BlockSpec(memory_space=pl.ANY)
    vmem = pl.BlockSpec(memory_space=pltpu.VMEM)
    S = jax.ShapeDtypeStruct
    per = width // 16
    count = len(ORDERS)
    small = [((2, per), f32), ((4, per), f32), ((2, cols // 16), f32), ((1, units // 16), f32)]
    scratch = small + [((rows, width), bf16)] * 3 + [
        ((rows, width), f32), ((rows, 128), f32), ((rows, width), f32), ((rows, 128), f32),
        ((2, units, rows), bf16), ((2, rows, units), bf16), ((width, rows), bf16), ((width, rows), bf16),
        ((2, cols, rows), bf16), ((2, rows, cols), bf16), ((2, rows, cols), bf16), ((2, rows, cols), bf16),
        ((2, units, width), bf16), ((2, width, units), bf16), ((2, cols, width), bf16), ((2, 3, width, cols), bf16),
        ((2, 3, rows, cols), bf16), ((count, 2, 16, per, TILE), bf16),
        ((count, 31, per, TILE), bf16), ((count, per, TILE), f32), ((6, 16, width), f32), ((5, 16, width), f32),
    ]
    return pl.pallas_call(
        backward_kernel,
        in_specs=[vmem] * 4 + [any_] * len(arrays),
        out_specs=[any_] * 10,
        out_shape=(
            S((2 * rows, width), bf16), S((rows, width), bf16), S((2 * per, width), f32), S((per, 2 * width), f32),
            S((3, per, cols), f32),
            S((cols // 16, width), f32), S((2, per), f32), S((4, per), f32), S((2, cols // 16), f32),
            S((1, units // 16), f32),
        ),
        scratch_shapes=[pltpu.VMEM(*s) for s in scratch] + [
            pltpu.SemaphoreType.DMA((24,)), pltpu.SemaphoreType.DMA((76,)), pltpu.SemaphoreType.DMA((44,)),
        ],
        compiler_params=pltpu.CompilerParams(
            vmem_limit_bytes=63 * 1024 * 1024, collective_id=1, has_side_effects=True
        ),
        name="backward",
    )(segr, gains, first_grad, b_qv, *arrays)


FINISH_PARTS = 4


def finish_kernel(*refs):
    grads_any, outs_any, others_any = refs[:3]
    count = (len(refs) - 8) // 3
    sources = refs[3:3 + count]
    wide_any, outs_to = refs[3 + count:5 + count]
    targets = refs[5 + count:5 + 2 * count]
    grads, wide, outs = refs[5 + 2 * count:8 + 2 * count]
    held = refs[8 + 2 * count:-2]
    load_sem, store_sem = refs[-2:]
    part = grads.shape[0] // FINISH_PARTS
    other = 1 - lax.axis_index("mp")
    loads, stores = [], []

    def copy(into, source, target, sem):
        into.append(pltpu.make_async_copy(source, target, sem.at[len(into)]))
        into[-1].start()

    def rows(ref, at):
        return ref.at[pl.ds(pl.multiple_of(at * part, part), part)]

    for at in range(FINISH_PARTS):
        copy(loads, rows(grads_any, at), rows(grads, at), load_sem)
    places = [2 * (1 - other), 2 * (1 - other) + 1, 2 * other, 2 * other + 1]
    for n, at in enumerate(places):
        copy(loads, rows((outs_any, others_any)[n // 2], n % 2), rows(outs, at), load_sem)
    for source, target in zip(sources, held):
        copy(loads, source, target, load_sem)
    for at in range(FINISH_PARTS):
        loads[at].wait()
        here = slice(at * part, (at + 1) * part)
        wide[here] = grads[here].astype(f32)
        copy(stores, rows(wide, at), rows(wide_any, at), store_sem)
    for n, at in enumerate(places):
        loads[FINISH_PARTS + n].wait()
        copy(stores, rows(outs, at), rows(outs_to, at), store_sem)
    for n in range(count):
        loads[2 * FINISH_PARTS + n].wait()
        copy(stores, held[n], targets[n], store_sem)
    for store in stores:
        store.wait()


def finish(grad_inputs, own_out, other_out, *arrays):
    any_ = pl.BlockSpec(memory_space=pl.ANY)
    results = (jax.ShapeDtypeStruct(grad_inputs.shape, f32), jax.ShapeDtypeStruct(grad_inputs.shape, bf16)) + tuple(
        jax.ShapeDtypeStruct(a.shape, a.dtype) for a in arrays
    )
    copies = 2 * FINISH_PARTS + len(arrays)
    return pl.pallas_call(
        finish_kernel,
        in_specs=[any_] * (3 + len(arrays)),
        out_specs=[any_] * len(results),
        out_shape=results,
        scratch_shapes=[
            pltpu.VMEM(grad_inputs.shape, bf16), pltpu.VMEM(grad_inputs.shape, f32), pltpu.VMEM(grad_inputs.shape, bf16),
        ] + [pltpu.VMEM(a.shape, a.dtype) for a in arrays] + [
            pltpu.SemaphoreType.DMA((copies,)), pltpu.SemaphoreType.DMA((copies,)),
        ],
        compiler_params=params(60),
        name="finish",
    )(grad_inputs, own_out, other_out, *arrays)


def swap_mp(values):
    return lax.ppermute(values, "mp", [(0, 1), (1, 0)])


def swap_dp(values, bit):
    size = lax.axis_size("dp")
    return lax.ppermute(values, "dp", [(at, at ^ bit) for at in range(size)])


def fetch(own, axis, place):
    size = own.shape[axis] // 4
    first = swap_mp(lax.dynamic_slice_in_dim(own, place * size, size, axis))
    second = swap_dp(first, 2)
    third = swap_dp(first, 1)
    fourth = swap_dp(second, 1)
    whole = jnp.zeros_like(own)
    for bits, part in ((0, first), (2, second), (1, third), (3, fourth)):
        whole = lax.dynamic_update_slice_in_dim(whole, part, (place ^ bits) * size, axis)
    return whole


def gather_rows(rows):
    size = lax.axis_size("dp")
    if size != 16:
        return lax.all_gather(rows, ("dp", "mp"), axis=0, tiled=True)
    rows = jnp.concatenate([rows, swap_mp(rows)], axis=0)
    for bit in (1, 2, 4, 8):
        rows = jnp.concatenate([rows, swap_dp(rows, bit)], axis=0)
    return rows


def both_halves(own, mp):
    other = swap_mp(own)
    return jnp.concatenate([jnp.where(mp == 0, own, other), jnp.where(mp == 0, other, own)], axis=0)


def add(a, b):
    return (a.astype(f32) + b.astype(f32)).astype(a.dtype)


def scatter_sum(keep, send, order):
    size = lax.axis_size("dp")
    if size != 16:
        rest = keep.shape[2:]
        both = jnp.stack([keep, send], axis=2)
        both = both.reshape((2, 16) + rest)
        mine = add(both[0], swap_mp(both[1]))
        return mine
    got = swap_dp(send, 1)
    rest = keep.shape[2:]
    names = ["x", "z1", "z0", "y"]
    keep = keep.reshape((2, 2, 2, 2) + rest)
    got = got.reshape((2, 2, 2, 2) + rest)
    bit_of = {"y": 2, "z0": 4, "z1": 8}
    for name in order:
        axis = names.index(name)
        names.remove(name)
        pick = lambda values, at: lax.index_in_dim(values, at, axis, keepdims=False)
        out = add(pick(keep, 1), pick(got, 1))
        out = swap_mp(out) if name == "x" else swap_dp(out, bit_of[name])
        keep = add(pick(keep, 0), pick(got, 0))
        got = out
    return add(keep, got)


def swap_order(values, axis, place):
    shape = values.shape
    split = values.reshape(shape[:axis] + (2, 2, 2, 2) + shape[axis + 1:])
    for at, bit in enumerate((8, 4, 2, 1)):
        low = lax.index_in_dim(split, 0, axis + at)
        high = lax.index_in_dim(split, 1, axis + at)
        flipped = jnp.concatenate([high, low], axis=axis + at)
        split = jnp.where((place & bit) != 0, flipped, split)
    return split.reshape(shape)


def shards(
    inputs, segment_ids, pair_index, w_qkv, bias_qv, w_out, w_in, bias_in, w_back,
    w_pool, norm_gains, shifts, logit_scale, out_grad,
):
    tok_rows, width = inputs.shape
    size = lax.axis_size("dp")
    dp, mp = lax.axis_index("dp"), lax.axis_index("mp")
    rows = tok_rows // 2
    blocks = rows // SEG_LEN
    place = dp % 4
    slots = 0 * dp
    pos = jnp.reshape(slots, (1,)).astype(jnp.int32)

    x = lax.dynamic_slice_in_dim(inputs, mp * rows, rows, 0)
    cot = lax.dynamic_slice_in_dim(out_grad, mp * rows, rows, 0)
    seg = lax.dynamic_slice_in_dim(segment_ids, mp * rows, rows, 0)
    segc, segr = seg.reshape(rows, 1), seg.reshape(1, rows)
    pairs = lax.dynamic_slice_in_dim(pair_index, mp * blocks, blocks, 0)

    cols = w_qkv.shape[2]
    units = w_in.shape[1]
    if size == 16:
        segr = segment_ids.reshape(1, -1)
        (
            own_out, w_qkv_p, w_out_p, w_in_p, w_back_p, q, k, v, n1, i1, lowt, xt, ctxt, actt, slope, n2, i2,
            loss_value, grad_scale, new_scale, first_grad, bias_qv_p, grad_pool, pool_bias,
        ) = forward(
            inputs, segr, w_qkv, bias_qv, bias_in.reshape(-1, 128),
            norm_gains, shifts, w_pool, logit_scale, pair_index, w_out, w_in, w_back,
        )
        results = backward(
            segr, norm_gains, first_grad, bias_qv_p, own_out,
            inputs, out_grad, n2, i2, n1, i1, actt, slope, lowt, xt, ctxt, q, k, v,
            w_back, w_back_p, w_in, w_in_p, w_out, w_out_p, w_qkv, w_qkv_p,
        )
        (
            grad_inputs, block_out, grad_back, grad_in, grad_qkv, grad_out, gains, shift_grads, grad_bias_qv,
            grad_bias_in, grad_pool, pool_bias,
        ) = finish(results[0], own_out, results[1], *results[2:], grad_pool, pool_bias)
        return (
            block_out, loss_value, grad_inputs, grad_qkv, grad_bias_qv, grad_out, grad_in,
            grad_bias_in[0], grad_back, grad_pool, gains, shift_grads, pool_bias[0], grad_scale, new_scale,
        )

    biases = swap_mp(bias_qv)
    bias_qv_p, bias_in_p = biases, swap_mp(bias_in)
    w_qkv_p = fetch(w_qkv, 1, place)
    w_out_p = fetch(w_out, 0, place)
    w_in_p = fetch(w_in, 0, place)
    w_back_p = fetch(w_back, 0, place)

    q_o, k_o, v_o, ctx_o = attention_half(x, w_qkv, bias_qv, segc, segr)
    q_p, k_p, v_p, ctx_p = attention_half(x, w_qkv_p, bias_qv_p, segc, segr)
    normed_one, inv_one, low_one = first_norm(ctx_o, ctx_p, w_out, w_out_p, x, norm_gains, shifts)
    act_o, slope_o = inner_half(low_one, w_in, bias_in.reshape(1, -1))
    part = branch_half(act_o, w_back)
    act_p, slope_p = inner_half(low_one, w_in_p, bias_in_p.reshape(1, -1))
    normed_two, inv_two, own_out = second_norm(act_p, w_back_p, part, normed_one, norm_gains, shifts)

    firsts = own_out.reshape(blocks, SEG_LEN, width)[:, 0]
    ids = jnp.broadcast_to(pairs.astype(f32)[:, None], (blocks, 128))
    rel = jnp.concatenate([gather_rows(firsts).astype(f32), gather_rows(ids)], axis=1)
    linear = dp * 2 + mp
    position = jnp.stack([linear if size == 16 else 0 * linear, linear]).astype(jnp.int32)
    loss_value, grad_scale, pre_all, pool_bias, first_grad, firsts_all = pair_loss(
        position, rel, w_pool, shifts[4:5], logit_scale
    )
    block_out = both_halves(own_out, mp)
    pool_rows = width // size
    grad_pool = lax.dot_general(
        lax.dynamic_slice_in_dim(firsts_all, dp * pool_rows, pool_rows, 1), pre_all, TN, preferred_element_type=f32
    )
    grad_pool_bias = lax.dynamic_slice_in_dim(pool_bias[0], dp * pool_rows, pool_rows, 0)

    grad_two, branch, sums_two = second_back(cot, first_grad, normed_two, inv_two, norm_gains)
    keep_bo, send_bo = back_weight(pos, act_o, branch)
    keep_bp, send_bp = back_weight(pos, act_p, branch)
    keep_io, send_io, bias_io, part_one = inner_back(pos, branch, w_back, slope_o, low_one, w_in, grad_two)
    keep_ip, send_ip, bias_ip, part_two = inner_back(pos, branch, w_back_p, slope_p, low_one, w_in_p, part_one)
    grad_one, sums_one, dc_o, dc_p, keep_w, send_w = first_back(
        pos, part_two, normed_one, inv_one, norm_gains, ctx_o, ctx_p, w_out, w_out_p
    )
    keep_qo, send_qo, bias_qo, in_one = attention_back(pos, x, w_qkv, segc, segr, q_o, k_o, v_o, dc_o, grad_one)
    keep_qp, send_qp, bias_qp, in_two = attention_back(pos, x, w_qkv_p, segc, segr, q_p, k_p, v_p, dc_p, in_one)

    both = lambda a, b: jnp.stack([a, b])
    mine_back = scatter_sum(both(keep_bo, keep_bp), both(send_bo, send_bp), ("x", "y", "z0", "z1"))
    mine_in = scatter_sum(both(keep_io, keep_ip), both(send_io, send_ip), ("y", "x", "z0", "z1"))
    mine_out = scatter_sum(keep_w, send_w, ("x", "y", "z0", "z1"))
    mine_qkv = scatter_sum(both(keep_qo, keep_qp), both(send_qo, send_qp), ("y", "x", "z0", "z1"))

    vectors = jnp.concatenate([sums_one[0:1], sums_two[0:1], sums_one[2:3], sums_one[1:2], sums_two[2:3], sums_two[1:2]])
    by_dp = vectors.reshape(6, 16, width // 16).transpose(1, 0, 2).reshape(16, -1)
    by_dp = jnp.broadcast_to(by_dp[None], (2,) + by_dp.shape)
    bias_q = both(bias_qo, bias_qp).reshape(2, 2, 16, cols // 16).transpose(0, 2, 1, 3).reshape(2, 16, -1)
    bias_i = both(bias_io, bias_ip).reshape(2, 16, units // 16)
    packed = jnp.concatenate([by_dp, bias_q, bias_i], axis=2)
    packed = swap_order(packed, 1, slots).reshape(2, 8, 2, -1)
    mine_small = scatter_sum(packed[:, :, 0], packed[:, :, 1], ("y", "x", "z0", "z1"))

    if size != 16:
        fold = lambda values: lax.psum_scatter(values, "dp", scatter_dimension=0, tiled=True)
        grad_back = fold(mine_back.reshape(units, width).astype(f32))
        grad_in = fold(mine_in.reshape(width, units).astype(f32))
        grad_qkv = fold(mine_qkv.transpose(0, 2, 1, 3).reshape(width, 3, cols).astype(f32)).transpose(1, 0, 2)
        small = mine_small
        n_vec = 6 * (width // 16)
        n_q = 2 * (cols // 16)
        n_i = units // 16
        vec = small[:, :n_vec].reshape(16, 6, -1).transpose(0, 2, 1).reshape(width, 6)
        vec = fold(vec).T
        grad_bias_qv = fold(small[:, n_vec:n_vec + n_q].reshape(16, 2, -1).transpose(0, 2, 1).reshape(cols, 2)).T
        grad_bias_in = fold(small[:, n_vec + n_q:n_vec + n_q + n_i].reshape(units))
        grad_out = fold(mine_out.reshape(cols, width).astype(f32))
    else:
        grad_back = mine_back.astype(f32)
        grad_in = mine_in.astype(f32)
        grad_qkv = mine_qkv.astype(f32)
        small = mine_small
        n_vec = 6 * (width // 16)
        n_q = 2 * (cols // 16)
        n_i = units // 16
        vec = small[:n_vec].reshape(6, -1)
        grad_bias_qv = small[n_vec:n_vec + n_q].reshape(2, -1)
        grad_bias_in = small[n_vec + n_q:n_vec + n_q + n_i]
        grad_out = mine_out.astype(f32)

    grad_inputs = both_halves(in_two.astype(bf16), mp).astype(f32)
    new_scale = logit_scale - step_rate * grad_scale
    return (
        block_out, loss_value, grad_inputs, grad_qkv, grad_bias_qv, grad_out, grad_in, grad_bias_in,
        grad_back, grad_pool, vec[:2], vec[2:], grad_pool_bias, grad_scale, new_scale,
    )


def solution(mesh):
    return jax.shard_map(
        shards,
        mesh=mesh,
        in_specs=(
            P("dp", None), P("dp"), P("dp"), P(None, None, "mp"), P(None, "mp"), P("mp", None), P(None, "mp"),
            P("mp"), P("mp", None), P(), P(), P(), P(), P("dp", None),
        ),
        out_specs=(
            P("dp", None), P(), P("dp", None), P(None, "dp", "mp"), P(None, ("mp", "dp")), P(("mp", "dp"), None),
            P("dp", "mp"), P(("mp", "dp")), P(("mp", "dp"), None), P("dp", None), P(None, "dp"), P(None, "dp"),
            P("dp"), P(), P(),
        ),
        check_vma=False,
    )
```

```python
from functools import partial

import jax
import jax.numpy as jnp
from jax import lax
from jax.experimental import pallas as pl
from jax.experimental.pallas import tpu as pltpu
from jax.sharding import PartitionSpec as P

HEAD_DIM = 64
SEG_LEN = 64
PAIR = 2 * HEAD_DIM
GROUP = 128

epsilon = 1e-12
margin = 0.3
step_rate = 0.1
masked_out = -1e30
f32 = jnp.float32
bf16 = jnp.bfloat16

NT = (((1,), (1,)), ((), ()))
TN = (((0,), (0,)), ((), ()))


def mm(a, b):
    return jnp.dot(a, b, preferred_element_type=f32)


def mm_nt(a, b):
    return lax.dot_general(a, b, NT, preferred_element_type=f32)


def mm_tn(a, b):
    return lax.dot_general(a, b, TN, preferred_element_type=f32)


def params(mib=40):
    return pltpu.CompilerParams(vmem_limit_bytes=mib * 1024 * 1024)


def cost(flops, moved):
    return pl.CostEstimate(flops=int(flops), bytes_accessed=int(moved), transcendentals=0)


def lane_masks():
    lane = lax.broadcasted_iota(jnp.int32, (1, PAIR), 1)
    first = (lane < HEAD_DIM).astype(f32)
    return first, 1.0 - first


def two_heads(rows):
    first, second = lane_masks()
    return jnp.concatenate([rows * first.astype(bf16), rows * second.astype(bf16)], axis=0)


def join_heads(both):
    first, second = lane_masks()
    half = both.shape[0] // 2
    return both[:half] * first + both[half:] * second


def pair_probs(q_two, k_pair, same):
    scores = mm_nt(q_two, k_pair) * (HEAD_DIM ** (-0.5))
    scores = jnp.where(same, scores, masked_out)
    shifted = jnp.exp(scores - jnp.max(scores, axis=1, keepdims=True))
    return shifted / jnp.sum(shifted, axis=1, keepdims=True)


def same_segment(seg_col, seg_row, rows):
    own = seg_col[rows, :]
    other = seg_row[:, rows]
    one = own == other
    return jnp.concatenate([one, one], axis=0)


def attention_kernel(x_ref, w_ref, b_ref, segc_ref, segr_ref, q_ref, k_ref, v_ref, c_ref):
    x = x_ref[...]
    q_ref[...] = (mm(x, w_ref[0]) + b_ref[0:1]).astype(bf16)
    k_ref[...] = mm(x, w_ref[1]).astype(bf16)
    v_ref[...] = (mm(x, w_ref[2]) + b_ref[1:2]).astype(bf16)
    for group in range(x.shape[0] // GROUP):
        rows = slice(group * GROUP, (group + 1) * GROUP)
        same = same_segment(segc_ref, segr_ref, rows)
        for pair in range(q_ref.shape[1] // PAIR):
            cols = slice(pair * PAIR, (pair + 1) * PAIR)
            probs = pair_probs(two_heads(q_ref[rows, cols]), k_ref[rows, cols], same)
            c_ref[rows, cols] = join_heads(mm(probs.astype(bf16), v_ref[rows, cols])).astype(bf16)


def attention_half(x, w, b, segc, segr):
    rows, cols = x.shape[0], w.shape[2]
    out = jax.ShapeDtypeStruct((rows, cols), bf16)
    return pl.pallas_call(
        attention_kernel,
        out_shape=(out,) * 4,
        compiler_params=params(),
        cost_estimate=cost(2 * rows * 768 * cols * 3 * 2, 6 * rows * cols * 2),
        name="attention",
    )(x, w, b, segc, segr)


def norm_rows(values):
    row_mean = jnp.mean(values, axis=-1, keepdims=True)
    centred = values - row_mean
    inv_std = lax.rsqrt(jnp.mean(centred * centred, axis=-1, keepdims=True) + epsilon)
    return centred * inv_std, inv_std


def norm_back(grad, normed, inv_std, gain):
    scaled = grad * gain
    return inv_std * (
        scaled
        - jnp.mean(scaled, axis=-1, keepdims=True)
        - normed * jnp.mean(scaled * normed, axis=-1, keepdims=True)
    )


def first_norm_kernel(co_ref, cp_ref, wo_ref, wp_ref, x_ref, g_ref, s_ref, n_ref, inv_ref, low_ref):
    for at in range(0, x_ref.shape[0], 128):
        rows = slice(at, at + 128)
        attended = mm(co_ref[rows], wo_ref[...]) + mm(cp_ref[rows], wp_ref[...]) + s_ref[0:1]
        normed, inv_std = norm_rows(x_ref[rows].astype(f32) + attended)
        n_ref[rows] = normed
        inv_ref[rows] = inv_std
        low_ref[rows] = (normed * g_ref[0:1] + s_ref[1:2]).astype(bf16)


def first_norm(ctx_o, ctx_p, wo, wp, x, gains, shifts):
    rows, width = x.shape
    return pl.pallas_call(
        first_norm_kernel,
        out_shape=(
            jax.ShapeDtypeStruct((rows, width), f32),
            jax.ShapeDtypeStruct((rows, 1), f32),
            jax.ShapeDtypeStruct((rows, width), bf16),
        ),
        compiler_params=params(),
        cost_estimate=cost(2 * rows * width * width, 12 * rows * width),
        name="first_norm",
    )(ctx_o, ctx_p, wo, wp, x, gains, shifts)


def inner_kernel(h_ref, w_ref, b_ref, act_ref, slope_ref):
    for at in range(0, h_ref.shape[0], 128):
        rows = slice(at, at + 128)
        inner = mm(h_ref[rows], w_ref[...]) + b_ref[...]
        cumulative = 0.5 * (1.0 + lax.erf(inner * 0.7071067811865476))
        density = jnp.exp(-0.5 * inner * inner) * 0.3989422804014327
        act_ref[rows] = (inner * cumulative).astype(bf16)
        slope_ref[rows] = (cumulative + inner * density).astype(bf16)


def inner_half(low, w, b):
    rows, width = low.shape
    units = w.shape[1]
    tile = 256
    out = jax.ShapeDtypeStruct((rows, units), bf16)
    return pl.pallas_call(
        inner_kernel,
        grid=(units // tile,),
        in_specs=[
            pl.BlockSpec((rows, width), lambda n: (0, 0)),
            pl.BlockSpec((width, tile), lambda n: (0, n)),
            pl.BlockSpec((1, tile), lambda n: (0, n)),
        ],
        out_specs=[pl.BlockSpec((rows, tile), lambda n: (0, n))] * 2,
        out_shape=(out, out),
        compiler_params=params(),
        cost_estimate=cost(4 * rows * width * units, 8 * rows * units),
        name="inner",
    )(low, w, b)


def branch_kernel(act_ref, w_ref, out_ref):
    for at in range(0, act_ref.shape[0], 128):
        rows = slice(at, at + 128)
        out_ref[rows] = mm(act_ref[rows], w_ref[...])


def branch_half(act, w):
    rows, units = act.shape
    width = w.shape[1]
    return pl.pallas_call(
        branch_kernel,
        out_shape=jax.ShapeDtypeStruct((rows, width), f32),
        compiler_params=params(),
        cost_estimate=cost(2 * rows * width * units, 4 * rows * units),
        name="branch",
    )(act, w)


def second_norm_kernel(act_ref, w_ref, part_ref, n1_ref, g_ref, s_ref, n_ref, inv_ref, out_ref):
    for at in range(0, act_ref.shape[0], 128):
        rows = slice(at, at + 128)
        branch = mm(act_ref[rows], w_ref[...]) + part_ref[rows] + s_ref[2:3]
        hidden_one = n1_ref[rows] * g_ref[0:1] + s_ref[1:2]
        normed, inv_std = norm_rows(hidden_one + branch)
        n_ref[rows] = normed
        inv_ref[rows] = inv_std
        out_ref[rows] = (normed * g_ref[1:2] + s_ref[3:4]).astype(bf16)


def second_norm(act, w, part, normed_one, gains, shifts):
    rows, units = act.shape
    width = w.shape[1]
    return pl.pallas_call(
        second_norm_kernel,
        out_shape=(
            jax.ShapeDtypeStruct((rows, width), f32),
            jax.ShapeDtypeStruct((rows, 1), f32),
            jax.ShapeDtypeStruct((rows, width), bf16),
        ),
        compiler_params=params(),
        cost_estimate=cost(2 * rows * width * units, 4 * rows * units),
        name="second_norm",
    )(act, w, part, normed_one, gains, shifts)


def loss_kernel(
    pos_ref, rel_ref, w_ref, bias_ref, scale_ref,
    loss_ref, gscale_ref, pre_ref, bias_grad_ref, first_grad_ref, firsts_out_ref,
    all_ref, pooled_ref, len_ref, unit_ref, lse_col_ref, lse_row_ref, pre_f_ref,
):
    @pl.loop(0, pooled_ref.shape[0] // 8)
    def _(slot):
        source = pl.multiple_of(slot * 8, 8)
        target = pl.multiple_of(jnp.bitwise_xor(slot, pos_ref[0]) * 8, 8)
        all_ref[pl.ds(target, 8), :] = rel_ref[pl.ds(source, 8), :].astype(f32)

    loss_passes(
        pos_ref[1], scale_ref[0], w_ref, bias_ref[...],
        loss_ref, gscale_ref, pre_ref, bias_grad_ref, first_grad_ref, firsts_out_ref,
        all_ref, pooled_ref, len_ref, unit_ref, lse_col_ref, lse_row_ref, pre_f_ref,
    )


def loss_passes(
    here, scale, w_ref, bias,
    loss_ref, gscale_ref, pre_ref, bias_grad_ref, first_grad_ref, firsts_out_ref,
    all_ref, pooled_ref, len_ref, unit_ref, lse_col_ref, lse_row_ref, pre_f_ref,
):
    count, width = pooled_ref.shape
    chunk = min(count, 256)
    steps = count // chunk

    def pool(at):
        firsts = all_ref[pl.ds(at, chunk), :width].astype(bf16)
        firsts_out_ref[pl.ds(at, chunk), :] = firsts
        pooled = jnp.tanh(mm(firsts, w_ref[...]) + bias)
        inv_len = lax.rsqrt(jnp.sum(pooled * pooled, axis=-1, keepdims=True) + 1e-06)
        pooled_ref[pl.ds(at, chunk), :] = pooled
        len_ref[pl.ds(at, chunk), :] = inv_len
        unit_ref[pl.ds(at, chunk), :] = (pooled * inv_len).astype(bf16)

    def positions(at):
        own = at + lax.broadcasted_iota(jnp.int32, (chunk, count), 0)
        other = lax.broadcasted_iota(jnp.int32, (chunk, count), 1)
        paired = all_ref[pl.ds(at, chunk), width:width + 1]
        positive = paired.astype(jnp.int32) == other
        return own == other, positive

    def logits_of(at):
        cosine = mm_nt(unit_ref[pl.ds(at, chunk), :], unit_ref[...])
        own, positive = positions(at)
        shifted = cosine - jnp.where(positive, margin, 0.0)
        return shifted, own, positive

    def first_pass(at, run):
        shifted, own, positive = logits_of(at)
        logits = jnp.where(own, masked_out, scale * shifted)
        top = jnp.max(logits, axis=1, keepdims=True)
        lse = top + jnp.log(jnp.sum(jnp.exp(logits - top), axis=1, keepdims=True))
        lse_col_ref[pl.ds(at, chunk), :] = lse
        eye = lax.broadcasted_iota(jnp.int32, (chunk, chunk), 0) == lax.broadcasted_iota(
            jnp.int32, (chunk, chunk), 1
        )
        lse_row_ref[:, pl.ds(at, chunk)] = jnp.sum(jnp.where(eye, lse, 0.0), axis=0, keepdims=True)
        return run + jnp.sum(lse) - jnp.sum(jnp.where(positive, logits, 0.0))

    def second_pass(at, run):
        run_scale, run_bias = run
        shifted, own, positive = logits_of(at)
        logits = scale * shifted
        factor = 1.0 / (2.0 * count)
        grad = (
            jnp.exp(logits - lse_col_ref[pl.ds(at, chunk), :])
            + jnp.exp(logits - lse_row_ref[...])
            - jnp.where(positive, 2.0, 0.0)
        ) * factor
        grad = jnp.where(own, 0.0, grad)
        run_scale = run_scale + jnp.sum(grad * shifted)
        unit_grad = 2.0 * mm((scale * grad).astype(bf16), unit_ref[...])
        pooled = pooled_ref[pl.ds(at, chunk), :]
        inv_len = len_ref[pl.ds(at, chunk), :]
        along = jnp.sum(pooled * unit_grad, axis=-1, keepdims=True)
        pooled_grad = inv_len * unit_grad - pooled * (inv_len * inv_len * inv_len) * along
        pre_grad = (pooled_grad * (1.0 - pooled * pooled)).astype(bf16)
        pre_ref[pl.ds(at, chunk), :] = pre_grad
        pre_f_ref[pl.ds(at, chunk), :] = pre_grad.astype(f32)
        return run_scale, run_bias + jnp.sum(pre_grad.astype(f32), axis=0, keepdims=True)

    def each(body, run):
        if steps == 1:
            return body(0, run)
        return lax.fori_loop(0, steps, lambda s, r: body(pl.multiple_of(s * chunk, chunk), r), run)

    each(lambda at, run: (pool(at), run)[1], 0)
    total = each(first_pass, jnp.float32(0.0))
    run_scale, run_bias = each(second_pass, (jnp.float32(0.0), jnp.zeros((1, width), f32)))
    loss_ref[0] = total / count
    gscale_ref[0] = run_scale
    bias_grad_ref[...] = run_bias
    own_rows = pre_f_ref[pl.ds(pl.multiple_of(here * 8, 8), 8), :].astype(bf16)
    first_grad_ref[...] = mm_nt(own_rows, w_ref[...])


def pair_loss(position, rel, w_pool, bias, scale):
    count, wide = rel.shape
    width = w_pool.shape[0]
    smem = pl.BlockSpec(memory_space=pltpu.SMEM)
    vmem = pl.BlockSpec(memory_space=pltpu.VMEM)
    return pl.pallas_call(
        loss_kernel,
        in_specs=[smem, vmem, vmem, vmem, smem],
        out_specs=[smem, smem, vmem, vmem, vmem, vmem],
        out_shape=(
            jax.ShapeDtypeStruct((1,), f32),
            jax.ShapeDtypeStruct((1,), f32),
            jax.ShapeDtypeStruct((count, width), bf16),
            jax.ShapeDtypeStruct((1, width), f32),
            jax.ShapeDtypeStruct((8, width), f32),
            jax.ShapeDtypeStruct((count, width), bf16),
        ),
        scratch_shapes=[
            pltpu.VMEM((count, wide), f32),
            pltpu.VMEM((count, width), f32),
            pltpu.VMEM((count, 1), f32),
            pltpu.VMEM((count, width), bf16),
            pltpu.VMEM((count, 1), f32),
            pltpu.VMEM((1, count), f32),
            pltpu.VMEM((count, width), f32),
        ],
        compiler_params=params(56),
        cost_estimate=cost(2e9, 4e6),
        name="pair_loss",
    )(position, rel, w_pool, bias, scale)


def put_slabs(pos_ref, source, keep_ref, send_ref, lead):
    slab = source.shape[0] // 16
    for place in range(16):
        at = pl.multiple_of(jnp.bitwise_xor(pos_ref[0], place) * slab, slab)
        target = send_ref if place % 2 else keep_ref
        target[lead + (place // 2,)] = source[pl.ds(at, slab), :].astype(bf16)


def second_back_kernel(
    og_ref, fg_ref, n_ref, inv_ref, g_ref, grad_ref, low_ref, sums_ref
):
    rows_all, width = og_ref.shape
    sums_ref[...] = jnp.zeros_like(sums_ref)
    for at in range(0, rows_all, 64):
        rows = slice(at, at + 64)
        block = at // 64
        is_first = lax.broadcasted_iota(jnp.int32, (64, width), 0) == 0
        grad = og_ref[rows].astype(f32) + jnp.where(is_first, fg_ref[block:block + 1], 0.0)
        normed = n_ref[rows]
        value = norm_back(grad, normed, inv_ref[rows], g_ref[1:2])
        low = value.astype(bf16)
        grad_ref[rows] = value
        low_ref[rows] = low
        sums_ref[0:1] += jnp.sum(grad * normed, axis=0, keepdims=True)
        sums_ref[1:2] += jnp.sum(grad, axis=0, keepdims=True)
        sums_ref[2:3] += jnp.sum(low.astype(f32), axis=0, keepdims=True)


def second_back(out_grad, first_grad, normed, inv_std, gains):
    rows, width = out_grad.shape
    return pl.pallas_call(
        second_back_kernel,
        out_shape=(
            jax.ShapeDtypeStruct((rows, width), f32),
            jax.ShapeDtypeStruct((rows, width), bf16),
            jax.ShapeDtypeStruct((8, width), f32),
        ),
        compiler_params=params(),
        cost_estimate=cost(20 * rows * width, 12 * rows * width),
        name="second_back",
    )(out_grad, first_grad, normed, inv_std, gains)


def slab_shape(rows, cols):
    return jax.ShapeDtypeStruct((8, rows // 16, cols), bf16)


def back_weight_kernel(pos_ref, act_ref, branch_ref, keep_ref, send_ref, whole):
    for at in range(0, whole.shape[0], 256):
        rows = slice(at, at + 256)
        whole[rows] = mm_tn(act_ref[:, rows], branch_ref[...])
    put_slabs(pos_ref, whole, keep_ref, send_ref, ())


def back_weight(pos, act, branch):
    rows, units = act.shape
    width = branch.shape[1]
    smem = pl.BlockSpec(memory_space=pltpu.SMEM)
    vmem = pl.BlockSpec(memory_space=pltpu.VMEM)
    return pl.pallas_call(
        back_weight_kernel,
        in_specs=[smem, vmem, vmem],
        out_specs=[vmem, vmem],
        out_shape=(slab_shape(units, width),) * 2,
        scratch_shapes=[pltpu.VMEM((units, width), f32)],
        compiler_params=params(),
        cost_estimate=cost(2 * rows * width * units, 4 * units * width),
        name="back_weight",
    )(pos, act, branch)


def inner_back_kernel(pos_ref, branch_ref, wb_ref, slope_ref, low_ref, wi_ref, part_ref,
                      keep_ref, send_ref, bias_ref, out_ref, grad, whole):
    units = slope_ref.shape[1]
    for at in range(0, units, 256):
        cols = slice(at, at + 256)
        inner_grad = (mm_nt(branch_ref[...], wb_ref[cols]) * slope_ref[:, cols].astype(f32)).astype(bf16)
        grad[:, cols] = inner_grad
        bias_ref[:, cols] = jnp.sum(inner_grad.astype(f32), axis=0, keepdims=True)
        whole[:, cols] = mm_tn(low_ref[...], inner_grad)
    put_slabs(pos_ref, whole, keep_ref, send_ref, ())
    for at in range(0, low_ref.shape[0], 128):
        rows = slice(at, at + 128)
        out_ref[rows] = part_ref[rows] + mm_nt(grad[rows], wi_ref[...])


def inner_back(pos, branch, w_back, slope, low, w_in, part):
    rows, units = slope.shape
    width = low.shape[1]
    smem = pl.BlockSpec(memory_space=pltpu.SMEM)
    vmem = pl.BlockSpec(memory_space=pltpu.VMEM)
    return pl.pallas_call(
        inner_back_kernel,
        in_specs=[smem] + [vmem] * 6,
        out_specs=[vmem] * 4,
        out_shape=(slab_shape(width, units),) * 2
        + (jax.ShapeDtypeStruct((1, units), f32), jax.ShapeDtypeStruct((rows, width), f32)),
        scratch_shapes=[pltpu.VMEM((rows, units), bf16), pltpu.VMEM((width, units), f32)],
        compiler_params=params(),
        cost_estimate=cost(6 * rows * width * units, 4 * units * width),
        name="inner_back",
    )(pos, branch, w_back, slope, low, w_in, part)


def first_back_kernel(pos_ref, grad_ref, n_ref, inv_ref, g_ref, co_ref, cp_ref, wo_ref, wp_ref,
                      one_ref, sums_ref, dco_ref, dcp_ref, keep_ref, send_ref, low, whole):
    width = grad_ref.shape[1]
    sums_ref[...] = jnp.zeros_like(sums_ref)
    for at in range(0, grad_ref.shape[0], 128):
        rows = slice(at, at + 128)
        grad = grad_ref[rows]
        normed = n_ref[rows]
        value = norm_back(grad, normed, inv_ref[rows], g_ref[0:1])
        low_rows = value.astype(bf16)
        one_ref[rows] = value
        low[rows] = low_rows
        dco_ref[rows] = mm_nt(low_rows, wo_ref[...]).astype(bf16)
        dcp_ref[rows] = mm_nt(low_rows, wp_ref[...]).astype(bf16)
        sums_ref[0:1] += jnp.sum(grad * normed, axis=0, keepdims=True)
        sums_ref[1:2] += jnp.sum(grad, axis=0, keepdims=True)
        sums_ref[2:3] += jnp.sum(low_rows.astype(f32), axis=0, keepdims=True)
    for side, ctx_ref in enumerate((co_ref, cp_ref)):
        whole[...] = mm_tn(ctx_ref[...], low[...])
        put_slabs(pos_ref, whole, keep_ref.at[side], send_ref.at[side], ())


def first_back(pos, grad, normed, inv_std, gains, ctx_o, ctx_p, wo, wp):
    rows, width = grad.shape
    cols = ctx_o.shape[1]
    smem = pl.BlockSpec(memory_space=pltpu.SMEM)
    vmem = pl.BlockSpec(memory_space=pltpu.VMEM)
    return pl.pallas_call(
        first_back_kernel,
        in_specs=[smem] + [vmem] * 8,
        out_specs=[vmem] * 6,
        out_shape=(
            jax.ShapeDtypeStruct((rows, width), f32),
            jax.ShapeDtypeStruct((8, width), f32),
            jax.ShapeDtypeStruct((rows, cols), bf16),
            jax.ShapeDtypeStruct((rows, cols), bf16),
        )
        + (jax.ShapeDtypeStruct((2, 8, cols // 16, width), bf16),) * 2,
        scratch_shapes=[pltpu.VMEM((rows, width), bf16), pltpu.VMEM((cols, width), f32)],
        compiler_params=params(),
        cost_estimate=cost(8 * rows * width * cols, 12 * rows * width),
        name="first_back",
    )(pos, grad, normed, inv_std, gains, ctx_o, ctx_p, wo, wp)


def attention_back_kernel(pos_ref, x_ref, w_ref, segc_ref, segr_ref, q_ref, k_ref, v_ref, dc_ref, part_ref,
                          keep_ref, send_ref, bias_ref, out_ref, dq, dk, dv, whole):
    scale = HEAD_DIM ** (-0.5)
    for group in range(x_ref.shape[0] // GROUP):
        rows = slice(group * GROUP, (group + 1) * GROUP)
        same = same_segment(segc_ref, segr_ref, rows)
        for pair in range(q_ref.shape[1] // PAIR):
            cols = slice(pair * PAIR, (pair + 1) * PAIR)
            q_two = two_heads(q_ref[rows, cols])
            dc_two = two_heads(dc_ref[rows, cols])
            k_pair = k_ref[rows, cols]
            probs = pair_probs(q_two, k_pair, same)
            prob_grad = mm_nt(dc_two, v_ref[rows, cols])
            score_grad = (
                probs * (prob_grad - jnp.sum(prob_grad * probs, axis=1, keepdims=True))
            ).astype(bf16)
            dq[rows, cols] = (join_heads(mm(score_grad, k_pair)) * scale).astype(bf16)
            dk[rows, cols] = (mm_tn(score_grad, q_two) * scale).astype(bf16)
            dv[rows, cols] = mm_tn(probs.astype(bf16), dc_two).astype(bf16)
    bias_ref[0:1] = jnp.sum(dq[...].astype(f32), axis=0, keepdims=True)
    bias_ref[1:2] = jnp.sum(dv[...].astype(f32), axis=0, keepdims=True)
    for s, grad in enumerate((dq, dk, dv)):
        whole[...] = mm_tn(x_ref[...], grad[...])
        put_slabs_at(pos_ref, whole, keep_ref, send_ref, s)
    for at in range(0, x_ref.shape[0], 128):
        rows = slice(at, at + 128)
        out_ref[rows] = (
            part_ref[rows] + mm_nt(dq[rows], w_ref[0]) + mm_nt(dk[rows], w_ref[1]) + mm_nt(dv[rows], w_ref[2])
        )


def put_slabs_at(pos_ref, source, keep_ref, send_ref, s):
    slab = source.shape[0] // 16
    for place in range(16):
        at = pl.multiple_of(jnp.bitwise_xor(pos_ref[0], place) * slab, slab)
        target = send_ref if place % 2 else keep_ref
        target[place // 2, s] = source[pl.ds(at, slab), :].astype(bf16)


def attention_back(pos, x, w, segc, segr, q, k, v, dc, part):
    rows, width = x.shape
    cols = q.shape[1]
    smem = pl.BlockSpec(memory_space=pltpu.SMEM)
    vmem = pl.BlockSpec(memory_space=pltpu.VMEM)
    slabs = jax.ShapeDtypeStruct((8, 3, width // 16, cols), bf16)
    return pl.pallas_call(
        attention_back_kernel,
        in_specs=[smem] + [vmem] * 9,
        out_specs=[vmem] * 4,
        out_shape=(slabs, slabs, jax.ShapeDtypeStruct((2, cols), f32), jax.ShapeDtypeStruct((rows, width), f32)),
        scratch_shapes=[pltpu.VMEM((rows, cols), bf16)] * 3 + [pltpu.VMEM((width, cols), f32)],
        compiler_params=params(),
        cost_estimate=cost(20 * rows * width * cols, 4 * 3 * width * cols),
        name="attention_back",
    )(pos, x, w, segc, segr, q, k, v, dc, part)


def flip(value, bit):
    return value + bit - 2 * bit * ((value // bit) % 2)


class Copies:
    def __init__(self, send, recv, local):
        self.send, self.recv, self.local = send, recv, local
        self.sent, self.kept, self.ring = [], [], send.shape[0]

    def remote(self, source, target, device):
        at = len(self.sent)
        if at >= self.ring:
            self.sent[at - self.ring].wait_send()
        copy = pltpu.make_async_remote_copy(
            src_ref=source, dst_ref=target, send_sem=self.send.at[at % self.ring], recv_sem=self.recv.at[at],
            device_id=device, device_id_type=pl.DeviceIdType.MESH,
        )
        copy.start()
        self.sent.append(copy)
        return copy

    def here(self, source, target):
        copy = pltpu.make_async_copy(source, target, self.local.at[len(self.kept)])
        copy.start()
        self.kept.append(copy)
        return copy


def greet(devices):
    barrier = pltpu.get_barrier_semaphore()
    for device in devices:
        pl.semaphore_signal(barrier, inc=1, device_id=device, device_id_type=pl.DeviceIdType.MESH)
    pl.semaphore_wait(barrier, len(devices))


def same_block(row):
    across = jnp.broadcast_to(row.astype(f32), (GROUP, GROUP))
    return across == across.T


def arrive(*copies):
    for copy in copies:
        copy.wait_recv()


N_CHUNK = 3


def forward_kernel(
    segr_ref, b_qv_ref, b_in_ref, g_ref, s_ref, scale_ref, pairs_ref,
    x_any, w_pool_any, w_qkv_any, w_out_any, w_in_any, w_back_any,
    block_out, p_qkv, p_out_any, p_in_any, p_back_any, q_any, k_any, v_any, n1_any, i1_any, lowt_any, xt_any, ctxt_any,
    actt_any, slope_any, n2_any, i2_any,
    loss_ref, gscale_ref, new_scale_ref, first_any, b_qv_p, pool_any, pool_bias_any,
    first_grad_ref, pool_ref, pool_bias_ref, x_ref, w_pool_ref, w_qkv_ref, w_out, w_in, w_back, p_out, p_in, p_back, b_in_p, q, k, v, qf, kf, vf, ctx_far, ctx_o, ctx_p,
    n1, i1, low, act, slope, part, n2, i2, own_out, lowt, xt, ctxt, actt, ahead, ahead_got, gathered, ids,
    pre_ref, bias_grad_ref, firsts_out_ref, all_ref, pooled_ref, len_ref, unit_ref, lse_col_ref, lse_row_ref, pre_f_ref,
    send_sem, recv_sem, local_sem,
):
    dp, mp = lax.axis_index("dp"), lax.axis_index("mp")
    rows = q.shape[0]
    width = x_ref.shape[1]
    units = w_in.shape[1]
    near = {"x": {"mp": 1 - mp}, "y": {"dp": flip(dp, 2)}, "z": {"dp": flip(dp, 4)}, "c": {"dp": flip(dp, 1)}}
    far = ({"dp": flip(dp, 8)}, {"dp": flip(flip(dp, 4), 8)})
    run = Copies(send_sem, recv_sem, local_sem)
    own = dp % 8
    bit = {"y": 2, "z": 4}

    out_block, in_block, unit_chunk = w_out.shape[0] // 8, width // 8, units // N_CHUNK
    back_block = unit_chunk // 8

    def out_at(ref):
        return lambda b: ref.at[pl.ds(pl.multiple_of(b * out_block, 16), out_block)]

    def in_at(ref, n):
        return lambda b: ref.at[pl.ds(pl.multiple_of(b * in_block, 16), in_block), pl.ds(n * unit_chunk, unit_chunk)]

    def back_at(ref, n):
        return lambda b: ref.at[pl.ds(pl.multiple_of(n * unit_chunk + b * back_block, 16), back_block)]

    def qkv_at(ref, n):
        return lambda b: ref.at[:, pl.ds(pl.multiple_of((2 * b + n) * in_block, 16), in_block)]

    routes = ("zy", "zy", "yz", "zy", "yz", "zy", "yz")
    chunks = [(out_at(w_out_any), out_at(p_out), routes[0])]
    chunks += [(in_at(w_in_any, n), in_at(p_in, n), routes[1 + n]) for n in range(N_CHUNK)]
    chunks += [(back_at(w_back_any, n), back_at(p_back, n), routes[1 + N_CHUNK + n]) for n in range(N_CHUNK)]
    chunks += [(qkv_at(w_qkv_any, n), qkv_at(p_qkv, n), "yz"[n]) for n in range(2)]
    hops = [[None] * 4 for _ in chunks]

    def step(at, stage):
        source, target, route = chunks[at]
        first = own if len(route) == 2 else dp % 2 + 2 * ((dp // bit[route]) % 2)
        if stage == 0:
            hops[at][0] = [run.remote(source(first), target(first), near["x"])]
            return
        for copy in hops[at][stage - 1]:
            copy.wait_recv()
        one = flip(first, bit[route[0]] if len(route) == 2 else 2)
        blocks = [first, one]
        if len(route) == 2:
            blocks += [flip(b, bit[route[1]]) for b in blocks]
        if stage == 1:
            hops[at][1] = [run.remote(target(first), target(first), near[route[0]])]
        elif stage == len(route) + 1:
            hops[at][stage] = [run.remote(target(b), target(b), near["c"]) for b in blocks]
        elif stage == 2:
            hops[at][2] = [run.remote(target(b), target(b), near[route[1]]) for b in blocks[:2]]

    loads = [
        run.here(a, b)
        for a, b in (
            (x_any, x_ref), (w_qkv_any, w_qkv_ref), (w_out_any, w_out), (w_in_any, w_in), (w_back_any, w_back),
            (w_pool_any, w_pool_ref),
        )
    ]
    z, y, c = dp // 4, (dp // 2) % 2, dp % 2
    row_of = lax.broadcasted_iota(jnp.int32, (8, 128), 0)
    paired = jnp.zeros((8, 128), f32)
    for at in range(8):
        paired = jnp.where(row_of == at, pairs_ref[mp * 8 + at].astype(f32), paired)
    ids[z, y, c, mp] = paired
    greet(list(near.values()) + list(far))
    pair_hops = [[run.remote(ids.at[z, y, c, mp], ids.at[z, y, c, mp], near["x"])]]
    step(0, 0)
    b_copies = [run.remote(b_in_ref, b_in_p, near["x"]), run.remote(b_qv_ref, b_qv_p, near["x"])]

    def project(base, q_to, k_to, v_to):
        x = x_ref[pl.ds(base, rows)]
        q_to[...] = (mm(x, w_qkv_ref[0]) + b_qv_ref[0:1]).astype(bf16)
        k_to[...] = mm(x, w_qkv_ref[1]).astype(bf16)
        v_to[...] = (mm(x, w_qkv_ref[2]) + b_qv_ref[1:2]).astype(bf16)

    def attend(base, q_from, k_from, v_from, target):
        for group in range(rows // GROUP):
            at = slice(group * GROUP, (group + 1) * GROUP)
            one = same_block(segr_ref[:, pl.ds(pl.multiple_of(base + group * GROUP, GROUP), GROUP)])
            same = jnp.concatenate([one, one], axis=0)
            for pair in range(q_from.shape[1] // PAIR):
                cols = slice(pair * PAIR, (pair + 1) * PAIR)
                probs = pair_probs(two_heads(q_from[at, cols]), k_from[at, cols], same)
                target[at, cols] = join_heads(mm(probs.astype(bf16), v_from[at, cols])).astype(bf16)

    far_base = pl.multiple_of((1 - mp) * rows, rows)
    own_base = pl.multiple_of(mp * rows, rows)
    half = width // 2
    flight = {}

    def firsts_of(ref):
        return jnp.concatenate([ref[at:at + 1].astype(f32) for at in range(0, rows, SEG_LEN)], axis=0)

    def gelu_parts(value):
        cumulative = 0.5 * (1.0 + lax.erf(value * 0.7071067811865476))
        density = jnp.exp(-0.5 * value * value) * 0.3989422804014327
        return (value * cumulative).astype(bf16), cumulative + value * density

    def bias_of(b, at):
        return jnp.concatenate([b[at // 128:at // 128 + 1], b[at // 128 + 1:at // 128 + 2]], axis=1)

    def far_tokens():
        loads[0].wait()
        loads[1].wait()
        project(far_base, qf, kf, vf)
        attend(far_base, qf, kf, vf, ctx_far)

    def own_tokens():
        attend(own_base, q, k, v, ctx_o)
        for a, b in ((q, q_any), (k, k_any), (v, v_any)):
            run.here(a, b)

    def send_context(part):
        some = pl.ds(part * GROUP, GROUP)
        flight["context", part] = run.remote(ctx_far.at[some], ctx_p.at[some], near["x"])

    def ahead_out():
        loads[2].wait()
        both = jnp.concatenate([firsts_of(ctx_o), firsts_of(ctx_far)], axis=0).astype(bf16)
        ahead[0] = mm(both, w_out[...])
        flight["ahead"] = run.remote(ahead.at[0, pl.ds(8, 8)], ahead_got.at[0], near["x"])

    def ahead_norm():
        arrive(flight["ahead"])
        x = jnp.concatenate(
            [x_ref[pl.ds(pl.multiple_of(own_base + at, SEG_LEN), 16)][0:1].astype(f32) for at in range(0, rows, SEG_LEN)],
            axis=0,
        )
        hidden = norm_rows(x + ahead[0, 0:8] + ahead_got[0] + s_ref[0:1])[0] * g_ref[0:1] + s_ref[1:2]
        ahead[3, 0:8] = hidden
        ahead[1, 0:8] = hidden.astype(bf16).astype(f32)
        flight["ahead"] = run.remote(ahead.at[1, pl.ds(0, 8)], ahead.at[1, pl.ds(8, 8)], near["x"])

    def ahead_units():
        loads[3].wait()
        loads[4].wait()
        arrive(flight["ahead"])
        both = ahead[1].astype(bf16)
        total = jnp.zeros((16, width), f32)
        for at in range(0, units, 256):
            inside = gelu_parts(mm(both, w_in[:, at:at + 256]) + bias_of(b_in_ref, at))[0]
            total = total + mm(inside, w_back[at:at + 256])
        ahead[2] = total
        flight["ahead"] = run.remote(ahead.at[2, pl.ds(8, 8)], ahead_got.at[1], near["x"])

    def ahead_last():
        arrive(flight["ahead"])
        normed = norm_rows(ahead[3, 0:8] + (ahead[2, 0:8] + ahead_got[1] + s_ref[2:3]))[0]
        firsts = (normed * g_ref[1:2] + s_ref[3:4]).astype(bf16).astype(f32)
        gathered[z, y, c, mp] = jnp.concatenate([firsts[:, :half], firsts[:, half:]], axis=0).astype(bf16)
        slot = gathered.at[z, y, c, mp]
        flight["gather"] = [run.remote(slot, slot, near["x"])]

    def gather(hop):
        arrive(*flight["gather"])
        slot = (gathered.at[z, y, c], gathered.at[:, y, c], gathered.at[:, :, c])[hop]
        devices = ((far[1], far[0], near["z"]), (near["y"],), (near["c"],))[hop]
        flight["gather"] = [run.remote(slot, slot, device) for device in devices]

    def pair_hop(hop):
        arrive(*pair_hops[hop])
        slot = (ids.at[z, y, c], ids.at[:, y, c], ids.at[:, :, c])[hop]
        devices = ((far[1], far[0], near["z"]), (near["y"],), (near["c"],))[hop]
        pair_hops.append([run.remote(slot, slot, device) for device in devices])

    def turn():
        for at in range(0, rows, 128):
            here = slice(at, at + 128)
            xt[:, here] = x_ref[pl.ds(pl.multiple_of(own_base + at, 128), 128)].T
            ctxt[0, :, here] = ctx_o[here].T

    def own_out_part():
        part[...] = mm(ctx_o[...], w_out[...])

    def first_norm():
        arrive(*[flight["context", at] for at in range(rows // GROUP)])
        for at in range(0, rows, 128):
            here = slice(at, at + 128)
            x = x_ref[pl.ds(pl.multiple_of(own_base + at, 128), 128)].astype(f32)
            normed, inv_std = norm_rows(x + part[here] + mm(ctx_p[here], p_out[...]) + s_ref[0:1])
            n1[here] = normed
            i1[here] = jnp.broadcast_to(inv_std, (128, 128))
            rounded = (normed * g_ref[0:1] + s_ref[1:2]).astype(bf16)
            low[here] = rounded
            lowt[:, here] = rounded.T
            ctxt[1, :, here] = ctx_p[here].T
        for a, b in ((p_out, p_out_any), (n1, n1_any), (i1, i1_any), (lowt, lowt_any), (xt, xt_any), (ctxt, ctxt_any)):
            run.here(a, b)

    def inner(side, n):
        w, b = ((w_in, b_in_ref), (p_in, b_in_p))[side]
        if side == 1 and n == 0:
            arrive(*b_copies)
        for at in range(n * unit_chunk, (n + 1) * unit_chunk, 256):
            cols = slice(at, at + 256)
            bias = bias_of(b, at)
            for top in range(0, rows, 128):
                here = slice(top, top + 128)
                rounded, slopes = gelu_parts(mm(low[here], w[:, cols]) + bias)
                act[side, here, cols] = rounded
                actt[side, cols, here] = rounded.T
                slope[side, here, cols] = slopes.astype(bf16)
        if side == 1 and n == N_CHUNK - 1:
            for a, b in ((actt, actt_any), (slope, slope_any), (p_in, p_in_any)):
                run.here(a, b)

    def branch(side, n):
        w = (w_back, p_back)[side]
        cols = slice(n * unit_chunk, (n + 1) * unit_chunk)
        for top in range(0, rows, 128):
            here = slice(top, top + 128)
            value = mm(act[side, here, cols], w[cols])
            part[here] = value if (side, n) == (0, 0) else part[here] + value

    def second_norm():
        last = slice((N_CHUNK - 1) * unit_chunk, units)
        for at in range(0, rows, 64):
            here = slice(at, at + 64)
            value = mm(act[1, here, last], p_back[last]) + part[here] + s_ref[2:3]
            normed, inv_std = norm_rows(n1[here] * g_ref[0:1] + s_ref[1:2] + value)
            n2[here] = normed
            i2[here] = jnp.broadcast_to(inv_std, (64, 128))
            own_out[here] = (normed * g_ref[1:2] + s_ref[3:4]).astype(bf16)
        for a, b in ((n2, n2_any), (i2, i2_any), (p_back, p_back_any), (own_out, block_out)):
            run.here(a, b)

    far_tokens()
    step(1, 0)
    project(own_base, q, k, v)
    step(0, 1)
    pair_hop(0)
    own_tokens()
    step(2, 0)
    ahead_out()
    turn()
    own_out_part()
    step(1, 1)
    step(3, 0)
    step(0, 2)
    step(4, 0)
    step(2, 1)
    ahead_norm()
    step(1, 2)
    pair_hop(1)
    send_context(0)
    step(3, 1)
    step(0, 3)
    step(5, 0)
    step(4, 1)
    ahead_units()
    step(6, 0)
    step(0, 4)
    step(2, 2)
    step(3, 2)
    step(5, 1)
    send_context(3)
    step(1, 3)
    ahead_last()
    step(1, 4)
    send_context(2)
    step(4, 2)
    step(6, 1)
    send_context(1)
    step(2, 3)
    gather(0)
    step(2, 4)
    step(7, 0)
    step(3, 3)
    step(5, 2)
    step(3, 4)
    step(6, 2)
    first_norm()
    pair_hop(2)
    inner(0, 0)
    step(8, 0)
    step(4, 3)
    inner(0, 1)
    inner(0, 2)
    step(4, 4)
    gather(1)
    branch(0, 0)
    branch(0, 1)
    branch(0, 2)
    step(5, 3)
    step(7, 1)
    inner(1, 0)
    inner(1, 1)
    step(5, 4)
    step(6, 3)
    inner(1, 2)
    branch(1, 0)
    gather(2)
    branch(1, 1)
    step(6, 4)
    step(8, 1)
    second_norm()
    arrive(*pair_hops[3])
    arrive(*flight["gather"])
    loads[5].wait()

    @pl.loop(0, 32)
    def _(at):
        slot = (at // 8, (at // 4) % 2, (at // 2) % 2, at % 2)
        values = gathered[slot].astype(f32)
        here = pl.ds(pl.multiple_of(at * 8, 8), 8)
        all_ref[here, :half] = values[:8]
        all_ref[here, half:width] = values[8:]
        all_ref[here, width:] = ids[slot]

    loss_passes(
        dp * 2 + mp, scale_ref[0], w_pool_ref, s_ref[4:5],
        loss_ref, gscale_ref, pre_ref, bias_grad_ref, first_grad_ref, firsts_out_ref,
        all_ref, pooled_ref, len_ref, unit_ref, lse_col_ref, lse_row_ref, pre_f_ref,
    )
    new_scale_ref[0] = scale_ref[0] - step_rate * gscale_ref[0]
    per = width // 16
    own_firsts = mm(firsts_out_ref[...], pick(width, dp * per, per).astype(bf16)).astype(bf16)
    pool_ref[...] = mm_tn(own_firsts, pre_ref[...])
    pool_bias_ref[...] = exact(bias_grad_ref[...], pick(width, dp * per, per))
    for a, b in ((first_grad_ref, first_any), (pool_ref, pool_any), (pool_bias_ref, pool_bias_any)):
        run.here(a, b)
    arrive(*hops[7][1], *hops[8][1])
    for copy in run.sent[-run.ring:]:
        copy.wait_send()
    for copy in run.kept[len(loads):]:
        copy.wait()


def forward(x, segr, w_qkv, b_qv, b_in, gains, shifts, w_pool, scale, pairs, w_out, w_in, w_back):
    rows, width = x.shape[0] // 2, x.shape[1]
    cols, units = w_qkv.shape[2], w_in.shape[1]
    count = 2 * lax.axis_size("dp") * 8
    any_ = pl.BlockSpec(memory_space=pl.ANY)
    smem = pl.BlockSpec(memory_space=pltpu.SMEM)
    vmem = pl.BlockSpec(memory_space=pltpu.VMEM)
    S = jax.ShapeDtypeStruct
    head = (rows, cols)
    kept = [
        ((rows, width), bf16), (w_qkv.shape, bf16), (w_out.shape, bf16), (w_in.shape, bf16), (w_back.shape, bf16),
        (head, bf16), (head, bf16), (head, bf16),
        ((rows, width), f32), ((rows, 128), f32), ((width, rows), bf16), ((width, rows), bf16), ((2, cols, rows), bf16),
        ((2, units, rows), bf16), ((2, rows, units), bf16), ((rows, width), f32), ((rows, 128), f32),
    ]
    scratch = [
        ((8, width), f32), ((width // 16, width), f32), ((1, width // 16), f32),
        (x.shape, bf16), (w_pool.shape, bf16), (w_qkv.shape, bf16),
        (w_out.shape, bf16), (w_in.shape, bf16), (w_back.shape, bf16),
        (w_out.shape, bf16), (w_in.shape, bf16), (w_back.shape, bf16), (b_in.shape, f32),
    ] + [(head, bf16)] * 9 + [
        ((rows, width), f32), ((rows, 128), f32), ((rows, width), bf16),
        ((2, rows, units), bf16), ((2, rows, units), bf16), ((rows, width), f32), ((rows, width), f32),
        ((rows, 128), f32), ((rows, width), bf16),
        ((width, rows), bf16), ((width, rows), bf16), ((2, cols, rows), bf16), ((2, units, rows), bf16),
        ((4, 16, width), f32), ((2, 8, width), f32), ((4, 2, 2, 2, 16, width // 2), bf16), ((4, 2, 2, 2, 8, 128), f32),
        ((count, width), bf16), ((1, width), f32), ((count, width), bf16),
        ((count, width + 128), f32), ((count, width), f32), ((count, 1), f32), ((count, width), bf16),
        ((count, 1), f32), ((1, count), f32), ((count, width), f32),
    ]
    return pl.pallas_call(
        forward_kernel,
        in_specs=[vmem] * 5 + [smem] * 2 + [any_] * 6,
        out_specs=[any_] * len(kept) + [smem] * 3 + [any_] * 4,
        out_shape=tuple(S(*k) for k in kept) + (
            S((1,), f32), S((1,), f32), S((1,), f32), S((8, width), f32), S(b_qv.shape, f32),
            S((width // 16, width), f32), S((1, width // 16), f32),
        ),
        scratch_shapes=[pltpu.VMEM(*s) for s in scratch] + [
            pltpu.SemaphoreType.DMA((48,)), pltpu.SemaphoreType.DMA((90,)), pltpu.SemaphoreType.DMA((26,)),
        ],
        compiler_params=pltpu.CompilerParams(
            vmem_limit_bytes=56 * 1024 * 1024, collective_id=0, has_side_effects=True
        ),
        name="forward",
    )(segr, b_qv, b_in, gains, shifts, scale, pairs, x, w_pool, w_qkv, w_out, w_in, w_back)


def pick(size, start, count):
    return (
        lax.broadcasted_iota(jnp.int32, (size, count), 0)
        == start + lax.broadcasted_iota(jnp.int32, (size, count), 1)
    ).astype(f32)


def exact(a, b):
    return jnp.dot(a, b, preferred_element_type=f32, precision=lax.Precision.HIGHEST)


ORDERS = (
    ("z", "x", "y", "w"), ("y", "x", "q"), ("y", "z", "w", "x"),
    ("z", "x", "y", "w"), ("z", "x", "w", "y"), ("y", "z", "x", "w"),
    ("y", "z", "x", "w"), ("x", "z", "y", "w"), ("y", "x", "z", "w"),
    ("y", "z", "x", "w"), ("x", "y", "z", "w"), ("y", "x", "q"),
)
TILE = 384
PARTS = 4


def backward_kernel(
    segr_ref, g_ref, first_grad_ref, b_qv_ref,
    out_any, x_any, og_any, n2_any, i2_any, n1_any, i1_any, act_any, slope_any, low_any, xt_any, ctx_any, q_any, k_any, v_any,
    wb_o_any, wb_p_any, wi_o_any, wi_p_any, wo_o_any, wo_p_any, wq_o_any, wq_p_any,
    grad_in_any, out_other, o_back, o_in, o_qkv, o_out, a_gains, a_shifts, a_bqv, a_bin,
    o_gains, o_shifts, o_bqv, o_bin, one_buf, two_buf, three_buf, grad, i2, n1, i1, act, slope, low, xt, ctx, q, k, v, wb, wi, wo, wq, deltas,
    unit, got, ready, sums, sums_got,
    send_sem, recv_sem, local_sem,
):
    dp, mp = lax.axis_index("dp"), lax.axis_index("mp")
    rows, width = one_buf.shape
    units = slope.shape[2]
    cols = q.shape[2]
    per = width // 16
    own_base = pl.multiple_of(mp * rows, rows)
    near = {
        "x": {"mp": 1 - mp}, "y": {"dp": flip(dp, 2)}, "z": {"dp": flip(dp, 4)}, "w": {"dp": flip(dp, 8)},
        "c": {"dp": flip(dp, 1)},
    }
    quad = (near["z"], near["w"], {"dp": flip(flip(dp, 4), 8)})
    run = Copies(send_sem, recv_sem, local_sem)
    own_rows = lambda ref: ref.at[pl.ds(own_base, rows)]
    pending, results = {}, []

    def load(*pairs):
        for source, target, name in pairs:
            pending.setdefault(name, []).append(run.here(source, target))

    def need(*names):
        for name in names:
            for copy in pending.pop(name, ()):
                copy.wait()

    load((own_rows(og_any), one_buf, "two"), (n2_any, grad, "two"), (i2_any, i2, "two"))
    load((act_any, act, "act"), (wb_o_any, wb.at[0], "wb"), (wb_p_any, wb.at[1], "wb"), (slope_any, slope, "slope"))

    greet(list(near.values()) + [quad[2]])
    flight = {}
    bits = {"y": 2, "z": 4, "w": 8}

    def rel(name, side, dest):
        return side if name == "x" else (dest // bits[name] + dp // bits[name]) % 2

    def put(at, side, dest, value):
        spot, left = 0, 16
        for name in ORDERS[at]:
            left = left // (4 if name == "q" else 2)
            spot = spot + left * (2 * rel("w", side, dest) + rel("z", side, dest) if name == "q" else rel(name, side, dest))
        unit[at, (dest + dp) % 2, spot] = value.astype(bf16)

    def shape_of(at, stage):
        start, left = 0, 32
        for name in ("c",) + ORDERS[at][:stage]:
            held = left
            left = held // (4 if name == "q" else 2)
            begins, start = start, start + held - left
        return held, left, begins

    def begin(at):
        flight[at, 0] = [run.remote(unit.at[at, 1], got.at[at, pl.ds(0, 16)], near["c"])]

    def step(at, stage):
        arrive(*flight[at, stage - 1])
        held, count, begins = shape_of(at, stage - 1)
        mine = unit.at[at, 0]

        def added(n):
            if held == 2 * count:
                return mine[n] + got[at, begins + n]
            total = mine[n].astype(f32)
            for part in range(3):
                total = total + got[at, begins + part * count + n].astype(f32)
            return total.astype(bf16)

        if count == 1:
            total = mine[0].astype(f32)
            for part in range(held - 1):
                total = total + got[at, begins + part].astype(f32)
            ready[at] = total
            if at < 4:
                target = o_back.at[pl.ds(at % 2 * per, per), pl.ds(at // 2 * TILE, TILE)]
            elif at < 8:
                target = o_in.at[:, pl.ds((at - 4) * TILE, TILE)]
            elif at < 11:
                target = o_qkv.at[at - 8]
            else:
                results.append(run.here(ready.at[at, pl.ds(0, per // 2)], o_out.at[:, pl.ds(0, cols)]))
                results.append(run.here(ready.at[at, pl.ds(per // 2, per // 2)], o_out.at[:, pl.ds(cols, cols)]))
                return
            results.append(run.here(ready.at[at], target))
            return
        _, after, begins_next = shape_of(at, stage)
        for n in range(after, count):
            mine[n] = added(n)
        name = ORDERS[at][stage - 1]
        devices = quad if name == "q" else (near[name],)
        flight[at, stage] = [
            run.remote(
                mine.at[pl.ds((part + 1) * after, after)], got.at[at, pl.ds(begins_next + part * after, after)], device
            )
            for part, device in enumerate(devices)
        ]
        for n in range(after):
            mine[n] = added(n)

    def sum_step(stage):
        if stage:
            flight["sums", stage - 1].wait_recv()
            sums[stage] = sums[stage - 1] + sums_got[stage - 1]
        if stage < 5:
            name = ("c", "x", "y", "z", "w")[stage]
            flight["sums", stage] = run.remote(sums.at[stage], sums_got.at[stage], near[name])

    def norm_grads(source, extra, normed_ref, inv_ref, gain, low_ref, places):
        gain_sum, shift_sum, low_sum = 0.0, 0.0, 0.0
        for at in range(0, rows, 64):
            here = slice(at, at + 64)
            value = source[here].astype(f32)
            if extra is not None:
                is_first = lax.broadcasted_iota(jnp.int32, (64, width), 0) == 0
                value = value + jnp.where(is_first, extra[at // 64:at // 64 + 1], 0.0)
            normed = normed_ref[here]
            out = norm_back(value, normed, inv_ref[here, 0:1], gain)
            rounded = out.astype(bf16)
            grad[here] = out
            low_ref[here] = rounded
            gain_sum += jnp.sum(value * normed, axis=0, keepdims=True)
            shift_sum += jnp.sum(value, axis=0, keepdims=True)
            low_sum += jnp.sum(rounded.astype(f32), axis=0, keepdims=True)
        for place, value in zip(places, (gain_sum, shift_sum, low_sum)):
            sums[0, place:place + 1] = value

    def second_norm():
        need("two")
        sums[0] = jnp.zeros(sums.shape[1:], f32)
        norm_grads(one_buf, first_grad_ref, grad, i2, g_ref[1:2], two_buf, (1, 5, 4))
        load((wi_o_any, wi.at[0], "wi"), (wi_p_any, wi.at[1], "wi"), (low_any, low, "low"))
        load((n1_any, n1, "one"), (i1_any, i1, "one"))

    def back_weight(half):
        need("act")
        for side in range(2):
            for top in range(0, units, TILE):
                tile = mm(act[side, top:top + TILE], two_buf[:, half * cols:(half + 1) * cols])
                for at in range(0, TILE, per):
                    put(2 * half + at // per % 2, side, (top + at) // (2 * per), tile[at:at + per])

    def inner_grads(side):
        need("wb", "slope")
        owner = mp + side - 2 * mp * side
        for at in range(0, units, 256):
            here = slice(at, at + 256)
            value = (mm_nt(two_buf[...], wb[side, here]) * slope[side, :, here].astype(f32)).astype(bf16)
            slope[side, :, here] = value
            sums[0, pl.ds(8 + 2 * owner + at // width, 1), at % width:at % width + 256] = jnp.sum(
                value.astype(f32), axis=0, keepdims=True
            )
        if side == 0:
            load((ctx_any, ctx, "ctx"), (wo_o_any, wo.at[0], "wo"), (wo_p_any, wo.at[1], "wo"))
            load((own_rows(x_any), three_buf, "x"))
            flight["wq"] = []
            for quarter in (dp % 2, dp % 2 + 2):
                some = pl.ds(pl.multiple_of(quarter * (width // 4), 16), width // 4)
                flight["wq"].append(run.remote(wq_p_any.at[:, some], wq.at[1, :, some], near["c"]))
                load((wq_p_any.at[:, some], wq.at[1, :, some], "wq_p"))

    def feed_back():
        need("wi")
        for at in range(0, width, 256):
            here = slice(at, at + 256)
            grad[:, here] = grad[:, here] + mm_nt(slope[0], wi[0, here]) + mm_nt(slope[1], wi[1, here])
        load((q_any, q.at[0], "qkv"), (k_any, k.at[0], "qkv"), (v_any, v.at[0], "qkv"))
        load((xt_any, xt, "xt"), (wq_o_any, wq.at[0], "wq_o"))

    def first_norm_back():
        need("one")
        norm_grads(grad, None, n1, i1, g_ref[0:1], one_buf, (0, 3, 2))

    def in_weight(half):
        need("low")
        for at in range(2 * half, 2 * half + 2):
            for side in range(2):
                for top in range(0, width, TILE):
                    tile = mm(low[top:top + TILE], slope[side, :, at * TILE:(at + 1) * TILE])
                    for row in range(0, TILE, per):
                        put(4 + at, side, (top + row) // per, tile[row:row + per])

    def out_weight():
        need("ctx")
        for side in range(2):
            tile = mm(ctx[side], one_buf[...])
            for dest in range(16):
                part = tile[dest * per // 2:(dest + 1) * per // 2]
                put(11, side, dest, jnp.concatenate([part[:, :cols], part[:, cols:]], axis=0))

    def context_grads():
        need("wo")
        for side in range(2):
            two_buf[:, side * cols:(side + 1) * cols] = mm_nt(one_buf[...], wo[side]).astype(bf16)

    def again():
        need("x", "wq_p")
        arrive(*flight["wq"])
        q[1] = (mm(three_buf[...], wq[1, 0]) + b_qv_ref[0:1]).astype(bf16)
        k[1] = mm(three_buf[...], wq[1, 1]).astype(bf16)
        v[1] = (mm(three_buf[...], wq[1, 2]) + b_qv_ref[1:2]).astype(bf16)

    def attend_back(side, groups):
        need("qkv")
        scale = HEAD_DIM ** (-0.5)
        for group in groups:
            at = slice(group * GROUP, (group + 1) * GROUP)
            one = same_block(segr_ref[:, pl.ds(pl.multiple_of(own_base + group * GROUP, GROUP), GROUP)])
            same = jnp.concatenate([one, one], axis=1)
            for pair in range(cols // PAIR):
                lanes = slice(pair * PAIR, (pair + 1) * PAIR)
                q_two = two_heads(q[side, at, lanes])
                dc_two = two_heads(two_buf[at, side * cols + pair * PAIR:side * cols + (pair + 1) * PAIR])
                k_pair, v_pair = k[side, at, lanes], v[side, at, lanes]
                scores = jnp.where(same, mm_nt(k_pair, q_two) * scale, masked_out)
                shifted = jnp.exp(scores - jnp.max(scores, axis=0, keepdims=True))
                probs = shifted / jnp.sum(shifted, axis=0, keepdims=True)
                prob_grad = mm_nt(v_pair, dc_two)
                score_grad = (
                    probs * (prob_grad - jnp.sum(prob_grad * probs, axis=0, keepdims=True))
                ).astype(bf16)
                deltas[side, 0, at, lanes] = (join_heads(mm_tn(score_grad, k_pair)) * scale).astype(bf16)
                deltas[side, 1, at, lanes] = (mm(score_grad, q_two) * scale).astype(bf16)
                deltas[side, 2, at, lanes] = mm(probs.astype(bf16), dc_two).astype(bf16)

    def qkv_weight(s):
        need("xt")
        for side in range(2):
            for top in range(0, width, TILE):
                tile = mm(xt[top:top + TILE], deltas[side, s])
                for at in range(0, TILE, per):
                    put(8 + s, side, (top + at) // per, tile[at:at + per])
            if s != 1:
                owner = mp + side - 2 * mp * side
                lanes = pl.ds(pl.multiple_of(owner * cols, 128), cols)
                sums[0, 6 + s // 2:7 + s // 2, lanes] = jnp.sum(deltas[side, s].astype(f32), axis=0, keepdims=True)

    def input_grads():
        need("wq_o", "wq_p")
        for at in range(0, width, 256):
            here = slice(at, at + 256)
            value = grad[:, here]
            for side in range(2):
                for s in range(3):
                    value = value + mm_nt(deltas[side, s], wq[side, s, here])
            three_buf[:, here] = value.astype(bf16)
        results.append(run.here(three_buf, own_rows(grad_in_any)))

    share = rows // PARTS

    def send_out(part):
        some = pl.ds(part * share, share)
        flight["out", part] = run.remote(out_any.at[some], out_other.at[some], near["x"])

    def send_inputs(part):
        some = pl.ds(pl.multiple_of(own_base + part * share, share), share)
        flight["inputs", part] = run.remote(
            three_buf.at[pl.ds(part * share, share)], grad_in_any.at[some], near["x"]
        )

    send_out(0)
    second_norm()
    back_weight(0)
    begin(0)
    begin(1)
    send_out(1)
    inner_grads(1)
    step(0, 1)
    back_weight(1)
    begin(2)
    begin(3)
    send_out(2)
    step(1, 1)
    inner_grads(0)
    in_weight(0)
    begin(4)
    begin(5)
    step(2, 1)
    send_out(3)
    step(3, 1)
    feed_back()
    step(5, 1)
    step(4, 1)
    step(0, 2)
    again()
    step(1, 2)
    first_norm_back()
    context_grads()
    in_weight(1)
    begin(6)
    begin(7)
    step(3, 2)
    step(0, 3)
    attend_back(1, (0, 1))
    step(2, 2)
    step(6, 1)
    attend_back(1, (2, 3))
    step(7, 1)
    step(1, 3)
    step(4, 2)
    attend_back(0, (2, 3))
    step(5, 2)
    step(3, 3)
    attend_back(0, (0, 1))
    step(2, 3)
    step(0, 4)
    qkv_weight(0)
    begin(8)
    qkv_weight(2)
    begin(10)
    sum_step(0)
    step(1, 4)
    qkv_weight(1)
    begin(9)
    step(8, 1)
    out_weight()
    begin(11)
    sum_step(1)
    step(7, 2)
    step(5, 3)
    step(10, 1)
    step(6, 2)
    step(9, 1)
    input_grads()
    sum_step(2)
    step(11, 1)
    step(4, 3)
    step(3, 4)
    step(2, 4)
    step(5, 4)
    step(0, 5)
    step(7, 3)
    step(8, 2)
    step(6, 3)
    step(10, 2)
    step(2, 5)
    send_inputs(0)
    step(4, 4)
    step(9, 2)
    sum_step(3)
    step(8, 3)
    step(3, 5)
    step(6, 4)
    step(5, 5)
    send_inputs(1)
    step(9, 3)
    sum_step(4)
    step(11, 2)
    step(8, 4)
    step(7, 4)
    step(6, 5)
    step(10, 3)
    send_inputs(2)
    step(9, 4)
    sum_step(5)
    total = sums[5]
    vectors = exact(total[0:8], pick(width, dp * per, per))
    o_gains[...] = vectors[0:2]
    o_shifts[...] = vectors[2:6]
    o_bqv[...] = exact(total[0:8], pick(width, mp * cols + dp * (per // 2), per // 2))[6:8]
    few = units // 16
    o_bin[...] = exact(sums[5, pl.ds(8 + 2 * mp + dp // 8, 1), :], pick(width, (dp % 8) * few, few))
    for source, target in ((o_gains, a_gains), (o_shifts, a_shifts), (o_bqv, a_bqv), (o_bin, a_bin)):
        results.append(run.here(source, target))
    step(8, 5)
    step(4, 5)
    step(11, 3)
    step(7, 5)
    send_inputs(3)
    step(10, 4)
    step(9, 5)
    step(11, 4)
    step(10, 5)
    for part in range(PARTS):
        arrive(flight["out", part], flight["inputs", part])
    for copy in run.sent[-run.ring:]:
        copy.wait_send()
    for copy in results:
        copy.wait()


def backward(segr, gains, first_grad, b_qv, *arrays):
    rows, width = arrays[3].shape
    units = arrays[8].shape[2]
    cols = arrays[12].shape[1]
    any_ = pl.BlockSpec(memory_space=pl.ANY)
    vmem = pl.BlockSpec(memory_space=pltpu.VMEM)
    S = jax.ShapeDtypeStruct
    per = width // 16
    count = len(ORDERS)
    small = [((2, per), f32), ((4, per), f32), ((2, cols // 16), f32), ((1, units // 16), f32)]
    scratch = small + [((rows, width), bf16)] * 3 + [
        ((rows, width), f32), ((rows, 128), f32), ((rows, width), f32), ((rows, 128), f32),
        ((2, units, rows), bf16), ((2, rows, units), bf16), ((width, rows), bf16), ((width, rows), bf16),
        ((2, cols, rows), bf16), ((2, rows, cols), bf16), ((2, rows, cols), bf16), ((2, rows, cols), bf16),
        ((2, units, width), bf16), ((2, width, units), bf16), ((2, cols, width), bf16), ((2, 3, width, cols), bf16),
        ((2, 3, rows, cols), bf16), ((count, 2, 16, per, TILE), bf16),
        ((count, 31, per, TILE), bf16), ((count, per, TILE), f32), ((6, 16, width), f32), ((5, 16, width), f32),
    ]
    return pl.pallas_call(
        backward_kernel,
        in_specs=[vmem] * 4 + [any_] * len(arrays),
        out_specs=[any_] * 10,
        out_shape=(
            S((2 * rows, width), bf16), S((rows, width), bf16), S((2 * per, width), f32), S((per, 2 * width), f32),
            S((3, per, cols), f32),
            S((cols // 16, width), f32), S((2, per), f32), S((4, per), f32), S((2, cols // 16), f32),
            S((1, units // 16), f32),
        ),
        scratch_shapes=[pltpu.VMEM(*s) for s in scratch] + [
            pltpu.SemaphoreType.DMA((24,)), pltpu.SemaphoreType.DMA((78,)), pltpu.SemaphoreType.DMA((44,)),
        ],
        compiler_params=pltpu.CompilerParams(
            vmem_limit_bytes=63 * 1024 * 1024, collective_id=1, has_side_effects=True
        ),
        name="backward",
    )(segr, gains, first_grad, b_qv, *arrays)


FINISH_PARTS = 4


def finish_kernel(*refs):
    grads_any, outs_any, others_any = refs[:3]
    count = (len(refs) - 8) // 3
    sources = refs[3:3 + count]
    wide_any, outs_to = refs[3 + count:5 + count]
    targets = refs[5 + count:5 + 2 * count]
    grads, wide, outs = refs[5 + 2 * count:8 + 2 * count]
    held = refs[8 + 2 * count:-2]
    load_sem, store_sem = refs[-2:]
    part = grads.shape[0] // FINISH_PARTS
    other = 1 - lax.axis_index("mp")
    loads, stores = [], []

    def copy(into, source, target, sem):
        into.append(pltpu.make_async_copy(source, target, sem.at[len(into)]))
        into[-1].start()

    def rows(ref, at):
        return ref.at[pl.ds(pl.multiple_of(at * part, part), part)]

    for at in range(FINISH_PARTS):
        copy(loads, rows(grads_any, at), rows(grads, at), load_sem)
    places = [2 * (1 - other), 2 * (1 - other) + 1, 2 * other, 2 * other + 1]
    for n, at in enumerate(places):
        copy(loads, rows((outs_any, others_any)[n // 2], n % 2), rows(outs, at), load_sem)
    for source, target in zip(sources, held):
        copy(loads, source, target, load_sem)
    for at in range(FINISH_PARTS):
        loads[at].wait()
        here = slice(at * part, (at + 1) * part)
        wide[here] = grads[here].astype(f32)
        copy(stores, rows(wide, at), rows(wide_any, at), store_sem)
    for n, at in enumerate(places):
        loads[FINISH_PARTS + n].wait()
        copy(stores, rows(outs, at), rows(outs_to, at), store_sem)
    for n in range(count):
        loads[2 * FINISH_PARTS + n].wait()
        copy(stores, held[n], targets[n], store_sem)
    for store in stores:
        store.wait()


def finish(grad_inputs, own_out, other_out, *arrays):
    any_ = pl.BlockSpec(memory_space=pl.ANY)
    results = (jax.ShapeDtypeStruct(grad_inputs.shape, f32), jax.ShapeDtypeStruct(grad_inputs.shape, bf16)) + tuple(
        jax.ShapeDtypeStruct(a.shape, a.dtype) for a in arrays
    )
    copies = 2 * FINISH_PARTS + len(arrays)
    return pl.pallas_call(
        finish_kernel,
        in_specs=[any_] * (3 + len(arrays)),
        out_specs=[any_] * len(results),
        out_shape=results,
        scratch_shapes=[
            pltpu.VMEM(grad_inputs.shape, bf16), pltpu.VMEM(grad_inputs.shape, f32), pltpu.VMEM(grad_inputs.shape, bf16),
        ] + [pltpu.VMEM(a.shape, a.dtype) for a in arrays] + [
            pltpu.SemaphoreType.DMA((copies,)), pltpu.SemaphoreType.DMA((copies,)),
        ],
        compiler_params=params(60),
        name="finish",
    )(grad_inputs, own_out, other_out, *arrays)


def swap_mp(values):
    return lax.ppermute(values, "mp", [(0, 1), (1, 0)])


def swap_dp(values, bit):
    size = lax.axis_size("dp")
    return lax.ppermute(values, "dp", [(at, at ^ bit) for at in range(size)])


def fetch(own, axis, place):
    size = own.shape[axis] // 4
    first = swap_mp(lax.dynamic_slice_in_dim(own, place * size, size, axis))
    second = swap_dp(first, 2)
    third = swap_dp(first, 1)
    fourth = swap_dp(second, 1)
    whole = jnp.zeros_like(own)
    for bits, part in ((0, first), (2, second), (1, third), (3, fourth)):
        whole = lax.dynamic_update_slice_in_dim(whole, part, (place ^ bits) * size, axis)
    return whole


def gather_rows(rows):
    size = lax.axis_size("dp")
    if size != 16:
        return lax.all_gather(rows, ("dp", "mp"), axis=0, tiled=True)
    rows = jnp.concatenate([rows, swap_mp(rows)], axis=0)
    for bit in (1, 2, 4, 8):
        rows = jnp.concatenate([rows, swap_dp(rows, bit)], axis=0)
    return rows


def both_halves(own, mp):
    other = swap_mp(own)
    return jnp.concatenate([jnp.where(mp == 0, own, other), jnp.where(mp == 0, other, own)], axis=0)


def add(a, b):
    return (a.astype(f32) + b.astype(f32)).astype(a.dtype)


def scatter_sum(keep, send, order):
    size = lax.axis_size("dp")
    if size != 16:
        rest = keep.shape[2:]
        both = jnp.stack([keep, send], axis=2)
        both = both.reshape((2, 16) + rest)
        mine = add(both[0], swap_mp(both[1]))
        return mine
    got = swap_dp(send, 1)
    rest = keep.shape[2:]
    names = ["x", "z1", "z0", "y"]
    keep = keep.reshape((2, 2, 2, 2) + rest)
    got = got.reshape((2, 2, 2, 2) + rest)
    bit_of = {"y": 2, "z0": 4, "z1": 8}
    for name in order:
        axis = names.index(name)
        names.remove(name)
        pick = lambda values, at: lax.index_in_dim(values, at, axis, keepdims=False)
        out = add(pick(keep, 1), pick(got, 1))
        out = swap_mp(out) if name == "x" else swap_dp(out, bit_of[name])
        keep = add(pick(keep, 0), pick(got, 0))
        got = out
    return add(keep, got)


def swap_order(values, axis, place):
    shape = values.shape
    split = values.reshape(shape[:axis] + (2, 2, 2, 2) + shape[axis + 1:])
    for at, bit in enumerate((8, 4, 2, 1)):
        low = lax.index_in_dim(split, 0, axis + at)
        high = lax.index_in_dim(split, 1, axis + at)
        flipped = jnp.concatenate([high, low], axis=axis + at)
        split = jnp.where((place & bit) != 0, flipped, split)
    return split.reshape(shape)


def shards(
    inputs, segment_ids, pair_index, w_qkv, bias_qv, w_out, w_in, bias_in, w_back,
    w_pool, norm_gains, shifts, logit_scale, out_grad,
):
    tok_rows, width = inputs.shape
    size = lax.axis_size("dp")
    dp, mp = lax.axis_index("dp"), lax.axis_index("mp")
    rows = tok_rows // 2
    blocks = rows // SEG_LEN
    place = dp % 4
    slots = 0 * dp
    pos = jnp.reshape(slots, (1,)).astype(jnp.int32)

    x = lax.dynamic_slice_in_dim(inputs, mp * rows, rows, 0)
    cot = lax.dynamic_slice_in_dim(out_grad, mp * rows, rows, 0)
    seg = lax.dynamic_slice_in_dim(segment_ids, mp * rows, rows, 0)
    segc, segr = seg.reshape(rows, 1), seg.reshape(1, rows)
    pairs = lax.dynamic_slice_in_dim(pair_index, mp * blocks, blocks, 0)

    cols = w_qkv.shape[2]
    units = w_in.shape[1]
    if size == 16:
        segr = segment_ids.reshape(1, -1)
        (
            own_out, w_qkv_p, w_out_p, w_in_p, w_back_p, q, k, v, n1, i1, lowt, xt, ctxt, actt, slope, n2, i2,
            loss_value, grad_scale, new_scale, first_grad, bias_qv_p, grad_pool, pool_bias,
        ) = forward(
            inputs, segr, w_qkv, bias_qv, bias_in.reshape(-1, 128),
            norm_gains, shifts, w_pool, logit_scale, pair_index, w_out, w_in, w_back,
        )
        results = backward(
            segr, norm_gains, first_grad, bias_qv_p, own_out,
            inputs, out_grad, n2, i2, n1, i1, actt, slope, lowt, xt, ctxt, q, k, v,
            w_back, w_back_p, w_in, w_in_p, w_out, w_out_p, w_qkv, w_qkv_p,
        )
        (
            grad_inputs, block_out, grad_back, grad_in, grad_qkv, grad_out, gains, shift_grads, grad_bias_qv,
            grad_bias_in, grad_pool, pool_bias,
        ) = finish(results[0], own_out, results[1], *results[2:], grad_pool, pool_bias)
        return (
            block_out, loss_value, grad_inputs, grad_qkv, grad_bias_qv, grad_out, grad_in,
            grad_bias_in[0], grad_back, grad_pool, gains, shift_grads, pool_bias[0], grad_scale, new_scale,
        )

    biases = swap_mp(bias_qv)
    bias_qv_p, bias_in_p = biases, swap_mp(bias_in)
    w_qkv_p = fetch(w_qkv, 1, place)
    w_out_p = fetch(w_out, 0, place)
    w_in_p = fetch(w_in, 0, place)
    w_back_p = fetch(w_back, 0, place)

    q_o, k_o, v_o, ctx_o = attention_half(x, w_qkv, bias_qv, segc, segr)
    q_p, k_p, v_p, ctx_p = attention_half(x, w_qkv_p, bias_qv_p, segc, segr)
    normed_one, inv_one, low_one = first_norm(ctx_o, ctx_p, w_out, w_out_p, x, norm_gains, shifts)
    act_o, slope_o = inner_half(low_one, w_in, bias_in.reshape(1, -1))
    part = branch_half(act_o, w_back)
    act_p, slope_p = inner_half(low_one, w_in_p, bias_in_p.reshape(1, -1))
    normed_two, inv_two, own_out = second_norm(act_p, w_back_p, part, normed_one, norm_gains, shifts)

    firsts = own_out.reshape(blocks, SEG_LEN, width)[:, 0]
    ids = jnp.broadcast_to(pairs.astype(f32)[:, None], (blocks, 128))
    rel = jnp.concatenate([gather_rows(firsts).astype(f32), gather_rows(ids)], axis=1)
    linear = dp * 2 + mp
    position = jnp.stack([linear if size == 16 else 0 * linear, linear]).astype(jnp.int32)
    loss_value, grad_scale, pre_all, pool_bias, first_grad, firsts_all = pair_loss(
        position, rel, w_pool, shifts[4:5], logit_scale
    )
    block_out = both_halves(own_out, mp)
    pool_rows = width // size
    grad_pool = lax.dot_general(
        lax.dynamic_slice_in_dim(firsts_all, dp * pool_rows, pool_rows, 1), pre_all, TN, preferred_element_type=f32
    )
    grad_pool_bias = lax.dynamic_slice_in_dim(pool_bias[0], dp * pool_rows, pool_rows, 0)

    grad_two, branch, sums_two = second_back(cot, first_grad, normed_two, inv_two, norm_gains)
    keep_bo, send_bo = back_weight(pos, act_o, branch)
    keep_bp, send_bp = back_weight(pos, act_p, branch)
    keep_io, send_io, bias_io, part_one = inner_back(pos, branch, w_back, slope_o, low_one, w_in, grad_two)
    keep_ip, send_ip, bias_ip, part_two = inner_back(pos, branch, w_back_p, slope_p, low_one, w_in_p, part_one)
    grad_one, sums_one, dc_o, dc_p, keep_w, send_w = first_back(
        pos, part_two, normed_one, inv_one, norm_gains, ctx_o, ctx_p, w_out, w_out_p
    )
    keep_qo, send_qo, bias_qo, in_one = attention_back(pos, x, w_qkv, segc, segr, q_o, k_o, v_o, dc_o, grad_one)
    keep_qp, send_qp, bias_qp, in_two = attention_back(pos, x, w_qkv_p, segc, segr, q_p, k_p, v_p, dc_p, in_one)

    both = lambda a, b: jnp.stack([a, b])
    mine_back = scatter_sum(both(keep_bo, keep_bp), both(send_bo, send_bp), ("x", "y", "z0", "z1"))
    mine_in = scatter_sum(both(keep_io, keep_ip), both(send_io, send_ip), ("y", "x", "z0", "z1"))
    mine_out = scatter_sum(keep_w, send_w, ("x", "y", "z0", "z1"))
    mine_qkv = scatter_sum(both(keep_qo, keep_qp), both(send_qo, send_qp), ("y", "x", "z0", "z1"))

    vectors = jnp.concatenate([sums_one[0:1], sums_two[0:1], sums_one[2:3], sums_one[1:2], sums_two[2:3], sums_two[1:2]])
    by_dp = vectors.reshape(6, 16, width // 16).transpose(1, 0, 2).reshape(16, -1)
    by_dp = jnp.broadcast_to(by_dp[None], (2,) + by_dp.shape)
    bias_q = both(bias_qo, bias_qp).reshape(2, 2, 16, cols // 16).transpose(0, 2, 1, 3).reshape(2, 16, -1)
    bias_i = both(bias_io, bias_ip).reshape(2, 16, units // 16)
    packed = jnp.concatenate([by_dp, bias_q, bias_i], axis=2)
    packed = swap_order(packed, 1, slots).reshape(2, 8, 2, -1)
    mine_small = scatter_sum(packed[:, :, 0], packed[:, :, 1], ("y", "x", "z0", "z1"))

    if size != 16:
        fold = lambda values: lax.psum_scatter(values, "dp", scatter_dimension=0, tiled=True)
        grad_back = fold(mine_back.reshape(units, width).astype(f32))
        grad_in = fold(mine_in.reshape(width, units).astype(f32))
        grad_qkv = fold(mine_qkv.transpose(0, 2, 1, 3).reshape(width, 3, cols).astype(f32)).transpose(1, 0, 2)
        small = mine_small
        n_vec = 6 * (width // 16)
        n_q = 2 * (cols // 16)
        n_i = units // 16
        vec = small[:, :n_vec].reshape(16, 6, -1).transpose(0, 2, 1).reshape(width, 6)
        vec = fold(vec).T
        grad_bias_qv = fold(small[:, n_vec:n_vec + n_q].reshape(16, 2, -1).transpose(0, 2, 1).reshape(cols, 2)).T
        grad_bias_in = fold(small[:, n_vec + n_q:n_vec + n_q + n_i].reshape(units))
        grad_out = fold(mine_out.reshape(cols, width).astype(f32))
    else:
        grad_back = mine_back.astype(f32)
        grad_in = mine_in.astype(f32)
        grad_qkv = mine_qkv.astype(f32)
        small = mine_small
        n_vec = 6 * (width // 16)
        n_q = 2 * (cols // 16)
        n_i = units // 16
        vec = small[:n_vec].reshape(6, -1)
        grad_bias_qv = small[n_vec:n_vec + n_q].reshape(2, -1)
        grad_bias_in = small[n_vec + n_q:n_vec + n_q + n_i]
        grad_out = mine_out.astype(f32)

    grad_inputs = both_halves(in_two.astype(bf16), mp).astype(f32)
    new_scale = logit_scale - step_rate * grad_scale
    return (
        block_out, loss_value, grad_inputs, grad_qkv, grad_bias_qv, grad_out, grad_in, grad_bias_in,
        grad_back, grad_pool, vec[:2], vec[2:], grad_pool_bias, grad_scale, new_scale,
    )


def solution(mesh):
    return jax.shard_map(
        shards,
        mesh=mesh,
        in_specs=(
            P("dp", None), P("dp"), P("dp"), P(None, None, "mp"), P(None, "mp"), P("mp", None), P(None, "mp"),
            P("mp"), P("mp", None), P(), P(), P(), P(), P("dp", None),
        ),
        out_specs=(
            P("dp", None), P(), P("dp", None), P(None, "dp", "mp"), P(None, ("mp", "dp")), P(("mp", "dp"), None),
            P("dp", "mp"), P(("mp", "dp")), P(("mp", "dp"), None), P("dp", None), P(None, "dp"), P(None, "dp"),
            P("dp"), P(), P(),
        ),
        check_vma=False,
    )
```

```python
from functools import partial

import jax
import jax.numpy as jnp
from jax import lax
from jax.experimental import pallas as pl
from jax.experimental.pallas import tpu as pltpu
from jax.sharding import PartitionSpec as P

HEAD_DIM = 64
SEG_LEN = 64
PAIR = 2 * HEAD_DIM
GROUP = 128

epsilon = 1e-12
margin = 0.3
step_rate = 0.1
masked_out = -1e30
f32 = jnp.float32
bf16 = jnp.bfloat16

NT = (((1,), (1,)), ((), ()))
TN = (((0,), (0,)), ((), ()))


def mm(a, b):
    return jnp.dot(a, b, preferred_element_type=f32)


def mm_nt(a, b):
    return lax.dot_general(a, b, NT, preferred_element_type=f32)


def mm_tn(a, b):
    return lax.dot_general(a, b, TN, preferred_element_type=f32)


def params(mib=40):
    return pltpu.CompilerParams(vmem_limit_bytes=mib * 1024 * 1024)


def cost(flops, moved):
    return pl.CostEstimate(flops=int(flops), bytes_accessed=int(moved), transcendentals=0)


def lane_masks():
    lane = lax.broadcasted_iota(jnp.int32, (1, PAIR), 1)
    first = (lane < HEAD_DIM).astype(f32)
    return first, 1.0 - first


def two_heads(rows):
    first, second = lane_masks()
    return jnp.concatenate([rows * first.astype(bf16), rows * second.astype(bf16)], axis=0)


def join_heads(both):
    first, second = lane_masks()
    half = both.shape[0] // 2
    return both[:half] * first + both[half:] * second


def pair_probs(q_two, k_pair, same):
    scores = mm_nt(q_two, k_pair) * (HEAD_DIM ** (-0.5))
    scores = jnp.where(same, scores, masked_out)
    shifted = jnp.exp(scores - jnp.max(scores, axis=1, keepdims=True))
    return shifted / jnp.sum(shifted, axis=1, keepdims=True)


def same_segment(seg_col, seg_row, rows):
    own = seg_col[rows, :]
    other = seg_row[:, rows]
    one = own == other
    return jnp.concatenate([one, one], axis=0)


def attention_kernel(x_ref, w_ref, b_ref, segc_ref, segr_ref, q_ref, k_ref, v_ref, c_ref):
    x = x_ref[...]
    q_ref[...] = (mm(x, w_ref[0]) + b_ref[0:1]).astype(bf16)
    k_ref[...] = mm(x, w_ref[1]).astype(bf16)
    v_ref[...] = (mm(x, w_ref[2]) + b_ref[1:2]).astype(bf16)
    for group in range(x.shape[0] // GROUP):
        rows = slice(group * GROUP, (group + 1) * GROUP)
        same = same_segment(segc_ref, segr_ref, rows)
        for pair in range(q_ref.shape[1] // PAIR):
            cols = slice(pair * PAIR, (pair + 1) * PAIR)
            probs = pair_probs(two_heads(q_ref[rows, cols]), k_ref[rows, cols], same)
            c_ref[rows, cols] = join_heads(mm(probs.astype(bf16), v_ref[rows, cols])).astype(bf16)


def attention_half(x, w, b, segc, segr):
    rows, cols = x.shape[0], w.shape[2]
    out = jax.ShapeDtypeStruct((rows, cols), bf16)
    return pl.pallas_call(
        attention_kernel,
        out_shape=(out,) * 4,
        compiler_params=params(),
        cost_estimate=cost(2 * rows * 768 * cols * 3 * 2, 6 * rows * cols * 2),
        name="attention",
    )(x, w, b, segc, segr)


def norm_rows(values):
    row_mean = jnp.mean(values, axis=-1, keepdims=True)
    centred = values - row_mean
    inv_std = lax.rsqrt(jnp.mean(centred * centred, axis=-1, keepdims=True) + epsilon)
    return centred * inv_std, inv_std


def norm_back(grad, normed, inv_std, gain):
    scaled = grad * gain
    return inv_std * (
        scaled
        - jnp.mean(scaled, axis=-1, keepdims=True)
        - normed * jnp.mean(scaled * normed, axis=-1, keepdims=True)
    )


def first_norm_kernel(co_ref, cp_ref, wo_ref, wp_ref, x_ref, g_ref, s_ref, n_ref, inv_ref, low_ref):
    for at in range(0, x_ref.shape[0], 128):
        rows = slice(at, at + 128)
        attended = mm(co_ref[rows], wo_ref[...]) + mm(cp_ref[rows], wp_ref[...]) + s_ref[0:1]
        normed, inv_std = norm_rows(x_ref[rows].astype(f32) + attended)
        n_ref[rows] = normed
        inv_ref[rows] = inv_std
        low_ref[rows] = (normed * g_ref[0:1] + s_ref[1:2]).astype(bf16)


def first_norm(ctx_o, ctx_p, wo, wp, x, gains, shifts):
    rows, width = x.shape
    return pl.pallas_call(
        first_norm_kernel,
        out_shape=(
            jax.ShapeDtypeStruct((rows, width), f32),
            jax.ShapeDtypeStruct((rows, 1), f32),
            jax.ShapeDtypeStruct((rows, width), bf16),
        ),
        compiler_params=params(),
        cost_estimate=cost(2 * rows * width * width, 12 * rows * width),
        name="first_norm",
    )(ctx_o, ctx_p, wo, wp, x, gains, shifts)


def inner_kernel(h_ref, w_ref, b_ref, act_ref, slope_ref):
    for at in range(0, h_ref.shape[0], 128):
        rows = slice(at, at + 128)
        inner = mm(h_ref[rows], w_ref[...]) + b_ref[...]
        cumulative = 0.5 * (1.0 + lax.erf(inner * 0.7071067811865476))
        density = jnp.exp(-0.5 * inner * inner) * 0.3989422804014327
        act_ref[rows] = (inner * cumulative).astype(bf16)
        slope_ref[rows] = (cumulative + inner * density).astype(bf16)


def inner_half(low, w, b):
    rows, width = low.shape
    units = w.shape[1]
    tile = 256
    out = jax.ShapeDtypeStruct((rows, units), bf16)
    return pl.pallas_call(
        inner_kernel,
        grid=(units // tile,),
        in_specs=[
            pl.BlockSpec((rows, width), lambda n: (0, 0)),
            pl.BlockSpec((width, tile), lambda n: (0, n)),
            pl.BlockSpec((1, tile), lambda n: (0, n)),
        ],
        out_specs=[pl.BlockSpec((rows, tile), lambda n: (0, n))] * 2,
        out_shape=(out, out),
        compiler_params=params(),
        cost_estimate=cost(4 * rows * width * units, 8 * rows * units),
        name="inner",
    )(low, w, b)


def branch_kernel(act_ref, w_ref, out_ref):
    for at in range(0, act_ref.shape[0], 128):
        rows = slice(at, at + 128)
        out_ref[rows] = mm(act_ref[rows], w_ref[...])


def branch_half(act, w):
    rows, units = act.shape
    width = w.shape[1]
    return pl.pallas_call(
        branch_kernel,
        out_shape=jax.ShapeDtypeStruct((rows, width), f32),
        compiler_params=params(),
        cost_estimate=cost(2 * rows * width * units, 4 * rows * units),
        name="branch",
    )(act, w)


def second_norm_kernel(act_ref, w_ref, part_ref, n1_ref, g_ref, s_ref, n_ref, inv_ref, out_ref):
    for at in range(0, act_ref.shape[0], 128):
        rows = slice(at, at + 128)
        branch = mm(act_ref[rows], w_ref[...]) + part_ref[rows] + s_ref[2:3]
        hidden_one = n1_ref[rows] * g_ref[0:1] + s_ref[1:2]
        normed, inv_std = norm_rows(hidden_one + branch)
        n_ref[rows] = normed
        inv_ref[rows] = inv_std
        out_ref[rows] = (normed * g_ref[1:2] + s_ref[3:4]).astype(bf16)


def second_norm(act, w, part, normed_one, gains, shifts):
    rows, units = act.shape
    width = w.shape[1]
    return pl.pallas_call(
        second_norm_kernel,
        out_shape=(
            jax.ShapeDtypeStruct((rows, width), f32),
            jax.ShapeDtypeStruct((rows, 1), f32),
            jax.ShapeDtypeStruct((rows, width), bf16),
        ),
        compiler_params=params(),
        cost_estimate=cost(2 * rows * width * units, 4 * rows * units),
        name="second_norm",
    )(act, w, part, normed_one, gains, shifts)


def loss_kernel(
    pos_ref, rel_ref, w_ref, bias_ref, scale_ref,
    loss_ref, gscale_ref, pre_ref, bias_grad_ref, first_grad_ref, firsts_out_ref,
    all_ref, pooled_ref, len_ref, unit_ref, lse_col_ref, lse_row_ref, pre_f_ref,
):
    @pl.loop(0, pooled_ref.shape[0] // 8)
    def _(slot):
        source = pl.multiple_of(slot * 8, 8)
        target = pl.multiple_of(jnp.bitwise_xor(slot, pos_ref[0]) * 8, 8)
        all_ref[pl.ds(target, 8), :] = rel_ref[pl.ds(source, 8), :].astype(f32)

    loss_passes(
        pos_ref[1], scale_ref[0], w_ref, bias_ref[...],
        loss_ref, gscale_ref, pre_ref, bias_grad_ref, first_grad_ref, firsts_out_ref,
        all_ref, pooled_ref, len_ref, unit_ref, lse_col_ref, lse_row_ref, pre_f_ref,
    )


def loss_passes(
    here, scale, w_ref, bias,
    loss_ref, gscale_ref, pre_ref, bias_grad_ref, first_grad_ref, firsts_out_ref,
    all_ref, pooled_ref, len_ref, unit_ref, lse_col_ref, lse_row_ref, pre_f_ref,
):
    count, width = pooled_ref.shape
    chunk = min(count, 256)
    steps = count // chunk

    def pool(at):
        firsts = all_ref[pl.ds(at, chunk), :width].astype(bf16)
        firsts_out_ref[pl.ds(at, chunk), :] = firsts
        pooled = jnp.tanh(mm(firsts, w_ref[...]) + bias)
        inv_len = lax.rsqrt(jnp.sum(pooled * pooled, axis=-1, keepdims=True) + 1e-06)
        pooled_ref[pl.ds(at, chunk), :] = pooled
        len_ref[pl.ds(at, chunk), :] = inv_len
        unit_ref[pl.ds(at, chunk), :] = (pooled * inv_len).astype(bf16)

    def positions(at):
        own = at + lax.broadcasted_iota(jnp.int32, (chunk, count), 0)
        other = lax.broadcasted_iota(jnp.int32, (chunk, count), 1)
        paired = all_ref[pl.ds(at, chunk), width:width + 1]
        positive = paired.astype(jnp.int32) == other
        return own == other, positive

    def logits_of(at):
        cosine = mm_nt(unit_ref[pl.ds(at, chunk), :], unit_ref[...])
        own, positive = positions(at)
        shifted = cosine - jnp.where(positive, margin, 0.0)
        return shifted, own, positive

    def first_pass(at, run):
        shifted, own, positive = logits_of(at)
        logits = jnp.where(own, masked_out, scale * shifted)
        top = jnp.max(logits, axis=1, keepdims=True)
        lse = top + jnp.log(jnp.sum(jnp.exp(logits - top), axis=1, keepdims=True))
        lse_col_ref[pl.ds(at, chunk), :] = lse
        eye = lax.broadcasted_iota(jnp.int32, (chunk, chunk), 0) == lax.broadcasted_iota(
            jnp.int32, (chunk, chunk), 1
        )
        lse_row_ref[:, pl.ds(at, chunk)] = jnp.sum(jnp.where(eye, lse, 0.0), axis=0, keepdims=True)
        return run + jnp.sum(lse) - jnp.sum(jnp.where(positive, logits, 0.0))

    def second_pass(at, run):
        run_scale, run_bias = run
        shifted, own, positive = logits_of(at)
        logits = scale * shifted
        factor = 1.0 / (2.0 * count)
        grad = (
            jnp.exp(logits - lse_col_ref[pl.ds(at, chunk), :])
            + jnp.exp(logits - lse_row_ref[...])
            - jnp.where(positive, 2.0, 0.0)
        ) * factor
        grad = jnp.where(own, 0.0, grad)
        run_scale = run_scale + jnp.sum(grad * shifted)
        unit_grad = 2.0 * mm((scale * grad).astype(bf16), unit_ref[...])
        pooled = pooled_ref[pl.ds(at, chunk), :]
        inv_len = len_ref[pl.ds(at, chunk), :]
        along = jnp.sum(pooled * unit_grad, axis=-1, keepdims=True)
        pooled_grad = inv_len * unit_grad - pooled * (inv_len * inv_len * inv_len) * along
        pre_grad = (pooled_grad * (1.0 - pooled * pooled)).astype(bf16)
        pre_ref[pl.ds(at, chunk), :] = pre_grad
        pre_f_ref[pl.ds(at, chunk), :] = pre_grad.astype(f32)
        return run_scale, run_bias + jnp.sum(pre_grad.astype(f32), axis=0, keepdims=True)

    def each(body, run):
        if steps == 1:
            return body(0, run)
        return lax.fori_loop(0, steps, lambda s, r: body(pl.multiple_of(s * chunk, chunk), r), run)

    each(lambda at, run: (pool(at), run)[1], 0)
    total = each(first_pass, jnp.float32(0.0))
    run_scale, run_bias = each(second_pass, (jnp.float32(0.0), jnp.zeros((1, width), f32)))
    loss_ref[0] = total / count
    gscale_ref[0] = run_scale
    bias_grad_ref[...] = run_bias
    own_rows = pre_f_ref[pl.ds(pl.multiple_of(here * 8, 8), 8), :].astype(bf16)
    first_grad_ref[...] = mm_nt(own_rows, w_ref[...])


def pair_loss(position, rel, w_pool, bias, scale):
    count, wide = rel.shape
    width = w_pool.shape[0]
    smem = pl.BlockSpec(memory_space=pltpu.SMEM)
    vmem = pl.BlockSpec(memory_space=pltpu.VMEM)
    return pl.pallas_call(
        loss_kernel,
        in_specs=[smem, vmem, vmem, vmem, smem],
        out_specs=[smem, smem, vmem, vmem, vmem, vmem],
        out_shape=(
            jax.ShapeDtypeStruct((1,), f32),
            jax.ShapeDtypeStruct((1,), f32),
            jax.ShapeDtypeStruct((count, width), bf16),
            jax.ShapeDtypeStruct((1, width), f32),
            jax.ShapeDtypeStruct((8, width), f32),
            jax.ShapeDtypeStruct((count, width), bf16),
        ),
        scratch_shapes=[
            pltpu.VMEM((count, wide), f32),
            pltpu.VMEM((count, width), f32),
            pltpu.VMEM((count, 1), f32),
            pltpu.VMEM((count, width), bf16),
            pltpu.VMEM((count, 1), f32),
            pltpu.VMEM((1, count), f32),
            pltpu.VMEM((count, width), f32),
        ],
        compiler_params=params(56),
        cost_estimate=cost(2e9, 4e6),
        name="pair_loss",
    )(position, rel, w_pool, bias, scale)


def put_slabs(pos_ref, source, keep_ref, send_ref, lead):
    slab = source.shape[0] // 16
    for place in range(16):
        at = pl.multiple_of(jnp.bitwise_xor(pos_ref[0], place) * slab, slab)
        target = send_ref if place % 2 else keep_ref
        target[lead + (place // 2,)] = source[pl.ds(at, slab), :].astype(bf16)


def second_back_kernel(
    og_ref, fg_ref, n_ref, inv_ref, g_ref, grad_ref, low_ref, sums_ref
):
    rows_all, width = og_ref.shape
    sums_ref[...] = jnp.zeros_like(sums_ref)
    for at in range(0, rows_all, 64):
        rows = slice(at, at + 64)
        block = at // 64
        is_first = lax.broadcasted_iota(jnp.int32, (64, width), 0) == 0
        grad = og_ref[rows].astype(f32) + jnp.where(is_first, fg_ref[block:block + 1], 0.0)
        normed = n_ref[rows]
        value = norm_back(grad, normed, inv_ref[rows], g_ref[1:2])
        low = value.astype(bf16)
        grad_ref[rows] = value
        low_ref[rows] = low
        sums_ref[0:1] += jnp.sum(grad * normed, axis=0, keepdims=True)
        sums_ref[1:2] += jnp.sum(grad, axis=0, keepdims=True)
        sums_ref[2:3] += jnp.sum(low.astype(f32), axis=0, keepdims=True)


def second_back(out_grad, first_grad, normed, inv_std, gains):
    rows, width = out_grad.shape
    return pl.pallas_call(
        second_back_kernel,
        out_shape=(
            jax.ShapeDtypeStruct((rows, width), f32),
            jax.ShapeDtypeStruct((rows, width), bf16),
            jax.ShapeDtypeStruct((8, width), f32),
        ),
        compiler_params=params(),
        cost_estimate=cost(20 * rows * width, 12 * rows * width),
        name="second_back",
    )(out_grad, first_grad, normed, inv_std, gains)


def slab_shape(rows, cols):
    return jax.ShapeDtypeStruct((8, rows // 16, cols), bf16)


def back_weight_kernel(pos_ref, act_ref, branch_ref, keep_ref, send_ref, whole):
    for at in range(0, whole.shape[0], 256):
        rows = slice(at, at + 256)
        whole[rows] = mm_tn(act_ref[:, rows], branch_ref[...])
    put_slabs(pos_ref, whole, keep_ref, send_ref, ())


def back_weight(pos, act, branch):
    rows, units = act.shape
    width = branch.shape[1]
    smem = pl.BlockSpec(memory_space=pltpu.SMEM)
    vmem = pl.BlockSpec(memory_space=pltpu.VMEM)
    return pl.pallas_call(
        back_weight_kernel,
        in_specs=[smem, vmem, vmem],
        out_specs=[vmem, vmem],
        out_shape=(slab_shape(units, width),) * 2,
        scratch_shapes=[pltpu.VMEM((units, width), f32)],
        compiler_params=params(),
        cost_estimate=cost(2 * rows * width * units, 4 * units * width),
        name="back_weight",
    )(pos, act, branch)


def inner_back_kernel(pos_ref, branch_ref, wb_ref, slope_ref, low_ref, wi_ref, part_ref,
                      keep_ref, send_ref, bias_ref, out_ref, grad, whole):
    units = slope_ref.shape[1]
    for at in range(0, units, 256):
        cols = slice(at, at + 256)
        inner_grad = (mm_nt(branch_ref[...], wb_ref[cols]) * slope_ref[:, cols].astype(f32)).astype(bf16)
        grad[:, cols] = inner_grad
        bias_ref[:, cols] = jnp.sum(inner_grad.astype(f32), axis=0, keepdims=True)
        whole[:, cols] = mm_tn(low_ref[...], inner_grad)
    put_slabs(pos_ref, whole, keep_ref, send_ref, ())
    for at in range(0, low_ref.shape[0], 128):
        rows = slice(at, at + 128)
        out_ref[rows] = part_ref[rows] + mm_nt(grad[rows], wi_ref[...])


def inner_back(pos, branch, w_back, slope, low, w_in, part):
    rows, units = slope.shape
    width = low.shape[1]
    smem = pl.BlockSpec(memory_space=pltpu.SMEM)
    vmem = pl.BlockSpec(memory_space=pltpu.VMEM)
    return pl.pallas_call(
        inner_back_kernel,
        in_specs=[smem] + [vmem] * 6,
        out_specs=[vmem] * 4,
        out_shape=(slab_shape(width, units),) * 2
        + (jax.ShapeDtypeStruct((1, units), f32), jax.ShapeDtypeStruct((rows, width), f32)),
        scratch_shapes=[pltpu.VMEM((rows, units), bf16), pltpu.VMEM((width, units), f32)],
        compiler_params=params(),
        cost_estimate=cost(6 * rows * width * units, 4 * units * width),
        name="inner_back",
    )(pos, branch, w_back, slope, low, w_in, part)


def first_back_kernel(pos_ref, grad_ref, n_ref, inv_ref, g_ref, co_ref, cp_ref, wo_ref, wp_ref,
                      one_ref, sums_ref, dco_ref, dcp_ref, keep_ref, send_ref, low, whole):
    width = grad_ref.shape[1]
    sums_ref[...] = jnp.zeros_like(sums_ref)
    for at in range(0, grad_ref.shape[0], 128):
        rows = slice(at, at + 128)
        grad = grad_ref[rows]
        normed = n_ref[rows]
        value = norm_back(grad, normed, inv_ref[rows], g_ref[0:1])
        low_rows = value.astype(bf16)
        one_ref[rows] = value
        low[rows] = low_rows
        dco_ref[rows] = mm_nt(low_rows, wo_ref[...]).astype(bf16)
        dcp_ref[rows] = mm_nt(low_rows, wp_ref[...]).astype(bf16)
        sums_ref[0:1] += jnp.sum(grad * normed, axis=0, keepdims=True)
        sums_ref[1:2] += jnp.sum(grad, axis=0, keepdims=True)
        sums_ref[2:3] += jnp.sum(low_rows.astype(f32), axis=0, keepdims=True)
    for side, ctx_ref in enumerate((co_ref, cp_ref)):
        whole[...] = mm_tn(ctx_ref[...], low[...])
        put_slabs(pos_ref, whole, keep_ref.at[side], send_ref.at[side], ())


def first_back(pos, grad, normed, inv_std, gains, ctx_o, ctx_p, wo, wp):
    rows, width = grad.shape
    cols = ctx_o.shape[1]
    smem = pl.BlockSpec(memory_space=pltpu.SMEM)
    vmem = pl.BlockSpec(memory_space=pltpu.VMEM)
    return pl.pallas_call(
        first_back_kernel,
        in_specs=[smem] + [vmem] * 8,
        out_specs=[vmem] * 6,
        out_shape=(
            jax.ShapeDtypeStruct((rows, width), f32),
            jax.ShapeDtypeStruct((8, width), f32),
            jax.ShapeDtypeStruct((rows, cols), bf16),
            jax.ShapeDtypeStruct((rows, cols), bf16),
        )
        + (jax.ShapeDtypeStruct((2, 8, cols // 16, width), bf16),) * 2,
        scratch_shapes=[pltpu.VMEM((rows, width), bf16), pltpu.VMEM((cols, width), f32)],
        compiler_params=params(),
        cost_estimate=cost(8 * rows * width * cols, 12 * rows * width),
        name="first_back",
    )(pos, grad, normed, inv_std, gains, ctx_o, ctx_p, wo, wp)


def attention_back_kernel(pos_ref, x_ref, w_ref, segc_ref, segr_ref, q_ref, k_ref, v_ref, dc_ref, part_ref,
                          keep_ref, send_ref, bias_ref, out_ref, dq, dk, dv, whole):
    scale = HEAD_DIM ** (-0.5)
    for group in range(x_ref.shape[0] // GROUP):
        rows = slice(group * GROUP, (group + 1) * GROUP)
        same = same_segment(segc_ref, segr_ref, rows)
        for pair in range(q_ref.shape[1] // PAIR):
            cols = slice(pair * PAIR, (pair + 1) * PAIR)
            q_two = two_heads(q_ref[rows, cols])
            dc_two = two_heads(dc_ref[rows, cols])
            k_pair = k_ref[rows, cols]
            probs = pair_probs(q_two, k_pair, same)
            prob_grad = mm_nt(dc_two, v_ref[rows, cols])
            score_grad = (
                probs * (prob_grad - jnp.sum(prob_grad * probs, axis=1, keepdims=True))
            ).astype(bf16)
            dq[rows, cols] = (join_heads(mm(score_grad, k_pair)) * scale).astype(bf16)
            dk[rows, cols] = (mm_tn(score_grad, q_two) * scale).astype(bf16)
            dv[rows, cols] = mm_tn(probs.astype(bf16), dc_two).astype(bf16)
    bias_ref[0:1] = jnp.sum(dq[...].astype(f32), axis=0, keepdims=True)
    bias_ref[1:2] = jnp.sum(dv[...].astype(f32), axis=0, keepdims=True)
    for s, grad in enumerate((dq, dk, dv)):
        whole[...] = mm_tn(x_ref[...], grad[...])
        put_slabs_at(pos_ref, whole, keep_ref, send_ref, s)
    for at in range(0, x_ref.shape[0], 128):
        rows = slice(at, at + 128)
        out_ref[rows] = (
            part_ref[rows] + mm_nt(dq[rows], w_ref[0]) + mm_nt(dk[rows], w_ref[1]) + mm_nt(dv[rows], w_ref[2])
        )


def put_slabs_at(pos_ref, source, keep_ref, send_ref, s):
    slab = source.shape[0] // 16
    for place in range(16):
        at = pl.multiple_of(jnp.bitwise_xor(pos_ref[0], place) * slab, slab)
        target = send_ref if place % 2 else keep_ref
        target[place // 2, s] = source[pl.ds(at, slab), :].astype(bf16)


def attention_back(pos, x, w, segc, segr, q, k, v, dc, part):
    rows, width = x.shape
    cols = q.shape[1]
    smem = pl.BlockSpec(memory_space=pltpu.SMEM)
    vmem = pl.BlockSpec(memory_space=pltpu.VMEM)
    slabs = jax.ShapeDtypeStruct((8, 3, width // 16, cols), bf16)
    return pl.pallas_call(
        attention_back_kernel,
        in_specs=[smem] + [vmem] * 9,
        out_specs=[vmem] * 4,
        out_shape=(slabs, slabs, jax.ShapeDtypeStruct((2, cols), f32), jax.ShapeDtypeStruct((rows, width), f32)),
        scratch_shapes=[pltpu.VMEM((rows, cols), bf16)] * 3 + [pltpu.VMEM((width, cols), f32)],
        compiler_params=params(),
        cost_estimate=cost(20 * rows * width * cols, 4 * 3 * width * cols),
        name="attention_back",
    )(pos, x, w, segc, segr, q, k, v, dc, part)


def flip(value, bit):
    return value + bit - 2 * bit * ((value // bit) % 2)


class Copies:
    def __init__(self, send, recv, local):
        self.send, self.recv, self.local = send, recv, local
        self.sent, self.kept, self.ring = [], [], send.shape[0]

    def remote(self, source, target, device):
        at = len(self.sent)
        if at >= self.ring:
            self.sent[at - self.ring].wait_send()
        copy = pltpu.make_async_remote_copy(
            src_ref=source, dst_ref=target, send_sem=self.send.at[at % self.ring], recv_sem=self.recv.at[at],
            device_id=device, device_id_type=pl.DeviceIdType.MESH,
        )
        copy.start()
        self.sent.append(copy)
        return copy

    def here(self, source, target):
        copy = pltpu.make_async_copy(source, target, self.local.at[len(self.kept)])
        copy.start()
        self.kept.append(copy)
        return copy


def greet(devices):
    barrier = pltpu.get_barrier_semaphore()
    for device in devices:
        pl.semaphore_signal(barrier, inc=1, device_id=device, device_id_type=pl.DeviceIdType.MESH)
    pl.semaphore_wait(barrier, len(devices))


def same_block(row):
    across = jnp.broadcast_to(row.astype(f32), (GROUP, GROUP))
    return across == across.T


def arrive(*copies):
    for copy in copies:
        copy.wait_recv()


N_CHUNK = 3


def forward_kernel(
    segr_ref, b_qv_ref, b_in_ref, g_ref, s_ref, scale_ref, pairs_ref,
    x_any, w_pool_any, w_qkv_any, w_out_any, w_in_any, w_back_any,
    block_out, p_qkv, p_out_any, p_in_any, p_back_any, q_any, k_any, v_any, n1_any, i1_any, lowt_any, xt_any, ctxt_any,
    actt_any, slope_any, n2_any, i2_any,
    loss_ref, gscale_ref, new_scale_ref, first_any, b_qv_p, pool_any, pool_bias_any,
    first_grad_ref, pool_ref, pool_bias_ref, x_ref, w_pool_ref, w_qkv_ref, w_out, w_in, w_back, p_out, p_in, p_back, b_in_p, q, k, v, qf, kf, vf, ctx_far, ctx_o, ctx_p,
    n1, i1, low, act, slope, part, n2, i2, own_out, lowt, xt, ctxt, actt, ahead, ahead_got, gathered, ids,
    pre_ref, bias_grad_ref, firsts_out_ref, all_ref, pooled_ref, len_ref, unit_ref, lse_col_ref, lse_row_ref, pre_f_ref,
    send_sem, recv_sem, local_sem,
):
    dp, mp = lax.axis_index("dp"), lax.axis_index("mp")
    rows = q.shape[0]
    width = x_ref.shape[1]
    units = w_in.shape[1]
    near = {"x": {"mp": 1 - mp}, "y": {"dp": flip(dp, 2)}, "z": {"dp": flip(dp, 4)}, "c": {"dp": flip(dp, 1)}}
    far = ({"dp": flip(dp, 8)}, {"dp": flip(flip(dp, 4), 8)})
    run = Copies(send_sem, recv_sem, local_sem)
    own = dp % 8
    bit = {"y": 2, "z": 4}

    out_block, in_block, unit_chunk = w_out.shape[0] // 8, width // 8, units // N_CHUNK
    back_block = unit_chunk // 8

    def out_at(ref):
        return lambda b: ref.at[pl.ds(pl.multiple_of(b * out_block, 16), out_block)]

    def in_at(ref, n):
        return lambda b: ref.at[pl.ds(pl.multiple_of(b * in_block, 16), in_block), pl.ds(n * unit_chunk, unit_chunk)]

    def back_at(ref, n):
        return lambda b: ref.at[pl.ds(pl.multiple_of(n * unit_chunk + b * back_block, 16), back_block)]

    def qkv_at(ref, n):
        return lambda b: ref.at[:, pl.ds(pl.multiple_of((2 * b + n) * in_block, 16), in_block)]

    routes = ("zy", "zy", "yz", "zy", "yz", "zy", "yz")
    chunks = [(out_at(w_out_any), out_at(p_out), routes[0])]
    chunks += [(in_at(w_in_any, n), in_at(p_in, n), routes[1 + n]) for n in range(N_CHUNK)]
    chunks += [(back_at(w_back_any, n), back_at(p_back, n), routes[1 + N_CHUNK + n]) for n in range(N_CHUNK)]
    chunks += [(qkv_at(w_qkv_any, n), qkv_at(p_qkv, n), "yz"[n]) for n in range(2)]
    hops = [[None] * 4 for _ in chunks]

    def step(at, stage):
        source, target, route = chunks[at]
        first = own if len(route) == 2 else dp % 2 + 2 * ((dp // bit[route]) % 2)
        if stage == 0:
            hops[at][0] = [run.remote(source(first), target(first), near["x"])]
            return
        for copy in hops[at][stage - 1]:
            copy.wait_recv()
        one = flip(first, bit[route[0]] if len(route) == 2 else 2)
        blocks = [first, one]
        if len(route) == 2:
            blocks += [flip(b, bit[route[1]]) for b in blocks]
        if stage == 1:
            hops[at][1] = [run.remote(target(first), target(first), near[route[0]])]
        elif stage == len(route) + 1:
            hops[at][stage] = [run.remote(target(b), target(b), near["c"]) for b in blocks]
        elif stage == 2:
            hops[at][2] = [run.remote(target(b), target(b), near[route[1]]) for b in blocks[:2]]

    loads = [
        run.here(a, b)
        for a, b in (
            (x_any, x_ref), (w_qkv_any, w_qkv_ref), (w_out_any, w_out), (w_in_any, w_in), (w_back_any, w_back),
            (w_pool_any, w_pool_ref),
        )
    ]
    z, y, c = dp // 4, (dp // 2) % 2, dp % 2
    row_of = lax.broadcasted_iota(jnp.int32, (8, 128), 0)
    paired = jnp.zeros((8, 128), f32)
    for at in range(8):
        paired = jnp.where(row_of == at, pairs_ref[mp * 8 + at].astype(f32), paired)
    ids[z, y, c, mp] = paired
    greet(list(near.values()) + list(far))
    pair_hops = [[run.remote(ids.at[z, y, c, mp], ids.at[z, y, c, mp], near["x"])]]
    step(0, 0)
    b_copies = [run.remote(b_in_ref, b_in_p, near["x"]), run.remote(b_qv_ref, b_qv_p, near["x"])]

    def project(base, q_to, k_to, v_to):
        x = x_ref[pl.ds(base, rows)]
        q_to[...] = (mm(x, w_qkv_ref[0]) + b_qv_ref[0:1]).astype(bf16)
        k_to[...] = mm(x, w_qkv_ref[1]).astype(bf16)
        v_to[...] = (mm(x, w_qkv_ref[2]) + b_qv_ref[1:2]).astype(bf16)

    def attend(base, q_from, k_from, v_from, target):
        for group in range(rows // GROUP):
            at = slice(group * GROUP, (group + 1) * GROUP)
            one = same_block(segr_ref[:, pl.ds(pl.multiple_of(base + group * GROUP, GROUP), GROUP)])
            same = jnp.concatenate([one, one], axis=0)
            for pair in range(q_from.shape[1] // PAIR):
                cols = slice(pair * PAIR, (pair + 1) * PAIR)
                probs = pair_probs(two_heads(q_from[at, cols]), k_from[at, cols], same)
                target[at, cols] = join_heads(mm(probs.astype(bf16), v_from[at, cols])).astype(bf16)

    far_base = pl.multiple_of((1 - mp) * rows, rows)
    own_base = pl.multiple_of(mp * rows, rows)
    half = width // 2
    flight = {}

    def firsts_of(ref):
        return jnp.concatenate([ref[at:at + 1].astype(f32) for at in range(0, rows, SEG_LEN)], axis=0)

    def gelu_parts(value):
        cumulative = 0.5 * (1.0 + lax.erf(value * 0.7071067811865476))
        density = jnp.exp(-0.5 * value * value) * 0.3989422804014327
        return (value * cumulative).astype(bf16), cumulative + value * density

    def bias_of(b, at):
        return jnp.concatenate([b[at // 128:at // 128 + 1], b[at // 128 + 1:at // 128 + 2]], axis=1)

    def far_tokens():
        loads[0].wait()
        loads[1].wait()
        project(far_base, qf, kf, vf)
        attend(far_base, qf, kf, vf, ctx_far)

    def own_tokens():
        attend(own_base, q, k, v, ctx_o)
        for a, b in ((q, q_any), (k, k_any), (v, v_any)):
            run.here(a, b)

    def send_context(part):
        some = pl.ds(part * GROUP, GROUP)
        flight["context", part] = run.remote(ctx_far.at[some], ctx_p.at[some], near["x"])

    def ahead_out():
        loads[2].wait()
        both = jnp.concatenate([firsts_of(ctx_o), firsts_of(ctx_far)], axis=0).astype(bf16)
        ahead[0] = mm(both, w_out[...])
        flight["ahead"] = run.remote(ahead.at[0, pl.ds(8, 8)], ahead_got.at[0], near["x"])

    def ahead_norm():
        arrive(flight["ahead"])
        x = jnp.concatenate(
            [x_ref[pl.ds(pl.multiple_of(own_base + at, SEG_LEN), 16)][0:1].astype(f32) for at in range(0, rows, SEG_LEN)],
            axis=0,
        )
        hidden = norm_rows(x + ahead[0, 0:8] + ahead_got[0] + s_ref[0:1])[0] * g_ref[0:1] + s_ref[1:2]
        ahead[3, 0:8] = hidden
        ahead[1, 0:8] = hidden.astype(bf16).astype(f32)
        flight["ahead"] = run.remote(ahead.at[1, pl.ds(0, 8)], ahead.at[1, pl.ds(8, 8)], near["x"])

    def ahead_units():
        loads[3].wait()
        loads[4].wait()
        arrive(flight["ahead"])
        both = ahead[1].astype(bf16)
        total = jnp.zeros((16, width), f32)
        for at in range(0, units, 256):
            inside = gelu_parts(mm(both, w_in[:, at:at + 256]) + bias_of(b_in_ref, at))[0]
            total = total + mm(inside, w_back[at:at + 256])
        ahead[2] = total
        flight["ahead"] = run.remote(ahead.at[2, pl.ds(8, 8)], ahead_got.at[1], near["x"])

    def ahead_last():
        arrive(flight["ahead"])
        normed = norm_rows(ahead[3, 0:8] + (ahead[2, 0:8] + ahead_got[1] + s_ref[2:3]))[0]
        firsts = (normed * g_ref[1:2] + s_ref[3:4]).astype(bf16).astype(f32)
        gathered[z, y, c, mp] = jnp.concatenate([firsts[:, :half], firsts[:, half:]], axis=0).astype(bf16)
        slot = gathered.at[z, y, c, mp]
        flight["gather"] = [run.remote(slot, slot, near["x"])]

    def gather(hop):
        arrive(*flight["gather"])
        slot = (gathered.at[z, y, c], gathered.at[:, y, c], gathered.at[:, :, c])[hop]
        devices = ((far[1], far[0], near["z"]), (near["y"],), (near["c"],))[hop]
        flight["gather"] = [run.remote(slot, slot, device) for device in devices]

    def pair_hop(hop):
        arrive(*pair_hops[hop])
        slot = (ids.at[z, y, c], ids.at[:, y, c], ids.at[:, :, c])[hop]
        devices = ((far[1], far[0], near["z"]), (near["y"],), (near["c"],))[hop]
        pair_hops.append([run.remote(slot, slot, device) for device in devices])

    def turn():
        for at in range(0, rows, 128):
            here = slice(at, at + 128)
            xt[:, here] = x_ref[pl.ds(pl.multiple_of(own_base + at, 128), 128)].T
            ctxt[0, :, here] = ctx_o[here].T

    def own_out_part():
        part[...] = mm(ctx_o[...], w_out[...])

    def first_norm():
        arrive(*[flight["context", at] for at in range(rows // GROUP)])
        for at in range(0, rows, 128):
            here = slice(at, at + 128)
            x = x_ref[pl.ds(pl.multiple_of(own_base + at, 128), 128)].astype(f32)
            normed, inv_std = norm_rows(x + part[here] + mm(ctx_p[here], p_out[...]) + s_ref[0:1])
            n1[here] = normed
            i1[here] = jnp.broadcast_to(inv_std, (128, 128))
            rounded = (normed * g_ref[0:1] + s_ref[1:2]).astype(bf16)
            low[here] = rounded
            lowt[:, here] = rounded.T
            ctxt[1, :, here] = ctx_p[here].T
        for a, b in ((p_out, p_out_any), (n1, n1_any), (i1, i1_any), (lowt, lowt_any), (xt, xt_any), (ctxt, ctxt_any)):
            run.here(a, b)

    def inner(side, n):
        w, b = ((w_in, b_in_ref), (p_in, b_in_p))[side]
        if side == 1 and n == 0:
            arrive(*b_copies)
        for at in range(n * unit_chunk, (n + 1) * unit_chunk, 256):
            cols = slice(at, at + 256)
            bias = bias_of(b, at)
            for top in range(0, rows, 128):
                here = slice(top, top + 128)
                rounded, slopes = gelu_parts(mm(low[here], w[:, cols]) + bias)
                act[side, here, cols] = rounded
                actt[side, cols, here] = rounded.T
                slope[side, here, cols] = slopes.astype(bf16)
        if side == 1 and n == N_CHUNK - 1:
            for a, b in ((actt, actt_any), (slope, slope_any), (p_in, p_in_any)):
                run.here(a, b)

    def branch(side, n):
        w = (w_back, p_back)[side]
        cols = slice(n * unit_chunk, (n + 1) * unit_chunk)
        for top in range(0, rows, 128):
            here = slice(top, top + 128)
            value = mm(act[side, here, cols], w[cols])
            part[here] = value if (side, n) == (0, 0) else part[here] + value

    def second_norm():
        last = slice((N_CHUNK - 1) * unit_chunk, units)
        for at in range(0, rows, 64):
            here = slice(at, at + 64)
            value = mm(act[1, here, last], p_back[last]) + part[here] + s_ref[2:3]
            normed, inv_std = norm_rows(n1[here] * g_ref[0:1] + s_ref[1:2] + value)
            n2[here] = normed
            i2[here] = jnp.broadcast_to(inv_std, (64, 128))
            own_out[here] = (normed * g_ref[1:2] + s_ref[3:4]).astype(bf16)
        for a, b in ((n2, n2_any), (i2, i2_any), (p_back, p_back_any), (own_out, block_out)):
            run.here(a, b)

    far_tokens()
    step(1, 0)
    project(own_base, q, k, v)
    step(0, 1)
    pair_hop(0)
    own_tokens()
    step(2, 0)
    ahead_out()
    turn()
    own_out_part()
    step(1, 1)
    step(3, 0)
    step(0, 2)
    step(4, 0)
    step(2, 1)
    ahead_norm()
    step(1, 2)
    pair_hop(1)
    send_context(0)
    step(3, 1)
    step(0, 3)
    step(5, 0)
    step(4, 1)
    ahead_units()
    step(6, 0)
    step(0, 4)
    step(2, 2)
    step(3, 2)
    step(5, 1)
    send_context(3)
    step(1, 3)
    ahead_last()
    step(1, 4)
    send_context(2)
    step(4, 2)
    step(6, 1)
    send_context(1)
    step(2, 3)
    gather(0)
    step(2, 4)
    step(7, 0)
    step(3, 3)
    step(5, 2)
    step(3, 4)
    step(6, 2)
    first_norm()
    pair_hop(2)
    inner(0, 0)
    step(8, 0)
    step(4, 3)
    inner(0, 1)
    inner(0, 2)
    step(4, 4)
    gather(1)
    branch(0, 0)
    branch(0, 1)
    branch(0, 2)
    step(5, 3)
    step(7, 1)
    inner(1, 0)
    inner(1, 1)
    step(5, 4)
    step(6, 3)
    inner(1, 2)
    branch(1, 0)
    gather(2)
    branch(1, 1)
    step(6, 4)
    step(8, 1)
    second_norm()
    arrive(*pair_hops[3])
    arrive(*flight["gather"])
    loads[5].wait()

    @pl.loop(0, 32)
    def _(at):
        slot = (at // 8, (at // 4) % 2, (at // 2) % 2, at % 2)
        values = gathered[slot].astype(f32)
        here = pl.ds(pl.multiple_of(at * 8, 8), 8)
        all_ref[here, :half] = values[:8]
        all_ref[here, half:width] = values[8:]
        all_ref[here, width:] = ids[slot]

    loss_passes(
        dp * 2 + mp, scale_ref[0], w_pool_ref, s_ref[4:5],
        loss_ref, gscale_ref, pre_ref, bias_grad_ref, first_grad_ref, firsts_out_ref,
        all_ref, pooled_ref, len_ref, unit_ref, lse_col_ref, lse_row_ref, pre_f_ref,
    )
    new_scale_ref[0] = scale_ref[0] - step_rate * gscale_ref[0]
    per = width // 16
    own_firsts = mm(firsts_out_ref[...], pick(width, dp * per, per).astype(bf16)).astype(bf16)
    pool_ref[...] = mm_tn(own_firsts, pre_ref[...])
    pool_bias_ref[...] = exact(bias_grad_ref[...], pick(width, dp * per, per))
    for a, b in ((first_grad_ref, first_any), (pool_ref, pool_any), (pool_bias_ref, pool_bias_any)):
        run.here(a, b)
    arrive(*hops[7][1], *hops[8][1])
    for copy in run.sent[-run.ring:]:
        copy.wait_send()
    for copy in run.kept[len(loads):]:
        copy.wait()


def forward(x, segr, w_qkv, b_qv, b_in, gains, shifts, w_pool, scale, pairs, w_out, w_in, w_back):
    rows, width = x.shape[0] // 2, x.shape[1]
    cols, units = w_qkv.shape[2], w_in.shape[1]
    count = 2 * lax.axis_size("dp") * 8
    any_ = pl.BlockSpec(memory_space=pl.ANY)
    smem = pl.BlockSpec(memory_space=pltpu.SMEM)
    vmem = pl.BlockSpec(memory_space=pltpu.VMEM)
    S = jax.ShapeDtypeStruct
    head = (rows, cols)
    kept = [
        ((rows, width), bf16), (w_qkv.shape, bf16), (w_out.shape, bf16), (w_in.shape, bf16), (w_back.shape, bf16),
        (head, bf16), (head, bf16), (head, bf16),
        ((rows, width), f32), ((rows, 128), f32), ((width, rows), bf16), ((width, rows), bf16), ((2, cols, rows), bf16),
        ((2, units, rows), bf16), ((2, rows, units), bf16), ((rows, width), f32), ((rows, 128), f32),
    ]
    scratch = [
        ((8, width), f32), ((width // 16, width), f32), ((1, width // 16), f32),
        (x.shape, bf16), (w_pool.shape, bf16), (w_qkv.shape, bf16),
        (w_out.shape, bf16), (w_in.shape, bf16), (w_back.shape, bf16),
        (w_out.shape, bf16), (w_in.shape, bf16), (w_back.shape, bf16), (b_in.shape, f32),
    ] + [(head, bf16)] * 9 + [
        ((rows, width), f32), ((rows, 128), f32), ((rows, width), bf16),
        ((2, rows, units), bf16), ((2, rows, units), bf16), ((rows, width), f32), ((rows, width), f32),
        ((rows, 128), f32), ((rows, width), bf16),
        ((width, rows), bf16), ((width, rows), bf16), ((2, cols, rows), bf16), ((2, units, rows), bf16),
        ((4, 16, width), f32), ((2, 8, width), f32), ((4, 2, 2, 2, 16, width // 2), bf16), ((4, 2, 2, 2, 8, 128), f32),
        ((count, width), bf16), ((1, width), f32), ((count, width), bf16),
        ((count, width + 128), f32), ((count, width), f32), ((count, 1), f32), ((count, width), bf16),
        ((count, 1), f32), ((1, count), f32), ((count, width), f32),
    ]
    return pl.pallas_call(
        forward_kernel,
        in_specs=[vmem] * 5 + [smem] * 2 + [any_] * 6,
        out_specs=[any_] * len(kept) + [smem] * 3 + [any_] * 4,
        out_shape=tuple(S(*k) for k in kept) + (
            S((1,), f32), S((1,), f32), S((1,), f32), S((8, width), f32), S(b_qv.shape, f32),
            S((width // 16, width), f32), S((1, width // 16), f32),
        ),
        scratch_shapes=[pltpu.VMEM(*s) for s in scratch] + [
            pltpu.SemaphoreType.DMA((48,)), pltpu.SemaphoreType.DMA((82,)), pltpu.SemaphoreType.DMA((26,)),
        ],
        compiler_params=pltpu.CompilerParams(
            vmem_limit_bytes=56 * 1024 * 1024, collective_id=0, has_side_effects=True
        ),
        name="forward",
    )(segr, b_qv, b_in, gains, shifts, scale, pairs, x, w_pool, w_qkv, w_out, w_in, w_back)


def pick(size, start, count):
    return (
        lax.broadcasted_iota(jnp.int32, (size, count), 0)
        == start + lax.broadcasted_iota(jnp.int32, (size, count), 1)
    ).astype(f32)


def exact(a, b):
    return jnp.dot(a, b, preferred_element_type=f32, precision=lax.Precision.HIGHEST)


ORDERS = (
    ("z", "x", "y", "w"), ("y", "x", "q"), ("y", "z", "w", "x"),
    ("z", "x", "y", "w"), ("z", "x", "w", "y"), ("y", "z", "x", "w"),
    ("y", "z", "x", "w"), ("x", "z", "y", "w"), ("y", "x", "z", "w"),
    ("y", "z", "x", "w"), ("x", "y", "z", "w"), ("y", "x", "q"),
)
TILE = 384
PARTS = 4


def backward_kernel(
    segr_ref, g_ref, first_grad_ref, b_qv_ref,
    out_any, x_any, og_any, n2_any, i2_any, n1_any, i1_any, act_any, slope_any, low_any, xt_any, ctx_any, q_any, k_any, v_any,
    wb_o_any, wb_p_any, wi_o_any, wi_p_any, wo_o_any, wo_p_any, wq_o_any, wq_p_any,
    grad_in_any, out_other, o_back, o_in, o_qkv, o_out, a_gains, a_shifts, a_bqv, a_bin,
    o_gains, o_shifts, o_bqv, o_bin, one_buf, two_buf, three_buf, grad, i2, n1, i1, act, slope, low, xt, ctx, q, k, v, wb, wi, wo, wq, deltas,
    unit, got, ready, sums, sums_got,
    send_sem, recv_sem, local_sem,
):
    dp, mp = lax.axis_index("dp"), lax.axis_index("mp")
    rows, width = one_buf.shape
    units = slope.shape[2]
    cols = q.shape[2]
    per = width // 16
    own_base = pl.multiple_of(mp * rows, rows)
    near = {
        "x": {"mp": 1 - mp}, "y": {"dp": flip(dp, 2)}, "z": {"dp": flip(dp, 4)}, "w": {"dp": flip(dp, 8)},
        "c": {"dp": flip(dp, 1)},
    }
    quad = (near["z"], near["w"], {"dp": flip(flip(dp, 4), 8)})
    run = Copies(send_sem, recv_sem, local_sem)
    own_rows = lambda ref: ref.at[pl.ds(own_base, rows)]
    pending, results = {}, []

    def load(*pairs):
        for source, target, name in pairs:
            pending.setdefault(name, []).append(run.here(source, target))

    def need(*names):
        for name in names:
            for copy in pending.pop(name, ()):
                copy.wait()

    load((own_rows(og_any), one_buf, "two"), (n2_any, grad, "two"), (i2_any, i2, "two"))
    load((act_any, act, "act"), (wb_o_any, wb.at[0], "wb"), (wb_p_any, wb.at[1], "wb"), (slope_any, slope, "slope"))

    greet(list(near.values()) + [quad[2]])
    flight = {}
    bits = {"y": 2, "z": 4, "w": 8}

    def rel(name, side, dest):
        return side if name == "x" else (dest // bits[name] + dp // bits[name]) % 2

    def put(at, side, dest, value):
        spot, left = 0, 16
        for name in ORDERS[at]:
            left = left // (4 if name == "q" else 2)
            spot = spot + left * (2 * rel("w", side, dest) + rel("z", side, dest) if name == "q" else rel(name, side, dest))
        unit[at, (dest + dp) % 2, spot] = value.astype(bf16)

    def shape_of(at, stage):
        start, left = 0, 32
        for name in ("c",) + ORDERS[at][:stage]:
            held = left
            left = held // (4 if name == "q" else 2)
            begins, start = start, start + held - left
        return held, left, begins

    def begin(at):
        flight[at, 0] = [run.remote(unit.at[at, 1], got.at[at, pl.ds(0, 16)], near["c"])]

    def step(at, stage):
        arrive(*flight[at, stage - 1])
        held, count, begins = shape_of(at, stage - 1)
        mine = unit.at[at, 0]

        def added(n):
            if held == 2 * count:
                return mine[n] + got[at, begins + n]
            total = mine[n].astype(f32)
            for part in range(3):
                total = total + got[at, begins + part * count + n].astype(f32)
            return total.astype(bf16)

        if count == 1:
            total = mine[0].astype(f32)
            for part in range(held - 1):
                total = total + got[at, begins + part].astype(f32)
            ready[at] = total
            if at < 4:
                target = o_back.at[pl.ds(at % 2 * per, per), pl.ds(at // 2 * TILE, TILE)]
            elif at < 8:
                target = o_in.at[:, pl.ds((at - 4) * TILE, TILE)]
            elif at < 11:
                target = o_qkv.at[at - 8]
            else:
                results.append(run.here(ready.at[at, pl.ds(0, per // 2)], o_out.at[:, pl.ds(0, cols)]))
                results.append(run.here(ready.at[at, pl.ds(per // 2, per // 2)], o_out.at[:, pl.ds(cols, cols)]))
                return
            results.append(run.here(ready.at[at], target))
            return
        _, after, begins_next = shape_of(at, stage)
        for n in range(after, count):
            mine[n] = added(n)
        name = ORDERS[at][stage - 1]
        devices = quad if name == "q" else (near[name],)
        flight[at, stage] = [
            run.remote(
                mine.at[pl.ds((part + 1) * after, after)], got.at[at, pl.ds(begins_next + part * after, after)], device
            )
            for part, device in enumerate(devices)
        ]
        for n in range(after):
            mine[n] = added(n)

    def sum_step(stage):
        if stage:
            flight["sums", stage - 1].wait_recv()
            sums[stage] = sums[stage - 1] + sums_got[stage - 1]
        if stage < 5:
            name = ("c", "x", "y", "z", "w")[stage]
            flight["sums", stage] = run.remote(sums.at[stage], sums_got.at[stage], near[name])

    def norm_grads(source, extra, normed_ref, inv_ref, gain, low_ref, places):
        gain_sum, shift_sum, low_sum = 0.0, 0.0, 0.0
        for at in range(0, rows, 64):
            here = slice(at, at + 64)
            value = source[here].astype(f32)
            if extra is not None:
                is_first = lax.broadcasted_iota(jnp.int32, (64, width), 0) == 0
                value = value + jnp.where(is_first, extra[at // 64:at // 64 + 1], 0.0)
            normed = normed_ref[here]
            out = norm_back(value, normed, inv_ref[here, 0:1], gain)
            rounded = out.astype(bf16)
            grad[here] = out
            low_ref[here] = rounded
            gain_sum += jnp.sum(value * normed, axis=0, keepdims=True)
            shift_sum += jnp.sum(value, axis=0, keepdims=True)
            low_sum += jnp.sum(rounded.astype(f32), axis=0, keepdims=True)
        for place, value in zip(places, (gain_sum, shift_sum, low_sum)):
            sums[0, place:place + 1] = value

    def second_norm():
        need("two")
        sums[0] = jnp.zeros(sums.shape[1:], f32)
        norm_grads(one_buf, first_grad_ref, grad, i2, g_ref[1:2], two_buf, (1, 5, 4))
        load((wi_o_any, wi.at[0], "wi"), (wi_p_any, wi.at[1], "wi"), (low_any, low, "low"))
        load((n1_any, n1, "one"), (i1_any, i1, "one"))

    def back_weight(half):
        need("act")
        for side in range(2):
            for top in range(0, units, TILE):
                tile = mm(act[side, top:top + TILE], two_buf[:, half * cols:(half + 1) * cols])
                for at in range(0, TILE, per):
                    put(2 * half + at // per % 2, side, (top + at) // (2 * per), tile[at:at + per])

    def inner_grads(side):
        need("wb", "slope")
        owner = mp + side - 2 * mp * side
        for at in range(0, units, 256):
            here = slice(at, at + 256)
            value = (mm_nt(two_buf[...], wb[side, here]) * slope[side, :, here].astype(f32)).astype(bf16)
            slope[side, :, here] = value
            sums[0, pl.ds(8 + 2 * owner + at // width, 1), at % width:at % width + 256] = jnp.sum(
                value.astype(f32), axis=0, keepdims=True
            )
        if side == 0:
            load((ctx_any, ctx, "ctx"), (wo_o_any, wo.at[0], "wo"), (wo_p_any, wo.at[1], "wo"))
            load((own_rows(x_any), three_buf, "x"))
            flight["wq"] = []
            for quarter in (dp % 2, dp % 2 + 2):
                some = pl.ds(pl.multiple_of(quarter * (width // 4), 16), width // 4)
                flight["wq"].append(run.remote(wq_p_any.at[:, some], wq.at[1, :, some], near["c"]))
                load((wq_p_any.at[:, some], wq.at[1, :, some], "wq_p"))

    def feed_back():
        need("wi")
        for at in range(0, width, 256):
            here = slice(at, at + 256)
            grad[:, here] = grad[:, here] + mm_nt(slope[0], wi[0, here]) + mm_nt(slope[1], wi[1, here])
        load((q_any, q.at[0], "qkv"), (k_any, k.at[0], "qkv"), (v_any, v.at[0], "qkv"))
        load((xt_any, xt, "xt"), (wq_o_any, wq.at[0], "wq_o"))

    def first_norm_back():
        need("one")
        norm_grads(grad, None, n1, i1, g_ref[0:1], one_buf, (0, 3, 2))

    def in_weight(half):
        need("low")
        for at in range(2 * half, 2 * half + 2):
            for side in range(2):
                for top in range(0, width, TILE):
                    tile = mm(low[top:top + TILE], slope[side, :, at * TILE:(at + 1) * TILE])
                    for row in range(0, TILE, per):
                        put(4 + at, side, (top + row) // per, tile[row:row + per])

    def out_weight():
        need("ctx")
        for side in range(2):
            tile = mm(ctx[side], one_buf[...])
            for dest in range(16):
                part = tile[dest * per // 2:(dest + 1) * per // 2]
                put(11, side, dest, jnp.concatenate([part[:, :cols], part[:, cols:]], axis=0))

    def context_grads():
        need("wo")
        for side in range(2):
            two_buf[:, side * cols:(side + 1) * cols] = mm_nt(one_buf[...], wo[side]).astype(bf16)

    def again():
        need("x", "wq_p")
        arrive(*flight["wq"])
        q[1] = (mm(three_buf[...], wq[1, 0]) + b_qv_ref[0:1]).astype(bf16)
        k[1] = mm(three_buf[...], wq[1, 1]).astype(bf16)
        v[1] = (mm(three_buf[...], wq[1, 2]) + b_qv_ref[1:2]).astype(bf16)

    def attend_back(side, groups):
        need("qkv")
        scale = HEAD_DIM ** (-0.5)
        for group in groups:
            at = slice(group * GROUP, (group + 1) * GROUP)
            one = same_block(segr_ref[:, pl.ds(pl.multiple_of(own_base + group * GROUP, GROUP), GROUP)])
            same = jnp.concatenate([one, one], axis=1)
            for pair in range(cols // PAIR):
                lanes = slice(pair * PAIR, (pair + 1) * PAIR)
                q_two = two_heads(q[side, at, lanes])
                dc_two = two_heads(two_buf[at, side * cols + pair * PAIR:side * cols + (pair + 1) * PAIR])
                k_pair, v_pair = k[side, at, lanes], v[side, at, lanes]
                scores = jnp.where(same, mm_nt(k_pair, q_two) * scale, masked_out)
                shifted = jnp.exp(scores - jnp.max(scores, axis=0, keepdims=True))
                probs = shifted / jnp.sum(shifted, axis=0, keepdims=True)
                prob_grad = mm_nt(v_pair, dc_two)
                score_grad = (
                    probs * (prob_grad - jnp.sum(prob_grad * probs, axis=0, keepdims=True))
                ).astype(bf16)
                deltas[side, 0, at, lanes] = (join_heads(mm_tn(score_grad, k_pair)) * scale).astype(bf16)
                deltas[side, 1, at, lanes] = (mm(score_grad, q_two) * scale).astype(bf16)
                deltas[side, 2, at, lanes] = mm(probs.astype(bf16), dc_two).astype(bf16)

    def qkv_weight(s):
        need("xt")
        for side in range(2):
            for top in range(0, width, TILE):
                tile = mm(xt[top:top + TILE], deltas[side, s])
                for at in range(0, TILE, per):
                    put(8 + s, side, (top + at) // per, tile[at:at + per])
            if s != 1:
                owner = mp + side - 2 * mp * side
                lanes = pl.ds(pl.multiple_of(owner * cols, 128), cols)
                sums[0, 6 + s // 2:7 + s // 2, lanes] = jnp.sum(deltas[side, s].astype(f32), axis=0, keepdims=True)

    def input_grads():
        need("wq_o", "wq_p")
        for at in range(0, width, 256):
            here = slice(at, at + 256)
            value = grad[:, here]
            for side in range(2):
                for s in range(3):
                    value = value + mm_nt(deltas[side, s], wq[side, s, here])
            three_buf[:, here] = value.astype(bf16)
        results.append(run.here(three_buf, own_rows(grad_in_any)))

    share = rows // PARTS

    def send_out(part):
        some = pl.ds(part * share, share)
        flight["out", part] = run.remote(out_any.at[some], out_other.at[some], near["x"])

    def send_inputs(part):
        some = pl.ds(pl.multiple_of(own_base + part * share, share), share)
        flight["inputs", part] = run.remote(
            three_buf.at[pl.ds(part * share, share)], grad_in_any.at[some], near["x"]
        )

    send_out(0)
    second_norm()
    back_weight(0)
    begin(0)
    begin(1)
    send_out(1)
    inner_grads(1)
    step(0, 1)
    back_weight(1)
    begin(2)
    begin(3)
    send_out(2)
    step(1, 1)
    inner_grads(0)
    in_weight(0)
    begin(4)
    begin(5)
    step(2, 1)
    send_out(3)
    step(3, 1)
    feed_back()
    step(5, 1)
    step(4, 1)
    step(0, 2)
    again()
    step(1, 2)
    first_norm_back()
    context_grads()
    in_weight(1)
    begin(6)
    begin(7)
    step(3, 2)
    step(0, 3)
    attend_back(1, (0, 1))
    step(2, 2)
    step(6, 1)
    attend_back(1, (2, 3))
    step(7, 1)
    step(1, 3)
    step(4, 2)
    attend_back(0, (2, 3))
    step(5, 2)
    step(3, 3)
    attend_back(0, (0, 1))
    step(2, 3)
    step(0, 4)
    qkv_weight(0)
    begin(8)
    qkv_weight(2)
    begin(10)
    sum_step(0)
    step(1, 4)
    qkv_weight(1)
    begin(9)
    step(8, 1)
    out_weight()
    begin(11)
    sum_step(1)
    step(7, 2)
    step(5, 3)
    step(10, 1)
    step(6, 2)
    step(9, 1)
    input_grads()
    sum_step(2)
    step(11, 1)
    step(4, 3)
    step(3, 4)
    step(2, 4)
    step(5, 4)
    step(0, 5)
    step(7, 3)
    step(8, 2)
    step(6, 3)
    step(10, 2)
    step(2, 5)
    send_inputs(0)
    step(4, 4)
    step(9, 2)
    sum_step(3)
    step(8, 3)
    step(3, 5)
    step(6, 4)
    step(5, 5)
    send_inputs(1)
    step(9, 3)
    sum_step(4)
    step(11, 2)
    send_inputs(2)
    send_inputs(3)
    step(8, 4)
    step(7, 4)
    step(6, 5)
    step(10, 3)
    step(9, 4)
    sum_step(5)
    total = sums[5]
    vectors = exact(total[0:8], pick(width, dp * per, per))
    o_gains[...] = vectors[0:2]
    o_shifts[...] = vectors[2:6]
    o_bqv[...] = exact(total[0:8], pick(width, mp * cols + dp * (per // 2), per // 2))[6:8]
    few = units // 16
    o_bin[...] = exact(sums[5, pl.ds(8 + 2 * mp + dp // 8, 1), :], pick(width, (dp % 8) * few, few))
    for source, target in ((o_gains, a_gains), (o_shifts, a_shifts), (o_bqv, a_bqv), (o_bin, a_bin)):
        results.append(run.here(source, target))
    step(8, 5)
    step(4, 5)
    step(11, 3)
    step(7, 5)
    step(10, 4)
    step(9, 5)
    step(11, 4)
    step(10, 5)
    for part in range(PARTS):
        arrive(flight["out", part], flight["inputs", part])
    for copy in run.sent[-run.ring:]:
        copy.wait_send()
    for copy in results:
        copy.wait()


def backward(segr, gains, first_grad, b_qv, *arrays):
    rows, width = arrays[3].shape
    units = arrays[8].shape[2]
    cols = arrays[12].shape[1]
    any_ = pl.BlockSpec(memory_space=pl.ANY)
    vmem = pl.BlockSpec(memory_space=pltpu.VMEM)
    S = jax.ShapeDtypeStruct
    per = width // 16
    count = len(ORDERS)
    small = [((2, per), f32), ((4, per), f32), ((2, cols // 16), f32), ((1, units // 16), f32)]
    scratch = small + [((rows, width), bf16)] * 3 + [
        ((rows, width), f32), ((rows, 128), f32), ((rows, width), f32), ((rows, 128), f32),
        ((2, units, rows), bf16), ((2, rows, units), bf16), ((width, rows), bf16), ((width, rows), bf16),
        ((2, cols, rows), bf16), ((2, rows, cols), bf16), ((2, rows, cols), bf16), ((2, rows, cols), bf16),
        ((2, units, width), bf16), ((2, width, units), bf16), ((2, cols, width), bf16), ((2, 3, width, cols), bf16),
        ((2, 3, rows, cols), bf16), ((count, 2, 16, per, TILE), bf16),
        ((count, 31, per, TILE), bf16), ((count, per, TILE), f32), ((6, 16, width), f32), ((5, 16, width), f32),
    ]
    return pl.pallas_call(
        backward_kernel,
        in_specs=[vmem] * 4 + [any_] * len(arrays),
        out_specs=[any_] * 10,
        out_shape=(
            S((2 * rows, width), bf16), S((rows, width), bf16), S((2 * per, width), f32), S((per, 2 * width), f32),
            S((3, per, cols), f32),
            S((cols // 16, width), f32), S((2, per), f32), S((4, per), f32), S((2, cols // 16), f32),
            S((1, units // 16), f32),
        ),
        scratch_shapes=[pltpu.VMEM(*s) for s in scratch] + [
            pltpu.SemaphoreType.DMA((24,)), pltpu.SemaphoreType.DMA((78,)), pltpu.SemaphoreType.DMA((42,)),
        ],
        compiler_params=pltpu.CompilerParams(
            vmem_limit_bytes=63 * 1024 * 1024, collective_id=1, has_side_effects=True
        ),
        name="backward",
    )(segr, gains, first_grad, b_qv, *arrays)


FINISH_PARTS = 4


def finish_kernel(*refs):
    grads_any, outs_any, others_any = refs[:3]
    count = (len(refs) - 8) // 3
    sources = refs[3:3 + count]
    wide_any, outs_to = refs[3 + count:5 + count]
    targets = refs[5 + count:5 + 2 * count]
    grads, wide, outs = refs[5 + 2 * count:8 + 2 * count]
    held = refs[8 + 2 * count:-2]
    load_sem, store_sem = refs[-2:]
    part = grads.shape[0] // FINISH_PARTS
    other = 1 - lax.axis_index("mp")
    loads, stores = [], []

    def copy(into, source, target, sem):
        into.append(pltpu.make_async_copy(source, target, sem.at[len(into)]))
        into[-1].start()

    def rows(ref, at):
        return ref.at[pl.ds(pl.multiple_of(at * part, part), part)]

    for at in range(FINISH_PARTS):
        copy(loads, rows(grads_any, at), rows(grads, at), load_sem)
    places = [2 * (1 - other), 2 * (1 - other) + 1, 2 * other, 2 * other + 1]
    for n, at in enumerate(places):
        copy(loads, rows((outs_any, others_any)[n // 2], n % 2), rows(outs, at), load_sem)
    for source, target in zip(sources, held):
        copy(loads, source, target, load_sem)
    for at in range(FINISH_PARTS):
        loads[at].wait()
        here = slice(at * part, (at + 1) * part)
        wide[here] = grads[here].astype(f32)
        copy(stores, rows(wide, at), rows(wide_any, at), store_sem)
    for n, at in enumerate(places):
        loads[FINISH_PARTS + n].wait()
        copy(stores, rows(outs, at), rows(outs_to, at), store_sem)
    for n in range(count):
        loads[2 * FINISH_PARTS + n].wait()
        copy(stores, held[n], targets[n], store_sem)
    for store in stores:
        store.wait()


def finish(grad_inputs, own_out, other_out, *arrays):
    any_ = pl.BlockSpec(memory_space=pl.ANY)
    results = (jax.ShapeDtypeStruct(grad_inputs.shape, f32), jax.ShapeDtypeStruct(grad_inputs.shape, bf16)) + tuple(
        jax.ShapeDtypeStruct(a.shape, a.dtype) for a in arrays
    )
    copies = 2 * FINISH_PARTS + len(arrays)
    return pl.pallas_call(
        finish_kernel,
        in_specs=[any_] * (3 + len(arrays)),
        out_specs=[any_] * len(results),
        out_shape=results,
        scratch_shapes=[
            pltpu.VMEM(grad_inputs.shape, bf16), pltpu.VMEM(grad_inputs.shape, f32), pltpu.VMEM(grad_inputs.shape, bf16),
        ] + [pltpu.VMEM(a.shape, a.dtype) for a in arrays] + [
            pltpu.SemaphoreType.DMA((copies,)), pltpu.SemaphoreType.DMA((copies,)),
        ],
        compiler_params=params(60),
        name="finish",
    )(grad_inputs, own_out, other_out, *arrays)


def swap_mp(values):
    return lax.ppermute(values, "mp", [(0, 1), (1, 0)])


def swap_dp(values, bit):
    size = lax.axis_size("dp")
    return lax.ppermute(values, "dp", [(at, at ^ bit) for at in range(size)])


def fetch(own, axis, place):
    size = own.shape[axis] // 4
    first = swap_mp(lax.dynamic_slice_in_dim(own, place * size, size, axis))
    second = swap_dp(first, 2)
    third = swap_dp(first, 1)
    fourth = swap_dp(second, 1)
    whole = jnp.zeros_like(own)
    for bits, part in ((0, first), (2, second), (1, third), (3, fourth)):
        whole = lax.dynamic_update_slice_in_dim(whole, part, (place ^ bits) * size, axis)
    return whole


def gather_rows(rows):
    size = lax.axis_size("dp")
    if size != 16:
        return lax.all_gather(rows, ("dp", "mp"), axis=0, tiled=True)
    rows = jnp.concatenate([rows, swap_mp(rows)], axis=0)
    for bit in (1, 2, 4, 8):
        rows = jnp.concatenate([rows, swap_dp(rows, bit)], axis=0)
    return rows


def both_halves(own, mp):
    other = swap_mp(own)
    return jnp.concatenate([jnp.where(mp == 0, own, other), jnp.where(mp == 0, other, own)], axis=0)


def add(a, b):
    return (a.astype(f32) + b.astype(f32)).astype(a.dtype)


def scatter_sum(keep, send, order):
    size = lax.axis_size("dp")
    if size != 16:
        rest = keep.shape[2:]
        both = jnp.stack([keep, send], axis=2)
        both = both.reshape((2, 16) + rest)
        mine = add(both[0], swap_mp(both[1]))
        return mine
    got = swap_dp(send, 1)
    rest = keep.shape[2:]
    names = ["x", "z1", "z0", "y"]
    keep = keep.reshape((2, 2, 2, 2) + rest)
    got = got.reshape((2, 2, 2, 2) + rest)
    bit_of = {"y": 2, "z0": 4, "z1": 8}
    for name in order:
        axis = names.index(name)
        names.remove(name)
        pick = lambda values, at: lax.index_in_dim(values, at, axis, keepdims=False)
        out = add(pick(keep, 1), pick(got, 1))
        out = swap_mp(out) if name == "x" else swap_dp(out, bit_of[name])
        keep = add(pick(keep, 0), pick(got, 0))
        got = out
    return add(keep, got)


def swap_order(values, axis, place):
    shape = values.shape
    split = values.reshape(shape[:axis] + (2, 2, 2, 2) + shape[axis + 1:])
    for at, bit in enumerate((8, 4, 2, 1)):
        low = lax.index_in_dim(split, 0, axis + at)
        high = lax.index_in_dim(split, 1, axis + at)
        flipped = jnp.concatenate([high, low], axis=axis + at)
        split = jnp.where((place & bit) != 0, flipped, split)
    return split.reshape(shape)


def shards(
    inputs, segment_ids, pair_index, w_qkv, bias_qv, w_out, w_in, bias_in, w_back,
    w_pool, norm_gains, shifts, logit_scale, out_grad,
):
    tok_rows, width = inputs.shape
    size = lax.axis_size("dp")
    dp, mp = lax.axis_index("dp"), lax.axis_index("mp")
    rows = tok_rows // 2
    blocks = rows // SEG_LEN
    place = dp % 4
    slots = 0 * dp
    pos = jnp.reshape(slots, (1,)).astype(jnp.int32)

    x = lax.dynamic_slice_in_dim(inputs, mp * rows, rows, 0)
    cot = lax.dynamic_slice_in_dim(out_grad, mp * rows, rows, 0)
    seg = lax.dynamic_slice_in_dim(segment_ids, mp * rows, rows, 0)
    segc, segr = seg.reshape(rows, 1), seg.reshape(1, rows)
    pairs = lax.dynamic_slice_in_dim(pair_index, mp * blocks, blocks, 0)

    cols = w_qkv.shape[2]
    units = w_in.shape[1]
    if size == 16:
        segr = segment_ids.reshape(1, -1)
        (
            own_out, w_qkv_p, w_out_p, w_in_p, w_back_p, q, k, v, n1, i1, lowt, xt, ctxt, actt, slope, n2, i2,
            loss_value, grad_scale, new_scale, first_grad, bias_qv_p, grad_pool, pool_bias,
        ) = forward(
            inputs, segr, w_qkv, bias_qv, bias_in.reshape(-1, 128),
            norm_gains, shifts, w_pool, logit_scale, pair_index, w_out, w_in, w_back,
        )
        results = backward(
            segr, norm_gains, first_grad, bias_qv_p, own_out,
            inputs, out_grad, n2, i2, n1, i1, actt, slope, lowt, xt, ctxt, q, k, v,
            w_back, w_back_p, w_in, w_in_p, w_out, w_out_p, w_qkv, w_qkv_p,
        )
        (
            grad_inputs, block_out, grad_back, grad_in, grad_qkv, grad_out, gains, shift_grads, grad_bias_qv,
            grad_bias_in, grad_pool, pool_bias,
        ) = finish(results[0], own_out, results[1], *results[2:], grad_pool, pool_bias)
        return (
            block_out, loss_value, grad_inputs, grad_qkv, grad_bias_qv, grad_out, grad_in,
            grad_bias_in[0], grad_back, grad_pool, gains, shift_grads, pool_bias[0], grad_scale, new_scale,
        )

    biases = swap_mp(bias_qv)
    bias_qv_p, bias_in_p = biases, swap_mp(bias_in)
    w_qkv_p = fetch(w_qkv, 1, place)
    w_out_p = fetch(w_out, 0, place)
    w_in_p = fetch(w_in, 0, place)
    w_back_p = fetch(w_back, 0, place)

    q_o, k_o, v_o, ctx_o = attention_half(x, w_qkv, bias_qv, segc, segr)
    q_p, k_p, v_p, ctx_p = attention_half(x, w_qkv_p, bias_qv_p, segc, segr)
    normed_one, inv_one, low_one = first_norm(ctx_o, ctx_p, w_out, w_out_p, x, norm_gains, shifts)
    act_o, slope_o = inner_half(low_one, w_in, bias_in.reshape(1, -1))
    part = branch_half(act_o, w_back)
    act_p, slope_p = inner_half(low_one, w_in_p, bias_in_p.reshape(1, -1))
    normed_two, inv_two, own_out = second_norm(act_p, w_back_p, part, normed_one, norm_gains, shifts)

    firsts = own_out.reshape(blocks, SEG_LEN, width)[:, 0]
    ids = jnp.broadcast_to(pairs.astype(f32)[:, None], (blocks, 128))
    rel = jnp.concatenate([gather_rows(firsts).astype(f32), gather_rows(ids)], axis=1)
    linear = dp * 2 + mp
    position = jnp.stack([linear if size == 16 else 0 * linear, linear]).astype(jnp.int32)
    loss_value, grad_scale, pre_all, pool_bias, first_grad, firsts_all = pair_loss(
        position, rel, w_pool, shifts[4:5], logit_scale
    )
    block_out = both_halves(own_out, mp)
    pool_rows = width // size
    grad_pool = lax.dot_general(
        lax.dynamic_slice_in_dim(firsts_all, dp * pool_rows, pool_rows, 1), pre_all, TN, preferred_element_type=f32
    )
    grad_pool_bias = lax.dynamic_slice_in_dim(pool_bias[0], dp * pool_rows, pool_rows, 0)

    grad_two, branch, sums_two = second_back(cot, first_grad, normed_two, inv_two, norm_gains)
    keep_bo, send_bo = back_weight(pos, act_o, branch)
    keep_bp, send_bp = back_weight(pos, act_p, branch)
    keep_io, send_io, bias_io, part_one = inner_back(pos, branch, w_back, slope_o, low_one, w_in, grad_two)
    keep_ip, send_ip, bias_ip, part_two = inner_back(pos, branch, w_back_p, slope_p, low_one, w_in_p, part_one)
    grad_one, sums_one, dc_o, dc_p, keep_w, send_w = first_back(
        pos, part_two, normed_one, inv_one, norm_gains, ctx_o, ctx_p, w_out, w_out_p
    )
    keep_qo, send_qo, bias_qo, in_one = attention_back(pos, x, w_qkv, segc, segr, q_o, k_o, v_o, dc_o, grad_one)
    keep_qp, send_qp, bias_qp, in_two = attention_back(pos, x, w_qkv_p, segc, segr, q_p, k_p, v_p, dc_p, in_one)

    both = lambda a, b: jnp.stack([a, b])
    mine_back = scatter_sum(both(keep_bo, keep_bp), both(send_bo, send_bp), ("x", "y", "z0", "z1"))
    mine_in = scatter_sum(both(keep_io, keep_ip), both(send_io, send_ip), ("y", "x", "z0", "z1"))
    mine_out = scatter_sum(keep_w, send_w, ("x", "y", "z0", "z1"))
    mine_qkv = scatter_sum(both(keep_qo, keep_qp), both(send_qo, send_qp), ("y", "x", "z0", "z1"))

    vectors = jnp.concatenate([sums_one[0:1], sums_two[0:1], sums_one[2:3], sums_one[1:2], sums_two[2:3], sums_two[1:2]])
    by_dp = vectors.reshape(6, 16, width // 16).transpose(1, 0, 2).reshape(16, -1)
    by_dp = jnp.broadcast_to(by_dp[None], (2,) + by_dp.shape)
    bias_q = both(bias_qo, bias_qp).reshape(2, 2, 16, cols // 16).transpose(0, 2, 1, 3).reshape(2, 16, -1)
    bias_i = both(bias_io, bias_ip).reshape(2, 16, units // 16)
    packed = jnp.concatenate([by_dp, bias_q, bias_i], axis=2)
    packed = swap_order(packed, 1, slots).reshape(2, 8, 2, -1)
    mine_small = scatter_sum(packed[:, :, 0], packed[:, :, 1], ("y", "x", "z0", "z1"))

    if size != 16:
        fold = lambda values: lax.psum_scatter(values, "dp", scatter_dimension=0, tiled=True)
        grad_back = fold(mine_back.reshape(units, width).astype(f32))
        grad_in = fold(mine_in.reshape(width, units).astype(f32))
        grad_qkv = fold(mine_qkv.transpose(0, 2, 1, 3).reshape(width, 3, cols).astype(f32)).transpose(1, 0, 2)
        small = mine_small
        n_vec = 6 * (width // 16)
        n_q = 2 * (cols // 16)
        n_i = units // 16
        vec = small[:, :n_vec].reshape(16, 6, -1).transpose(0, 2, 1).reshape(width, 6)
        vec = fold(vec).T
        grad_bias_qv = fold(small[:, n_vec:n_vec + n_q].reshape(16, 2, -1).transpose(0, 2, 1).reshape(cols, 2)).T
        grad_bias_in = fold(small[:, n_vec + n_q:n_vec + n_q + n_i].reshape(units))
        grad_out = fold(mine_out.reshape(cols, width).astype(f32))
    else:
        grad_back = mine_back.astype(f32)
        grad_in = mine_in.astype(f32)
        grad_qkv = mine_qkv.astype(f32)
        small = mine_small
        n_vec = 6 * (width // 16)
        n_q = 2 * (cols // 16)
        n_i = units // 16
        vec = small[:n_vec].reshape(6, -1)
        grad_bias_qv = small[n_vec:n_vec + n_q].reshape(2, -1)
        grad_bias_in = small[n_vec + n_q:n_vec + n_q + n_i]
        grad_out = mine_out.astype(f32)

    grad_inputs = both_halves(in_two.astype(bf16), mp).astype(f32)
    new_scale = logit_scale - step_rate * grad_scale
    return (
        block_out, loss_value, grad_inputs, grad_qkv, grad_bias_qv, grad_out, grad_in, grad_bias_in,
        grad_back, grad_pool, vec[:2], vec[2:], grad_pool_bias, grad_scale, new_scale,
    )


def solution(mesh):
    return jax.shard_map(
        shards,
        mesh=mesh,
        in_specs=(
            P("dp", None), P("dp"), P("dp"), P(None, None, "mp"), P(None, "mp"), P("mp", None), P(None, "mp"),
            P("mp"), P("mp", None), P(), P(), P(), P(), P("dp", None),
        ),
        out_specs=(
            P("dp", None), P(), P("dp", None), P(None, "dp", "mp"), P(None, ("mp", "dp")), P(("mp", "dp"), None),
            P("dp", "mp"), P(("mp", "dp")), P(("mp", "dp"), None), P("dp", None), P(None, "dp"), P(None, "dp"),
            P("dp"), P(), P(),
        ),
        check_vma=False,
    )
```
